32 devices in a mesh: blk: 4 (over y, x), seq: 8 (over z, core).
Axes of the slice: x: 2, y: 2, z: 4, core: 2. Of those that a mesh axis runs over, the one named last changes fastest.
Arguments:
- tokens: bfloat16 [16, 2048, 768], P('seq', 'blk'), may hold values from -6 to 6
- seq_len: int32 [16], P('seq'), may hold values from 1024 to 2048, as said below
- ln1_gain: bfloat16 [768], P(('blk', 'seq')), may hold values from 0.5 to 1.5
- ln1_shift: bfloat16 [768], P(('blk', 'seq')), may hold values from -2.5 to 2.5
- w_qkv: bfloat16 [768, 2304], P(('blk', 'seq')), may hold values from -0.21875 to 0.21875
- w_out: bfloat16 [768, 768], P(('blk', 'seq')), may hold values from -2.5 to 2.5
- ln2_gain: bfloat16 [768], P(('blk', 'seq')), may hold values from 0.5 to 1.5
- ln2_shift: bfloat16 [768], P(('blk', 'seq')), may hold values from -2.5 to 2.5
- w_up: bfloat16 [768, 3072], P(('blk', 'seq')), may hold values from -0.21875 to 0.21875
- w_down: bfloat16 [3072, 768], P(('blk', 'seq')), may hold values from -0.109375 to 0.109375
- cotangent: bfloat16 [16, 2048, 768], P('seq', 'blk'), may hold values from -6 to 6
Outputs:
- output: bfloat16 [16, 2048, 768], P('seq', 'blk')
- grad_tokens: float32 [16, 2048, 768], P('seq', 'blk')
- grad_ln1_gain: float32 [768], P(('blk', 'seq'))
- grad_ln1_shift: float32 [768], P(('blk', 'seq'))
- grad_w_qkv: float32 [768, 2304], P(('blk', 'seq'))
- grad_w_out: float32 [768, 768], P(('blk', 'seq'))
- grad_ln2_gain: float32 [768], P(('blk', 'seq'))
- grad_ln2_shift: float32 [768], P(('blk', 'seq'))
- grad_w_up: float32 [768, 3072], P(('blk', 'seq'))
- grad_w_down: float32 [3072, 768], P(('blk', 'seq'))
The draws below stay inside these ranges and needn't reach their ends.
Inputs may be any that keep to these rules, and one draw needn't show every extreme that they name: `seq_len`: positions at or beyond a sequence's length are padding; in every draw some sequence has exactly 2048 positions and some exactly 1024.
All inputs are finite; a program needn't handle non-finite values.
Results may differ from the reference program's by a relative error of at most 0.02.
Values may be sent and summed in bfloat16 or wider, within the bound.
A program may use at most 448 MiB of HBM per device.

```python
import jax
import jax.numpy as jnp
from jax import lax

D = 768
HEADS = 12
FF = 3072
TOK = 2048
SEQS = 16


def draw_seq_len(key, part):
    key = jax.random.fold_in(key, 11)
    key_group, key_short, key_first, key_second = jax.random.split(key, 4)
    long_group = jax.random.randint(key_group, (SEQS,), 0, 2)
    short_len = jax.random.randint(key_short, (SEQS,), TOK // 2, TOK)
    lengths = jnp.where(long_group == 1, TOK, short_len)
    first_pick = jax.random.randint(key_first, (), 0, SEQS)
    second_pick = (first_pick + 1 + jax.random.randint(key_second, (), 0, SEQS - 1)) % SEQS
    indices = jnp.arange(SEQS, dtype=jnp.int32)
    lengths = jnp.where(indices == first_pick, TOK, lengths)
    lengths = jnp.where(indices == second_pick, TOK // 2, lengths)
    return lengths.astype(jnp.int32)


def shard_levels(stream_key, extent, cuts, smallest, high):
    factor_of = 1.0
    for dim, shards_of in cuts:
        draws = jax.random.uniform(jax.random.fold_in(jax.random.fold_in(stream_key, 6), dim), (shards_of,), jnp.float32, smallest / len(cuts), high / len(cuts))
        factor_of = factor_of * jnp.repeat(jnp.exp(draws), extent[dim] // shards_of).reshape((-1,) + (1,) * (len(extent) - 1 - dim))
    return factor_of


def normal_values(rng, dims, scale, bound, cuts=(), kind=jnp.bfloat16):
    level = shard_levels(rng, dims, cuts, -0.22, 0.18) if cuts else 1.0
    entries = jax.random.normal(rng, dims, jnp.float32) * scale * level
    return jnp.minimum(jnp.maximum(entries, -bound), bound).astype(kind)


def setup_inputs(seed: int = 0) -> dict:
    streams_of = jax.random.split(jax.random.key(seed), 12)
    return {
        "tokens": normal_values(streams_of[0], (SEQS, TOK, D), 1.0, 6.0, ((0, 8), (1, 4))),
        "seq_len": draw_seq_len(jax.random.fold_in(streams_of[11], 71), 0),
        "ln1_gain": jnp.clip(1.0 + 0.1 * jax.random.normal(streams_of[2], (D,), jnp.float32), 0.5, 1.5).astype(jnp.bfloat16),
        "ln1_shift": normal_values(streams_of[3], (D,), 0.2, 2.5, ((0, 32),)),
        "w_qkv": normal_values(streams_of[4], (D, 3 * D), D ** -0.5, 0.21875, ((0, 32),)),
        "w_out": normal_values(streams_of[5], (D, D), (D // 128) ** -0.5, 2.5, ((0, 32),)),
        "ln2_gain": jnp.clip(1.0 + 0.1 * jax.random.normal(streams_of[6], (D,), jnp.float32), 0.5, 1.5).astype(jnp.bfloat16),
        "ln2_shift": normal_values(streams_of[7], (D,), 0.2, 2.5, ((0, 32),)),
        "w_up": normal_values(streams_of[8], (D, FF), D ** -0.5, 0.21875, ((0, 32),)),
        "w_down": normal_values(streams_of[9], (FF, D), FF ** -0.5, 0.109375, ((0, 32),)),
        "cotangent": normal_values(streams_of[10], (SEQS, TOK, D), 1.0, 6.0, ((0, 8), (1, 4))),
    }


@jax.custom_vjp
def low(v):
    return lax.optimization_barrier(v.astype(jnp.bfloat16)).astype(jnp.float32)

@jax.custom_vjp
def low_back(v):
    return v

def low_keep(v):
    return (low(v), None)

def low_pass(kept, grad):
    return (grad,)

def back_keep(v):
    return (v, None)

def back_low(kept, grad):
    return (low(grad),)
low.defvjp(low_keep, low_pass)
low_back.defvjp(back_keep, back_low)

def matmul(left, right):
    return jnp.dot(left, right, precision=lax.Precision.HIGHEST)

def normalize(values, gain, shift):
    center = lax.optimization_barrier(jnp.mean(values, axis=-1, keepdims=True))
    offsets = values - center
    spread = lax.optimization_barrier(jnp.mean(offsets * offsets, axis=-1, keepdims=True))
    return offsets * lax.rsqrt(spread + 1e-05) * gain + shift

def signed_attention(queries, key_vecs, val_vecs):
    length = queries.shape[0]
    tile_rows = min(512, length)
    positions = jnp.arange(length, dtype=jnp.int32)

    def one_block(block_id):
        first_row = (block_id * tile_rows).astype(jnp.int32)
        query_rows = lax.dynamic_slice_in_dim(queries, first_row, tile_rows, 0)
        scores = low_back(jnp.einsum('qhd,khd->hqk', query_rows, key_vecs, precision=lax.Precision.HIGHEST) * 0.125)
        row_pos = first_row + jnp.arange(tile_rows, dtype=jnp.int32)
        allowed = positions[None, :] <= row_pos[:, None]
        soft_mag = jnp.sqrt(scores * scores + 1.0)
        soft_sign = scores / soft_mag
        magnitude = jnp.where(allowed, soft_mag, -1e+30)
        row_peak = lax.optimization_barrier(jnp.max(magnitude, axis=-1, keepdims=True))
        weights = jnp.where(allowed, jnp.exp(magnitude - row_peak), 0.0)
        normed_weights = weights / lax.optimization_barrier(jnp.sum(weights, axis=-1, keepdims=True))
        signed = low(normed_weights * soft_sign)
        return jnp.einsum('hqk,khd->qhd', signed, val_vecs, precision=lax.Precision.HIGHEST)
    outputs = lax.map(jax.checkpoint(one_block), jnp.arange(length // tile_rows, dtype=jnp.int32))
    return outputs.reshape(length, -1)

def sequence_layer(inputs, live_rows, ln1_gain, ln1_shift, w_qkv, w_out, ln2_gain, ln2_shift, w_up, w_down):
    model_width = inputs.shape[1]
    normed_one = low(normalize(inputs, ln1_gain, ln1_shift))
    projected = matmul(normed_one, w_qkv)
    queries = low_back(low(projected[:, :model_width]))
    key_vecs = low_back(low(projected[:, model_width:2 * model_width]))
    val_vecs = low_back(low(projected[:, 2 * model_width:]))
    shaped = (inputs.shape[0], HEADS, model_width // HEADS)
    attended = signed_attention(queries.reshape(shaped), key_vecs.reshape(shaped), val_vecs.reshape(shaped))
    attended = low_back(low(attended))
    branch = low_back(matmul(attended, w_out)) * live_rows
    middle = inputs + branch
    normed_two = low(normalize(middle, ln2_gain, ln2_shift))
    hidden_pre = low_back(matmul(normed_two, w_up))
    hidden = low(jax.nn.gelu(hidden_pre, approximate=True))
    return middle + low_back(matmul(hidden, w_down))

def reference(tokens, seq_len, ln1_gain, ln1_shift, w_qkv, w_out, ln2_gain, ln2_shift, w_up, w_down, cotangent):
    params = tuple((weight_arg.astype(jnp.float32) for weight_arg in (ln1_gain, ln1_shift, w_qkv, w_out, ln2_gain, ln2_shift, w_up, w_down)))
    positions = jnp.arange(TOK, dtype=jnp.int32)

    def per_sequence(totals, packed):
        inputs, length, grad_top = packed
        live_rows = (positions < length.astype(jnp.int32)).astype(jnp.float32)[:, None]

        def layer_fn(values, *weight_all):
            return sequence_layer(values, live_rows, *weight_all)
        result, pullback = jax.vjp(layer_fn, inputs.astype(jnp.float32), *params)
        grads = pullback(grad_top.astype(jnp.float32))
        totals = tuple((running + update for running, update in zip(totals, grads[1:])))
        return (totals, (result.astype(jnp.bfloat16), grads[0]))
    start_sums = tuple((jnp.zeros_like(weight_arg) for weight_arg in params))
    totals, (outputs, input_grads) = lax.scan(per_sequence, start_sums, (tokens, seq_len, cotangent))
    return (outputs, input_grads, totals[0], totals[1], totals[2], totals[3], totals[4], totals[5], totals[6], totals[7])
```

```python
import functools

import jax
import jax.numpy as jnp
from jax import lax
from jax.experimental import pallas as pl
from jax.experimental.pallas import tpu as pltpu
from jax.sharding import PartitionSpec as P

HEADS = 12
VMEM_LIMIT = 60 * 2**20


def dot_nt(left, right):
    return lax.dot_general(left, right, (((1,), (1,)), ((), ())), preferred_element_type=jnp.float32)


def dot_nn(left, right):
    return lax.dot_general(left, right, (((1,), (0,)), ((), ())), preferred_element_type=jnp.float32)


def split_heads(dst, src):
    low = lax.broadcasted_iota(jnp.int32, src.shape, 1) < 64
    dst[0] = jnp.where(low, src, jnp.zeros_like(src))
    dst[1] = jnp.where(low, jnp.zeros_like(src), src)


def causal(bk, bq, kj, qi):
    kpos = kj * bk + lax.broadcasted_iota(jnp.int32, (bk, bq), 0)
    qpos = qi * bq + lax.broadcasted_iota(jnp.int32, (bk, bq), 1)
    return kpos <= qpos


def fwd_kernel(bq, bk, q_ref, k_ref, v_ref, att_ref, lse_ref, kh, vt):
    length = q_ref.shape[0]
    split_heads(kh, k_ref[...])
    vt[...] = v_ref[...].astype(jnp.float32).T.astype(jnp.bfloat16)
    ratio = bq // bk

    def q_step(qi, _):
        q_rows = q_ref[pl.ds(pl.multiple_of(qi * bq, bq), bq), :]

        def one(kj, state, masked):
            at = pl.ds(pl.multiple_of(kj * bk, bk), bk)
            out = []
            for h in range(2):
                peak, total, acc = state[3 * h : 3 * h + 3]
                s = dot_nt(kh[h, at, :], q_rows)
                u = s * s + 1.0
                inv = lax.rsqrt(u)
                mag = u * inv
                if masked:
                    mag = jnp.where(causal(bk, bq, kj, qi), mag, -1e30)
                new = jnp.maximum(peak, jnp.max(mag, axis=0, keepdims=True))
                p = jnp.exp(mag - new)
                alpha = jnp.exp(peak - new)
                total = total * alpha + jnp.sum(p, axis=0, keepdims=True)
                signed = (p * (s * inv)).astype(jnp.bfloat16)
                acc = acc * alpha + dot_nn(vt[64 * h : 64 * h + 64, at], signed)
                out += [new, total, acc]
            return tuple(out)

        zero = (
            jnp.full((1, bq), -1e30, jnp.float32),
            jnp.zeros((1, bq), jnp.float32),
            jnp.zeros((64, bq), jnp.float32),
        )
        state = zero + zero
        for r in range(ratio):
            state = one(qi * ratio + r, state, True)
        state = lax.fori_loop(0, qi * ratio, lambda kj, st: one(kj, st, False), state)
        rows = pl.ds(pl.multiple_of(qi * bq, bq), bq)
        both = []
        for h in range(2):
            peak, total, acc = state[3 * h : 3 * h + 3]
            both.append(acc / total)
            lse_ref[0, h : h + 1, rows] = peak + jnp.log(total)
        att_ref[rows, :] = jnp.concatenate(both, 0).T.astype(jnp.bfloat16)
        return 0

    lax.fori_loop(0, length // bq, q_step, 0)


def attend(qkv, bq=256, bk=256):
    length, width = qkv.shape
    pairs = width // 384
    return pl.pallas_call(
        functools.partial(fwd_kernel, bq, bk),
        grid=(pairs,),
        out_shape=(
            jax.ShapeDtypeStruct((length, 128 * pairs), jnp.bfloat16),
            jax.ShapeDtypeStruct((pairs, 8, length), jnp.float32),
        ),
        in_specs=[pl.BlockSpec((length, 128), lambda p, n=n: (0, n * pairs + p)) for n in range(3)],
        out_specs=(
            pl.BlockSpec((length, 128), lambda p: (0, p)),
            pl.BlockSpec((1, 8, length), lambda p: (p, 0, 0)),
        ),
        scratch_shapes=[
            pltpu.VMEM((2, length, 128), jnp.bfloat16),
            pltpu.VMEM((128, length), jnp.bfloat16),
        ],
        compiler_params=pltpu.CompilerParams(vmem_limit_bytes=VMEM_LIMIT),
    )(qkv, qkv, qkv)


def bwd_kernel(bq, bk, pairs, q_ref, k_ref, v_ref, g_ref, att_ref, lse_ref, out_ref, kh, vh, qh, gh, kt, delta, dqt, dk, dv):
    pair = pl.program_id(0)
    length = q_ref.shape[0]
    width = 128 * pairs
    split_heads(kh, k_ref[...])
    split_heads(vh, v_ref[...])
    split_heads(qh, q_ref[...])
    split_heads(gh, g_ref[...])
    kt[...] = k_ref[...].astype(jnp.float32).T.astype(jnp.bfloat16)
    prod = (g_ref[...].astype(jnp.float32) * att_ref[...].astype(jnp.float32)).T
    delta[0:1, :] = jnp.sum(prod[:64], axis=0, keepdims=True)
    delta[1:2, :] = jnp.sum(prod[64:], axis=0, keepdims=True)
    dqt[...] = jnp.zeros_like(dqt)

    def k_step(kj, _):
        at = pl.ds(pl.multiple_of(kj * bk, bk), bk)

        def one(qi, masked):
            rows = pl.ds(pl.multiple_of(qi * bq, bq), bq)
            q_rows = q_ref[rows, :]
            g_rows = g_ref[rows, :]
            add_k = add_v = None
            for h in range(2):
                s = dot_nt(kh[h, at, :], q_rows)
                dp = dot_nt(vh[h, at, :], g_rows)
                u = s * s + 1.0
                inv = lax.rsqrt(u)
                arg = u * inv - lse_ref[0, h : h + 1, rows]
                if masked:
                    arg = jnp.where(causal(bk, bq, kj, qi), arg, -1e30)
                p = jnp.exp(arg)
                sgn = s * inv
                t = inv * inv * (inv - 1.0) + 1.0
                ds = (p * (dp * t - sgn * delta[h : h + 1, rows])).astype(jnp.bfloat16)
                signed = (p * sgn).astype(jnp.bfloat16)
                one_v = dot_nn(signed, gh[h, rows, :])
                one_k = dot_nn(ds, qh[h, rows, :])
                add_v = one_v if h == 0 else add_v + one_v
                add_k = one_k if h == 0 else add_k + one_k
                dqt[64 * h : 64 * h + 64, rows] += dot_nn(kt[64 * h : 64 * h + 64, at], ds)
            return add_k, add_v

        first = one(kj, True)
        dk[...], dv[...] = first

        def more(qi, _):
            add_k, add_v = one(qi, False)
            dk[...] += add_k
            dv[...] += add_v
            return 0

        lax.fori_loop(kj + 1, length // bq, more, 0)
        out_ref[at, pl.ds(pl.multiple_of(width + pair * 128, 128), 128)] = dk[...].astype(jnp.bfloat16)
        out_ref[at, pl.ds(pl.multiple_of(2 * width + pair * 128, 128), 128)] = dv[...].astype(jnp.bfloat16)
        return 0

    lax.fori_loop(0, length // bk, k_step, 0)
    out_ref[:, pl.ds(pl.multiple_of(pair * 128, 128), 128)] = (dqt[...] * 0.125).T.astype(jnp.bfloat16)


def attend_back(qkv, g_att, att, lse, bq=256, bk=256):
    length, width = qkv.shape
    pairs = width // 384
    return pl.pallas_call(
        functools.partial(bwd_kernel, bq, bk, pairs),
        grid=(pairs,),
        out_shape=jax.ShapeDtypeStruct((length, width), jnp.bfloat16),
        in_specs=[pl.BlockSpec((length, 128), lambda p, n=n: (0, n * pairs + p)) for n in range(3)]
        + [pl.BlockSpec((length, 128), lambda p: (0, p))] * 2
        + [pl.BlockSpec((1, 8, length), lambda p: (p, 0, 0))],
        out_specs=pl.BlockSpec((length, width), lambda p: (0, 0)),
        scratch_shapes=[pltpu.VMEM((2, length, 128), jnp.bfloat16)] * 4
        + [
            pltpu.VMEM((128, length), jnp.bfloat16),
            pltpu.VMEM((8, length), jnp.float32),
            pltpu.VMEM((128, length), jnp.float32),
            pltpu.VMEM((bk, 128), jnp.float32),
            pltpu.VMEM((bk, 128), jnp.float32),
        ],
        compiler_params=pltpu.CompilerParams(vmem_limit_bytes=VMEM_LIMIT),
    )(qkv, qkv, qkv, g_att, att, lse)


MESH = pl.DeviceIdType.MESH


class Place:
    def __init__(self, blocks, lanes, seqs):
        self.blocks, self.depth, self.seqs = blocks, lanes // 2, seqs
        self.share = blocks // seqs
        self.bits = max(1, blocks.bit_length() - 1)
        self.blk = lax.axis_index("blk")
        lane = lax.axis_index("seq")
        self.z, self.core = lane // 2, lane % 2
        flat = self.blk * 2 + self.core
        self.seq, self.part = flat // self.share, flat % self.share

    def at(self, blk, z, core):
        return (blk, z * 2 + core)

    def bit(self, part, step):
        return 1 << ((part + step) % self.bits)


def greet(devices):
    barrier = pltpu.get_barrier_semaphore()
    for device in devices:
        pl.semaphore_signal(barrier, inc=1, device_id=device, device_id_type=MESH)
    pl.semaphore_wait(barrier, len(devices))


def send(src, dst, send_sem, recv_sem, device):
    copy = pltpu.make_async_remote_copy(
        src_ref=src, dst_ref=dst, send_sem=send_sem, recv_sem=recv_sem, device_id=device, device_id_type=MESH
    )
    copy.start()
    return copy


def arrived(ref, sem):
    pltpu.make_async_copy(ref, ref, sem).wait()


def gather_kernel(sizes, shapes, *refs):
    place = Place(*sizes)
    blocks, depth, seqs, share, bits = place.blocks, place.depth, place.seqs, place.share, place.bits
    count = len(shapes)
    tok, cot = refs[0], refs[1]
    shards = refs[2 : 2 + count]
    refs = refs[2 + count :]
    tok_all, cot_own = refs[0], refs[1]
    fulls = refs[2 : 2 + count]
    cols = refs[2 + count]
    tok_s, tok_r, near_s, near_r, cot_s, cot_r, z_s, z_r, b_s, b_r, c_s, c_r, loc = refs[3 + count :]
    blk, z, core, seq, part = place.blk, place.z, place.core, place.seq, place.part
    per_seq = share // 2
    per_part = blocks // share
    sibling = place.at(blk, z, 1 - core)
    peers = [place.at(blk, lax.rem(z + k, depth), core) for k in range(1, depth)]
    for m in range(1, blocks):
        peers += [place.at(blk ^ m, z, 0), place.at(blk ^ m, z, 1)]
    greet(peers + [sibling])

    copies = []
    local = []
    home_core = seq // seqs
    for i in range(seqs):
        for h in range(per_seq):
            target = (core * seqs + i) * per_seq + h

            def away(i=i, h=h, target=target):
                send(tok.at[i], tok_all.at[blk], tok_s.at[i * per_seq + h], tok_r.at[blk], place.at(target, z, core))

            def here(i=i):
                pltpu.make_async_copy(tok.at[i], tok_all.at[blk], loc.at[0]).start()

            pl.when(target != blk)(away)
            pl.when(target == blk)(here)
    for a in range(count):
        full, shard = fulls[a], shards[a]
        for k in range(1, depth):
            copies.append(
                send(shard, full.at[blk, z, core], z_s.at[a, k - 1], z_r.at[a, k - 1], place.at(blk, lax.rem(z + k, depth), core))
            )
        own = pltpu.make_async_copy(shard, full.at[blk, z, core], loc.at[1 + a])
        own.start()
        local.append(own)

    def level(k):
        return lax.rem(z + depth - k, depth)

    def spans(k):
        masks, out, seen = [0], [], 0
        for t in range(bits):
            bit = place.bit(k, t)
            out.append((bit, list(masks), seen))
            seen += len(masks)
            masks += [m ^ bit for m in masks]
        return out

    def forward(a, k, t):
        bit, masks, seen = spans(k)[t]
        for n, m in enumerate(masks):
            src = shards[a] if (m == 0 and k == 0) else fulls[a].at[blk ^ m, level(k), core]
            copies.append(
                send(
                    src,
                    fulls[a].at[blk ^ m, level(k), core],
                    b_s.at[a, k, seen + n],
                    b_r.at[a, k, seen + n],
                    place.at(blk ^ bit, z, core),
                )
            )

    def received(a, k, t):
        bit, masks, seen = spans(k)[t]
        for n, m in enumerate(masks):
            arrived(fulls[a].at[blk ^ bit ^ m, level(k), core], b_r.at[a, k, seen + n])

    for a in range(count):
        forward(a, 0, 0)
    for i in range(seqs):
        owner = (core * seqs + i) * share + blk // per_part
        slot = lax.rem(blk, per_part)

        def away(i=i, owner=owner, slot=slot):
            send(cot.at[i], cot_own.at[slot], cot_s.at[i], cot_r.at[slot], place.at(owner // 2, z, owner % 2))

        def here(i=i, slot=slot):
            pltpu.make_async_copy(cot.at[i], cot_own.at[slot], loc.at[1 + count]).start()

        pl.when(owner != blk * 2 + core)(away)
        pl.when(owner == blk * 2 + core)(here)

    for a in range(count):
        for k in range(1, depth):
            arrived(fulls[a].at[blk, level(k), core], z_r.at[a, k - 1])
            forward(a, k, 0)
    @pl.when(core == home_core)
    def _():
        for p in range(blocks):
            @pl.when(p != blk)
            def _():
                arrived(tok_all.at[p], tok_r.at[p])

            @pl.when(p == blk)
            def _():
                arrived(tok_all.at[p], loc.at[0])

            send(tok_all.at[p], tok_all.at[p], near_s.at[p], near_r.at[p], sibling)
        for p in range(blocks):
            arrived(tok_all.at[p], near_s.at[p])

    @pl.when(core != home_core)
    def _():
        for p in range(blocks):
            arrived(tok_all.at[p], near_r.at[p])

    for own in local:
        own.wait()
    group = lax.rem(blk * 2 + 1 - core, share)
    for a in range(count):
        for t in range(bits):
            for k in range(depth):
                received(a, k, t)
                if t + 1 < bits:
                    forward(a, k, t + 1)
                elif a == 0:
                    copies.append(
                        send(
                            fulls[0].at[:, level(k), core, group],
                            cols.at[:, level(k), core],
                            c_s.at[a, k],
                            c_r.at[a, k],
                            sibling,
                        )
                    )
                    keep = pltpu.make_async_copy(
                        fulls[0].at[:, level(k), core, part], cols.at[:, level(k), core], loc.at[2 + count + k]
                    )
                    keep.start()
                    local.append(keep)
                else:
                    held = fulls[a].at[:, level(k), core]
                    copies.append(send(held, held, c_s.at[a, k], c_r.at[a, k], sibling))
    for a in range(count):
        for k in range(depth):
            if a == 0:
                arrived(cols.at[:, level(k), 1 - core], c_r.at[a, k])
            else:
                arrived(fulls[a].at[:, level(k), 1 - core], c_r.at[a, k])
    for keep in local[count:]:
        keep.wait()
    for copy in copies:
        copy.wait_send()
    for i in range(seqs):
        for h in range(per_seq):
            target = (core * seqs + i) * per_seq + h

            @pl.when(target != blk)
            def _(i=i, h=h):
                arrived(tok.at[i], tok_s.at[i * per_seq + h])

            @pl.when((target == blk) & (core != home_core))
            def _():
                arrived(tok_all.at[blk], loc.at[0])

        owner = (core * seqs + i) * share + blk // per_part

        @pl.when(owner != blk * 2 + core)
        def _(i=i):
            arrived(cot.at[i], cot_s.at[i])

    for t in range(per_part):
        source = part * per_part + t
        mine = (source == blk) & (home_core == core)

        @pl.when(mine)
        def _(t=t):
            arrived(cot_own.at[t], loc.at[1 + count])

        @pl.when(jnp.logical_not(mine))
        def _(t=t):
            arrived(cot_own.at[t], cot_r.at[t])


def gather(sizes, tok, cot, shards):
    blocks, lanes, seqs = sizes
    depth, share = lanes // 2, blocks // seqs
    count = len(shards)
    rows, width = tok.shape[1:]
    any_space = pl.BlockSpec(memory_space=pl.ANY)
    outs = [
        jax.ShapeDtypeStruct((blocks, rows, width), tok.dtype),
        jax.ShapeDtypeStruct((blocks // share, rows, width), cot.dtype),
    ]
    outs += [jax.ShapeDtypeStruct((blocks, depth, 2) + s.shape, s.dtype) for s in shards]
    outs += [jax.ShapeDtypeStruct((blocks, depth, 2) + shards[0].shape[1:], shards[0].dtype)]
    sem = pltpu.SemaphoreType.DMA
    return pl.pallas_call(
        functools.partial(gather_kernel, sizes, [s.shape for s in shards]),
        out_shape=outs,
        in_specs=[any_space] * (2 + count),
        out_specs=[any_space] * len(outs),
        scratch_shapes=[
            sem((seqs * share // 2,)),
            sem((blocks,)),
            sem((blocks,)),
            sem((blocks,)),
            sem((seqs,)),
            sem((blocks // share,)),
            sem((count, depth - 1)),
            sem((count, depth - 1)),
            sem((count, depth, blocks - 1)),
            sem((count, depth, blocks - 1)),
            sem((count, depth)),
            sem((count, depth)),
            sem((2 + count + depth,)),
        ],
        compiler_params=pltpu.CompilerParams(collective_id=0, has_side_effects=True, vmem_limit_bytes=VMEM_LIMIT),
    )(tok, cot, *shards)


def reduce_kernel(sizes, kinds, moves, *refs):
    place = Place(*sizes)
    blocks, depth, seqs, share, bits = place.blocks, place.depth, place.seqs, place.share, place.bits
    blk, z, core, seq, part = place.blk, place.z, place.core, place.seq, place.part
    count = len(kinds)
    per_part = blocks // share
    grads, refs = refs[:count], refs[count:]
    rows_in, refs = refs[:moves], refs[moves:]
    sums, refs = refs[:count], refs[count:]
    rows_out, refs = refs[:moves], refs[moves:]
    held, refs = refs[:count], refs[count:]
    near, refs = refs[:count], refs[count:]
    wide, refs = refs[:count], refs[count:]
    tall, refs = refs[:count], refs[count:]
    m_s, m_r, z_s, z_r, b_s, b_r, c_s, c_r, loc = refs
    sibling = place.at(blk, z, 1 - core)
    peers = [place.at(blk, lax.rem(z + k, depth), core) for k in range(1, depth)]
    for m in range(1, blocks):
        peers += [place.at(blk ^ m, z, 0), place.at(blk ^ m, z, 1)]
    greet(peers + [sibling])
    order = list(range(1, depth)) + [0]
    copies, local = [], {}

    def level(k):
        return lax.rem(z + k, depth)

    other = lax.rem(blk * 2 + 1 - core, share)
    for a in range(count):
        if kinds[a] == "columns" and share > 2:
            for g in range(share):

                @pl.when((g != part) & (g != other))
                def _(a=a, g=g):
                    held[a][:, :, g] = jnp.zeros(held[a].shape[:2] + held[a].shape[3:], held[a].dtype)

    for a in range(count):
        for k in order:
            if kinds[a] == "columns":
                mine = held[a].at[:, level(k), part]
                there = held[a].at[:, level(k), part]
            else:
                mine = held[a].at[:, level(k)]
                there = near[a].at[:, level(k)]
            copies.append(send(grads[a].at[:, level(k), 1 - core], there, c_s.at[a, k], c_r.at[a, k], sibling))
            keep = pltpu.make_async_copy(grads[a].at[:, level(k), core], mine, loc.at[a, k])
            keep.start()
            local[a, k] = keep
    for j in range(moves):
        for t in range(per_part):
            source = part * per_part + t
            mine = (source == blk) & (seq // seqs == core)

            @pl.when(mine)
            def _(j=j, t=t):
                pltpu.make_async_copy(rows_in[j].at[t], rows_out[j].at[lax.rem(seq, seqs)], loc.at[count, j]).start()

            @pl.when(jnp.logical_not(mine))
            def _(j=j, t=t, source=source):
                slot = lax.rem(seq, seqs)
                send(rows_in[j].at[t], rows_out[j].at[slot], m_s.at[j, t], m_r.at[j, slot], place.at(source, z, seq // seqs))

    def spans(k):
        out, seen = [], 0
        for t in range(bits):
            bit = place.bit(k, t)
            later = [place.bit(k, u) for u in range(t + 1, bits)]
            masks = [0]
            for other in later:
                masks += [m ^ other for m in masks]
            out.append((bit, masks, seen))
            seen += len(masks)
        return out

    def add(into, first, second):
        total = first[...].astype(jnp.float32) + second[...].astype(jnp.float32)
        into[...] = total.astype(into.dtype)

    def forward(a, k, t):
        bit, masks, seen = spans(k)[t]
        for n, m in enumerate(masks):
            copies.append(
                send(
                    held[a].at[blk ^ bit ^ m, level(k)],
                    wide[a].at[k, seen + n],
                    b_s.at[a, k, seen + n],
                    b_r.at[a, k, seen + n],
                    place.at(blk ^ bit, z, core),
                )
            )

    def received(a, k, t):
        bit, masks, seen = spans(k)[t]
        for n, m in enumerate(masks):
            arrived(wide[a].at[k, seen + n], b_r.at[a, k, seen + n])
            mine = held[a].at[blk ^ m, level(k)]
            add(mine, mine, wide[a].at[k, seen + n])

    for a in range(count):
        for k in order:
            local[a, k].wait()
            if kinds[a] == "columns":
                arrived(held[a].at[:, level(k), other], c_r.at[a, k])
            else:
                arrived(near[a].at[:, level(k)], c_r.at[a, k])

                def one(b, _):
                    mine = held[a].at[b, level(k)]
                    add(mine, mine, near[a].at[b, level(k)])
                    return 0

                lax.fori_loop(0, blocks, one, 0)
            forward(a, k, 0)
    for a in range(count):
        for t in range(bits):
            for k in order:
                received(a, k, t)
                if t + 1 < bits:
                    forward(a, k, t + 1)
                elif k > 0:
                    copies.append(
                        send(
                            held[a].at[blk, level(k)],
                            tall[a].at[k - 1],
                            z_s.at[a, k - 1],
                            z_r.at[a, k - 1],
                            place.at(blk, level(k), core),
                        )
                    )
    for a in range(count):
        total = held[a][blk, z].astype(jnp.float32)
        for k in range(1, depth):
            arrived(tall[a].at[k - 1], z_r.at[a, k - 1])
            total = total + tall[a][k - 1].astype(jnp.float32)
        sums[a][...] = total
    for copy in copies:
        copy.wait_send()
    for j in range(moves):
        for t in range(per_part):
            source = part * per_part + t
            mine = (source == blk) & (seq // seqs == core)

            @pl.when(mine)
            def _(j=j, t=t):
                arrived(rows_in[j].at[t], loc.at[count, j])

            @pl.when(jnp.logical_not(mine))
            def _(j=j, t=t):
                arrived(rows_in[j].at[t], m_s.at[j, t])

        for i in range(seqs):
            owner = (core * seqs + i) * share + blk // per_part

            @pl.when(owner != blk * 2 + core)
            def _(j=j, i=i):
                arrived(rows_out[j].at[i], m_r.at[j, i])


def reduce(sizes, grads, kinds, rows, cid):
    blocks, lanes, seqs = sizes
    depth, share = lanes // 2, blocks // seqs
    count, moves = len(grads), len(rows)
    any_space = pl.BlockSpec(memory_space=pl.ANY)
    in_vmem = pl.BlockSpec(memory_space=pltpu.VMEM)
    chunks = [((share,) if kind == "columns" else ()) + g.shape[3:] for g, kind in zip(grads, kinds)]
    types = [g.dtype for g in grads]
    sem = pltpu.SemaphoreType.DMA
    out = [jax.ShapeDtypeStruct(c, jnp.float32) for c in chunks]
    out += [jax.ShapeDtypeStruct((seqs,) + r.shape[1:], r.dtype) for r in rows]
    return pl.pallas_call(
        functools.partial(reduce_kernel, sizes, kinds, moves),
        out_shape=out,
        in_specs=[any_space] * (count + moves),
        out_specs=[in_vmem] * count + [any_space] * moves,
        scratch_shapes=[pltpu.VMEM((blocks, depth) + c, t) for c, t in zip(chunks, types)]
        + [
            pltpu.VMEM((1, 1, 8, 128) if kind == "columns" else (blocks, depth) + c, t)
            for c, t, kind in zip(chunks, types, kinds)
        ]
        + [pltpu.VMEM((depth, blocks - 1) + c, t) for c, t in zip(chunks, types)]
        + [pltpu.VMEM((depth - 1,) + c, t) for c, t in zip(chunks, types)]
        + [
            sem((max(1, moves), blocks // share)),
            sem((max(1, moves), seqs)),
            sem((count, depth - 1)),
            sem((count, depth - 1)),
            sem((count, depth, blocks - 1)),
            sem((count, depth, blocks - 1)),
            sem((count, depth)),
            sem((count, depth)),
            sem((count + 1, max(depth, moves))),
        ],
        compiler_params=pltpu.CompilerParams(collective_id=cid, has_side_effects=True, vmem_limit_bytes=VMEM_LIMIT),
    )(*grads, *rows)


def normalize(values, gain, shift):
    center = jnp.mean(values, axis=-1, keepdims=True)
    offsets = values - center
    spread = jnp.mean(offsets * offsets, axis=-1, keepdims=True)
    return offsets * lax.rsqrt(spread + 1e-05) * gain + shift


def dot(left, right, at_left, at_right):
    return lax.dot_general(left, right, (((at_left,), (at_right,)), ((), ())), preferred_element_type=jnp.float32)


def swap(values, share, blocks, lanes, part):
    flat = blocks * lanes

    def number(blk, z, core):
        return blk * lanes + z * 2 + core

    pieces = [lax.dynamic_index_in_dim(values, part, 0, False)]
    for step in range(1, share):
        pairs = []
        for blk in range(blocks):
            for z in range(lanes // 2):
                for core in range(2):
                    other = (blk * 2 + core) ^ step
                    pairs.append((number(blk, z, core), number(other // 2, z, other % 2)))
        piece = lax.dynamic_index_in_dim(values, part ^ step, 0, False)
        pieces.append(lax.ppermute(piece, ("blk", "seq"), pairs))
    ordered = []
    for g in range(share):
        got = pieces[0]
        for step in range(1, share):
            got = jnp.where((part ^ step) == g, pieces[step], got)
        ordered.append(got)
    return ordered


def shards(sizes, tokens, seq_len, ln1_gain, ln1_shift, w_qkv, w_out, ln2_gain, ln2_shift, w_up, w_down, cotangent):
    blocks, lanes, seqs = sizes
    devices = blocks * lanes
    place = Place(*sizes)
    share, part = place.share, place.part
    model = tokens.shape[2]
    length = blocks * tokens.shape[1]
    rows = length // share
    owned = w_qkv.shape[0]
    cols = model // share
    wide = -(-cols // 128) * 128
    real = cols // 64

    grouped = w_qkv.reshape(owned, 3, share, cols)
    grouped = jnp.pad(grouped, ((0, 0), (0, 0), (0, 0), (0, wide - cols)))
    grouped = jnp.transpose(grouped, (2, 0, 1, 3)).reshape(share, owned, 3 * wide)
    vec = jnp.stack([ln1_gain, ln1_shift, ln2_gain, ln2_shift]).astype(jnp.float32)
    vec = jnp.pad(vec, ((0, 4), (0, 128 - owned)))
    vec = vec.at[4, :seqs].set(seq_len.astype(jnp.float32))
    outs = gather(sizes, tokens, cotangent, [grouped, vec, w_out, w_up, w_down])
    tok_all, cot_own, _, vec_all, out_full, up_full, down_full, qkv_cols = outs
    out_full, up_full, qkv_cols = [a.reshape(model, -1) for a in (out_full, up_full, qkv_cols)]
    down_full = down_full.reshape(-1, model)
    params = jnp.swapaxes(vec_all.reshape(devices, 8, 128)[:, :4, :owned], 0, 1).reshape(4, model)
    gain_one, shift_one, gain_two, shift_two = params
    lens = lax.dynamic_index_in_dim(vec_all[0], place.z, 0, False)[:, 4, :seqs].reshape(2 * seqs)
    my_len = lax.dynamic_index_in_dim(lens, place.seq, 0, False)

    inputs = tok_all.reshape(length, model).astype(jnp.float32)
    normed = normalize(inputs, gain_one, shift_one).astype(jnp.bfloat16)
    scale = jnp.where(jnp.arange(3 * wide) < wide, 0.125, 1.0)
    qkv = (dot(normed, qkv_cols, 1, 0) * scale).astype(jnp.bfloat16)
    att, lse = attend(qkv, 512, 512)
    att_parts = swap(att[:, :cols].reshape(share, rows, cols), share, blocks, lanes, part)
    att_own = jnp.concatenate(att_parts, -1)

    mine = lax.dynamic_slice_in_dim(tok_all.reshape(length, model), part * rows, rows, 0).astype(jnp.float32)
    positions = part * rows + jnp.arange(rows, dtype=jnp.int32)
    live = (positions.astype(jnp.float32) < my_len).astype(jnp.float32)[:, None]
    middle = mine + live * dot(att_own, out_full, 1, 0)
    normed_two = normalize(middle, gain_two, shift_two).astype(jnp.bfloat16)
    pre = dot(normed_two, up_full, 1, 0)
    hidden = jax.nn.gelu(pre, approximate=True).astype(jnp.bfloat16)
    result = (middle + dot(hidden, down_full, 1, 0)).astype(jnp.bfloat16)
    top = cot_own.reshape(rows, model)
    grad_down = dot(hidden, top, 0, 0).astype(jnp.bfloat16)
    grad_hidden = dot(top, down_full, 1, 1)
    pull = jax.vjp(lambda v: jax.nn.gelu(v, approximate=True), pre)[1]
    grad_pre = pull(grad_hidden)[0].astype(jnp.bfloat16)
    grad_up = dot(normed_two, grad_pre, 0, 0).astype(jnp.bfloat16)
    grad_two = dot(grad_pre, up_full, 1, 1)
    pull_two = jax.vjp(normalize, middle, gain_two, shift_two)[1]
    grad_norm, grad_gain_two, grad_shift_two = pull_two(grad_two)
    grad_mid = top.astype(jnp.float32) + grad_norm
    branch = (live * grad_mid).astype(jnp.bfloat16)
    grad_out = dot(att_own, branch, 0, 0).astype(jnp.bfloat16)
    g_att = dot(branch, out_full, 1, 1).astype(jnp.bfloat16)
    g_parts = swap(jnp.stack([g_att[:, g * cols : (g + 1) * cols] for g in range(share)]), share, blocks, lanes, part)
    g_heads = jnp.pad(jnp.concatenate(g_parts, 0), ((0, 0), (0, wide - cols)))
    g_qkv = attend_back(qkv, g_heads, att, lse, 512, 512)
    grad_qkv = dot(normed, g_qkv, 0, 0).astype(jnp.bfloat16)
    partial = dot(g_qkv * 1, qkv_cols, 1, 1)
    one_parts = swap(partial.astype(jnp.bfloat16).reshape(share, rows, model), share, blocks, lanes, part)
    grad_one = one_parts[0].astype(jnp.float32)
    for other in one_parts[1:]:
        grad_one = grad_one + other.astype(jnp.float32)
    pull_one = jax.vjp(normalize, mine, gain_one, shift_one)[1]
    grad_norm, grad_gain_one, grad_shift_one = pull_one(grad_one)
    grad_tokens = (grad_mid + grad_norm).astype(jnp.bfloat16)

    vec_grads = jnp.stack([grad_gain_one, grad_shift_one, grad_gain_two, grad_shift_two]).reshape(4, devices, owned)
    vec_grads = jnp.pad(jnp.swapaxes(vec_grads, 0, 1), ((0, 0), (0, 4), (0, 128 - owned)))

    def cut(values):
        return values.reshape((blocks, lanes // 2, 2, -1) + values.shape[1:])

    per_part = blocks // share
    done = reduce(
        sizes,
        [cut(grad_qkv), vec_grads.reshape(blocks, lanes // 2, 2, 8, 128), cut(grad_out), cut(grad_up), cut(grad_down)],
        ["columns", "rows", "rows", "rows", "rows"],
        [result.reshape(per_part, -1, model), grad_tokens.reshape(per_part, -1, model)],
        1,
    )
    sum_qkv, sum_vec, sum_out, sum_up, sum_down, result, grad_tokens = done
    sum_qkv = jnp.transpose(sum_qkv.reshape(share, owned, 3, wide)[..., :cols], (1, 2, 0, 3)).reshape(owned, 3 * model)
    return (
        result,
        grad_tokens.astype(jnp.float32),
        sum_vec[0, :owned],
        sum_vec[1, :owned],
        sum_qkv,
        sum_out,
        sum_vec[2, :owned],
        sum_vec[3, :owned],
        sum_up,
        sum_down,
    )


def solution(mesh):
    blocks, lanes = mesh.shape["blk"], mesh.shape["seq"]
    whole = P(("blk", "seq"))
    rows = P(("blk", "seq"), None)
    tokens = P("seq", "blk", None)

    def run(*args):
        seqs = args[0].shape[0] // lanes
        return jax.shard_map(
            functools.partial(shards, (blocks, lanes, seqs)),
            mesh=mesh,
            in_specs=(tokens, P("seq"), whole, whole, rows, rows, whole, whole, rows, rows, tokens),
            out_specs=(tokens, tokens, whole, whole, rows, rows, whole, whole, rows, rows),
            check_vma=False,
        )(*args)

    return run
```

```python
import functools

import jax
import jax.numpy as jnp
from jax import lax
from jax.experimental import pallas as pl
from jax.experimental.pallas import tpu as pltpu
from jax.sharding import PartitionSpec as P

HEADS = 12
VMEM_LIMIT = 60 * 2**20


MESH = pl.DeviceIdType.MESH
DMA = pltpu.SemaphoreType.DMA
ANYWHERE = pl.BlockSpec(memory_space=pl.ANY)


class Place:
    def __init__(self, blocks, lanes, seqs):
        self.blocks, self.depth, self.seqs = blocks, lanes // 2, seqs
        self.share = blocks // seqs
        self.per_part = blocks // self.share
        self.bits = max(1, blocks.bit_length() - 1)
        self.blk = lax.axis_index("blk")
        lane = lax.axis_index("seq")
        self.z, self.core = lane // 2, lane % 2
        flat = self.blk * 2 + self.core
        self.seq, self.part = flat // self.share, flat % self.share
        self.home = self.seq // seqs
        self.other = lax.rem(self.blk * 2 + 1 - self.core, self.share)

    def at(self, blk, z, core):
        return (blk, z * 2 + core)

    def sibling(self):
        return self.at(self.blk, self.z, 1 - self.core)

    def peers(self, along_z, along_blk):
        out = [self.sibling()]
        if along_z:
            out += [self.at(self.blk, lax.rem(self.z + k, self.depth), self.core) for k in range(1, self.depth)]
        if along_blk:
            for m in range(1, self.blocks):
                out += [self.at(self.blk ^ m, self.z, 0), self.at(self.blk ^ m, self.z, 1)]
        return out

    def bit(self, part, step):
        return 1 << ((part + step) % self.bits)

    def widen(self, k):
        masks, out, seen = [0], [], 0
        for t in range(self.bits):
            bit = self.bit(k, t)
            out.append((bit, list(masks), seen))
            seen += len(masks)
            masks += [m ^ bit for m in masks]
        return out

    def narrow(self, k):
        out, seen = [], 0
        for t in range(self.bits):
            masks = [0]
            for u in range(t + 1, self.bits):
                masks += [m ^ self.bit(k, u) for m in masks]
            out.append((self.bit(k, t), masks, seen))
            seen += len(masks)
        return out


def greet(devices):
    barrier = pltpu.get_barrier_semaphore()
    for device in devices:
        pl.semaphore_signal(barrier, inc=1, device_id=device, device_id_type=MESH)
    pl.semaphore_wait(barrier, len(devices))


def send(src, dst, send_sem, recv_sem, device):
    pltpu.make_async_remote_copy(
        src_ref=src, dst_ref=dst, send_sem=send_sem, recv_sem=recv_sem, device_id=device, device_id_type=MESH
    ).start()


def arrived(ref, sem):
    pltpu.make_async_copy(ref, ref, sem).wait()


def gather_kernel(sizes, early, late, *refs):
    place = Place(*sizes)
    blocks, depth, seqs, share, bits = place.blocks, place.depth, place.seqs, place.share, place.bits
    blk, z, core, home = place.blk, place.z, place.core, place.home
    count = early + late
    tok, shards, refs = refs[0], refs[1 : 1 + count], refs[1 + count :]
    tok_all, fulls, refs = refs[0], refs[1 : 1 + count], refs[1 + count :]
    cols = refs[0]
    tok_s, tok_r, near_s, near_r, z_s, z_r, b_s, b_r, c_s, c_r, loc = refs[1:]
    per_seq = share // 2
    greet(place.peers(True, True))
    waits = []

    def level(k):
        return lax.rem(z + depth - k, depth)

    def slot(a, depth_at):
        return fulls[a].at[blk, depth_at, core] if a < early else fulls[a].at[depth_at]

    for a in range(early):
        for k in range(1, depth):
            send(shards[a], slot(a, z), z_s.at[a, k - 1], z_r.at[a, k - 1], place.at(blk, lax.rem(z + k, depth), core))
            waits.append((shards[a], z_s.at[a, k - 1]))
    for i in range(seqs):
        for h in range(per_seq):
            target = (core * seqs + i) * per_seq + h

            @pl.when(target != blk)
            def _(i=i, h=h, target=target):
                send(tok.at[i], tok_all.at[blk], tok_s.at[i * per_seq + h], tok_r.at[blk], place.at(target, z, core))

            @pl.when(target == blk)
            def _(i=i):
                pltpu.make_async_copy(tok.at[i], tok_all.at[blk], loc.at[0]).start()

    def forward(a, k, t):
        bit, masks, seen = place.widen(k)[t]
        for n, m in enumerate(masks):
            src = shards[a] if (m == 0 and k == 0) else fulls[a].at[blk ^ m, level(k), core]
            there = fulls[a].at[blk ^ m, level(k), core]
            send(src, there, b_s.at[a, k, seen + n], b_r.at[a, k, seen + n], place.at(blk ^ bit, z, core))
            waits.append((shards[a], b_s.at[a, k, seen + n]))

    def received(a, k, t):
        bit, masks, seen = place.widen(k)[t]
        for n, m in enumerate(masks):
            arrived(fulls[a].at[blk ^ bit ^ m, level(k), core], b_r.at[a, k, seen + n])

    for a in range(early):
        forward(a, 0, 0)
    for a in range(count):
        pltpu.make_async_copy(shards[a], slot(a, z), loc.at[1 + a]).start()
    for k in range(1, depth):
        for a in range(early):
            arrived(slot(a, level(k)), z_r.at[a, k - 1])
            forward(a, k, 0)

    for a in range(early, count):
        for k in range(1, depth):
            send(shards[a], slot(a, z), z_s.at[a, k - 1], z_r.at[a, k - 1], place.at(blk, lax.rem(z + k, depth), core))
            waits.append((shards[a], z_s.at[a, k - 1]))
    @pl.when(core == home)
    def _():
        for p in range(blocks):

            @pl.when(p != blk)
            def _():
                arrived(tok_all.at[p], tok_r.at[p])

            @pl.when(p == blk)
            def _():
                arrived(tok_all.at[p], loc.at[0])

            send(tok_all.at[p], tok_all.at[p], near_s.at[p], near_r.at[p], place.sibling())

    for a in range(early):
        arrived(shards[a], loc.at[1 + a])
    for k in range(depth):
        for t in range(bits):
            for a in range(early):
                received(a, k, t)
                if t + 1 < bits:
                    forward(a, k, t + 1)
                elif a == 0:
                    send(
                        fulls[0].at[:, level(k), core, place.other],
                        cols.at[:, level(k), core],
                        c_s.at[a, k],
                        c_r.at[a, k],
                        place.sibling(),
                    )
                    waits.append((cols.at[:, 0, 0], c_s.at[a, k]))
                    pltpu.make_async_copy(
                        fulls[0].at[:, level(k), core, place.part], cols.at[:, level(k), core], loc.at[1 + count + k]
                    ).start()
                    waits.append((cols.at[:, 0, 0], loc.at[1 + count + k]))
                else:
                    held = fulls[a].at[:, level(k), core]
                    send(held, held, c_s.at[a, k], c_r.at[a, k], place.sibling())
                    waits.append((fulls[a].at[:, 0, 0], c_s.at[a, k]))
    for k in range(depth):
        for a in range(early):
            full = cols if a == 0 else fulls[a]
            arrived(full.at[:, level(k), 1 - core], c_r.at[a, k])
    for a in range(early, count):
        arrived(shards[a], loc.at[1 + a])
        for k in range(1, depth):
            arrived(slot(a, level(k)), z_r.at[a, k - 1])
    for ref, sem in waits:
        arrived(ref, sem)

    @pl.when(core == home)
    def _():
        for p in range(blocks):
            arrived(tok_all.at[p], near_s.at[p])

    @pl.when(core != home)
    def _():
        for p in range(blocks):
            arrived(tok_all.at[p], near_r.at[p])

    for i in range(seqs):
        for h in range(per_seq):
            target = (core * seqs + i) * per_seq + h

            @pl.when(target != blk)
            def _(i=i, h=h):
                arrived(tok.at[i], tok_s.at[i * per_seq + h])


def gather(sizes, tok, shards, late_shards):
    blocks, lanes, seqs = sizes
    depth, share = lanes // 2, blocks // seqs
    early, late = len(shards), len(late_shards)
    count = early + late
    rows, width = tok.shape[1:]
    outs = [jax.ShapeDtypeStruct((blocks, rows, width), tok.dtype)]
    outs += [jax.ShapeDtypeStruct((blocks, depth, 2) + s.shape, s.dtype) for s in shards]
    outs += [jax.ShapeDtypeStruct((depth,) + s.shape, s.dtype) for s in late_shards]
    outs += [jax.ShapeDtypeStruct((blocks, depth, 2) + shards[0].shape[1:], shards[0].dtype)]
    return pl.pallas_call(
        functools.partial(gather_kernel, sizes, early, late),
        out_shape=outs,
        in_specs=[ANYWHERE] * (1 + count),
        out_specs=[ANYWHERE] * len(outs),
        scratch_shapes=[
            DMA((seqs * share // 2,)),
            DMA((blocks,)),
            DMA((blocks,)),
            DMA((blocks,)),
            DMA((count, depth - 1)),
            DMA((count, depth - 1)),
            DMA((early, depth, blocks - 1)),
            DMA((early, depth, blocks - 1)),
            DMA((early, depth)),
            DMA((early, depth)),
            DMA((1 + count + depth,)),
        ],
        compiler_params=pltpu.CompilerParams(collective_id=0, has_side_effects=True, vmem_limit_bytes=VMEM_LIMIT),
    )(tok, *shards, *late_shards)


class Spread:
    def __init__(self, place, cot, tall, cot_own, fulls, sems):
        self.place, self.cot, self.tall, self.cot_own, self.fulls = place, cot, tall, cot_own, fulls
        self.b_s, self.b_r, self.c_s, self.c_r, self.cot_s, self.cot_r, self.loc = sems
        self.count = len(fulls)

    @staticmethod
    def sems(count, blocks, depth, seqs):
        return [
            DMA((count, depth, blocks - 1)),
            DMA((count, depth, blocks - 1)),
            DMA((count,)),
            DMA((count,)),
            DMA((seqs,)),
            DMA((blocks,)),
            DMA((count + 1,)),
        ]

    def start(self):
        place = self.place
        greet(place.peers(False, True))
        for a in range(self.count):
            for k in range(place.depth):
                self.forward(a, k, 0)
            pltpu.make_async_copy(self.tall[a], self.fulls[a].at[place.blk, :, place.core], self.loc.at[a]).start()

    def forward(self, a, k, t):
        place = self.place
        bit, masks, seen = place.widen(k)[t]
        for n, m in enumerate(masks):
            there = self.fulls[a].at[place.blk ^ m, k, place.core]
            src = self.tall[a].at[k] if m == 0 else there
            sems = self.b_s.at[a, k, seen + n], self.b_r.at[a, k, seen + n]
            send(src, there, *sems, place.at(place.blk ^ bit, place.z, place.core))

    def step(self, a, t):
        place = self.place
        for k in range(place.depth):
            bit, masks, seen = place.widen(k)[t]
            for n, m in enumerate(masks):
                arrived(self.fulls[a].at[place.blk ^ bit ^ m, k, place.core], self.b_r.at[a, k, seen + n])
            if t + 1 < place.bits:
                self.forward(a, k, t + 1)
        if t + 1 == place.bits:
            arrived(self.tall[a], self.loc.at[a])
            held = self.fulls[a].at[:, :, place.core]
            send(held, held, self.c_s.at[a], self.c_r.at[a], place.sibling())

    def rows(self):
        place = self.place
        for i in range(place.seqs):
            owner = (place.core * place.seqs + i) * place.share + place.blk // place.per_part
            slot = lax.rem(place.blk, place.per_part)
            mine = owner == place.blk * 2 + place.core

            @pl.when(jnp.logical_not(mine))
            def _(i=i, owner=owner, slot=slot):
                sems = self.cot_s.at[i], self.cot_r.at[slot]
                send(self.cot.at[i], self.cot_own.at[slot], *sems, place.at(owner // 2, place.z, owner % 2))

            @pl.when(mine)
            def _(i=i, slot=slot):
                pltpu.make_async_copy(self.cot.at[i], self.cot_own.at[slot], self.loc.at[self.count]).start()

    def finish(self):
        place = self.place
        for a in range(self.count):
            arrived(self.fulls[a].at[:, :, 1 - place.core], self.c_r.at[a])
            arrived(self.fulls[a].at[:, :, place.core], self.c_s.at[a])
            for k in range(place.depth):
                for n in range(place.blocks - 1):
                    arrived(self.tall[a].at[k], self.b_s.at[a, k, n])
        for i in range(place.seqs):
            owner = (place.core * place.seqs + i) * place.share + place.blk // place.per_part

            @pl.when(owner != place.blk * 2 + place.core)
            def _(i=i):
                arrived(self.cot.at[i], self.cot_s.at[i])

        for t in range(place.per_part):
            mine = (place.part * place.per_part + t == place.blk) & (place.home == place.core)

            @pl.when(mine)
            def _(t=t):
                arrived(self.cot_own.at[t], self.loc.at[self.count])

            @pl.when(jnp.logical_not(mine))
            def _(t=t):
                arrived(self.cot_own.at[t], self.cot_r.at[t])


class Fold:
    def __init__(self, place, kinds, grads, rows_in, sums, rows_out, scratch):
        self.place, self.kinds, self.grads = place, kinds, grads
        self.rows_in, self.sums, self.rows_out = rows_in, sums, rows_out
        self.count, self.moves = len(kinds), len(rows_in)
        n = self.count
        self.held, self.near, self.wide, self.tall = (scratch[i * n : i * n + n] for i in range(4))
        self.m_s, self.m_r, self.z_s, self.z_r, self.b_s, self.b_r, self.c_s, self.c_r, self.loc = scratch[4 * n :]
        self.order = list(range(1, place.depth)) + [0]
        self.units = [(a, k) for a in range(n) for k in self.order]

    @staticmethod
    def scratch(sizes, chunks, types, kinds, moves):
        blocks, lanes, seqs = sizes
        depth, share, count = lanes // 2, blocks // seqs, len(chunks)
        out = [pltpu.VMEM((blocks, depth) + c, t) for c, t in zip(chunks, types)]
        out += [
            pltpu.VMEM((1, 1, 8, 128) if kind == "columns" else (blocks, depth) + c, t)
            for c, t, kind in zip(chunks, types, kinds)
        ]
        out += [pltpu.VMEM((depth, blocks - 1) + c, t) for c, t in zip(chunks, types)]
        out += [pltpu.VMEM((depth - 1,) + c, t) for c, t in zip(chunks, types)]
        return out + [
            DMA((max(1, moves), blocks // share)),
            DMA((max(1, moves), seqs)),
            DMA((count, depth - 1)),
            DMA((count, depth - 1)),
            DMA((count, depth, blocks - 1)),
            DMA((count, depth, blocks - 1)),
            DMA((count, depth)),
            DMA((count, depth)),
            DMA((count + 1, max(depth, moves))),
        ]

    def level(self, k):
        return lax.rem(self.place.z + k, self.place.depth)

    def greet(self):
        greet(self.place.peers(True, True))

    def clear(self):
        place = self.place
        for a in range(self.count):
            if self.kinds[a] == "columns" and place.share > 2:
                held = self.held[a]
                for g in range(place.share):

                    @pl.when((g != place.part) & (g != place.other))
                    def _(held=held, g=g):
                        held[:, :, g] = jnp.zeros(held.shape[:2] + held.shape[3:], held.dtype)

    def start(self, a, k):
        place = self.place
        if self.kinds[a] == "columns":
            mine = there = self.held[a].at[:, self.level(k), place.part]
        else:
            mine = self.held[a].at[:, self.level(k)]
            there = self.near[a].at[:, self.level(k)]
        theirs = self.grads[a].at[:, self.level(k), 1 - place.core]
        send(theirs, there, self.c_s.at[a, k], self.c_r.at[a, k], place.sibling())
        pltpu.make_async_copy(self.grads[a].at[:, self.level(k), place.core], mine, self.loc.at[a, k]).start()

    def add(self, into, second):
        total = into[...].astype(jnp.float32) + second[...].astype(jnp.float32)
        into[...] = total.astype(into.dtype)

    def forward(self, a, k, t):
        place = self.place
        bit, masks, seen = place.narrow(k)[t]
        for n, m in enumerate(masks):
            sems = self.b_s.at[a, k, seen + n], self.b_r.at[a, k, seen + n]
            block = self.held[a].at[place.blk ^ bit ^ m, self.level(k)]
            send(block, self.wide[a].at[k, seen + n], *sems, place.at(place.blk ^ bit, place.z, place.core))

    def join(self, a, k):
        place = self.place
        if self.kinds[a] == "columns":
            arrived(self.held[a].at[:, self.level(k), place.part], self.loc.at[a, k])
            arrived(self.held[a].at[:, self.level(k), place.other], self.c_r.at[a, k])
        else:
            arrived(self.held[a].at[:, self.level(k)], self.loc.at[a, k])
            arrived(self.near[a].at[:, self.level(k)], self.c_r.at[a, k])

            def one(b, _):
                self.add(self.held[a].at[b, self.level(k)], self.near[a].at[b, self.level(k)])
                return 0

            lax.fori_loop(0, place.blocks, one, 0)
        self.forward(a, k, 0)

    def step(self, a, k, t):
        place = self.place
        bit, masks, seen = place.narrow(k)[t]
        for n, m in enumerate(masks):
            arrived(self.wide[a].at[k, seen + n], self.b_r.at[a, k, seen + n])
            self.add(self.held[a].at[place.blk ^ m, self.level(k)], self.wide[a].at[k, seen + n])
        if t + 1 < place.bits:
            self.forward(a, k, t + 1)
        elif k > 0:
            sems = self.z_s.at[a, k - 1], self.z_r.at[a, k - 1]
            block = self.held[a].at[place.blk, self.level(k)]
            send(block, self.tall[a].at[k - 1], *sems, place.at(place.blk, self.level(k), place.core))

    def total(self, a):
        place = self.place
        value = self.held[a][place.blk, place.z].astype(jnp.float32)
        for k in range(1, place.depth):
            arrived(self.tall[a].at[k - 1], self.z_r.at[a, k - 1])
            value = value + self.tall[a][k - 1].astype(jnp.float32)
        self.sums[a][...] = value

    def rows(self, j):
        place = self.place
        slot = lax.rem(place.seq, place.seqs)
        for t in range(place.per_part):
            source = place.part * place.per_part + t
            mine = (source == place.blk) & (place.home == place.core)

            @pl.when(mine)
            def _(t=t):
                pltpu.make_async_copy(self.rows_in[j].at[t], self.rows_out[j].at[slot], self.loc.at[self.count, j]).start()

            @pl.when(jnp.logical_not(mine))
            def _(t=t, source=source):
                sems = self.m_s.at[j, t], self.m_r.at[j, slot]
                send(self.rows_in[j].at[t], self.rows_out[j].at[slot], *sems, place.at(source, place.z, place.home))

    def finish(self):
        place = self.place
        for a, k in self.units:
            if self.kinds[a] == "columns":
                arrived(self.held[a].at[:, 0, 0], self.c_s.at[a, k])
            else:
                arrived(self.held[a].at[:, 0], self.c_s.at[a, k])
            for n in range(place.blocks - 1):
                arrived(self.held[a].at[0, 0], self.b_s.at[a, k, n])
            if k > 0:
                arrived(self.held[a].at[0, 0], self.z_s.at[a, k - 1])
        for j in range(self.moves):
            for t in range(place.per_part):
                mine = (place.part * place.per_part + t == place.blk) & (place.home == place.core)

                @pl.when(mine)
                def _(j=j, t=t):
                    arrived(self.rows_in[j].at[t], self.loc.at[self.count, j])

                @pl.when(jnp.logical_not(mine))
                def _(j=j, t=t):
                    arrived(self.rows_in[j].at[t], self.m_s.at[j, t])

            for i in range(place.seqs):
                owner = (place.core * place.seqs + i) * place.share + place.blk // place.per_part

                @pl.when(owner != place.blk * 2 + place.core)
                def _(j=j, i=i):
                    arrived(self.rows_out[j].at[i], self.m_r.at[j, i])


def fold_shapes(sizes, grads, kinds, rows):
    blocks, _, seqs = sizes
    share = blocks // seqs
    chunks = [((share,) if kind == "columns" else ()) + g.shape[3:] for g, kind in zip(grads, kinds)]
    scratch = Fold.scratch(sizes, chunks, [g.dtype for g in grads], kinds, len(rows))
    out = [jax.ShapeDtypeStruct(c, jnp.float32) for c in chunks]
    moved = [jax.ShapeDtypeStruct((seqs,) + r.shape[1:], r.dtype) for r in rows]
    return out, moved, scratch


def reduce_kernel(sizes, kinds, moves, *refs):
    count = len(kinds)
    ends = [count, count + moves, 2 * count + moves, 2 * (count + moves)]
    fold = Fold(
        Place(*sizes), kinds, refs[: ends[0]], refs[ends[0] : ends[1]], refs[ends[1] : ends[2]], refs[ends[2] : ends[3]], refs[ends[3] :]
    )
    fold.greet()
    fold.clear()
    for a, k in fold.units:
        fold.start(a, k)
    for j in range(moves):
        fold.rows(j)
    for a, k in fold.units:
        fold.join(a, k)
    for t in range(fold.place.bits):
        for a, k in fold.units:
            fold.step(a, k, t)
    for a in range(count):
        fold.total(a)
    fold.finish()


def reduce(sizes, grads, kinds, rows, cid):
    count, moves = len(grads), len(rows)
    out, moved, scratch = fold_shapes(sizes, grads, kinds, rows)
    return pl.pallas_call(
        functools.partial(reduce_kernel, sizes, kinds, moves),
        out_shape=out + moved,
        in_specs=[ANYWHERE] * (count + moves),
        out_specs=[pl.BlockSpec(memory_space=pltpu.VMEM)] * count + [ANYWHERE] * moves,
        scratch_shapes=scratch,
        compiler_params=pltpu.CompilerParams(collective_id=cid, has_side_effects=True, vmem_limit_bytes=VMEM_LIMIT),
    )(*grads, *rows)


def dot_nt(left, right):
    return lax.dot_general(left, right, (((1,), (1,)), ((), ())), preferred_element_type=jnp.float32)


def dot_nn(left, right):
    return lax.dot_general(left, right, (((1,), (0,)), ((), ())), preferred_element_type=jnp.float32)


def split_heads(dst, src):
    low = lax.broadcasted_iota(jnp.int32, src.shape, 1) < 64
    dst[0] = jnp.where(low, src, jnp.zeros_like(src))
    dst[1] = jnp.where(low, jnp.zeros_like(src), src)


def causal(bk, bq, kj, qi):
    kpos = kj * bk + lax.broadcasted_iota(jnp.int32, (bk, bq), 0)
    qpos = qi * bq + lax.broadcasted_iota(jnp.int32, (bk, bq), 1)
    return kpos <= qpos


def plan(tasks, points):
    out = {}
    for where, call in tasks:
        out.setdefault(min(points - 1, int(where * points)), []).append(call)
    return out


def pump(todo, point):
    for at, calls in todo.items():

        @pl.when(point == at)
        def _(calls=calls):
            for call in calls:
                call()


def fwd_kernel(sizes, late, block, pairs, *refs):
    q_ref, k_ref, v_ref, cot = refs[:4]
    tall, refs = refs[4 : 4 + late], refs[4 + late :]
    att_ref, lse_ref, cot_own = refs[:3]
    fulls, refs = refs[3 : 3 + late], refs[3 + late :]
    kh, vt, sems = refs[0], refs[1], refs[2:]
    pair = pl.program_id(0)
    length = q_ref.shape[0]
    count = length // block
    spread = Spread(Place(*sizes), cot, tall, cot_own, fulls, sems)
    bits = spread.place.bits
    steps = [(a, t) for t in range(bits) for a in range(late)]
    tasks = [(0.15 + 0.75 * n / len(steps), functools.partial(spread.step, a, t)) for n, (a, t) in enumerate(steps)]
    tasks.insert(late, (tasks[late - 1][0], spread.rows))
    todo = plan(tasks, pairs * count)

    @pl.when(pair == 0)
    def _():
        spread.start()

    split_heads(kh, k_ref[...])
    vt[...] = v_ref[...].astype(jnp.float32).T.astype(jnp.bfloat16)

    def q_step(qi, _):
        rows = pl.ds(pl.multiple_of(qi * block, block), block)
        q_rows = q_ref[rows, :]

        def one(kj, state, masked):
            at = pl.ds(pl.multiple_of(kj * block, block), block)
            out = []
            for h in range(2):
                peak, total, acc = state[3 * h : 3 * h + 3]
                s = dot_nt(kh[h, at, :], q_rows)
                u = s * s + 1.0
                inv = lax.rsqrt(u)
                mag = u * inv
                if masked:
                    mag = jnp.where(causal(block, block, kj, qi), mag, -1e30)
                new = jnp.maximum(peak, jnp.max(mag, axis=0, keepdims=True))
                p = jnp.exp(mag - new)
                alpha = jnp.exp(peak - new)
                total = total * alpha + jnp.sum(p, axis=0, keepdims=True)
                signed = (p * (s * inv)).astype(jnp.bfloat16)
                acc = acc * alpha + dot_nn(vt[64 * h : 64 * h + 64, at], signed)
                out += [new, total, acc]
            return tuple(out)

        zero = (
            jnp.full((1, block), -1e30, jnp.float32),
            jnp.zeros((1, block), jnp.float32),
            jnp.zeros((64, block), jnp.float32),
        )
        state = one(qi, zero + zero, True)
        state = lax.fori_loop(0, qi, lambda kj, st: one(kj, st, False), state)
        both = []
        for h in range(2):
            peak, total, acc = state[3 * h : 3 * h + 3]
            both.append(acc / total)
            lse_ref[0, h : h + 1, rows] = peak + jnp.log(total)
        att_ref[rows, :] = jnp.concatenate(both, 0).T.astype(jnp.bfloat16)
        pump(todo, pair * count + qi)
        return 0

    lax.fori_loop(0, count, q_step, 0)

    @pl.when(pair == pairs - 1)
    def _():
        spread.finish()


def attend(sizes, qkv, cot, tall, block):
    blocks, lanes, seqs = sizes
    share = blocks // seqs
    length, width = qkv.shape
    pairs = width // 384
    return pl.pallas_call(
        functools.partial(fwd_kernel, sizes, len(tall), block, pairs),
        grid=(pairs,),
        out_shape=[
            jax.ShapeDtypeStruct((length, 128 * pairs), jnp.bfloat16),
            jax.ShapeDtypeStruct((pairs, 8, length), jnp.float32),
            jax.ShapeDtypeStruct((blocks // share,) + cot.shape[1:], cot.dtype),
        ]
        + [jax.ShapeDtypeStruct((blocks, lanes // 2, 2) + a.shape[1:], a.dtype) for a in tall],
        in_specs=[pl.BlockSpec((length, 128), lambda p, n=n: (0, n * pairs + p)) for n in range(3)]
        + [ANYWHERE] * (1 + len(tall)),
        out_specs=[pl.BlockSpec((length, 128), lambda p: (0, p)), pl.BlockSpec((1, 8, length), lambda p: (p, 0, 0))]
        + [ANYWHERE] * (1 + len(tall)),
        scratch_shapes=[pltpu.VMEM((2, length, 128), jnp.bfloat16), pltpu.VMEM((128, length), jnp.bfloat16)]
        + Spread.sems(len(tall), blocks, lanes // 2, seqs),
        compiler_params=pltpu.CompilerParams(collective_id=1, has_side_effects=True, vmem_limit_bytes=VMEM_LIMIT),
    )(qkv, qkv, qkv, cot, *tall)


def bwd_kernel(sizes, kinds, moves, block, pairs, *refs):
    many = len(kinds)
    q_ref, k_ref, v_ref, g_ref, att_ref, lse_ref = refs[:6]
    grads, rows_in, refs = refs[6 : 6 + many], refs[6 + many : 6 + many + moves], refs[6 + many + moves :]
    out_ref = refs[0]
    sums, rows_out, refs = refs[1 : 1 + many], refs[1 + many : 1 + many + moves], refs[1 + many + moves :]
    kh, vh, qh, gh, kt, delta, dqt, dk, dv = refs[:9]
    fold = Fold(Place(*sizes), kinds, grads, rows_in, sums, rows_out, refs[9:])
    pair = pl.program_id(0)
    length = q_ref.shape[0]
    width = 128 * pairs
    count = length // block
    per_pair = count * (count + 1) // 2
    bits, units = fold.place.bits, len(fold.units)
    tasks = []
    for n, (a, k) in enumerate(fold.units):
        tasks.append((0.02 + 0.45 * n / units, functools.partial(fold.join, a, k)))
        for t in range(bits):
            where = 0.1 + 0.08 * t + (0.6 + 0.1 * t / bits) * n / units
            tasks.append((where, functools.partial(fold.step, a, k, t)))
    for j in range(moves):
        tasks.append((0.5, functools.partial(fold.rows, j)))
    tasks.sort(key=lambda task: task[0])
    todo = plan(tasks, pairs * per_pair)

    @pl.when(pair == 0)
    def _():
        fold.greet()
        for a, k in fold.units:
            fold.start(a, k)

    split_heads(kh, k_ref[...])
    split_heads(vh, v_ref[...])
    split_heads(qh, q_ref[...])
    split_heads(gh, g_ref[...])
    kt[...] = k_ref[...].astype(jnp.float32).T.astype(jnp.bfloat16)
    prod = (g_ref[...].astype(jnp.float32) * att_ref[...].astype(jnp.float32)).T
    delta[0:1, :] = jnp.sum(prod[:64], axis=0, keepdims=True)
    delta[1:2, :] = jnp.sum(prod[64:], axis=0, keepdims=True)
    dqt[...] = jnp.zeros_like(dqt)

    def k_step(kj, _):
        at = pl.ds(pl.multiple_of(kj * block, block), block)

        def one(qi, masked):
            rows = pl.ds(pl.multiple_of(qi * block, block), block)
            q_rows = q_ref[rows, :]
            g_rows = g_ref[rows, :]
            add_k = add_v = None
            for h in range(2):
                s = dot_nt(kh[h, at, :], q_rows)
                dp = dot_nt(vh[h, at, :], g_rows)
                u = s * s + 1.0
                inv = lax.rsqrt(u)
                arg = u * inv - lse_ref[0, h : h + 1, rows]
                if masked:
                    arg = jnp.where(causal(block, block, kj, qi), arg, -1e30)
                p = jnp.exp(arg)
                sgn = s * inv
                t = inv * inv * (inv - 1.0) + 1.0
                ds = (p * (dp * t - sgn * delta[h : h + 1, rows])).astype(jnp.bfloat16)
                signed = (p * sgn).astype(jnp.bfloat16)
                one_v = dot_nn(signed, gh[h, rows, :])
                one_k = dot_nn(ds, qh[h, rows, :])
                add_v = one_v if h == 0 else add_v + one_v
                add_k = one_k if h == 0 else add_k + one_k
                dqt[64 * h : 64 * h + 64, rows] += dot_nn(kt[64 * h : 64 * h + 64, at], ds)
            return add_k, add_v

        def more(qi, _):
            @pl.when(qi == kj)
            def _():
                dk[...], dv[...] = one(qi, True)

            @pl.when(qi != kj)
            def _():
                add_k, add_v = one(qi, False)
                dk[...] += add_k
                dv[...] += add_v

            pump(todo, pair * per_pair + kj * count - kj * (kj - 1) // 2 + qi - kj)
            return 0

        lax.fori_loop(kj, count, more, 0)
        out_ref[at, pl.ds(pl.multiple_of(width + pair * 128, 128), 128)] = dk[...].astype(jnp.bfloat16)
        out_ref[at, pl.ds(pl.multiple_of(2 * width + pair * 128, 128), 128)] = dv[...].astype(jnp.bfloat16)
        return 0

    lax.fori_loop(0, count, k_step, 0)
    out_ref[:, pl.ds(pl.multiple_of(pair * 128, 128), 128)] = (dqt[...] * 0.125).T.astype(jnp.bfloat16)

    @pl.when(pair == pairs - 1)
    def _():
        for a in range(many):
            fold.total(a)
        fold.finish()


def attend_back(sizes, qkv, g_att, att, lse, grads, rows, block):
    length, width = qkv.shape
    pairs = width // 384
    kinds = ["rows"] * len(grads)
    out, moved, scratch = fold_shapes(sizes, grads, kinds, rows)
    in_vmem = pl.BlockSpec(memory_space=pltpu.VMEM)
    return pl.pallas_call(
        functools.partial(bwd_kernel, sizes, kinds, len(rows), block, pairs),
        grid=(pairs,),
        out_shape=[jax.ShapeDtypeStruct((length, width), jnp.bfloat16)] + out + moved,
        in_specs=[pl.BlockSpec((length, 128), lambda p, n=n: (0, n * pairs + p)) for n in range(3)]
        + [pl.BlockSpec((length, 128), lambda p: (0, p))] * 2
        + [pl.BlockSpec((1, 8, length), lambda p: (p, 0, 0))]
        + [ANYWHERE] * (len(grads) + len(rows)),
        out_specs=[pl.BlockSpec((length, width), lambda p: (0, 0))] + [in_vmem] * len(out) + [ANYWHERE] * len(moved),
        scratch_shapes=[pltpu.VMEM((2, length, 128), jnp.bfloat16)] * 4
        + [
            pltpu.VMEM((128, length), jnp.bfloat16),
            pltpu.VMEM((8, length), jnp.float32),
            pltpu.VMEM((128, length), jnp.float32),
            pltpu.VMEM((block, 128), jnp.float32),
            pltpu.VMEM((block, 128), jnp.float32),
        ]
        + scratch,
        compiler_params=pltpu.CompilerParams(collective_id=2, has_side_effects=True, vmem_limit_bytes=VMEM_LIMIT),
    )(qkv, qkv, qkv, g_att, att, lse, *grads, *rows)


def normalize(values, gain, shift):
    center = jnp.mean(values, axis=-1, keepdims=True)
    offsets = values - center
    spread = jnp.mean(offsets * offsets, axis=-1, keepdims=True)
    return offsets * lax.rsqrt(spread + 1e-05) * gain + shift


def dot(left, right, at_left, at_right):
    return lax.dot_general(left, right, (((at_left,), (at_right,)), ((), ())), preferred_element_type=jnp.float32)


def swap(values, share, blocks, lanes, part):
    flat = blocks * lanes

    def number(blk, z, core):
        return blk * lanes + z * 2 + core

    pieces = [lax.dynamic_index_in_dim(values, part, 0, False)]
    for step in range(1, share):
        pairs = []
        for blk in range(blocks):
            for z in range(lanes // 2):
                for core in range(2):
                    other = (blk * 2 + core) ^ step
                    pairs.append((number(blk, z, core), number(other // 2, z, other % 2)))
        piece = lax.dynamic_index_in_dim(values, part ^ step, 0, False)
        pieces.append(lax.ppermute(piece, ("blk", "seq"), pairs))
    ordered = []
    for g in range(share):
        got = pieces[0]
        for step in range(1, share):
            got = jnp.where((part ^ step) == g, pieces[step], got)
        ordered.append(got)
    return ordered


def shards(sizes, tokens, seq_len, ln1_gain, ln1_shift, w_qkv, w_out, ln2_gain, ln2_shift, w_up, w_down, cotangent):
    blocks, lanes, seqs = sizes
    devices = blocks * lanes
    place = Place(*sizes)
    share, part = place.share, place.part
    model = tokens.shape[2]
    length = blocks * tokens.shape[1]
    rows = length // share
    owned = w_qkv.shape[0]
    cols = model // share
    wide = -(-cols // 128) * 128
    real = cols // 64

    grouped = w_qkv.reshape(owned, 3, share, cols)
    grouped = jnp.pad(grouped, ((0, 0), (0, 0), (0, 0), (0, wide - cols)))
    grouped = jnp.transpose(grouped, (2, 0, 1, 3)).reshape(share, owned, 3 * wide)
    vec = jnp.stack([ln1_gain, ln1_shift, ln2_gain, ln2_shift]).astype(jnp.float32)
    vec = jnp.pad(vec, ((0, 4), (0, 128 - owned)))
    vec = vec.at[4, :seqs].set(seq_len.astype(jnp.float32))
    outs = gather(sizes, tokens, [grouped, vec], [w_out, w_up, w_down])
    tok_all, _, vec_all, *tall, qkv_cols = outs
    qkv_cols = qkv_cols.reshape(model, -1)
    params = jnp.swapaxes(vec_all.reshape(devices, 8, 128)[:, :4, :owned], 0, 1).reshape(4, model)
    gain_one, shift_one, gain_two, shift_two = params
    lens = lax.dynamic_index_in_dim(vec_all[0], place.z, 0, False)[:, 4, :seqs].reshape(2 * seqs)
    my_len = lax.dynamic_index_in_dim(lens, place.seq, 0, False)

    inputs = tok_all.reshape(length, model).astype(jnp.float32)
    normed = normalize(inputs, gain_one, shift_one).astype(jnp.bfloat16)
    scale = jnp.where(jnp.arange(3 * wide) < wide, 0.125, 1.0)
    qkv = (dot(normed, qkv_cols, 1, 0) * scale).astype(jnp.bfloat16)
    att, lse, cot_own, out_full, up_full, down_full = attend(sizes, qkv, cotangent, tall, 512)
    out_full, up_full, down_full = [a.reshape(model, -1) for a in (out_full, up_full)] + [down_full.reshape(-1, model)]
    att_parts = swap(att[:, :cols].reshape(share, rows, cols), share, blocks, lanes, part)
    att_own = jnp.concatenate(att_parts, -1)

    mine = lax.dynamic_slice_in_dim(tok_all.reshape(length, model), part * rows, rows, 0).astype(jnp.float32)
    positions = part * rows + jnp.arange(rows, dtype=jnp.int32)
    live = (positions.astype(jnp.float32) < my_len).astype(jnp.float32)[:, None]
    middle = mine + live * dot(att_own, out_full, 1, 0)
    normed_two = normalize(middle, gain_two, shift_two).astype(jnp.bfloat16)
    pre = dot(normed_two, up_full, 1, 0)
    hidden = jax.nn.gelu(pre, approximate=True).astype(jnp.bfloat16)
    result = (middle + dot(hidden, down_full, 1, 0)).astype(jnp.bfloat16)
    top = cot_own.reshape(rows, model)
    grad_down = dot(hidden, top, 0, 0).astype(jnp.bfloat16)
    grad_hidden = dot(top, down_full, 1, 1)
    pull = jax.vjp(lambda v: jax.nn.gelu(v, approximate=True), pre)[1]
    grad_pre = pull(grad_hidden)[0].astype(jnp.bfloat16)
    grad_up = dot(normed_two, grad_pre, 0, 0).astype(jnp.bfloat16)
    grad_two = dot(grad_pre, up_full, 1, 1)
    pull_two = jax.vjp(normalize, middle, gain_two, shift_two)[1]
    grad_norm, grad_gain_two, grad_shift_two = pull_two(grad_two)
    grad_mid = top.astype(jnp.float32) + grad_norm
    branch = (live * grad_mid).astype(jnp.bfloat16)
    grad_out = dot(att_own, branch, 0, 0).astype(jnp.bfloat16)
    g_att = dot(branch, out_full, 1, 1).astype(jnp.bfloat16)
    g_parts = swap(jnp.stack([g_att[:, g * cols : (g + 1) * cols] for g in range(share)]), share, blocks, lanes, part)
    g_heads = jnp.pad(jnp.concatenate(g_parts, 0), ((0, 0), (0, wide - cols)))
    per_part = blocks // share

    def cut(values):
        return values.reshape((blocks, lanes // 2, 2, -1) + values.shape[1:])

    g_qkv, sum_out, sum_up, sum_down, result = attend_back(
        sizes,
        qkv,
        g_heads,
        att,
        lse,
        [cut(grad_out), cut(grad_up), cut(grad_down)],
        [result.reshape(per_part, -1, model)],
        512,
    )
    grad_qkv = dot(normed, g_qkv, 0, 0).astype(jnp.bfloat16)
    partial = dot(g_qkv, qkv_cols, 1, 1)
    one_parts = swap(partial.astype(jnp.bfloat16).reshape(share, rows, model), share, blocks, lanes, part)
    grad_one = one_parts[0].astype(jnp.float32)
    for other in one_parts[1:]:
        grad_one = grad_one + other.astype(jnp.float32)
    pull_one = jax.vjp(normalize, mine, gain_one, shift_one)[1]
    grad_norm, grad_gain_one, grad_shift_one = pull_one(grad_one)
    grad_tokens = (grad_mid + grad_norm).astype(jnp.bfloat16)

    vec_grads = jnp.stack([grad_gain_one, grad_shift_one, grad_gain_two, grad_shift_two]).reshape(4, devices, owned)
    vec_grads = jnp.pad(jnp.swapaxes(vec_grads, 0, 1), ((0, 0), (0, 4), (0, 128 - owned)))

    sum_qkv, sum_vec, grad_tokens = reduce(
        sizes,
        [cut(grad_qkv), vec_grads.reshape(blocks, lanes // 2, 2, 8, 128)],
        ["columns", "rows"],
        [grad_tokens.reshape(per_part, -1, model)],
        3,
    )
    sum_qkv = jnp.transpose(sum_qkv.reshape(share, owned, 3, wide)[..., :cols], (1, 2, 0, 3)).reshape(owned, 3 * model)
    return (
        result,
        grad_tokens.astype(jnp.float32),
        sum_vec[0, :owned],
        sum_vec[1, :owned],
        sum_qkv,
        sum_out,
        sum_vec[2, :owned],
        sum_vec[3, :owned],
        sum_up,
        sum_down,
    )


def solution(mesh):
    blocks, lanes = mesh.shape["blk"], mesh.shape["seq"]
    whole = P(("blk", "seq"))
    rows = P(("blk", "seq"), None)
    tokens = P("seq", "blk", None)

    def run(*args):
        seqs = args[0].shape[0] // lanes
        return jax.shard_map(
            functools.partial(shards, (blocks, lanes, seqs)),
            mesh=mesh,
            in_specs=(tokens, P("seq"), whole, whole, rows, rows, whole, whole, rows, rows, tokens),
            out_specs=(tokens, tokens, whole, whole, rows, rows, whole, whole, rows, rows),
            check_vma=False,
        )(*args)

    return run
```

```python
import functools

import jax
import jax.numpy as jnp
from jax import lax
from jax.experimental import pallas as pl
from jax.experimental.pallas import tpu as pltpu
from jax.sharding import PartitionSpec as P

HEADS = 12
VMEM_LIMIT = 60 * 2**20


MESH = pl.DeviceIdType.MESH
DMA = pltpu.SemaphoreType.DMA
ANYWHERE = pl.BlockSpec(memory_space=pl.ANY)


class Place:
    def __init__(self, blocks, lanes, seqs):
        self.blocks, self.depth, self.seqs = blocks, lanes // 2, seqs
        self.share = blocks // seqs
        self.per_part = blocks // self.share
        self.bits = max(1, blocks.bit_length() - 1)
        self.blk = lax.axis_index("blk")
        lane = lax.axis_index("seq")
        self.z, self.core = lane // 2, lane % 2
        flat = self.blk * 2 + self.core
        self.seq, self.part = flat // self.share, flat % self.share
        self.home = self.seq // seqs
        self.other = lax.rem(self.blk * 2 + 1 - self.core, self.share)

    def at(self, blk, z, core):
        return (blk, z * 2 + core)

    def sibling(self):
        return self.at(self.blk, self.z, 1 - self.core)

    def peers(self, along_z, along_blk):
        out = [self.sibling()]
        if along_z:
            out += [self.at(self.blk, lax.rem(self.z + k, self.depth), self.core) for k in range(1, self.depth)]
        if along_blk:
            for m in range(1, self.blocks):
                out += [self.at(self.blk ^ m, self.z, 0), self.at(self.blk ^ m, self.z, 1)]
        return out

    def bit(self, part, step):
        return 1 << ((part + step) % self.bits)

    def widen(self, k):
        masks, out, seen = [0], [], 0
        for t in range(self.bits):
            bit = self.bit(k, t)
            out.append((bit, list(masks), seen))
            seen += len(masks)
            masks += [m ^ bit for m in masks]
        return out

    def narrow(self, k):
        out, seen = [], 0
        for t in range(self.bits):
            masks = [0]
            for u in range(t + 1, self.bits):
                masks += [m ^ self.bit(k, u) for m in masks]
            out.append((self.bit(k, t), masks, seen))
            seen += len(masks)
        return out


def greet(devices):
    barrier = pltpu.get_barrier_semaphore()
    for device in devices:
        pl.semaphore_signal(barrier, inc=1, device_id=device, device_id_type=MESH)
    pl.semaphore_wait(barrier, len(devices))


def send(src, dst, send_sem, recv_sem, device):
    pltpu.make_async_remote_copy(
        src_ref=src, dst_ref=dst, send_sem=send_sem, recv_sem=recv_sem, device_id=device, device_id_type=MESH
    ).start()


def arrived(ref, sem):
    pltpu.make_async_copy(ref, ref, sem).wait()


def gather_kernel(sizes, early, late, *refs):
    place = Place(*sizes)
    blocks, depth, seqs, share, bits = place.blocks, place.depth, place.seqs, place.share, place.bits
    blk, z, core, home = place.blk, place.z, place.core, place.home
    count = early + late
    tok, shards, refs = refs[0], refs[1 : 1 + count], refs[1 + count :]
    tok_all, fulls, refs = refs[0], refs[1 : 1 + count], refs[1 + count :]
    cols = refs[0]
    tok_s, tok_r, near_s, near_r, z_s, z_r, b_s, b_r, c_s, c_r, loc = refs[1:]
    per_seq = share // 2
    greet(place.peers(True, True))
    waits = []

    def level(k):
        return lax.rem(z + depth - k, depth)

    def slot(a, depth_at):
        return fulls[a].at[blk, depth_at, core] if a < early else fulls[a].at[depth_at]

    for a in range(early):
        for k in range(1, depth):
            send(shards[a], slot(a, z), z_s.at[a, k - 1], z_r.at[a, k - 1], place.at(blk, lax.rem(z + k, depth), core))
            waits.append((shards[a], z_s.at[a, k - 1]))
    for i in range(seqs):
        for h in range(per_seq):
            target = (core * seqs + i) * per_seq + h

            @pl.when(target != blk)
            def _(i=i, h=h, target=target):
                send(tok.at[i], tok_all.at[blk], tok_s.at[i * per_seq + h], tok_r.at[blk], place.at(target, z, core))

            @pl.when(target == blk)
            def _(i=i):
                pltpu.make_async_copy(tok.at[i], tok_all.at[blk], loc.at[0]).start()

    def forward(a, k, t):
        bit, masks, seen = place.widen(k)[t]
        for n, m in enumerate(masks):
            src = shards[a] if (m == 0 and k == 0) else fulls[a].at[blk ^ m, level(k), core]
            there = fulls[a].at[blk ^ m, level(k), core]
            send(src, there, b_s.at[a, k, seen + n], b_r.at[a, k, seen + n], place.at(blk ^ bit, z, core))
            waits.append((shards[a], b_s.at[a, k, seen + n]))

    def received(a, k, t):
        bit, masks, seen = place.widen(k)[t]
        for n, m in enumerate(masks):
            arrived(fulls[a].at[blk ^ bit ^ m, level(k), core], b_r.at[a, k, seen + n])

    for a in range(early):
        forward(a, 0, 0)
    for a in range(count):
        pltpu.make_async_copy(shards[a], slot(a, z), loc.at[1 + a]).start()
    for k in range(1, depth):
        for a in range(early):
            arrived(slot(a, level(k)), z_r.at[a, k - 1])
            forward(a, k, 0)

    for a in range(early, count):
        for k in range(1, depth):
            send(shards[a], slot(a, z), z_s.at[a, k - 1], z_r.at[a, k - 1], place.at(blk, lax.rem(z + k, depth), core))
            waits.append((shards[a], z_s.at[a, k - 1]))
    @pl.when(core == home)
    def _():
        for p in range(blocks):

            @pl.when(p != blk)
            def _():
                arrived(tok_all.at[p], tok_r.at[p])

            @pl.when(p == blk)
            def _():
                arrived(tok_all.at[p], loc.at[0])

            send(tok_all.at[p], tok_all.at[p], near_s.at[p], near_r.at[p], place.sibling())

    for a in range(early):
        arrived(shards[a], loc.at[1 + a])
    for k in range(depth):
        for t in range(bits):
            for a in range(early):
                received(a, k, t)
                if t + 1 < bits:
                    forward(a, k, t + 1)
                elif a == 0:
                    send(
                        fulls[0].at[:, level(k), core, place.other],
                        cols.at[:, level(k), core],
                        c_s.at[a, k],
                        c_r.at[a, k],
                        place.sibling(),
                    )
                    waits.append((cols.at[:, 0, 0], c_s.at[a, k]))
                    pltpu.make_async_copy(
                        fulls[0].at[:, level(k), core, place.part], cols.at[:, level(k), core], loc.at[1 + count + k]
                    ).start()
                    waits.append((cols.at[:, 0, 0], loc.at[1 + count + k]))
                else:
                    held = fulls[a].at[:, level(k), core]
                    send(held, held, c_s.at[a, k], c_r.at[a, k], place.sibling())
                    waits.append((fulls[a].at[:, 0, 0], c_s.at[a, k]))
    for k in range(depth):
        for a in range(early):
            full = cols if a == 0 else fulls[a]
            arrived(full.at[:, level(k), 1 - core], c_r.at[a, k])
    for a in range(early, count):
        arrived(shards[a], loc.at[1 + a])
        for k in range(1, depth):
            arrived(slot(a, level(k)), z_r.at[a, k - 1])
    for ref, sem in waits:
        arrived(ref, sem)

    @pl.when(core == home)
    def _():
        for p in range(blocks):
            arrived(tok_all.at[p], near_s.at[p])

    @pl.when(core != home)
    def _():
        for p in range(blocks):
            arrived(tok_all.at[p], near_r.at[p])

    for i in range(seqs):
        for h in range(per_seq):
            target = (core * seqs + i) * per_seq + h

            @pl.when(target != blk)
            def _(i=i, h=h):
                arrived(tok.at[i], tok_s.at[i * per_seq + h])


def gather(sizes, tok, shards, late_shards):
    blocks, lanes, seqs = sizes
    depth, share = lanes // 2, blocks // seqs
    early, late = len(shards), len(late_shards)
    count = early + late
    rows, width = tok.shape[1:]
    outs = [jax.ShapeDtypeStruct((blocks, rows, width), tok.dtype)]
    outs += [jax.ShapeDtypeStruct((blocks, depth, 2) + s.shape, s.dtype) for s in shards]
    outs += [jax.ShapeDtypeStruct((depth,) + s.shape, s.dtype) for s in late_shards]
    outs += [jax.ShapeDtypeStruct((blocks, depth, 2) + shards[0].shape[1:], shards[0].dtype)]
    return pl.pallas_call(
        functools.partial(gather_kernel, sizes, early, late),
        out_shape=outs,
        in_specs=[ANYWHERE] * (1 + count),
        out_specs=[ANYWHERE] * len(outs),
        scratch_shapes=[
            DMA((seqs * share // 2,)),
            DMA((blocks,)),
            DMA((blocks,)),
            DMA((blocks,)),
            DMA((count, depth - 1)),
            DMA((count, depth - 1)),
            DMA((early, depth, blocks - 1)),
            DMA((early, depth, blocks - 1)),
            DMA((early, depth)),
            DMA((early, depth)),
            DMA((1 + count + depth,)),
        ],
        compiler_params=pltpu.CompilerParams(collective_id=0, has_side_effects=True, vmem_limit_bytes=VMEM_LIMIT),
    )(tok, *shards, *late_shards)


class Spread:
    def __init__(self, place, tall, fulls, sems):
        self.place, self.tall, self.fulls = place, tall, fulls
        self.b_s, self.b_r, self.c_s, self.c_r, self.loc = sems
        self.count = len(fulls)

    @staticmethod
    def sems(count, blocks, depth):
        return [
            DMA((count, depth, blocks - 1)),
            DMA((count, depth, blocks - 1)),
            DMA((count,)),
            DMA((count,)),
            DMA((count,)),
        ]

    def start(self):
        place = self.place
        greet(place.peers(False, True))
        for a in range(self.count):
            for k in range(place.depth):
                self.forward(a, k, 0)
            pltpu.make_async_copy(self.tall[a], self.fulls[a].at[place.blk, :, place.core], self.loc.at[a]).start()

    def forward(self, a, k, t):
        place = self.place
        bit, masks, seen = place.widen(k)[t]
        for n, m in enumerate(masks):
            there = self.fulls[a].at[place.blk ^ m, k, place.core]
            src = self.tall[a].at[k] if m == 0 else there
            sems = self.b_s.at[a, k, seen + n], self.b_r.at[a, k, seen + n]
            send(src, there, *sems, place.at(place.blk ^ bit, place.z, place.core))

    def step(self, a, t):
        place = self.place
        for k in range(place.depth):
            bit, masks, seen = place.widen(k)[t]
            for n, m in enumerate(masks):
                arrived(self.fulls[a].at[place.blk ^ bit ^ m, k, place.core], self.b_r.at[a, k, seen + n])
            if t + 1 < place.bits:
                self.forward(a, k, t + 1)
        if t + 1 == place.bits:
            arrived(self.tall[a], self.loc.at[a])
            held = self.fulls[a].at[:, :, place.core]
            send(held, held, self.c_s.at[a], self.c_r.at[a], place.sibling())

    def finish(self):
        place = self.place
        for a in range(self.count):
            arrived(self.fulls[a].at[:, :, 1 - place.core], self.c_r.at[a])
            arrived(self.fulls[a].at[:, :, place.core], self.c_s.at[a])
            for k in range(place.depth):
                for n in range(place.blocks - 1):
                    arrived(self.tall[a].at[k], self.b_s.at[a, k, n])


class Fold:
    def __init__(self, place, kinds, grads, rows_in, sums, rows_out, scratch):
        self.place, self.kinds, self.grads = place, kinds, grads
        self.rows_in, self.sums, self.rows_out = rows_in, sums, rows_out
        self.count, self.moves = len(kinds), len(rows_in)
        n = self.count
        self.held, self.near, self.wide, self.tall = (scratch[i * n : i * n + n] for i in range(4))
        self.m_s, self.m_r, self.z_s, self.z_r, self.b_s, self.b_r, self.c_s, self.c_r, self.loc = scratch[4 * n :]
        self.order = list(range(1, place.depth)) + [0]
        self.units = [(a, k) for a in range(n) for k in self.order]

    @staticmethod
    def scratch(sizes, chunks, types, kinds, moves):
        blocks, lanes, seqs = sizes
        depth, share, count = lanes // 2, blocks // seqs, len(chunks)
        out = [pltpu.VMEM((blocks, depth) + c, t) for c, t in zip(chunks, types)]
        out += [
            pltpu.VMEM((1, 1, 8, 128) if kind == "columns" else (blocks, depth) + c, t)
            for c, t, kind in zip(chunks, types, kinds)
        ]
        out += [pltpu.VMEM((depth, blocks - 1) + c, t) for c, t in zip(chunks, types)]
        out += [pltpu.VMEM((depth - 1,) + c, t) for c, t in zip(chunks, types)]
        return out + [
            DMA((max(1, moves), blocks // share)),
            DMA((max(1, moves), seqs)),
            DMA((count, depth - 1)),
            DMA((count, depth - 1)),
            DMA((count, depth, blocks - 1)),
            DMA((count, depth, blocks - 1)),
            DMA((count, depth)),
            DMA((count, depth)),
            DMA((count + 1, max(depth, moves))),
        ]

    def level(self, k):
        return lax.rem(self.place.z + k, self.place.depth)

    def greet(self):
        greet(self.place.peers(True, True))

    def clear(self):
        place = self.place
        for a in range(self.count):
            if self.kinds[a] == "columns" and place.share > 2:
                held = self.held[a]
                for g in range(place.share):

                    @pl.when((g != place.part) & (g != place.other))
                    def _(held=held, g=g):
                        held[:, :, g] = jnp.zeros(held.shape[:2] + held.shape[3:], held.dtype)

    def start(self, a, k):
        place = self.place
        if self.kinds[a] == "columns":
            mine = there = self.held[a].at[:, self.level(k), place.part]
        else:
            mine = self.held[a].at[:, self.level(k)]
            there = self.near[a].at[:, self.level(k)]
        theirs = self.grads[a].at[:, self.level(k), 1 - place.core]
        send(theirs, there, self.c_s.at[a, k], self.c_r.at[a, k], place.sibling())
        pltpu.make_async_copy(self.grads[a].at[:, self.level(k), place.core], mine, self.loc.at[a, k]).start()

    def add(self, into, second):
        total = into[...].astype(jnp.float32) + second[...].astype(jnp.float32)
        into[...] = total.astype(into.dtype)

    def forward(self, a, k, t):
        place = self.place
        bit, masks, seen = place.narrow(k)[t]
        for n, m in enumerate(masks):
            sems = self.b_s.at[a, k, seen + n], self.b_r.at[a, k, seen + n]
            block = self.held[a].at[place.blk ^ bit ^ m, self.level(k)]
            send(block, self.wide[a].at[k, seen + n], *sems, place.at(place.blk ^ bit, place.z, place.core))

    def join(self, a, k):
        place = self.place
        if self.kinds[a] == "columns":
            arrived(self.held[a].at[:, self.level(k), place.part], self.loc.at[a, k])
            arrived(self.held[a].at[:, self.level(k), place.other], self.c_r.at[a, k])
        else:
            arrived(self.held[a].at[:, self.level(k)], self.loc.at[a, k])
            arrived(self.near[a].at[:, self.level(k)], self.c_r.at[a, k])

            def one(b, _):
                self.add(self.held[a].at[b, self.level(k)], self.near[a].at[b, self.level(k)])
                return 0

            lax.fori_loop(0, place.blocks, one, 0)
        self.forward(a, k, 0)

    def step(self, a, k, t):
        place = self.place
        bit, masks, seen = place.narrow(k)[t]
        for n, m in enumerate(masks):
            arrived(self.wide[a].at[k, seen + n], self.b_r.at[a, k, seen + n])
            self.add(self.held[a].at[place.blk ^ m, self.level(k)], self.wide[a].at[k, seen + n])
        if t + 1 < place.bits:
            self.forward(a, k, t + 1)
        elif k > 0:
            sems = self.z_s.at[a, k - 1], self.z_r.at[a, k - 1]
            block = self.held[a].at[place.blk, self.level(k)]
            send(block, self.tall[a].at[k - 1], *sems, place.at(place.blk, self.level(k), place.core))

    def total(self, a):
        place = self.place
        value = self.held[a][place.blk, place.z].astype(jnp.float32)
        for k in range(1, place.depth):
            arrived(self.tall[a].at[k - 1], self.z_r.at[a, k - 1])
            value = value + self.tall[a][k - 1].astype(jnp.float32)
        self.sums[a][...] = value

    def rows(self, j):
        place = self.place
        slot = lax.rem(place.seq, place.seqs)
        for t in range(place.per_part):
            source = place.part * place.per_part + t
            mine = (source == place.blk) & (place.home == place.core)

            @pl.when(mine)
            def _(t=t):
                pltpu.make_async_copy(self.rows_in[j].at[t], self.rows_out[j].at[slot], self.loc.at[self.count, j]).start()

            @pl.when(jnp.logical_not(mine))
            def _(t=t, source=source):
                sems = self.m_s.at[j, t], self.m_r.at[j, slot]
                send(self.rows_in[j].at[t], self.rows_out[j].at[slot], *sems, place.at(source, place.z, place.home))

    def finish(self):
        place = self.place
        for a, k in self.units:
            if self.kinds[a] == "columns":
                arrived(self.held[a].at[:, 0, 0], self.c_s.at[a, k])
            else:
                arrived(self.held[a].at[:, 0], self.c_s.at[a, k])
            for n in range(place.blocks - 1):
                arrived(self.held[a].at[0, 0], self.b_s.at[a, k, n])
            if k > 0:
                arrived(self.held[a].at[0, 0], self.z_s.at[a, k - 1])
        for j in range(self.moves):
            for t in range(place.per_part):
                mine = (place.part * place.per_part + t == place.blk) & (place.home == place.core)

                @pl.when(mine)
                def _(j=j, t=t):
                    arrived(self.rows_in[j].at[t], self.loc.at[self.count, j])

                @pl.when(jnp.logical_not(mine))
                def _(j=j, t=t):
                    arrived(self.rows_in[j].at[t], self.m_s.at[j, t])

            for i in range(place.seqs):
                owner = (place.core * place.seqs + i) * place.share + place.blk // place.per_part

                @pl.when(owner != place.blk * 2 + place.core)
                def _(j=j, i=i):
                    arrived(self.rows_out[j].at[i], self.m_r.at[j, i])


def fold_shapes(sizes, grads, kinds, rows):
    blocks, _, seqs = sizes
    share = blocks // seqs
    chunks = [((share,) if kind == "columns" else ()) + g.shape[3:] for g, kind in zip(grads, kinds)]
    scratch = Fold.scratch(sizes, chunks, [g.dtype for g in grads], kinds, len(rows))
    out = [jax.ShapeDtypeStruct(c, jnp.float32) for c in chunks]
    moved = [jax.ShapeDtypeStruct((seqs,) + r.shape[1:], r.dtype) for r in rows]
    return out, moved, scratch


def reduce_kernel(sizes, kinds, moves, *refs):
    count = len(kinds)
    ends = [count, count + moves, 2 * count + moves, 2 * (count + moves)]
    fold = Fold(
        Place(*sizes), kinds, refs[: ends[0]], refs[ends[0] : ends[1]], refs[ends[1] : ends[2]], refs[ends[2] : ends[3]], refs[ends[3] :]
    )
    fold.greet()
    fold.clear()
    for a, k in fold.units:
        fold.start(a, k)
    for j in range(moves):
        fold.rows(j)
    for a, k in fold.units:
        fold.join(a, k)
    for t in range(fold.place.bits):
        for a, k in fold.units:
            fold.step(a, k, t)
    for a in range(count):
        fold.total(a)
    fold.finish()


def reduce(sizes, grads, kinds, rows, cid):
    count, moves = len(grads), len(rows)
    out, moved, scratch = fold_shapes(sizes, grads, kinds, rows)
    return pl.pallas_call(
        functools.partial(reduce_kernel, sizes, kinds, moves),
        out_shape=out + moved,
        in_specs=[ANYWHERE] * (count + moves),
        out_specs=[pl.BlockSpec(memory_space=pltpu.VMEM)] * count + [ANYWHERE] * moves,
        scratch_shapes=scratch,
        compiler_params=pltpu.CompilerParams(collective_id=cid, has_side_effects=True, vmem_limit_bytes=VMEM_LIMIT),
    )(*grads, *rows)


def dot_nt(left, right):
    return lax.dot_general(left, right, (((1,), (1,)), ((), ())), preferred_element_type=jnp.float32)


def dot_nn(left, right):
    return lax.dot_general(left, right, (((1,), (0,)), ((), ())), preferred_element_type=jnp.float32)


def split_heads(dst, src):
    low = lax.broadcasted_iota(jnp.int32, src.shape, 1) < 64
    dst[0] = jnp.where(low, src, jnp.zeros_like(src))
    dst[1] = jnp.where(low, jnp.zeros_like(src), src)


def causal(bk, bq, kj, qi):
    kpos = kj * bk + lax.broadcasted_iota(jnp.int32, (bk, bq), 0)
    qpos = qi * bq + lax.broadcasted_iota(jnp.int32, (bk, bq), 1)
    return kpos <= qpos


def plan(tasks, points):
    out = {}
    for where, call in tasks:
        out.setdefault(min(points - 1, int(where * points)), []).append(call)
    return out


def pump(todo, point):
    for at, calls in todo.items():

        @pl.when(point == at)
        def _(calls=calls):
            for call in calls:
                call()


def fwd_kernel(sizes, late, block, pairs, *refs):
    q_ref, k_ref, v_ref = refs[:3]
    tall, refs = refs[3 : 3 + late], refs[3 + late :]
    att_ref, lse_ref = refs[:2]
    fulls, refs = refs[2 : 2 + late], refs[2 + late :]
    kh, vt, sems = refs[0], refs[1], refs[2:]
    pair = pl.program_id(0)
    length = q_ref.shape[0]
    count = length // block
    spread = Spread(Place(*sizes), tall, fulls, sems)
    bits = spread.place.bits
    steps = [(a, t) for t in range(bits) for a in range(late)]
    tasks = [(0.15 + 0.75 * n / len(steps), functools.partial(spread.step, a, t)) for n, (a, t) in enumerate(steps)]
    todo = plan(tasks, pairs * count)

    @pl.when(pair == 0)
    def _():
        spread.start()

    split_heads(kh, k_ref[...])
    vt[...] = v_ref[...].astype(jnp.float32).T.astype(jnp.bfloat16)

    def q_step(qi, _):
        rows = pl.ds(pl.multiple_of(qi * block, block), block)
        q_rows = q_ref[rows, :]

        def one(kj, state, masked):
            at = pl.ds(pl.multiple_of(kj * block, block), block)
            out = []
            for h in range(2):
                peak, total, acc = state[3 * h : 3 * h + 3]
                s = dot_nt(kh[h, at, :], q_rows)
                u = s * s + 1.0
                inv = lax.rsqrt(u)
                mag = u * inv
                if masked:
                    mag = jnp.where(causal(block, block, kj, qi), mag, -1e30)
                new = jnp.maximum(peak, jnp.max(mag, axis=0, keepdims=True))
                p = jnp.exp(mag - new)
                alpha = jnp.exp(peak - new)
                total = total * alpha + jnp.sum(p, axis=0, keepdims=True)
                signed = (p * (s * inv)).astype(jnp.bfloat16)
                acc = acc * alpha + dot_nn(vt[64 * h : 64 * h + 64, at], signed)
                out += [new, total, acc]
            return tuple(out)

        zero = (
            jnp.full((1, block), -1e30, jnp.float32),
            jnp.zeros((1, block), jnp.float32),
            jnp.zeros((64, block), jnp.float32),
        )
        state = one(qi, zero + zero, True)
        state = lax.fori_loop(0, qi, lambda kj, st: one(kj, st, False), state)
        both = []
        for h in range(2):
            peak, total, acc = state[3 * h : 3 * h + 3]
            both.append(acc / total)
            lse_ref[0, h : h + 1, rows] = peak + jnp.log(total)
        att_ref[rows, :] = jnp.concatenate(both, 0).T.astype(jnp.bfloat16)
        pump(todo, pair * count + qi)
        return 0

    lax.fori_loop(0, count, q_step, 0)

    @pl.when(pair == pairs - 1)
    def _():
        spread.finish()


def attend(sizes, qkv, tall, block):
    blocks, lanes, _ = sizes
    length, width = qkv.shape
    pairs = width // 384
    return pl.pallas_call(
        functools.partial(fwd_kernel, sizes, len(tall), block, pairs),
        grid=(pairs,),
        out_shape=[
            jax.ShapeDtypeStruct((length, 128 * pairs), jnp.bfloat16),
            jax.ShapeDtypeStruct((pairs, 8, length), jnp.float32),
        ]
        + [jax.ShapeDtypeStruct((blocks, lanes // 2, 2) + a.shape[1:], a.dtype) for a in tall],
        in_specs=[pl.BlockSpec((length, 128), lambda p, n=n: (0, n * pairs + p)) for n in range(3)]
        + [ANYWHERE] * len(tall),
        out_specs=[pl.BlockSpec((length, 128), lambda p: (0, p)), pl.BlockSpec((1, 8, length), lambda p: (p, 0, 0))]
        + [ANYWHERE] * len(tall),
        scratch_shapes=[pltpu.VMEM((2, length, 128), jnp.bfloat16), pltpu.VMEM((128, length), jnp.bfloat16)]
        + Spread.sems(len(tall), blocks, lanes // 2),
        compiler_params=pltpu.CompilerParams(collective_id=1, has_side_effects=True, vmem_limit_bytes=VMEM_LIMIT),
    )(qkv, qkv, qkv, *tall)


def bwd_kernel(sizes, kinds, moves, block, pairs, *refs):
    many = len(kinds)
    q_ref, k_ref, v_ref, g_ref, att_ref, lse_ref = refs[:6]
    grads, rows_in, refs = refs[6 : 6 + many], refs[6 + many : 6 + many + moves], refs[6 + many + moves :]
    out_ref = refs[0]
    sums, rows_out, refs = refs[1 : 1 + many], refs[1 + many : 1 + many + moves], refs[1 + many + moves :]
    kh, vh, qh, gh, kt, delta, dqt, dk, dv = refs[:9]
    fold = Fold(Place(*sizes), kinds, grads, rows_in, sums, rows_out, refs[9:])
    pair = pl.program_id(0)
    length = q_ref.shape[0]
    width = 128 * pairs
    count = length // block
    per_pair = count * (count + 1) // 2
    bits, units = fold.place.bits, len(fold.units)
    tasks = []
    for n, (a, k) in enumerate(fold.units):
        tasks.append((0.02 + 0.45 * n / units, functools.partial(fold.join, a, k)))
        for t in range(bits):
            where = 0.1 + 0.08 * t + (0.6 + 0.1 * t / bits) * n / units
            tasks.append((where, functools.partial(fold.step, a, k, t)))
    for j in range(moves):
        tasks.append((0.5, functools.partial(fold.rows, j)))
    tasks.sort(key=lambda task: task[0])
    todo = plan(tasks, pairs * per_pair)

    @pl.when(pair == 0)
    def _():
        fold.greet()
        for a, k in fold.units:
            fold.start(a, k)

    split_heads(kh, k_ref[...])
    split_heads(vh, v_ref[...])
    split_heads(qh, q_ref[...])
    split_heads(gh, g_ref[...])
    kt[...] = k_ref[...].astype(jnp.float32).T.astype(jnp.bfloat16)
    prod = (g_ref[...].astype(jnp.float32) * att_ref[...].astype(jnp.float32)).T
    delta[0:1, :] = jnp.sum(prod[:64], axis=0, keepdims=True)
    delta[1:2, :] = jnp.sum(prod[64:], axis=0, keepdims=True)
    dqt[...] = jnp.zeros_like(dqt)

    def k_step(kj, _):
        at = pl.ds(pl.multiple_of(kj * block, block), block)

        def one(qi, masked):
            rows = pl.ds(pl.multiple_of(qi * block, block), block)
            q_rows = q_ref[rows, :]
            g_rows = g_ref[rows, :]
            add_k = add_v = None
            for h in range(2):
                s = dot_nt(kh[h, at, :], q_rows)
                dp = dot_nt(vh[h, at, :], g_rows)
                u = s * s + 1.0
                inv = lax.rsqrt(u)
                arg = u * inv - lse_ref[0, h : h + 1, rows]
                if masked:
                    arg = jnp.where(causal(block, block, kj, qi), arg, -1e30)
                p = jnp.exp(arg)
                sgn = s * inv
                t = inv * inv * (inv - 1.0) + 1.0
                ds = (p * (dp * t - sgn * delta[h : h + 1, rows])).astype(jnp.bfloat16)
                signed = (p * sgn).astype(jnp.bfloat16)
                one_v = dot_nn(signed, gh[h, rows, :])
                one_k = dot_nn(ds, qh[h, rows, :])
                add_v = one_v if h == 0 else add_v + one_v
                add_k = one_k if h == 0 else add_k + one_k
                dqt[64 * h : 64 * h + 64, rows] += dot_nn(kt[64 * h : 64 * h + 64, at], ds)
            return add_k, add_v

        def more(qi, _):
            @pl.when(qi == kj)
            def _():
                dk[...], dv[...] = one(qi, True)

            @pl.when(qi != kj)
            def _():
                add_k, add_v = one(qi, False)
                dk[...] += add_k
                dv[...] += add_v

            pump(todo, pair * per_pair + kj * count - kj * (kj - 1) // 2 + qi - kj)
            return 0

        lax.fori_loop(kj, count, more, 0)
        out_ref[at, pl.ds(pl.multiple_of(width + pair * 128, 128), 128)] = dk[...].astype(jnp.bfloat16)
        out_ref[at, pl.ds(pl.multiple_of(2 * width + pair * 128, 128), 128)] = dv[...].astype(jnp.bfloat16)
        return 0

    lax.fori_loop(0, count, k_step, 0)
    out_ref[:, pl.ds(pl.multiple_of(pair * 128, 128), 128)] = (dqt[...] * 0.125).T.astype(jnp.bfloat16)

    @pl.when(pair == pairs - 1)
    def _():
        for a in range(many):
            fold.total(a)
        fold.finish()


def attend_back(sizes, qkv, g_att, att, lse, grads, rows, block):
    length, width = qkv.shape
    pairs = width // 384
    kinds = ["rows"] * len(grads)
    out, moved, scratch = fold_shapes(sizes, grads, kinds, rows)
    in_vmem = pl.BlockSpec(memory_space=pltpu.VMEM)
    return pl.pallas_call(
        functools.partial(bwd_kernel, sizes, kinds, len(rows), block, pairs),
        grid=(pairs,),
        out_shape=[jax.ShapeDtypeStruct((length, width), jnp.bfloat16)] + out + moved,
        in_specs=[pl.BlockSpec((length, 128), lambda p, n=n: (0, n * pairs + p)) for n in range(3)]
        + [pl.BlockSpec((length, 128), lambda p: (0, p))] * 2
        + [pl.BlockSpec((1, 8, length), lambda p: (p, 0, 0))]
        + [ANYWHERE] * (len(grads) + len(rows)),
        out_specs=[pl.BlockSpec((length, width), lambda p: (0, 0))] + [in_vmem] * len(out) + [ANYWHERE] * len(moved),
        scratch_shapes=[pltpu.VMEM((2, length, 128), jnp.bfloat16)] * 4
        + [
            pltpu.VMEM((128, length), jnp.bfloat16),
            pltpu.VMEM((8, length), jnp.float32),
            pltpu.VMEM((128, length), jnp.float32),
            pltpu.VMEM((block, 128), jnp.float32),
            pltpu.VMEM((block, 128), jnp.float32),
        ]
        + scratch,
        compiler_params=pltpu.CompilerParams(collective_id=2, has_side_effects=True, vmem_limit_bytes=VMEM_LIMIT),
    )(qkv, qkv, qkv, g_att, att, lse, *grads, *rows)


def dot_tn(left, right):
    return lax.dot_general(left, right, (((0,), (0,)), ((), ())), preferred_element_type=jnp.float32)


def centered(values):
    center = jnp.mean(values, axis=-1, keepdims=True)
    offsets = values - center
    spread = jnp.mean(offsets * offsets, axis=-1, keepdims=True)
    inverse = lax.rsqrt(spread + 1e-05)
    return offsets * inverse, inverse


def norm_back(values, grads, gain):
    unit, inverse = centered(values)
    scaled = grads * gain
    first = jnp.mean(scaled, axis=-1, keepdims=True)
    second = jnp.mean(scaled * unit, axis=-1, keepdims=True)
    back = inverse * (scaled - first - unit * second)
    return back, jnp.sum(grads * unit, axis=0, keepdims=True), jnp.sum(grads, axis=0, keepdims=True)


def gelu_parts(x):
    square = x * x
    half = 0.5 + 0.5 * jnp.tanh(0.7978845608028654 * x * (1.0 + 0.044715 * square))
    slope = half + x * (2.0 * half * (1.0 - half)) * (0.7978845608028654 + 0.1070322243 * square)
    return x * half, slope


def mlp_kernel(sizes, cols, tile, chunk, *refs):
    place = Place(*sizes)
    att, tok_all, cot, w_out, w_up, w_down, vec, live = refs[:8]
    result, g_heads, g_mid, g_out, g_up, g_down, g_vec = refs[8:15]
    (att_v, tok_v, cot_v, res_v, out_v, up_v, down_v, mid_v, n2_v, n2t_v, hid_v, slope_v, sum_v, ga_v) = refs[15:29]
    (st_out, st_up, st_down) = refs[29:32]
    a_s, a_r, g_s, g_r, cot_s, cot_r, m_s, m_r, loc, up_l, down_l, o_l = refs[32:]
    share, per_part, seqs = place.share, place.per_part, place.seqs
    part, blk, z, core = place.part, place.blk, place.z, place.core
    rows, model = mid_v.shape
    block = rows // per_part
    ff = up_v.shape[1]
    chunks, tiles = ff // chunk, rows // tile
    flat = blk * 2 + core
    partners = [((flat ^ k) // 2, z, (flat ^ k) % 2) for k in range(1, share)]
    slot_of = lax.rem(place.seq, seqs)
    greet(place.peers(False, True))
    for k in range(1, share):
        send(att.at[part ^ k], att_v.at[part], a_s.at[k - 1], a_r.at[k - 1], place.at(*partners[k - 1]))

    def local(src, dst, sem):
        pltpu.make_async_copy(src, dst, sem).start()

    local(att.at[part], att_v.at[part], loc.at[0])
    for t in range(per_part):
        local(tok_all.at[part * per_part + t], tok_v.at[t], loc.at[1 + t])
    local(w_out, out_v, loc.at[1 + per_part])
    for i in range(seqs):
        owner = (core * seqs + i) * share + blk // per_part
        slot = lax.rem(blk, per_part)

        @pl.when(owner != flat)
        def _(i=i, owner=owner, slot=slot):
            send(cot.at[i], cot_v.at[slot], cot_s.at[i], cot_r.at[slot], place.at(owner // 2, z, owner % 2))

        @pl.when(owner == flat)
        def _(i=i, slot=slot):
            local(cot.at[i], cot_v.at[slot], loc.at[2 + per_part])

    def span(f):
        return pl.ds(pl.multiple_of(f * chunk, chunk), chunk)

    for f in range(chunks):
        local(w_up.at[:, pl.ds(f * chunk, chunk)], up_v.at[:, pl.ds(f * chunk, chunk)], up_l.at[f])
        local(w_down.at[pl.ds(f * chunk, chunk)], down_v.at[pl.ds(f * chunk, chunk)], down_l.at[f])

    arrived(att_v.at[part], loc.at[0])
    for t in range(per_part):
        arrived(tok_v.at[t], loc.at[1 + t])
    arrived(out_v, loc.at[1 + per_part])
    for k in range(1, share):
        arrived(att_v.at[part ^ k], a_r.at[k - 1])
    gain, shift = vec[2:3, :], vec[3:4, :]
    per_block = block // tile

    def spot(i):
        return i // per_block, pl.ds(pl.multiple_of(lax.rem(i, per_block) * tile, tile), tile)

    def enter(i, _):
        at = pl.ds(pl.multiple_of(i * tile, tile), tile)
        branch = dot_nn(att_v[0, at, :cols], out_v[:cols, :])
        for g in range(1, share):
            branch = branch + dot_nn(att_v[g, at, :cols], out_v[g * cols : (g + 1) * cols, :])
        t, inside = spot(i)
        middle = tok_v[t, inside, :].astype(jnp.float32) + live[at, :] * branch
        mid_v[at, :] = middle
        unit, _ = centered(middle)
        normed = unit * gain + shift
        n2_v[at, :] = normed.astype(jnp.bfloat16)
        n2t_v[:, at] = normed.T.astype(jnp.bfloat16)
        return 0

    lax.fori_loop(0, tiles, enter, 0)
    sum_v[...] = mid_v[...]

    def up_step(f, _):
        arrived(up_v.at[:, span(f)], up_l.at[f])
        arrived(down_v.at[span(f)], down_l.at[f])
        hidden, slope = gelu_parts(dot_nn(n2_v[...], up_v[:, span(f)]))
        hidden = hidden.astype(jnp.bfloat16)
        hid_v[:, span(f)] = hidden
        slope_v[:, span(f)] = slope.astype(jnp.bfloat16)
        sum_v[...] += dot_nn(hidden, down_v[span(f), :])
        return 0

    lax.fori_loop(0, chunks, up_step, 0)
    for t in range(per_part):
        res_v[t] = sum_v[t * block : (t + 1) * block, :].astype(jnp.bfloat16)
        source = part * per_part + t
        mine = (source == blk) & (place.home == core)

        @pl.when(mine)
        def _(t=t):
            local(res_v.at[t], result.at[slot_of], loc.at[0])

        @pl.when(jnp.logical_not(mine))
        def _(t=t, source=source):
            send(res_v.at[t], result.at[slot_of], m_s.at[t], m_r.at[slot_of], place.at(source, z, place.home))

    for t in range(per_part):
        mine = (part * per_part + t == blk) & (place.home == core)

        @pl.when(mine)
        def _(t=t):
            arrived(cot_v.at[t], loc.at[2 + per_part])

        @pl.when(jnp.logical_not(mine))
        def _(t=t):
            arrived(cot_v.at[t], cot_r.at[t])

    sum_v[...] = jnp.zeros_like(sum_v)

    def back_step(f, _):
        top = cot_v[...].reshape(rows, model)
        grad_pre = (dot_nt(top, down_v[span(f), :]) * slope_v[:, span(f)].astype(jnp.float32)).astype(jnp.bfloat16)
        now = lax.rem(f, 2)

        @pl.when(f >= 2)
        def _():
            arrived(st_down.at[now], o_l.at[now])
            arrived(st_up.at[now], o_l.at[2 + now])

        st_down[now] = dot_tn(hid_v[:, span(f)], top).astype(jnp.bfloat16)
        st_up[now] = dot_nn(n2t_v[...], grad_pre).astype(jnp.bfloat16)
        local(st_down.at[now], g_down.at[span(f)], o_l.at[now])
        local(st_up.at[now], g_up.at[:, span(f)], o_l.at[2 + now])
        sum_v[...] += dot_nt(grad_pre, up_v[:, span(f)])
        return 0

    lax.fori_loop(0, chunks, back_step, 0)
    g_vec[...] = jnp.zeros_like(g_vec)

    def leave(i, _):
        at = pl.ds(pl.multiple_of(i * tile, tile), tile)
        t, inside = spot(i)
        back, d_gain, d_shift = norm_back(mid_v[at, :], sum_v[at, :], gain)
        g_vec[0:1, :] += d_gain
        g_vec[1:2, :] += d_shift
        total = cot_v[t, inside, :].astype(jnp.float32) + back
        mid_v[at, :] = total
        branch = (live[at, :] * total).astype(jnp.bfloat16)
        n2_v[at, :] = branch
        heads = dot_nt(branch, out_v[...]).astype(jnp.bfloat16)
        for g in range(share):
            if cols == ga_v.shape[2]:
                ga_v[g, at, :] = heads[:, g * cols : (g + 1) * cols]
            else:
                piece = heads[:, g * cols : (g + 1) * cols]
                ga_v[g, at, :] = jnp.concatenate([piece, jnp.zeros((tile, ga_v.shape[2] - cols), jnp.bfloat16)], 1)
        return 0

    lax.fori_loop(0, tiles, leave, 0)
    for k in range(1, share):
        send(ga_v.at[part ^ k], g_heads.at[part], g_s.at[k - 1], g_r.at[k - 1], place.at(*partners[k - 1]))
    local(ga_v.at[part], g_heads.at[part], loc.at[1])
    local(mid_v, g_mid, loc.at[2])
    for g in range(share):
        st_out[g * cols : (g + 1) * cols, :] = dot_tn(att_v[g, :, :cols], n2_v[...]).astype(jnp.bfloat16)
    local(st_out, g_out, loc.at[1 + per_part])
    for n in range(min(2, chunks)):
        arrived(st_down.at[n], o_l.at[n])
        arrived(st_up.at[n], o_l.at[2 + n])
    arrived(st_out, loc.at[1 + per_part])
    arrived(mid_v, loc.at[2])
    arrived(ga_v.at[part], loc.at[1])
    for k in range(1, share):
        arrived(att.at[part ^ k], a_s.at[k - 1])
        arrived(ga_v.at[part ^ k], g_s.at[k - 1])
        arrived(g_heads.at[part ^ k], g_r.at[k - 1])
    for i in range(seqs):
        owner = (core * seqs + i) * share + blk // per_part

        @pl.when(owner != flat)
        def _(i=i):
            arrived(cot.at[i], cot_s.at[i])
            arrived(result.at[i], m_r.at[i])

    for t in range(per_part):
        mine = (part * per_part + t == blk) & (place.home == core)

        @pl.when(mine)
        def _(t=t):
            arrived(res_v.at[t], loc.at[0])

        @pl.when(jnp.logical_not(mine))
        def _(t=t):
            arrived(res_v.at[t], m_s.at[t])


def feed_forward(sizes, cols, att, tok_all, cot, w_out, w_up, w_down, vec, live, tile, chunk):
    blocks, lanes, seqs = sizes
    share = blocks // seqs
    per_part = blocks // share
    block, model = tok_all.shape[1:]
    rows = per_part * block
    wide = att.shape[2]
    ff = w_up.shape[1]
    chunks = ff // chunk
    in_vmem = pl.BlockSpec(memory_space=pltpu.VMEM)
    low, full = jnp.bfloat16, jnp.float32
    return pl.pallas_call(
        functools.partial(mlp_kernel, sizes, cols, tile, chunk),
        out_shape=[
            jax.ShapeDtypeStruct((seqs, block, model), low),
            jax.ShapeDtypeStruct((share, rows, wide), low),
            jax.ShapeDtypeStruct((rows, model), full),
            jax.ShapeDtypeStruct((model, model), low),
            jax.ShapeDtypeStruct((model, ff), low),
            jax.ShapeDtypeStruct((ff, model), low),
            jax.ShapeDtypeStruct((8, model), full),
        ],
        in_specs=[ANYWHERE] * 6 + [in_vmem] * 2,
        out_specs=[ANYWHERE] * 6 + [in_vmem],
        scratch_shapes=[
            pltpu.VMEM((share, rows, wide), low),
            pltpu.VMEM((per_part, block, model), low),
            pltpu.VMEM((per_part, block, model), low),
            pltpu.VMEM((per_part, block, model), low),
            pltpu.VMEM((model, model), low),
            pltpu.VMEM((model, ff), low),
            pltpu.VMEM((ff, model), low),
            pltpu.VMEM((rows, model), full),
            pltpu.VMEM((rows, model), low),
            pltpu.VMEM((model, rows), low),
            pltpu.VMEM((rows, ff), low),
            pltpu.VMEM((rows, ff), low),
            pltpu.VMEM((rows, model), full),
            pltpu.VMEM((share, rows, wide), low),
            pltpu.VMEM((model, model), low),
            pltpu.VMEM((2, model, chunk), low),
            pltpu.VMEM((2, chunk, model), low),
            DMA((share,)),
            DMA((share,)),
            DMA((share,)),
            DMA((share,)),
            DMA((seqs,)),
            DMA((per_part,)),
            DMA((per_part,)),
            DMA((seqs,)),
            DMA((3 + per_part,)),
            DMA((chunks,)),
            DMA((chunks,)),
            DMA((4,)),
        ],
        compiler_params=pltpu.CompilerParams(collective_id=4, has_side_effects=True, vmem_limit_bytes=VMEM_LIMIT),
    )(att, tok_all, cot, w_out, w_up, w_down, vec, live)


def normalize(values, gain, shift):
    center = jnp.mean(values, axis=-1, keepdims=True)
    offsets = values - center
    spread = jnp.mean(offsets * offsets, axis=-1, keepdims=True)
    return offsets * lax.rsqrt(spread + 1e-05) * gain + shift


def dot(left, right, at_left, at_right):
    return lax.dot_general(left, right, (((at_left,), (at_right,)), ((), ())), preferred_element_type=jnp.float32)


def swap(values, share, blocks, lanes, part):
    flat = blocks * lanes

    def number(blk, z, core):
        return blk * lanes + z * 2 + core

    pieces = [lax.dynamic_index_in_dim(values, part, 0, False)]
    for step in range(1, share):
        pairs = []
        for blk in range(blocks):
            for z in range(lanes // 2):
                for core in range(2):
                    other = (blk * 2 + core) ^ step
                    pairs.append((number(blk, z, core), number(other // 2, z, other % 2)))
        piece = lax.dynamic_index_in_dim(values, part ^ step, 0, False)
        pieces.append(lax.ppermute(piece, ("blk", "seq"), pairs))
    ordered = []
    for g in range(share):
        got = pieces[0]
        for step in range(1, share):
            got = jnp.where((part ^ step) == g, pieces[step], got)
        ordered.append(got)
    return ordered


def shards(sizes, tokens, seq_len, ln1_gain, ln1_shift, w_qkv, w_out, ln2_gain, ln2_shift, w_up, w_down, cotangent):
    blocks, lanes, seqs = sizes
    devices = blocks * lanes
    place = Place(*sizes)
    share, part = place.share, place.part
    model = tokens.shape[2]
    length = blocks * tokens.shape[1]
    rows = length // share
    owned = w_qkv.shape[0]
    cols = model // share
    wide = -(-cols // 128) * 128
    real = cols // 64

    grouped = w_qkv.reshape(owned, 3, share, cols)
    grouped = jnp.pad(grouped, ((0, 0), (0, 0), (0, 0), (0, wide - cols)))
    grouped = jnp.transpose(grouped, (2, 0, 1, 3)).reshape(share, owned, 3 * wide)
    vec = jnp.stack([ln1_gain, ln1_shift, ln2_gain, ln2_shift]).astype(jnp.float32)
    vec = jnp.pad(vec, ((0, 4), (0, 128 - owned)))
    vec = vec.at[4, :seqs].set(seq_len.astype(jnp.float32))
    outs = gather(sizes, tokens, [grouped, vec], [w_out, w_up, w_down])
    tok_all, _, vec_all, *tall, qkv_cols = outs
    qkv_cols = qkv_cols.reshape(model, -1)
    params = jnp.swapaxes(vec_all.reshape(devices, 8, 128)[:, :4, :owned], 0, 1).reshape(4, model)
    gain_one, shift_one, gain_two, shift_two = params
    lens = lax.dynamic_index_in_dim(vec_all[0], place.z, 0, False)[:, 4, :seqs].reshape(2 * seqs)
    my_len = lax.dynamic_index_in_dim(lens, place.seq, 0, False)

    inputs = tok_all.reshape(length, model).astype(jnp.float32)
    normed = normalize(inputs, gain_one, shift_one).astype(jnp.bfloat16)
    scale = jnp.where(jnp.arange(3 * wide) < wide, 0.125, 1.0)
    qkv = (dot(normed, qkv_cols, 1, 0) * scale).astype(jnp.bfloat16)
    att, lse, out_full, up_full, down_full = attend(sizes, qkv, tall, 512)
    out_full, up_full, down_full = [a.reshape(model, -1) for a in (out_full, up_full)] + [down_full.reshape(-1, model)]
    positions = part * rows + jnp.arange(rows, dtype=jnp.int32)
    live = (positions.astype(jnp.float32) < my_len).astype(jnp.float32)[:, None]
    result, g_heads, grad_mid, grad_out, grad_up, grad_down, two_grads = feed_forward(
        sizes,
        cols,
        att.reshape(share, rows, wide),
        tok_all,
        cotangent,
        out_full,
        up_full,
        down_full,
        jnp.pad(params, ((0, 4), (0, 0))),
        live,
        min(256, tokens.shape[1]),
        min(512, w_up.shape[1]),
    )
    grad_gain_two, grad_shift_two = two_grads[0], two_grads[1]
    mine = lax.dynamic_slice_in_dim(tok_all.reshape(length, model), part * rows, rows, 0).astype(jnp.float32)
    per_part = blocks // share

    def cut(values):
        return values.reshape((blocks, lanes // 2, 2, -1) + values.shape[1:])

    g_qkv, sum_out, sum_up, sum_down = attend_back(
        sizes,
        qkv,
        g_heads.reshape(length, wide),
        att,
        lse,
        [cut(grad_out), cut(grad_up), cut(grad_down)],
        [],
        512,
    )
    grad_qkv = dot(normed, g_qkv, 0, 0).astype(jnp.bfloat16)
    partial = dot(g_qkv, qkv_cols, 1, 1)
    one_parts = swap(partial.astype(jnp.bfloat16).reshape(share, rows, model), share, blocks, lanes, part)
    grad_one = one_parts[0].astype(jnp.float32)
    for other in one_parts[1:]:
        grad_one = grad_one + other.astype(jnp.float32)
    pull_one = jax.vjp(normalize, mine, gain_one, shift_one)[1]
    grad_norm, grad_gain_one, grad_shift_one = pull_one(grad_one)
    grad_tokens = (grad_mid + grad_norm).astype(jnp.bfloat16)

    vec_grads = jnp.stack([grad_gain_one, grad_shift_one, grad_gain_two, grad_shift_two]).reshape(4, devices, owned)
    vec_grads = jnp.pad(jnp.swapaxes(vec_grads, 0, 1), ((0, 0), (0, 4), (0, 128 - owned)))

    sum_qkv, sum_vec, grad_tokens = reduce(
        sizes,
        [cut(grad_qkv), vec_grads.reshape(blocks, lanes // 2, 2, 8, 128)],
        ["columns", "rows"],
        [grad_tokens.reshape(per_part, -1, model)],
        3,
    )
    sum_qkv = jnp.transpose(sum_qkv.reshape(share, owned, 3, wide)[..., :cols], (1, 2, 0, 3)).reshape(owned, 3 * model)
    return (
        result,
        grad_tokens.astype(jnp.float32),
        sum_vec[0, :owned],
        sum_vec[1, :owned],
        sum_qkv,
        sum_out,
        sum_vec[2, :owned],
        sum_vec[3, :owned],
        sum_up,
        sum_down,
    )


def solution(mesh):
    blocks, lanes = mesh.shape["blk"], mesh.shape["seq"]
    whole = P(("blk", "seq"))
    rows = P(("blk", "seq"), None)
    tokens = P("seq", "blk", None)

    def run(*args):
        seqs = args[0].shape[0] // lanes
        return jax.shard_map(
            functools.partial(shards, (blocks, lanes, seqs)),
            mesh=mesh,
            in_specs=(tokens, P("seq"), whole, whole, rows, rows, whole, whole, rows, rows, tokens),
            out_specs=(tokens, tokens, whole, whole, rows, rows, whole, whole, rows, rows),
            check_vma=False,
        )(*args)

    return run
```

```python
import functools

import jax
import jax.numpy as jnp
from jax import lax
from jax.experimental import pallas as pl
from jax.experimental.pallas import tpu as pltpu
from jax.sharding import PartitionSpec as P

HEADS = 12
VMEM_LIMIT = 60 * 2**20


MESH = pl.DeviceIdType.MESH
DMA = pltpu.SemaphoreType.DMA
ANYWHERE = pl.BlockSpec(memory_space=pl.ANY)


class Place:
    def __init__(self, blocks, lanes, seqs):
        self.blocks, self.depth, self.seqs = blocks, lanes // 2, seqs
        self.share = blocks // seqs
        self.per_part = blocks // self.share
        self.bits = max(1, blocks.bit_length() - 1)
        self.blk = lax.axis_index("blk")
        lane = lax.axis_index("seq")
        self.z, self.core = lane // 2, lane % 2
        flat = self.blk * 2 + self.core
        self.seq, self.part = flat // self.share, flat % self.share
        self.home = self.seq // seqs
        self.other = lax.rem(self.blk * 2 + 1 - self.core, self.share)

    def at(self, blk, z, core):
        return (blk, z * 2 + core)

    def sibling(self):
        return self.at(self.blk, self.z, 1 - self.core)

    def peers(self, along_z, along_blk):
        out = [self.sibling()]
        if along_z:
            out += [self.at(self.blk, lax.rem(self.z + k, self.depth), self.core) for k in range(1, self.depth)]
        if along_blk:
            for m in range(1, self.blocks):
                out += [self.at(self.blk ^ m, self.z, 0), self.at(self.blk ^ m, self.z, 1)]
        return out

    def bit(self, part, step):
        return 1 << ((part + step) % self.bits)

    def widen(self, k):
        masks, out, seen = [0], [], 0
        for t in range(self.bits):
            bit = self.bit(k, t)
            out.append((bit, list(masks), seen))
            seen += len(masks)
            masks += [m ^ bit for m in masks]
        return out

    def narrow(self, k):
        out, seen = [], 0
        for t in range(self.bits):
            masks = [0]
            for u in range(t + 1, self.bits):
                masks += [m ^ self.bit(k, u) for m in masks]
            out.append((self.bit(k, t), masks, seen))
            seen += len(masks)
        return out


def greet(devices):
    barrier = pltpu.get_barrier_semaphore()
    for device in devices:
        pl.semaphore_signal(barrier, inc=1, device_id=device, device_id_type=MESH)
    pl.semaphore_wait(barrier, len(devices))


def send(src, dst, send_sem, recv_sem, device):
    pltpu.make_async_remote_copy(
        src_ref=src, dst_ref=dst, send_sem=send_sem, recv_sem=recv_sem, device_id=device, device_id_type=MESH
    ).start()


def arrived(ref, sem):
    pltpu.make_async_copy(ref, ref, sem).wait()


class Fold:
    def __init__(self, place, kinds, grads, rows_in, sums, rows_out, scratch):
        self.place, self.kinds, self.grads = place, kinds, grads
        self.rows_in, self.sums, self.rows_out = rows_in, sums, rows_out
        self.count, self.moves = len(kinds), len(rows_in)
        n = self.count
        self.held, self.near, self.wide, self.tall = (scratch[i * n : i * n + n] for i in range(4))
        self.m_s, self.m_r, self.z_s, self.z_r, self.b_s, self.b_r, self.c_s, self.c_r, self.loc = scratch[4 * n :]
        self.order = list(range(1, place.depth)) + [0]
        self.units = [(a, k) for a in range(n) for k in self.order]

    @staticmethod
    def scratch(sizes, chunks, types, kinds, moves):
        blocks, lanes, seqs = sizes
        depth, share, count = lanes // 2, blocks // seqs, len(chunks)
        out = [pltpu.VMEM((blocks, depth) + c, t) for c, t in zip(chunks, types)]
        out += [
            pltpu.VMEM((1, 1, 8, 128) if kind == "columns" else (blocks, depth) + c, t)
            for c, t, kind in zip(chunks, types, kinds)
        ]
        out += [pltpu.VMEM((depth, blocks - 1) + c, t) for c, t in zip(chunks, types)]
        out += [pltpu.VMEM((depth - 1,) + c, t) for c, t in zip(chunks, types)]
        return out + [
            DMA((max(1, moves), blocks // share)),
            DMA((max(1, moves), seqs)),
            DMA((count, depth - 1)),
            DMA((count, depth - 1)),
            DMA((count, depth, blocks - 1)),
            DMA((count, depth, blocks - 1)),
            DMA((count, depth)),
            DMA((count, depth)),
            DMA((count + 1, max(depth, moves))),
        ]

    def level(self, k):
        return lax.rem(self.place.z + k, self.place.depth)

    def greet(self):
        greet(self.place.peers(True, True))

    def clear(self):
        place = self.place
        for a in range(self.count):
            if self.kinds[a] == "columns" and place.share > 2:
                held = self.held[a]
                for g in range(place.share):

                    @pl.when((g != place.part) & (g != place.other))
                    def _(held=held, g=g):
                        held[:, :, g] = jnp.zeros(held.shape[:2] + held.shape[3:], held.dtype)

    def start(self, a, k):
        place = self.place
        if self.kinds[a] == "columns":
            mine = there = self.held[a].at[:, self.level(k), place.part]
        else:
            mine = self.held[a].at[:, self.level(k)]
            there = self.near[a].at[:, self.level(k)]
        theirs = self.grads[a].at[:, self.level(k), 1 - place.core]
        send(theirs, there, self.c_s.at[a, k], self.c_r.at[a, k], place.sibling())
        pltpu.make_async_copy(self.grads[a].at[:, self.level(k), place.core], mine, self.loc.at[a, k]).start()

    def add(self, into, second):
        total = into[...].astype(jnp.float32) + second[...].astype(jnp.float32)
        into[...] = total.astype(into.dtype)

    def forward(self, a, k, t):
        place = self.place
        bit, masks, seen = place.narrow(k)[t]
        for n, m in enumerate(masks):
            sems = self.b_s.at[a, k, seen + n], self.b_r.at[a, k, seen + n]
            block = self.held[a].at[place.blk ^ bit ^ m, self.level(k)]
            send(block, self.wide[a].at[k, seen + n], *sems, place.at(place.blk ^ bit, place.z, place.core))

    def join(self, a, k):
        place = self.place
        if self.kinds[a] == "columns":
            arrived(self.held[a].at[:, self.level(k), place.part], self.loc.at[a, k])
            arrived(self.held[a].at[:, self.level(k), place.other], self.c_r.at[a, k])
        else:
            arrived(self.held[a].at[:, self.level(k)], self.loc.at[a, k])
            arrived(self.near[a].at[:, self.level(k)], self.c_r.at[a, k])

            def one(b, _):
                self.add(self.held[a].at[b, self.level(k)], self.near[a].at[b, self.level(k)])
                return 0

            lax.fori_loop(0, place.blocks, one, 0)
        self.forward(a, k, 0)

    def step(self, a, k, t):
        place = self.place
        bit, masks, seen = place.narrow(k)[t]
        for n, m in enumerate(masks):
            arrived(self.wide[a].at[k, seen + n], self.b_r.at[a, k, seen + n])
            self.add(self.held[a].at[place.blk ^ m, self.level(k)], self.wide[a].at[k, seen + n])
        if t + 1 < place.bits:
            self.forward(a, k, t + 1)
        elif k > 0:
            sems = self.z_s.at[a, k - 1], self.z_r.at[a, k - 1]
            block = self.held[a].at[place.blk, self.level(k)]
            send(block, self.tall[a].at[k - 1], *sems, place.at(place.blk, self.level(k), place.core))

    def total(self, a):
        place = self.place
        value = self.held[a][place.blk, place.z].astype(jnp.float32)
        for k in range(1, place.depth):
            arrived(self.tall[a].at[k - 1], self.z_r.at[a, k - 1])
            value = value + self.tall[a][k - 1].astype(jnp.float32)
        self.sums[a][...] = value

    def rows(self, j):
        place = self.place
        slot = lax.rem(place.seq, place.seqs)
        for t in range(place.per_part):
            source = place.part * place.per_part + t
            mine = (source == place.blk) & (place.home == place.core)

            @pl.when(mine)
            def _(t=t):
                pltpu.make_async_copy(self.rows_in[j].at[t], self.rows_out[j].at[slot], self.loc.at[self.count, j]).start()

            @pl.when(jnp.logical_not(mine))
            def _(t=t, source=source):
                sems = self.m_s.at[j, t], self.m_r.at[j, slot]
                send(self.rows_in[j].at[t], self.rows_out[j].at[slot], *sems, place.at(source, place.z, place.home))

    def finish(self):
        place = self.place
        for a, k in self.units:
            if self.kinds[a] == "columns":
                arrived(self.held[a].at[:, 0, 0], self.c_s.at[a, k])
            else:
                arrived(self.held[a].at[:, 0], self.c_s.at[a, k])
            for n in range(place.blocks - 1):
                arrived(self.held[a].at[0, 0], self.b_s.at[a, k, n])
            if k > 0:
                arrived(self.held[a].at[0, 0], self.z_s.at[a, k - 1])
        for j in range(self.moves):
            for t in range(place.per_part):
                mine = (place.part * place.per_part + t == place.blk) & (place.home == place.core)

                @pl.when(mine)
                def _(j=j, t=t):
                    arrived(self.rows_in[j].at[t], self.loc.at[self.count, j])

                @pl.when(jnp.logical_not(mine))
                def _(j=j, t=t):
                    arrived(self.rows_in[j].at[t], self.m_s.at[j, t])

            for i in range(place.seqs):
                owner = (place.core * place.seqs + i) * place.share + place.blk // place.per_part

                @pl.when(owner != place.blk * 2 + place.core)
                def _(j=j, i=i):
                    arrived(self.rows_out[j].at[i], self.m_r.at[j, i])


def fold_shapes(sizes, grads, kinds, rows):
    blocks, _, seqs = sizes
    share = blocks // seqs
    chunks = [((share,) if kind == "columns" else ()) + g.shape[3:] for g, kind in zip(grads, kinds)]
    scratch = Fold.scratch(sizes, chunks, [g.dtype for g in grads], kinds, len(rows))
    out = [jax.ShapeDtypeStruct(c, jnp.float32) for c in chunks]
    moved = [jax.ShapeDtypeStruct((seqs,) + r.shape[1:], r.dtype) for r in rows]
    return out, moved, scratch


def dot_nt(left, right):
    return lax.dot_general(left, right, (((1,), (1,)), ((), ())), preferred_element_type=jnp.float32)


def dot_nn(left, right):
    return lax.dot_general(left, right, (((1,), (0,)), ((), ())), preferred_element_type=jnp.float32)


def split_heads(dst, src):
    low = lax.broadcasted_iota(jnp.int32, src.shape, 1) < 64
    dst[0] = jnp.where(low, src, jnp.zeros_like(src))
    dst[1] = jnp.where(low, jnp.zeros_like(src), src)


def causal(bk, bq, kj, qi):
    kpos = kj * bk + lax.broadcasted_iota(jnp.int32, (bk, bq), 0)
    qpos = qi * bq + lax.broadcasted_iota(jnp.int32, (bk, bq), 1)
    return kpos <= qpos


def plan(tasks, points):
    out = {}
    for where, call in tasks:
        out.setdefault(min(points - 1, int(where * points)), []).append(call)
    return out


def pump(todo, point):
    for at, calls in todo.items():

        @pl.when(point == at)
        def _(calls=calls):
            for call in calls:
                call()


class Total:
    def __init__(self, place, stages, from_z, from_blk, from_core, sems):
        self.place, self.stages = place, stages
        self.from_z, self.from_blk, self.from_core = from_z, from_blk, from_core
        self.z_s, self.z_r, self.b_s, self.b_r, self.c_s, self.c_r = sems

    @staticmethod
    def scratch(sizes, shape):
        blocks, lanes, _ = sizes
        depth, bits = lanes // 2, max(1, blocks.bit_length() - 1)
        return [
            pltpu.VMEM((2 + bits,) + shape, jnp.float32),
            pltpu.VMEM((depth - 1,) + shape, jnp.float32),
            pltpu.VMEM((bits,) + shape, jnp.float32),
            pltpu.VMEM(shape, jnp.float32),
            DMA((depth - 1,)),
            DMA((depth - 1,)),
            DMA((bits,)),
            DMA((bits,)),
            DMA((1,)),
            DMA((1,)),
        ]

    def start(self):
        place = self.place
        for k in range(1, place.depth):
            target = place.at(place.blk, lax.rem(place.z + k, place.depth), place.core)
            send(self.stages.at[0], self.from_z.at[k - 1], self.z_s.at[k - 1], self.z_r.at[k - 1], target)

    def step(self, n):
        place = self.place
        if n == 0:
            value = self.stages[0]
            for k in range(1, place.depth):
                arrived(self.from_z.at[k - 1], self.z_r.at[k - 1])
                value = value + self.from_z[k - 1]
        else:
            arrived(self.from_blk.at[n - 1], self.b_r.at[n - 1])
            value = self.stages[n] + self.from_blk[n - 1]
        self.stages[n + 1] = value
        if n < place.bits:
            target = place.at(place.blk ^ (1 << n), place.z, place.core)
            send(self.stages.at[n + 1], self.from_blk.at[n], self.b_s.at[n], self.b_r.at[n], target)
        else:
            send(self.stages.at[n + 1], self.from_core, self.c_s.at[0], self.c_r.at[0], place.sibling())

    def finish(self):
        place = self.place
        arrived(self.from_core, self.c_r.at[0])
        value = self.stages[place.bits + 1] + self.from_core[...]
        arrived(self.from_core, self.c_s.at[0])
        for n in range(place.bits):
            arrived(self.from_core, self.b_s.at[n])
        for k in range(1, place.depth):
            arrived(self.from_core, self.z_s.at[k - 1])
        return value


class Gather:
    def __init__(self, place, shard, full, sems, only=None):
        self.place, self.shard, self.full, self.only = place, shard, full, only
        self.z_s, self.z_r, self.b_s, self.b_r, self.c_s, self.c_r, self.loc = sems

    @staticmethod
    def sems(sizes):
        blocks, lanes, _ = sizes
        depth = lanes // 2
        return [
            DMA((depth,)),
            DMA((depth,)),
            DMA((depth, blocks - 1)),
            DMA((depth, blocks - 1)),
            DMA((depth,)),
            DMA((depth,)),
            DMA((1 + depth,)),
        ]

    def level(self, k):
        return lax.rem(self.place.z + self.place.depth - k, self.place.depth)

    def chunk(self, blk, k):
        return self.full.at[blk, self.level(k), self.place.core]

    def start(self):
        place = self.place
        for k in range(1, place.depth):
            target = place.at(place.blk, lax.rem(place.z + k, place.depth), place.core)
            send(self.shard, self.chunk(place.blk, 0), self.z_s.at[k], self.z_r.at[k], target)

    def keep(self):
        pltpu.make_async_copy(self.shard, self.chunk(self.place.blk, 0), self.loc.at[0]).start()

    def forward(self, k, t):
        place = self.place
        bit, masks, seen = place.widen(k)[t]
        for n, m in enumerate(masks):
            there = self.chunk(place.blk ^ m, k)
            src = self.shard if m == 0 and k == 0 else there
            send(src, there, self.b_s.at[k, seen + n], self.b_r.at[k, seen + n], place.at(place.blk ^ bit, place.z, place.core))

    def climb(self, k):
        if k > 0:
            arrived(self.chunk(self.place.blk, k), self.z_r.at[k])
        self.forward(k, 0)

    def step(self, k, t):
        place = self.place
        bit, masks, seen = place.widen(k)[t]
        for n, m in enumerate(masks):
            arrived(self.chunk(place.blk ^ bit ^ m, k), self.b_r.at[k, seen + n])
        if t + 1 < place.bits:
            self.forward(k, t + 1)
        else:
            self.swap(k)

    def swap(self, k):
        place = self.place
        if k == 0:
            arrived(self.shard, self.loc.at[0])
        if self.only is None:
            held = self.full.at[:, self.level(k), place.core]
            send(held, held, self.c_s.at[k], self.c_r.at[k], place.sibling())
        else:
            there = self.only.at[:, self.level(k), place.core]
            send(self.full.at[:, self.level(k), place.core, place.other], there, self.c_s.at[k], self.c_r.at[k], place.sibling())
            mine = self.full.at[:, self.level(k), place.core, place.part]
            pltpu.make_async_copy(mine, there, self.loc.at[1 + k]).start()

    def wait_swap(self, k):
        place = self.place
        if self.only is None:
            arrived(self.full.at[:, self.level(k), 1 - place.core], self.c_r.at[k])
        else:
            arrived(self.only.at[:, self.level(k), 1 - place.core], self.c_r.at[k])
            arrived(self.only.at[:, self.level(k), place.core], self.loc.at[1 + k])

    def finish(self):
        place = self.place
        for k in range(place.depth):
            if self.only is None:
                self.wait_swap(k)
                arrived(self.full.at[:, 0, 0], self.c_s.at[k])
            else:
                arrived(self.only.at[:, 0, 0], self.c_s.at[k])
            if k > 0:
                arrived(self.shard, self.z_s.at[k])
            for n in range(place.blocks - 1):
                arrived(self.shard, self.b_s.at[k, n])


class GatherAcross(Gather):
    def start(self):
        place = self.place
        for m in range(1, place.blocks):
            target = place.at(place.blk ^ m, place.z, place.core)
            send(self.shard, self.chunk(place.blk, 0), self.b_s.at[0, m - 1], self.b_r.at[0, m - 1], target)

    def climb(self):
        place = self.place
        for m in range(1, place.blocks):
            arrived(self.chunk(place.blk ^ m, 0), self.b_r.at[0, m - 1])
        arrived(self.shard, self.loc.at[0])
        held = self.full.at[:, place.z, place.core]
        for k in range(1, place.depth):
            target = place.at(place.blk, lax.rem(place.z + k, place.depth), place.core)
            send(held, held, self.z_s.at[k], self.z_r.at[k], target)
        self.pass_on(0)

    def pass_on(self, k):
        held = self.full.at[:, self.level(k), self.place.core]
        if k > 0:
            arrived(held, self.z_r.at[k])
        send(held, held, self.c_s.at[k], self.c_r.at[k], self.place.sibling())

    def finish(self):
        place = self.place
        for k in range(place.depth):
            self.wait_swap(k)
            arrived(self.full.at[:, 0, 0], self.c_s.at[k])
            if k > 0:
                arrived(self.full.at[:, 0, 0], self.z_s.at[k])
        for m in range(1, place.blocks):
            arrived(self.shard, self.b_s.at[0, m - 1])


def first_kernel(sizes, block, pairs, *refs):
    place = Place(*sizes)
    tok, vec, w_qkv, w_out, w_up, w_down = refs[:6]
    att_ref, lse_ref, tok_own, normed_out, qkv_out, cols_out, vec_out, stage, out_full, up_full, down_full = refs[6:17]
    tok_v, norm_v, norm_t, chunk_v, w32_v, cols_v, qkv_v, kh, vt, run_m, run_l, run_a = refs[17:29]
    tok_s, tok_r, near_s, near_r, loc = refs[29:34]
    total = Total(place, *refs[34:38], refs[38:44])
    qkv = Gather(place, w_qkv, stage, refs[44:51], chunk_v)
    outw = Gather(place, w_out, out_full, refs[51:58])
    upw = Gather(place, w_up, up_full, refs[58:65])
    downw = GatherAcross(place, w_down, down_full, refs[65:72])
    blocks, depth, seqs, share, bits = place.blocks, place.depth, place.seqs, place.share, place.bits
    blk, z, core, home = place.blk, place.z, place.core, place.home
    pair = pl.program_id(0)
    rows, model = tok_v.shape[1:]
    length = blocks * rows
    count = length // block
    owned = w_qkv.shape[1]
    per_seq = share // 2
    local = lambda src, dst, sem: pltpu.make_async_copy(src, dst, sem).start()

    @pl.when(pair == 0)
    def _():
        total.stages[0] = vec[...]
        greet(place.peers(True, True))
        total.start()
        qkv.start()
        for i in range(seqs):
            for h in range(per_seq):
                target = (core * seqs + i) * per_seq + h

                @pl.when(target != blk)
                def _(i=i, h=h, target=target):
                    sems = tok_s.at[i * per_seq + h], tok_r.at[blk]
                    send(tok.at[i], tok_v.at[blk], *sems, place.at(target, z, core))

                @pl.when(target == blk)
                def _(i=i):
                    local(tok.at[i], tok_v.at[blk], loc.at[0])

        qkv.forward(0, 0)
        for array in (qkv, outw, upw, downw):
            array.keep()
        for k in range(1, depth):
            qkv.climb(k)
        outw.start()
        upw.start()
        total.step(0)
        total.step(1)

        @pl.when(core == home)
        def _():
            for p in range(blocks):

                @pl.when(p != blk)
                def _():
                    arrived(tok_v.at[p], tok_r.at[p])

                @pl.when(p == blk)
                def _():
                    arrived(tok_v.at[p], loc.at[0])

                send(tok_v.at[p], tok_v.at[p], near_s.at[p], near_r.at[p], place.sibling())

        for n in range(2, bits + 1):
            total.step(n)
        for t in range(bits):
            for k in range(depth):
                qkv.step(k, t)
            if t == 0:
                downw.start()
        for array in (outw, upw):
            for k in range(depth):
                array.climb(k)
        vec_out[...] = total.finish()
        gain, shift = vec_out[0:1, :], vec_out[1:2, :]
        part_rows = min(rows, 128)

        for p in range(blocks):

            @pl.when(core != home)
            def _(p=p):
                arrived(tok_v.at[p], near_r.at[p])

            def norm(i, _, p=p):
                inside = pl.ds(pl.multiple_of(i * part_rows, part_rows), part_rows)
                unit, _ = centered(tok_v[p, inside, :].astype(jnp.float32))
                at = pl.ds(pl.multiple_of(p * rows + i * part_rows, part_rows), part_rows)
                normed = unit * gain + shift
                norm_v[at, :] = normed.astype(jnp.bfloat16)
                norm_t[:, at] = normed.T.astype(jnp.bfloat16)
                return 0

            lax.fori_loop(0, rows // part_rows, norm, 0)
        local(norm_t, normed_out, loc.at[1])
        for t in range(place.per_part):
            local(tok_v.at[place.part * place.per_part + t], tok_own.at[t], loc.at[2 + t])
        downw.climb()
        for k in range(depth):
            qkv.wait_swap(k)
        for b in range(blocks):
            for d in range(depth):
                for c in range(2):
                    index = (b * depth + d) * 2 + c
                    w32_v[index * owned : (index + 1) * owned, :] = chunk_v[b, d, c].astype(jnp.float32)
        cols_v[...] = w32_v[...].astype(jnp.bfloat16)
        local(cols_v, cols_out, loc.at[2 + place.per_part])

        def project(i, _):
            at = pl.ds(pl.multiple_of(i * block, block), block)
            normed = norm_v[at, :]
            scale = jnp.where(lax.broadcasted_iota(jnp.int32, (1, 384), 1) < 128, 0.125, 1.0)
            for n in range(pairs):
                value = dot_nn(normed, cols_v[:, n * 384 : (n + 1) * 384]) * scale
                qkv_v[at, n * 384 : (n + 1) * 384] = value.astype(jnp.bfloat16)
            return 0

        lax.fori_loop(0, count, project, 0)
        local(qkv_v, qkv_out, loc.at[3 + place.per_part])

    per_pair = count * (count + 1) // 2
    tasks = []
    levels = [(array, k) for array in (outw, upw) for k in range(depth)]
    for n, (array, k) in enumerate(levels):
        for t in range(bits):
            where = 0.3 * t + (0.05 + 0.15 * t) * n / len(levels)
            tasks.append((where, functools.partial(array.step, k, t)))
    for k in range(1, depth):
        tasks.append((0.6 + 0.25 * k / depth, functools.partial(downw.pass_on, k)))
    tasks.sort(key=lambda task: task[0])
    todo = plan(tasks, pairs * per_pair)

    def lanes_of(n):
        return pl.ds(pl.multiple_of(pair * 384 + n * 128, 128), 128)

    split_heads(kh, qkv_v[:, lanes_of(1)])
    vt[...] = qkv_v[:, lanes_of(2)].astype(jnp.float32).T.astype(jnp.bfloat16)

    def q_step(qi, _):
        at_q = pl.ds(pl.multiple_of(qi * block, block), block)
        run_m[...] = jnp.full_like(run_m, -1e30)
        run_l[...] = jnp.zeros_like(run_l)
        run_a[...] = jnp.zeros_like(run_a)

        def one(kj, masked):
            at = pl.ds(pl.multiple_of(kj * block, block), block)
            q_rows = qkv_v[at_q, lanes_of(0)]
            for h in range(2):
                peak, so_far = run_m[h : h + 1, :], run_l[h : h + 1, :]
                s = dot_nt(kh[h, at, :], q_rows)
                u = s * s + 1.0
                inv = lax.rsqrt(u)
                mag = u * inv
                if masked:
                    mag = jnp.where(causal(block, block, kj, qi), mag, -1e30)
                new = jnp.maximum(peak, jnp.max(mag, axis=0, keepdims=True))
                p = jnp.exp(mag - new)
                alpha = jnp.exp(peak - new)
                run_m[h : h + 1, :] = new
                run_l[h : h + 1, :] = so_far * alpha + jnp.sum(p, axis=0, keepdims=True)
                signed = (p * (s * inv)).astype(jnp.bfloat16)
                head = slice(64 * h, 64 * h + 64)
                run_a[head, :] = run_a[head, :] * alpha + dot_nn(vt[head, at], signed)

        def k_step(kj, _):
            @pl.when(kj == qi)
            def _():
                one(kj, True)

            @pl.when(kj != qi)
            def _():
                one(kj, False)

            pump(todo, pair * per_pair + qi * (qi + 1) // 2 + kj)
            return 0

        lax.fori_loop(0, qi + 1, k_step, 0)
        both = []
        for h in range(2):
            both.append(run_a[64 * h : 64 * h + 64, :] / run_l[h : h + 1, :])
            lse_ref[0, h : h + 1, at_q] = run_m[h : h + 1, :] + jnp.log(run_l[h : h + 1, :])
        att_ref[at_q, :] = jnp.concatenate(both, 0).T.astype(jnp.bfloat16)
        return 0

    lax.fori_loop(0, count, q_step, 0)

    @pl.when(pair == pairs - 1)
    def _():
        for array in (qkv, outw, upw, downw):
            array.finish()
        arrived(norm_t, loc.at[1])
        arrived(cols_v, loc.at[2 + place.per_part])
        arrived(qkv_v, loc.at[3 + place.per_part])
        for t in range(place.per_part):
            arrived(tok_own.at[t], loc.at[2 + t])

        @pl.when(core == home)
        def _():
            for p in range(blocks):
                arrived(tok_v.at[p], near_s.at[p])

        for i in range(seqs):
            for h in range(per_seq):
                target = (core * seqs + i) * per_seq + h

                @pl.when(target != blk)
                def _(i=i, h=h):
                    arrived(tok.at[i], tok_s.at[i * per_seq + h])

                @pl.when((target == blk) & (core != home))
                def _():
                    arrived(tok_v.at[blk], loc.at[0])


def first_half(sizes, tok, vec, w_qkv, w_out, w_up, w_down, block):
    blocks, lanes, seqs = sizes
    depth, share = lanes // 2, blocks // seqs
    per_part = blocks // share
    rows, model = tok.shape[1:]
    length = blocks * rows
    width = w_qkv.shape[2]
    pairs = width // 384
    low, full = jnp.bfloat16, jnp.float32
    shape = jax.ShapeDtypeStruct
    owners = (blocks, depth, 2)
    in_vmem = pl.BlockSpec(memory_space=pltpu.VMEM)
    return pl.pallas_call(
        functools.partial(first_kernel, sizes, block, pairs),
        grid=(pairs,),
        out_shape=[
            shape((length, 128 * pairs), low),
            shape((pairs, 8, length), full),
            shape((per_part, rows, model), low),
            shape((model, length), low),
            shape((length, width), low),
            shape((model, width), low),
            shape(vec.shape, full),
            shape(owners + w_qkv.shape, low),
            shape(owners + w_out.shape, low),
            shape(owners + w_up.shape, low),
            shape(owners + w_down.shape, low),
        ],
        in_specs=[ANYWHERE, in_vmem] + [ANYWHERE] * 4,
        out_specs=[pl.BlockSpec((length, 128), lambda p: (0, p)), pl.BlockSpec((1, 8, length), lambda p: (p, 0, 0))]
        + [ANYWHERE] * 4
        + [in_vmem]
        + [ANYWHERE] * 4,
        scratch_shapes=[
            pltpu.VMEM((blocks, rows, model), low),
            pltpu.VMEM((length, model), low),
            pltpu.VMEM((model, length), low),
            pltpu.VMEM(owners + w_qkv.shape[1:], low),
            pltpu.VMEM((model, width), full),
            pltpu.VMEM((model, width), low),
            pltpu.VMEM((length, width), low),
            pltpu.VMEM((2, length, 128), low),
            pltpu.VMEM((128, length), low),
            pltpu.VMEM((8, block), full),
            pltpu.VMEM((8, block), full),
            pltpu.VMEM((128, block), full),
            DMA((seqs * share // 2,)),
            DMA((blocks,)),
            DMA((blocks,)),
            DMA((blocks,)),
            DMA((4 + per_part,)),
        ]
        + Total.scratch(sizes, vec.shape)
        + Gather.sems(sizes) * 4,
        compiler_params=pltpu.CompilerParams(collective_id=0, has_side_effects=True, vmem_limit_bytes=VMEM_LIMIT),
    )(tok, vec, w_qkv, w_out, w_up, w_down)


def dot_tn(left, right):
    return lax.dot_general(left, right, (((0,), (0,)), ((), ())), preferred_element_type=jnp.float32)


def centered(values):
    center = jnp.mean(values, axis=-1, keepdims=True)
    offsets = values - center
    spread = jnp.mean(offsets * offsets, axis=-1, keepdims=True)
    inverse = lax.rsqrt(spread + 1e-05)
    return offsets * inverse, inverse


def norm_back(values, grads, gain):
    unit, inverse = centered(values)
    scaled = grads * gain
    first = jnp.mean(scaled, axis=-1, keepdims=True)
    second = jnp.mean(scaled * unit, axis=-1, keepdims=True)
    back = inverse * (scaled - first - unit * second)
    return back, jnp.sum(grads * unit, axis=0, keepdims=True), jnp.sum(grads, axis=0, keepdims=True)


def gelu_parts(x):
    square = x * x
    half = 0.5 + 0.5 * jnp.tanh(0.7978845608028654 * x * (1.0 + 0.044715 * square))
    slope = half + x * (2.0 * half * (1.0 - half)) * (0.7978845608028654 + 0.1070322243 * square)
    return x * half, slope


def mlp_kernel(sizes, cols, tile, chunk, *refs):
    place = Place(*sizes)
    att, tok_own, cot, w_out, w_up, w_down, vec, live = refs[:8]
    result, g_heads, g_mid, g_out, g_up, g_down, g_vec = refs[8:15]
    (att_v, tok_v, cot_v, res_v, out_v, up_v, down_v, mid_v, n2_v, n2t_v, hid_v, slope_v, sum_v, ga_v) = refs[15:29]
    (st_out, st_up, st_down) = refs[29:32]
    a_s, a_r, g_s, g_r, cot_s, cot_r, m_s, m_r, loc, up_l, down_l, o_l = refs[32:]
    share, per_part, seqs = place.share, place.per_part, place.seqs
    part, blk, z, core = place.part, place.blk, place.z, place.core
    rows, model = mid_v.shape
    block = rows // per_part
    ff = up_v.shape[1]
    chunks, tiles = ff // chunk, rows // tile
    flat = blk * 2 + core
    partners = [((flat ^ k) // 2, z, (flat ^ k) % 2) for k in range(1, share)]
    slot_of = lax.rem(place.seq, seqs)
    greet(place.peers(False, True))
    for k in range(1, share):
        send(att.at[part ^ k], att_v.at[part], a_s.at[k - 1], a_r.at[k - 1], place.at(*partners[k - 1]))

    def local(src, dst, sem):
        pltpu.make_async_copy(src, dst, sem).start()

    local(att.at[part], att_v.at[part], loc.at[0])
    for t in range(per_part):
        local(tok_own.at[t], tok_v.at[t], loc.at[1 + t])
    local(w_out, out_v, loc.at[1 + per_part])
    for i in range(seqs):
        owner = (core * seqs + i) * share + blk // per_part
        slot = lax.rem(blk, per_part)

        @pl.when(owner != flat)
        def _(i=i, owner=owner, slot=slot):
            send(cot.at[i], cot_v.at[slot], cot_s.at[i], cot_r.at[slot], place.at(owner // 2, z, owner % 2))

        @pl.when(owner == flat)
        def _(i=i, slot=slot):
            local(cot.at[i], cot_v.at[slot], loc.at[2 + per_part])

    def span(f):
        return pl.ds(pl.multiple_of(f * chunk, chunk), chunk)

    for f in range(chunks):
        local(w_up.at[:, pl.ds(f * chunk, chunk)], up_v.at[:, pl.ds(f * chunk, chunk)], up_l.at[f])
        local(w_down.at[pl.ds(f * chunk, chunk)], down_v.at[pl.ds(f * chunk, chunk)], down_l.at[f])

    arrived(att_v.at[part], loc.at[0])
    for t in range(per_part):
        arrived(tok_v.at[t], loc.at[1 + t])
    arrived(out_v, loc.at[1 + per_part])
    for k in range(1, share):
        arrived(att_v.at[part ^ k], a_r.at[k - 1])
    gain, shift = vec[2:3, :], vec[3:4, :]
    per_block = block // tile

    def spot(i):
        return i // per_block, pl.ds(pl.multiple_of(lax.rem(i, per_block) * tile, tile), tile)

    def enter(i, _):
        at = pl.ds(pl.multiple_of(i * tile, tile), tile)
        branch = dot_nn(att_v[0, at, :cols], out_v[:cols, :])
        for g in range(1, share):
            branch = branch + dot_nn(att_v[g, at, :cols], out_v[g * cols : (g + 1) * cols, :])
        t, inside = spot(i)
        middle = tok_v[t, inside, :].astype(jnp.float32) + live[at, :] * branch
        mid_v[at, :] = middle
        unit, _ = centered(middle)
        normed = unit * gain + shift
        n2_v[at, :] = normed.astype(jnp.bfloat16)
        n2t_v[:, at] = normed.T.astype(jnp.bfloat16)
        return 0

    lax.fori_loop(0, tiles, enter, 0)
    sum_v[...] = mid_v[...]

    def up_step(f, _):
        arrived(up_v.at[:, span(f)], up_l.at[f])
        arrived(down_v.at[span(f)], down_l.at[f])
        hidden, slope = gelu_parts(dot_nn(n2_v[...], up_v[:, span(f)]))
        hidden = hidden.astype(jnp.bfloat16)
        hid_v[:, span(f)] = hidden
        slope_v[:, span(f)] = slope.astype(jnp.bfloat16)
        sum_v[...] += dot_nn(hidden, down_v[span(f), :])
        return 0

    lax.fori_loop(0, chunks, up_step, 0)
    for t in range(per_part):
        res_v[t] = sum_v[t * block : (t + 1) * block, :].astype(jnp.bfloat16)
        source = part * per_part + t
        mine = (source == blk) & (place.home == core)

        @pl.when(mine)
        def _(t=t):
            local(res_v.at[t], result.at[slot_of], loc.at[0])

        @pl.when(jnp.logical_not(mine))
        def _(t=t, source=source):
            send(res_v.at[t], result.at[slot_of], m_s.at[t], m_r.at[slot_of], place.at(source, z, place.home))

    for t in range(per_part):
        mine = (part * per_part + t == blk) & (place.home == core)

        @pl.when(mine)
        def _(t=t):
            arrived(cot_v.at[t], loc.at[2 + per_part])

        @pl.when(jnp.logical_not(mine))
        def _(t=t):
            arrived(cot_v.at[t], cot_r.at[t])

    sum_v[...] = jnp.zeros_like(sum_v)

    def back_step(f, _):
        top = cot_v[...].reshape(rows, model)
        grad_pre = (dot_nt(top, down_v[span(f), :]) * slope_v[:, span(f)].astype(jnp.float32)).astype(jnp.bfloat16)
        now = lax.rem(f, 2)

        @pl.when(f >= 2)
        def _():
            arrived(st_down.at[now], o_l.at[now])
            arrived(st_up.at[now], o_l.at[2 + now])

        st_down[now] = dot_tn(hid_v[:, span(f)], top).astype(jnp.bfloat16)
        st_up[now] = dot_nn(n2t_v[...], grad_pre).astype(jnp.bfloat16)
        local(st_down.at[now], g_down.at[span(f)], o_l.at[now])
        local(st_up.at[now], g_up.at[:, span(f)], o_l.at[2 + now])
        sum_v[...] += dot_nt(grad_pre, up_v[:, span(f)])
        return 0

    lax.fori_loop(0, chunks, back_step, 0)
    g_vec[...] = jnp.zeros_like(g_vec)

    def leave(i, _):
        at = pl.ds(pl.multiple_of(i * tile, tile), tile)
        t, inside = spot(i)
        back, d_gain, d_shift = norm_back(mid_v[at, :], sum_v[at, :], gain)
        g_vec[0:1, :] += d_gain
        g_vec[1:2, :] += d_shift
        total = cot_v[t, inside, :].astype(jnp.float32) + back
        mid_v[at, :] = total
        branch = (live[at, :] * total).astype(jnp.bfloat16)
        n2_v[at, :] = branch
        heads = dot_nt(branch, out_v[...]).astype(jnp.bfloat16)
        for g in range(share):
            if cols == ga_v.shape[2]:
                ga_v[g, at, :] = heads[:, g * cols : (g + 1) * cols]
            else:
                piece = heads[:, g * cols : (g + 1) * cols]
                ga_v[g, at, :] = jnp.concatenate([piece, jnp.zeros((tile, ga_v.shape[2] - cols), jnp.bfloat16)], 1)
        return 0

    lax.fori_loop(0, tiles, leave, 0)
    for k in range(1, share):
        send(ga_v.at[part ^ k], g_heads.at[part], g_s.at[k - 1], g_r.at[k - 1], place.at(*partners[k - 1]))
    local(ga_v.at[part], g_heads.at[part], loc.at[1])
    local(mid_v, g_mid, loc.at[2])
    for g in range(share):
        st_out[g * cols : (g + 1) * cols, :] = dot_tn(att_v[g, :, :cols], n2_v[...]).astype(jnp.bfloat16)
    local(st_out, g_out, loc.at[1 + per_part])
    for n in range(min(2, chunks)):
        arrived(st_down.at[n], o_l.at[n])
        arrived(st_up.at[n], o_l.at[2 + n])
    arrived(st_out, loc.at[1 + per_part])
    arrived(mid_v, loc.at[2])
    arrived(ga_v.at[part], loc.at[1])
    for k in range(1, share):
        arrived(att.at[part ^ k], a_s.at[k - 1])
        arrived(ga_v.at[part ^ k], g_s.at[k - 1])
        arrived(g_heads.at[part ^ k], g_r.at[k - 1])
    for i in range(seqs):
        owner = (core * seqs + i) * share + blk // per_part

        @pl.when(owner != flat)
        def _(i=i):
            arrived(cot.at[i], cot_s.at[i])
            arrived(result.at[i], m_r.at[i])

    for t in range(per_part):
        mine = (part * per_part + t == blk) & (place.home == core)

        @pl.when(mine)
        def _(t=t):
            arrived(res_v.at[t], loc.at[0])

        @pl.when(jnp.logical_not(mine))
        def _(t=t):
            arrived(res_v.at[t], m_s.at[t])


def feed_forward(sizes, cols, att, tok_own, cot, w_out, w_up, w_down, vec, live, tile, chunk):
    blocks, lanes, seqs = sizes
    share = blocks // seqs
    per_part = blocks // share
    block, model = tok_own.shape[1:]
    rows = per_part * block
    wide = att.shape[2]
    ff = w_up.shape[1]
    chunks = ff // chunk
    in_vmem = pl.BlockSpec(memory_space=pltpu.VMEM)
    low, full = jnp.bfloat16, jnp.float32
    return pl.pallas_call(
        functools.partial(mlp_kernel, sizes, cols, tile, chunk),
        out_shape=[
            jax.ShapeDtypeStruct((seqs, block, model), low),
            jax.ShapeDtypeStruct((share, rows, wide), low),
            jax.ShapeDtypeStruct((rows, model), full),
            jax.ShapeDtypeStruct((model, model), low),
            jax.ShapeDtypeStruct((model, ff), low),
            jax.ShapeDtypeStruct((ff, model), low),
            jax.ShapeDtypeStruct((8, model), full),
        ],
        in_specs=[ANYWHERE] * 6 + [in_vmem] * 2,
        out_specs=[ANYWHERE] * 6 + [in_vmem],
        scratch_shapes=[
            pltpu.VMEM((share, rows, wide), low),
            pltpu.VMEM((per_part, block, model), low),
            pltpu.VMEM((per_part, block, model), low),
            pltpu.VMEM((per_part, block, model), low),
            pltpu.VMEM((model, model), low),
            pltpu.VMEM((model, ff), low),
            pltpu.VMEM((ff, model), low),
            pltpu.VMEM((rows, model), full),
            pltpu.VMEM((rows, model), low),
            pltpu.VMEM((model, rows), low),
            pltpu.VMEM((rows, ff), low),
            pltpu.VMEM((rows, ff), low),
            pltpu.VMEM((rows, model), full),
            pltpu.VMEM((share, rows, wide), low),
            pltpu.VMEM((model, model), low),
            pltpu.VMEM((2, model, chunk), low),
            pltpu.VMEM((2, chunk, model), low),
            DMA((share,)),
            DMA((share,)),
            DMA((share,)),
            DMA((share,)),
            DMA((seqs,)),
            DMA((per_part,)),
            DMA((per_part,)),
            DMA((seqs,)),
            DMA((3 + per_part,)),
            DMA((chunks,)),
            DMA((chunks,)),
            DMA((4,)),
        ],
        compiler_params=pltpu.CompilerParams(collective_id=4, has_side_effects=True, vmem_limit_bytes=VMEM_LIMIT),
    )(att, tok_own, cot, w_out, w_up, w_down, vec, live)


def last_kernel(sizes, block, pairs, *refs):
    place = Place(*sizes)
    blocks, depth, seqs, share, bits = place.blocks, place.depth, place.seqs, place.share, place.bits
    blk, z, core, part = place.blk, place.z, place.core, place.part
    per_part = place.per_part
    count = 3 + pairs
    q_ref, k_ref, v_ref, g_ref, att_ref, lse_ref = refs[:6]
    big, tok_own, g_mid, norm_t, cols, vec, two = refs[6:9], refs[9], refs[10], refs[11], refs[12], refs[13], refs[14]
    refs = refs[15:]
    sums, tok_out, vec_out, refs = refs[:count], refs[count], refs[count + 1], refs[count + 2 :]
    kh, vh, qh, gh, kt, delta, dqt, dk, dv = refs[:9]
    gq_v, own_v, norm_v, cols_v, tok_v, mid_v, out_v, part_v, got_v, sum_v = refs[9:19]
    p_s, p_r, t_s, t_r, loc = refs[19:24]
    total = Total(place, *refs[24:28], refs[28:34])
    kinds = ["rows"] * 3 + ["columns"] * pairs
    fold = Fold(place, kinds, list(big) + [own_v.at[p] for p in range(pairs)], [], sums, [], refs[34:])
    pair = pl.program_id(0)
    length = q_ref.shape[0]
    rows, model = mid_v.shape
    owned = own_v.shape[4]
    steps = length // block
    per_pair = steps * (steps + 1) // 2
    flat = blk * 2 + core
    partners = [((flat ^ k) // 2, z, (flat ^ k) % 2) for k in range(1, share)]
    slot_of = lax.rem(place.seq, seqs)
    local = lambda src, dst, sem: pltpu.make_async_copy(src, dst, sem).start()

    tasks = []
    units = [(a, k) for a in range(3) for k in fold.order]
    scale = 12.0 / len(units) / 80.0
    for n, (a, k) in enumerate(units):
        tasks.append(((3 + 1.3 * n) * scale, functools.partial(fold.join, a, k)))
        for t in range(bits):
            where = 8 + 6 * t + (3.2 + 0.4 * t) * n
            tasks.append((where * scale, functools.partial(fold.step, a, k, t)))
    for a in range(3):
        tasks.append((0.78 + 0.05 * a, functools.partial(fold.total, a)))
    for p in range(pairs - 1):
        for n, k in enumerate(fold.order):
            tasks.append(((p + 1.15) / pairs, functools.partial(fold.join, 3 + p, k)))
            for t in range(bits):
                where = p + 1.4 + 0.5 * t / bits + 0.1 * n / depth
                tasks.append((where / pairs, functools.partial(fold.step, 3 + p, k, t)))
    tasks.sort(key=lambda task: task[0])
    todo = plan(tasks, pairs * per_pair)

    @pl.when(pair == 0)
    def _():
        fold.greet()
        fold.clear()
        for a, k in units:
            fold.start(a, k)
        local(norm_t, norm_v, loc.at[0])
        local(cols, cols_v, loc.at[1])
        local(g_mid, mid_v, loc.at[2])
        local(tok_own, tok_v, loc.at[3])

    split_heads(kh, k_ref[...])
    split_heads(vh, v_ref[...])
    split_heads(qh, q_ref[...])
    split_heads(gh, g_ref[...])
    kt[...] = k_ref[...].astype(jnp.float32).T.astype(jnp.bfloat16)
    prod = (g_ref[...].astype(jnp.float32) * att_ref[...].astype(jnp.float32)).T
    delta[0:1, :] = jnp.sum(prod[:64], axis=0, keepdims=True)
    delta[1:2, :] = jnp.sum(prod[64:], axis=0, keepdims=True)
    dqt[...] = jnp.zeros_like(dqt)

    def k_step(kj, _):
        at = pl.ds(pl.multiple_of(kj * block, block), block)

        def one(qi, masked):
            at_q = pl.ds(pl.multiple_of(qi * block, block), block)
            q_rows = q_ref[at_q, :]
            g_rows = g_ref[at_q, :]
            add_k = add_v = None
            for h in range(2):
                s = dot_nt(kh[h, at, :], q_rows)
                dp = dot_nt(vh[h, at, :], g_rows)
                u = s * s + 1.0
                inv = lax.rsqrt(u)
                arg = u * inv - lse_ref[0, h : h + 1, at_q]
                if masked:
                    arg = jnp.where(causal(block, block, kj, qi), arg, -1e30)
                p = jnp.exp(arg)
                sgn = s * inv
                t = inv * inv * (inv - 1.0) + 1.0
                ds = (p * (dp * t - sgn * delta[h : h + 1, at_q])).astype(jnp.bfloat16)
                signed = (p * sgn).astype(jnp.bfloat16)
                one_v = dot_nn(signed, gh[h, at_q, :])
                one_k = dot_nn(ds, qh[h, at_q, :])
                add_v = one_v if h == 0 else add_v + one_v
                add_k = one_k if h == 0 else add_k + one_k
                dqt[64 * h : 64 * h + 64, at_q] += dot_nn(kt[64 * h : 64 * h + 64, at], ds)
            return add_k, add_v

        def more(qi, _):
            @pl.when(qi == kj)
            def _():
                dk[...], dv[...] = one(qi, True)

            @pl.when(qi != kj)
            def _():
                add_k, add_v = one(qi, False)
                dk[...] += add_k
                dv[...] += add_v

            pump(todo, pair * per_pair + kj * steps - kj * (kj - 1) // 2 + qi - kj)
            return 0

        lax.fori_loop(kj, steps, more, 0)
        gq_v[pair, at, 128:256] = dk[...].astype(jnp.bfloat16)
        gq_v[pair, at, 256:384] = dv[...].astype(jnp.bfloat16)
        return 0

    lax.fori_loop(0, steps, k_step, 0)
    gq_v[pair, :, 0:128] = (dqt[...] * 0.125).T.astype(jnp.bfloat16)

    @pl.when(pair == 0)
    def _():
        arrived(norm_v, loc.at[0])
        arrived(cols_v, loc.at[1])
        arrived(mid_v, loc.at[2])
        arrived(tok_v, loc.at[3])

    sum_v[...] = dot_nn(norm_v[...], gq_v[pair])
    for b in range(blocks):
        for d in range(depth):
            for c in range(2):
                first = ((b * depth + d) * 2 + c) * owned
                own_v[pair, b, d, c] = sum_v[first : first + owned, :].astype(jnp.bfloat16)
    for p in range(pairs):

        @pl.when(pair == p)
        def _(p=p):
            for k in fold.order:
                fold.start(3 + p, k)

    @pl.when(pair == pairs - 1)
    def _():
        mine = 3 + pairs - 1
        tile = min(256, block, rows)

        def input_grad(g, i):
            at = pl.ds(pl.multiple_of(g * rows + i * tile, tile), tile)
            value = dot_nt(gq_v[0, at, :], cols_v[:, 0:384])
            for p in range(1, pairs):
                value = value + dot_nt(gq_v[p, at, :], cols_v[:, p * 384 : (p + 1) * 384])
            return value

        for k in range(1, share):

            def away(i, _, k=k):
                at = pl.ds(pl.multiple_of(i * tile, tile), tile)
                part_v[k - 1, at, :] = input_grad(part ^ k, i).astype(jnp.bfloat16)
                return 0

            lax.fori_loop(0, rows // tile, away, 0)
            send(part_v.at[k - 1], got_v.at[k - 1], p_s.at[k - 1], p_r.at[k - 1], place.at(*partners[k - 1]))
        for k in fold.order:
            fold.join(mine, k)
        total.stages[0] = jnp.zeros(total.stages.shape[1:], jnp.float32)
        total.stages[0, 2:4, :] = two[0:2, :]
        gain = vec[0:1, :]
        per_block = rows // per_part // tile

        def leave(i, _):
            at = pl.ds(pl.multiple_of(i * tile, tile), tile)
            t = i // per_block
            inside = pl.ds(pl.multiple_of(lax.rem(i, per_block) * tile, tile), tile)
            value = input_grad(part, i)
            for k in range(1, share):
                value = value + got_v[k - 1, at, :].astype(jnp.float32)
            back, d_gain, d_shift = norm_back(tok_v[t, inside, :].astype(jnp.float32), value, gain)
            total.stages[0, 0:1, :] += d_gain
            total.stages[0, 1:2, :] += d_shift
            out_v[t, inside, :] = (mid_v[at, :] + back).astype(jnp.bfloat16)
            return 0

        for k in range(1, share):
            arrived(got_v.at[k - 1], p_r.at[k - 1])
        for t in range(per_part):
            lax.fori_loop(t * per_block, (t + 1) * per_block, leave, 0)
            source = part * per_part + t
            here = (source == blk) & (place.home == core)

            @pl.when(here)
            def _(t=t):
                local(out_v.at[t], tok_out.at[slot_of], loc.at[0])

            @pl.when(jnp.logical_not(here))
            def _(t=t, source=source):
                send(out_v.at[t], tok_out.at[slot_of], t_s.at[t], t_r.at[slot_of], place.at(source, z, place.home))

            if t == 0:
                for k in fold.order:
                    fold.step(mine, k, 0)
        total.start()
        for t in range(1, bits):
            for k in fold.order:
                fold.step(mine, k, t)
        for n in range(bits + 1):
            total.step(n)
        for p in range(pairs):
            fold.total(3 + p)
        vec_out[...] = total.finish()
        fold.finish()
        for k in range(1, share):
            arrived(part_v.at[k - 1], p_s.at[k - 1])
        for t in range(per_part):
            here = (part * per_part + t == blk) & (place.home == core)

            @pl.when(here)
            def _(t=t):
                arrived(out_v.at[t], loc.at[0])

            @pl.when(jnp.logical_not(here))
            def _(t=t):
                arrived(out_v.at[t], t_s.at[t])

        for i in range(seqs):
            owner = (core * seqs + i) * share + blk // per_part

            @pl.when(owner != flat)
            def _(i=i):
                arrived(tok_out.at[i], t_r.at[i])


def last_half(sizes, qkv, g_att, att, lse, big, tok_own, g_mid, norm_t, cols, vec, two, block):
    blocks, lanes, seqs = sizes
    depth, share = lanes // 2, blocks // seqs
    length, width = qkv.shape
    pairs = width // 384
    model = cols.shape[0]
    owned = model // (blocks * lanes)
    per_part, rows_in, _ = tok_own.shape
    rows = per_part * rows_in
    low, full = jnp.bfloat16, jnp.float32
    in_vmem = pl.BlockSpec(memory_space=pltpu.VMEM)
    own = jax.ShapeDtypeStruct((blocks, depth, 2, owned, 384), low)
    kinds = ["rows"] * 3 + ["columns"] * pairs
    out, _, scratch = fold_shapes(sizes, list(big) + [own] * pairs, kinds, [])
    return pl.pallas_call(
        functools.partial(last_kernel, sizes, block, pairs),
        grid=(pairs,),
        out_shape=out + [jax.ShapeDtypeStruct((seqs, rows_in, model), low), jax.ShapeDtypeStruct(vec.shape, full)],
        in_specs=[pl.BlockSpec((length, 128), lambda p, n=n: (0, 3 * p + n)) for n in range(3)]
        + [pl.BlockSpec((length, 128), lambda p: (0, p))] * 2
        + [pl.BlockSpec((1, 8, length), lambda p: (p, 0, 0))]
        + [ANYWHERE] * 7
        + [in_vmem] * 2,
        out_specs=[in_vmem] * len(out) + [ANYWHERE, in_vmem],
        scratch_shapes=[pltpu.VMEM((2, length, 128), low)] * 4
        + [
            pltpu.VMEM((128, length), low),
            pltpu.VMEM((8, length), full),
            pltpu.VMEM((128, length), full),
            pltpu.VMEM((block, 128), full),
            pltpu.VMEM((block, 128), full),
            pltpu.VMEM((pairs, length, 384), low),
            pltpu.VMEM((pairs,) + own.shape, low),
            pltpu.VMEM((model, length), low),
            pltpu.VMEM((model, width), low),
            pltpu.VMEM((per_part, rows_in, model), low),
            pltpu.VMEM((rows, model), full),
            pltpu.VMEM((per_part, rows_in, model), low),
            pltpu.VMEM((share - 1, rows, model), low),
            pltpu.VMEM((share - 1, rows, model), low),
            pltpu.VMEM((model, 384), full),
            DMA((share,)),
            DMA((share,)),
            DMA((per_part,)),
            DMA((seqs,)),
            DMA((4,)),
        ]
        + Total.scratch(sizes, vec.shape)
        + scratch,
        compiler_params=pltpu.CompilerParams(collective_id=2, has_side_effects=True, vmem_limit_bytes=63 * 2**20),
    )(qkv, qkv, qkv, g_att, att, lse, *big, tok_own, g_mid, norm_t, cols, vec, two)


def shards(sizes, tokens, seq_len, ln1_gain, ln1_shift, w_qkv, w_out, ln2_gain, ln2_shift, w_up, w_down, cotangent):
    blocks, lanes, seqs = sizes
    place = Place(*sizes)
    share, part = place.share, place.part
    model = tokens.shape[2]
    length = blocks * tokens.shape[1]
    rows = length // share
    owned = w_qkv.shape[0]
    cols = model // share
    wide = -(-cols // 128) * 128

    pairs = wide // 128
    grouped = jnp.pad(w_qkv.reshape(owned, 3, share, cols), ((0, 0), (0, 0), (0, 0), (0, wide - cols)))
    grouped = grouped.reshape(owned, 3, share, pairs, 128)
    grouped = jnp.transpose(grouped, (2, 0, 3, 1, 4)).reshape(share, owned, 3 * wide)
    flat = place.blk * lanes + lax.axis_index("seq")
    vec = jnp.zeros((8, model), jnp.float32)
    own = jnp.stack([ln1_gain, ln1_shift, ln2_gain, ln2_shift]).astype(jnp.float32)
    vec = lax.dynamic_update_slice(vec, own, (0, flat * owned))
    first = (place.blk == 0).astype(jnp.float32)
    vec = lax.dynamic_update_slice(vec, first * seq_len.astype(jnp.float32)[None], (4, lax.axis_index("seq") * seqs))
    outs = first_half(sizes, tokens, vec, grouped, w_out, w_up, w_down, min(512, rows))
    att, lse, tok_own, norm_t, qkv, qkv_cols, params, _, out_full, up_full, down_full = outs
    out_full, up_full = [a.reshape(model, -1) for a in (out_full, up_full)]
    down_full = down_full.reshape(-1, model)
    my_len = lax.dynamic_index_in_dim(params[4], place.z * 2 * seqs + place.seq, 0, False)

    positions = part * rows + jnp.arange(rows, dtype=jnp.int32)
    live = (positions.astype(jnp.float32) < my_len).astype(jnp.float32)[:, None]
    result, g_heads, grad_mid, grad_out, grad_up, grad_down, two_grads = feed_forward(
        sizes,
        cols,
        att.reshape(share, rows, wide),
        tok_own,
        cotangent,
        out_full,
        up_full,
        down_full,
        params,
        live,
        min(256, tokens.shape[1]),
        min(512, w_up.shape[1]),
    )

    def cut(values):
        return values.reshape((blocks, lanes // 2, 2, -1) + values.shape[1:])

    done = last_half(
        sizes,
        qkv,
        g_heads.reshape(length, wide),
        att,
        lse,
        [cut(grad_out), cut(grad_up), cut(grad_down)],
        tok_own,
        grad_mid,
        norm_t,
        qkv_cols,
        params,
        two_grads,
        min(512, rows),
    )
    sum_out, sum_up, sum_down, *sum_pairs, grad_tokens, vec_sum = done
    vec_own = lax.dynamic_slice_in_dim(vec_sum, flat * owned, owned, 1)
    sum_qkv = jnp.stack(sum_pairs).reshape(pairs, share, owned, 3, 128)
    sum_qkv = jnp.transpose(sum_qkv, (2, 3, 1, 0, 4)).reshape(owned, 3, share, wide)[..., :cols].reshape(owned, 3 * model)
    return (
        result,
        grad_tokens.astype(jnp.float32),
        vec_own[0],
        vec_own[1],
        sum_qkv,
        sum_out,
        vec_own[2],
        vec_own[3],
        sum_up,
        sum_down,
    )


def solution(mesh):
    blocks, lanes = mesh.shape["blk"], mesh.shape["seq"]
    whole = P(("blk", "seq"))
    rows = P(("blk", "seq"), None)
    tokens = P("seq", "blk", None)

    def run(*args):
        seqs = args[0].shape[0] // lanes
        return jax.shard_map(
            functools.partial(shards, (blocks, lanes, seqs)),
            mesh=mesh,
            in_specs=(tokens, P("seq"), whole, whole, rows, rows, whole, whole, rows, rows, tokens),
            out_specs=(tokens, tokens, whole, whole, rows, rows, whole, whole, rows, rows),
            check_vma=False,
        )(*args)

    return run
```

```python
import functools

import jax
import jax.numpy as jnp
from jax import lax
from jax.experimental import pallas as pl
from jax.experimental.pallas import tpu as pltpu
from jax.sharding import PartitionSpec as P

HEADS = 12
VMEM_LIMIT = 60 * 2**20


MESH = pl.DeviceIdType.MESH
DMA = pltpu.SemaphoreType.DMA
ANYWHERE = pl.BlockSpec(memory_space=pl.ANY)


class Place:
    def __init__(self, blocks, lanes, seqs):
        self.blocks, self.depth, self.seqs = blocks, lanes // 2, seqs
        self.share = blocks // seqs
        self.per_part = blocks // self.share
        self.bits = max(1, blocks.bit_length() - 1)
        self.blk = lax.axis_index("blk")
        lane = lax.axis_index("seq")
        self.z, self.core = lane // 2, lane % 2
        flat = self.blk * 2 + self.core
        self.seq, self.part = flat // self.share, flat % self.share
        self.home = self.seq // seqs
        self.other = lax.rem(self.blk * 2 + 1 - self.core, self.share)

    def at(self, blk, z, core):
        return (blk, z * 2 + core)

    def sibling(self):
        return self.at(self.blk, self.z, 1 - self.core)

    def peers(self, along_z, along_blk):
        out = [self.sibling()]
        if along_z:
            out += [self.at(self.blk, lax.rem(self.z + k, self.depth), self.core) for k in range(1, self.depth)]
        if along_blk:
            for m in range(1, self.blocks):
                out += [self.at(self.blk ^ m, self.z, 0), self.at(self.blk ^ m, self.z, 1)]
        return out

    def bit(self, part, step):
        return 1 << ((part + step) % self.bits)

    def widen(self, k):
        masks, out, seen = [0], [], 0
        for t in range(self.bits):
            bit = self.bit(k, t)
            out.append((bit, list(masks), seen))
            seen += len(masks)
            masks += [m ^ bit for m in masks]
        return out

    def narrow(self, k):
        out, seen = [], 0
        for t in range(self.bits):
            masks = [0]
            for u in range(t + 1, self.bits):
                masks += [m ^ self.bit(k, u) for m in masks]
            out.append((self.bit(k, t), masks, seen))
            seen += len(masks)
        return out


def greet(devices):
    barrier = pltpu.get_barrier_semaphore()
    for device in devices:
        pl.semaphore_signal(barrier, inc=1, device_id=device, device_id_type=MESH)
    pl.semaphore_wait(barrier, len(devices))


def send(src, dst, send_sem, recv_sem, device):
    pltpu.make_async_remote_copy(
        src_ref=src, dst_ref=dst, send_sem=send_sem, recv_sem=recv_sem, device_id=device, device_id_type=MESH
    ).start()


def arrived(ref, sem):
    pltpu.make_async_copy(ref, ref, sem).wait()


class Fold:
    def __init__(self, place, kinds, grads, rows_in, sums, rows_out, scratch):
        self.place, self.kinds, self.grads = place, kinds, grads
        self.rows_in, self.sums, self.rows_out = rows_in, sums, rows_out
        self.count, self.moves = len(kinds), len(rows_in)
        n = self.count
        self.held, self.near, self.wide, self.tall = (scratch[i * n : i * n + n] for i in range(4))
        self.m_s, self.m_r, self.z_s, self.z_r, self.b_s, self.b_r, self.c_s, self.c_r, self.loc = scratch[4 * n :]
        self.order = list(range(1, place.depth)) + [0]
        self.units = [(a, k) for a in range(n) for k in self.order]

    @staticmethod
    def scratch(sizes, chunks, types, kinds, moves):
        blocks, lanes, seqs = sizes
        depth, share, count = lanes // 2, blocks // seqs, len(chunks)
        out = [pltpu.VMEM((blocks, depth) + c, t) for c, t in zip(chunks, types)]
        out += [
            pltpu.VMEM((1, 1, 8, 128) if kind == "columns" else (blocks, depth) + c, t)
            for c, t, kind in zip(chunks, types, kinds)
        ]
        out += [pltpu.VMEM((depth, blocks - 1) + c, t) for c, t in zip(chunks, types)]
        out += [pltpu.VMEM((depth - 1,) + c, t) for c, t in zip(chunks, types)]
        return out + [
            DMA((max(1, moves), blocks // share)),
            DMA((max(1, moves), seqs)),
            DMA((count, depth - 1)),
            DMA((count, depth - 1)),
            DMA((count, depth, blocks - 1)),
            DMA((count, depth, blocks - 1)),
            DMA((count, depth)),
            DMA((count, depth)),
            DMA((count + 1, max(depth, moves))),
        ]

    def level(self, k):
        return lax.rem(self.place.z + k, self.place.depth)

    def greet(self):
        greet(self.place.peers(True, True))

    def clear(self):
        place = self.place
        for a in range(self.count):
            if self.kinds[a] == "columns" and place.share > 2:
                held = self.held[a]
                for g in range(place.share):

                    @pl.when((g != place.part) & (g != place.other))
                    def _(held=held, g=g):
                        held[:, :, g] = jnp.zeros(held.shape[:2] + held.shape[3:], held.dtype)

    def start(self, a, k):
        place = self.place
        if self.kinds[a] == "columns":
            mine = there = self.held[a].at[:, self.level(k), place.part]
        else:
            mine = self.held[a].at[:, self.level(k)]
            there = self.near[a].at[:, self.level(k)]
        theirs = self.grads[a].at[:, self.level(k), 1 - place.core]
        send(theirs, there, self.c_s.at[a, k], self.c_r.at[a, k], place.sibling())
        pltpu.make_async_copy(self.grads[a].at[:, self.level(k), place.core], mine, self.loc.at[a, k]).start()

    def add(self, into, second):
        total = into[...].astype(jnp.float32) + second[...].astype(jnp.float32)
        into[...] = total.astype(into.dtype)

    def forward(self, a, k, t):
        place = self.place
        bit, masks, seen = place.narrow(k)[t]
        for n, m in enumerate(masks):
            sems = self.b_s.at[a, k, seen + n], self.b_r.at[a, k, seen + n]
            block = self.held[a].at[place.blk ^ bit ^ m, self.level(k)]
            send(block, self.wide[a].at[k, seen + n], *sems, place.at(place.blk ^ bit, place.z, place.core))

    def join(self, a, k):
        place = self.place
        if self.kinds[a] == "columns":
            arrived(self.held[a].at[:, self.level(k), place.part], self.loc.at[a, k])
            arrived(self.held[a].at[:, self.level(k), place.other], self.c_r.at[a, k])
        else:
            arrived(self.held[a].at[:, self.level(k)], self.loc.at[a, k])
            arrived(self.near[a].at[:, self.level(k)], self.c_r.at[a, k])

            def one(b, _):
                self.add(self.held[a].at[b, self.level(k)], self.near[a].at[b, self.level(k)])
                return 0

            lax.fori_loop(0, place.blocks, one, 0)
        self.forward(a, k, 0)

    def step(self, a, k, t):
        place = self.place
        bit, masks, seen = place.narrow(k)[t]
        for n, m in enumerate(masks):
            arrived(self.wide[a].at[k, seen + n], self.b_r.at[a, k, seen + n])
            self.add(self.held[a].at[place.blk ^ m, self.level(k)], self.wide[a].at[k, seen + n])
        if t + 1 < place.bits:
            self.forward(a, k, t + 1)
        elif k > 0:
            sems = self.z_s.at[a, k - 1], self.z_r.at[a, k - 1]
            block = self.held[a].at[place.blk, self.level(k)]
            send(block, self.tall[a].at[k - 1], *sems, place.at(place.blk, self.level(k), place.core))

    def total(self, a):
        place = self.place
        value = self.held[a][place.blk, place.z].astype(jnp.float32)
        for k in range(1, place.depth):
            arrived(self.tall[a].at[k - 1], self.z_r.at[a, k - 1])
            value = value + self.tall[a][k - 1].astype(jnp.float32)
        self.sums[a][...] = value

    def rows(self, j):
        place = self.place
        slot = lax.rem(place.seq, place.seqs)
        for t in range(place.per_part):
            source = place.part * place.per_part + t
            mine = (source == place.blk) & (place.home == place.core)

            @pl.when(mine)
            def _(t=t):
                pltpu.make_async_copy(self.rows_in[j].at[t], self.rows_out[j].at[slot], self.loc.at[self.count, j]).start()

            @pl.when(jnp.logical_not(mine))
            def _(t=t, source=source):
                sems = self.m_s.at[j, t], self.m_r.at[j, slot]
                send(self.rows_in[j].at[t], self.rows_out[j].at[slot], *sems, place.at(source, place.z, place.home))

    def finish(self):
        place = self.place
        for a, k in self.units:
            if self.kinds[a] == "columns":
                arrived(self.held[a].at[:, 0, 0], self.c_s.at[a, k])
            else:
                arrived(self.held[a].at[:, 0], self.c_s.at[a, k])
            for n in range(place.blocks - 1):
                arrived(self.held[a].at[0, 0], self.b_s.at[a, k, n])
            if k > 0:
                arrived(self.held[a].at[0, 0], self.z_s.at[a, k - 1])
        for j in range(self.moves):
            for t in range(place.per_part):
                mine = (place.part * place.per_part + t == place.blk) & (place.home == place.core)

                @pl.when(mine)
                def _(j=j, t=t):
                    arrived(self.rows_in[j].at[t], self.loc.at[self.count, j])

                @pl.when(jnp.logical_not(mine))
                def _(j=j, t=t):
                    arrived(self.rows_in[j].at[t], self.m_s.at[j, t])

            for i in range(place.seqs):
                owner = (place.core * place.seqs + i) * place.share + place.blk // place.per_part

                @pl.when(owner != place.blk * 2 + place.core)
                def _(j=j, i=i):
                    arrived(self.rows_out[j].at[i], self.m_r.at[j, i])


def fold_shapes(sizes, grads, kinds, rows):
    blocks, _, seqs = sizes
    share = blocks // seqs
    chunks = [((share,) if kind == "columns" else ()) + g.shape[3:] for g, kind in zip(grads, kinds)]
    scratch = Fold.scratch(sizes, chunks, [g.dtype for g in grads], kinds, len(rows))
    out = [jax.ShapeDtypeStruct(c, jnp.float32) for c in chunks]
    moved = [jax.ShapeDtypeStruct((seqs,) + r.shape[1:], r.dtype) for r in rows]
    return out, moved, scratch


def dot_nt(left, right):
    return lax.dot_general(left, right, (((1,), (1,)), ((), ())), preferred_element_type=jnp.float32)


def dot_nn(left, right):
    return lax.dot_general(left, right, (((1,), (0,)), ((), ())), preferred_element_type=jnp.float32)


def split_heads(dst, src):
    low = lax.broadcasted_iota(jnp.int32, src.shape, 1) < 64
    dst[0] = jnp.where(low, src, jnp.zeros_like(src))
    dst[1] = jnp.where(low, jnp.zeros_like(src), src)


def causal(bk, bq, kj, qi):
    kpos = kj * bk + lax.broadcasted_iota(jnp.int32, (bk, bq), 0)
    qpos = qi * bq + lax.broadcasted_iota(jnp.int32, (bk, bq), 1)
    return kpos <= qpos


def plan(tasks, points):
    out = {}
    for where, call in tasks:
        out.setdefault(min(points - 1, int(where * points)), []).append(call)
    return out


def pump(todo, point):
    for at, calls in todo.items():

        @pl.when(point == at)
        def _(calls=calls):
            for call in calls:
                call()


class Total:
    def __init__(self, place, stages, from_z, from_blk, from_core, sems):
        self.place, self.stages = place, stages
        self.from_z, self.from_blk, self.from_core = from_z, from_blk, from_core
        self.z_s, self.z_r, self.b_s, self.b_r, self.c_s, self.c_r = sems

    @staticmethod
    def scratch(sizes, shape):
        blocks, lanes, _ = sizes
        depth, bits = lanes // 2, max(1, blocks.bit_length() - 1)
        return [
            pltpu.VMEM((2 + bits,) + shape, jnp.float32),
            pltpu.VMEM((depth - 1,) + shape, jnp.float32),
            pltpu.VMEM((bits,) + shape, jnp.float32),
            pltpu.VMEM(shape, jnp.float32),
            DMA((depth - 1,)),
            DMA((depth - 1,)),
            DMA((bits,)),
            DMA((bits,)),
            DMA((1,)),
            DMA((1,)),
        ]

    def start(self):
        place = self.place
        for k in range(1, place.depth):
            target = place.at(place.blk, lax.rem(place.z + k, place.depth), place.core)
            send(self.stages.at[0], self.from_z.at[k - 1], self.z_s.at[k - 1], self.z_r.at[k - 1], target)

    def step(self, n):
        place = self.place
        if n == 0:
            value = self.stages[0]
            for k in range(1, place.depth):
                arrived(self.from_z.at[k - 1], self.z_r.at[k - 1])
                value = value + self.from_z[k - 1]
        else:
            arrived(self.from_blk.at[n - 1], self.b_r.at[n - 1])
            value = self.stages[n] + self.from_blk[n - 1]
        self.stages[n + 1] = value
        if n < place.bits:
            target = place.at(place.blk ^ (1 << n), place.z, place.core)
            send(self.stages.at[n + 1], self.from_blk.at[n], self.b_s.at[n], self.b_r.at[n], target)
        else:
            send(self.stages.at[n + 1], self.from_core, self.c_s.at[0], self.c_r.at[0], place.sibling())

    def finish(self):
        place = self.place
        arrived(self.from_core, self.c_r.at[0])
        value = self.stages[place.bits + 1] + self.from_core[...]
        arrived(self.from_core, self.c_s.at[0])
        for n in range(place.bits):
            arrived(self.from_core, self.b_s.at[n])
        for k in range(1, place.depth):
            arrived(self.from_core, self.z_s.at[k - 1])
        return value


class Gather:
    def __init__(self, place, shard, full, sems, only=None, span=None):
        self.place, self.full, self.only = place, full, only
        self.tail = () if span is None else (pl.ds(*span),)
        self.shard = shard if span is None else shard.at[self.tail[0]]
        self.z_s, self.z_r, self.b_s, self.b_r, self.c_s, self.c_r, self.loc = sems

    @staticmethod
    def sems(sizes):
        blocks, lanes, _ = sizes
        depth = lanes // 2
        return [
            DMA((depth,)),
            DMA((depth,)),
            DMA((depth, blocks - 1)),
            DMA((depth, blocks - 1)),
            DMA((depth,)),
            DMA((depth,)),
            DMA((1 + depth,)),
        ]

    def level(self, k):
        return lax.rem(self.place.z + self.place.depth - k, self.place.depth)

    def lane(self, depth_at, core):
        return self.full.at[(slice(None), depth_at, core) + self.tail]

    def chunk(self, blk, k):
        return self.full.at[(blk, self.level(k), self.place.core) + self.tail]

    def start(self):
        place = self.place
        for k in range(1, place.depth):
            target = place.at(place.blk, lax.rem(place.z + k, place.depth), place.core)
            send(self.shard, self.chunk(place.blk, 0), self.z_s.at[k], self.z_r.at[k], target)

    def keep(self):
        pltpu.make_async_copy(self.shard, self.chunk(self.place.blk, 0), self.loc.at[0]).start()

    def forward(self, k, t):
        place = self.place
        bit, masks, seen = place.widen(k)[t]
        for n, m in enumerate(masks):
            there = self.chunk(place.blk ^ m, k)
            src = self.shard if m == 0 and k == 0 else there
            send(src, there, self.b_s.at[k, seen + n], self.b_r.at[k, seen + n], place.at(place.blk ^ bit, place.z, place.core))

    def climb(self, k):
        if k > 0:
            arrived(self.chunk(self.place.blk, k), self.z_r.at[k])
        self.forward(k, 0)

    def step(self, k, t):
        place = self.place
        bit, masks, seen = place.widen(k)[t]
        for n, m in enumerate(masks):
            arrived(self.chunk(place.blk ^ bit ^ m, k), self.b_r.at[k, seen + n])
        if t + 1 < place.bits:
            self.forward(k, t + 1)
        else:
            self.swap(k)

    def swap(self, k):
        place = self.place
        if k == 0:
            arrived(self.shard, self.loc.at[0])
        if self.only is None:
            held = self.lane(self.level(k), place.core)
            send(held, held, self.c_s.at[k], self.c_r.at[k], place.sibling())
        else:
            there = self.only.at[:, self.level(k), place.core]
            send(self.full.at[:, self.level(k), place.core, place.other], there, self.c_s.at[k], self.c_r.at[k], place.sibling())
            mine = self.full.at[:, self.level(k), place.core, place.part]
            pltpu.make_async_copy(mine, there, self.loc.at[1 + k]).start()

    def wait_swap(self, k):
        place = self.place
        if self.only is None:
            arrived(self.lane(self.level(k), 1 - place.core), self.c_r.at[k])
        else:
            arrived(self.only.at[:, self.level(k), 1 - place.core], self.c_r.at[k])
            arrived(self.only.at[:, self.level(k), place.core], self.loc.at[1 + k])

    def finish(self):
        place = self.place
        for k in range(place.depth):
            if self.only is None:
                self.wait_swap(k)
                arrived(self.lane(0, 0), self.c_s.at[k])
            else:
                arrived(self.only.at[:, 0, 0], self.c_s.at[k])
            if k > 0:
                arrived(self.shard, self.z_s.at[k])
            for n in range(place.blocks - 1):
                arrived(self.shard, self.b_s.at[k, n])


class GatherAcross(Gather):
    def start(self):
        place = self.place
        for m in range(1, place.blocks):
            target = place.at(place.blk ^ m, place.z, place.core)
            send(self.shard, self.chunk(place.blk, 0), self.b_s.at[0, m - 1], self.b_r.at[0, m - 1], target)

    def climb(self):
        place = self.place
        for m in range(1, place.blocks):
            arrived(self.chunk(place.blk ^ m, 0), self.b_r.at[0, m - 1])
        arrived(self.shard, self.loc.at[0])
        held = self.lane(place.z, place.core)
        for k in range(1, place.depth):
            target = place.at(place.blk, lax.rem(place.z + k, place.depth), place.core)
            send(held, held, self.z_s.at[k], self.z_r.at[k], target)
        self.pass_on(0)

    def pass_on(self, k):
        held = self.lane(self.level(k), self.place.core)
        if k > 0:
            arrived(held, self.z_r.at[k])
        send(held, held, self.c_s.at[k], self.c_r.at[k], self.place.sibling())

    def finish(self):
        place = self.place
        for k in range(place.depth):
            self.wait_swap(k)
            arrived(self.lane(0, 0), self.c_s.at[k])
            if k > 0:
                arrived(self.lane(0, 0), self.z_s.at[k])
        for m in range(1, place.blocks):
            arrived(self.shard, self.b_s.at[0, m - 1])


def first_kernel(sizes, block, pairs, *refs):
    place = Place(*sizes)
    tok, cot, vec, w_qkv, w_out, w_up, w_down = refs[:7]
    refs = refs[7:]
    att_ref, lse_ref, tok_own, cot_own, normed_out, qkv_out, cols_out, vec_out, stage, out_full, up_full, down_full = refs[:12]
    refs = refs[12:]
    tok_v, norm_v, norm_t, chunk_v, w32_v, cols_v, qkv_v, kh, vt, run_m, run_l, run_a = refs[:12]
    tok_s, tok_r, near_s, near_r, cot_s, cot_r, loc = refs[12:19]
    total = Total(place, *refs[19:23], refs[23:29])
    refs = refs[29:]
    late_rows = w_down.shape[0] // 3
    late_rows = late_rows if late_rows % 16 == 0 else 0
    early_rows = w_down.shape[0] - late_rows
    qkv = Gather(place, w_qkv, stage, refs[0:7], chunk_v)
    outw = Gather(place, w_out, out_full, refs[7:14])
    upw = Gather(place, w_up, up_full, refs[14:21])
    downw = GatherAcross(place, w_down, down_full, refs[21:28], span=(0, early_rows))
    climbers = [outw, upw]
    if late_rows:
        climbers.append(Gather(place, w_down, down_full, refs[28:35], span=(early_rows, late_rows)))
    arrays = [qkv, downw] + climbers
    blocks, depth, seqs, share, bits = place.blocks, place.depth, place.seqs, place.share, place.bits
    blk, z, core, home = place.blk, place.z, place.core, place.home
    pair = pl.program_id(0)
    rows, model = tok_v.shape[1:]
    length = blocks * rows
    count = length // block
    owned = w_qkv.shape[1]
    per_seq = share // 2
    local = lambda src, dst, sem: pltpu.make_async_copy(src, dst, sem).start()

    @pl.when(pair == 0)
    def _():
        total.stages[0] = vec[...]
        greet(place.peers(True, True))
        total.start()
        qkv.start()
        for i in range(seqs):
            for h in range(per_seq):
                target = (core * seqs + i) * per_seq + h

                @pl.when(target != blk)
                def _(i=i, h=h, target=target):
                    sems = tok_s.at[i * per_seq + h], tok_r.at[blk]
                    send(tok.at[i], tok_v.at[blk], *sems, place.at(target, z, core))

                @pl.when(target == blk)
                def _(i=i):
                    local(tok.at[i], tok_v.at[blk], loc.at[0])

        qkv.forward(0, 0)
        for array in arrays:
            array.keep()
        for k in range(1, depth):
            qkv.climb(k)
        for array in climbers:
            array.start()
        total.step(0)
        total.step(1)

        @pl.when(core == home)
        def _():
            for p in range(blocks):

                @pl.when(p != blk)
                def _():
                    arrived(tok_v.at[p], tok_r.at[p])

                @pl.when(p == blk)
                def _():
                    arrived(tok_v.at[p], loc.at[0])

                send(tok_v.at[p], tok_v.at[p], near_s.at[p], near_r.at[p], place.sibling())

        for n in range(2, bits + 1):
            total.step(n)
        for t in range(bits):
            for k in range(depth):
                qkv.step(k, t)
            if t == 0:
                downw.start()
        for array in climbers:
            for k in range(depth):
                array.climb(k)
        vec_out[...] = total.finish()
        gain, shift = vec_out[0:1, :], vec_out[1:2, :]
        part_rows = min(rows, 128)

        for p in range(blocks):

            @pl.when(core != home)
            def _(p=p):
                arrived(tok_v.at[p], near_r.at[p])

            def norm(i, _, p=p):
                inside = pl.ds(pl.multiple_of(i * part_rows, part_rows), part_rows)
                unit, _ = centered(tok_v[p, inside, :].astype(jnp.float32))
                at = pl.ds(pl.multiple_of(p * rows + i * part_rows, part_rows), part_rows)
                normed = unit * gain + shift
                norm_v[at, :] = normed.astype(jnp.bfloat16)
                norm_t[:, at] = normed.T.astype(jnp.bfloat16)
                return 0

            lax.fori_loop(0, rows // part_rows, norm, 0)
        local(norm_t, normed_out, loc.at[1])
        for t in range(place.per_part):
            local(tok_v.at[place.part * place.per_part + t], tok_own.at[t], loc.at[2 + t])
        downw.climb()
        for k in range(depth):
            qkv.wait_swap(k)
        for b in range(blocks):
            for d in range(depth):
                for c in range(2):
                    index = (b * depth + d) * 2 + c
                    w32_v[index * owned : (index + 1) * owned, :] = chunk_v[b, d, c].astype(jnp.float32)
        cols_v[...] = w32_v[...].astype(jnp.bfloat16)
        local(cols_v, cols_out, loc.at[2 + place.per_part])

        def project(i, _):
            at = pl.ds(pl.multiple_of(i * block, block), block)
            normed = norm_v[at, :]
            scale = jnp.where(lax.broadcasted_iota(jnp.int32, (1, 384), 1) < 128, 0.125, 1.0)
            for n in range(pairs):
                value = dot_nn(normed, cols_v[:, n * 384 : (n + 1) * 384]) * scale
                qkv_v[at, n * 384 : (n + 1) * 384] = value.astype(jnp.bfloat16)
            return 0

        lax.fori_loop(0, count, project, 0)
        local(qkv_v, qkv_out, loc.at[3 + place.per_part])

    per_pair = count * (count + 1) // 2
    tasks = []
    levels = [(array, k) for array in climbers for k in range(depth)]
    for n, (array, k) in enumerate(levels):
        for t in range(bits):
            where = 0.1 + 0.24 * t + (0.15 + 0.35 * t) * n / len(levels)
            tasks.append((where, functools.partial(array.step, k, t)))
    for k in range(1, depth):
        tasks.append((0.55 + 0.3 * k / depth, functools.partial(downw.pass_on, k)))

    def own_rows():
        for i in range(seqs):
            owner = (core * seqs + i) * share + blk // place.per_part
            slot = lax.rem(blk, place.per_part)

            @pl.when(owner != blk * 2 + core)
            def _(i=i, owner=owner, slot=slot):
                send(cot.at[i], cot_own.at[slot], cot_s.at[i], cot_r.at[slot], place.at(owner // 2, z, owner % 2))

            @pl.when(owner == blk * 2 + core)
            def _(i=i, slot=slot):
                local(cot.at[i], cot_own.at[slot], loc.at[4 + place.per_part])

    tasks.append((0.28, own_rows))
    tasks.sort(key=lambda task: task[0])
    todo = plan(tasks, pairs * per_pair)

    def lanes_of(n):
        return pl.ds(pl.multiple_of(pair * 384 + n * 128, 128), 128)

    split_heads(kh, qkv_v[:, lanes_of(1)])
    vt[...] = qkv_v[:, lanes_of(2)].astype(jnp.float32).T.astype(jnp.bfloat16)

    def q_step(qi, _):
        at_q = pl.ds(pl.multiple_of(qi * block, block), block)
        run_m[...] = jnp.full_like(run_m, -1e30)
        run_l[...] = jnp.zeros_like(run_l)
        run_a[...] = jnp.zeros_like(run_a)

        def one(kj, masked):
            at = pl.ds(pl.multiple_of(kj * block, block), block)
            q_rows = qkv_v[at_q, lanes_of(0)]
            scores = [dot_nt(kh[h, at, :], q_rows) for h in range(2)]
            weighed = []
            for h in range(2):
                peak, so_far = run_m[h : h + 1, :], run_l[h : h + 1, :]
                s = scores[h]
                u = s * s + 1.0
                inv = lax.rsqrt(u)
                mag = u * inv
                if masked:
                    mag = jnp.where(causal(block, block, kj, qi), mag, -1e30)
                new = jnp.maximum(peak, jnp.max(mag, axis=0, keepdims=True))
                p = jnp.exp(mag - new)
                alpha = jnp.exp(peak - new)
                run_m[h : h + 1, :] = new
                run_l[h : h + 1, :] = so_far * alpha + jnp.sum(p, axis=0, keepdims=True)
                weighed.append((alpha, (p * (s * inv)).astype(jnp.bfloat16)))
            for h in range(2):
                alpha, signed = weighed[h]
                head = slice(64 * h, 64 * h + 64)
                run_a[head, :] = run_a[head, :] * alpha + dot_nn(vt[head, at], signed)

        def k_step(kj, _):
            @pl.when(kj == qi)
            def _():
                one(kj, True)

            @pl.when(kj != qi)
            def _():
                one(kj, False)

            pump(todo, pair * per_pair + qi * (qi + 1) // 2 + kj)
            return 0

        lax.fori_loop(0, qi + 1, k_step, 0)
        both = []
        for h in range(2):
            both.append(run_a[64 * h : 64 * h + 64, :] / run_l[h : h + 1, :])
            lse_ref[0, h : h + 1, at_q] = run_m[h : h + 1, :] + jnp.log(run_l[h : h + 1, :])
        att_ref[at_q, :] = jnp.concatenate(both, 0).T.astype(jnp.bfloat16)
        return 0

    lax.fori_loop(0, count, q_step, 0)

    @pl.when(pair == pairs - 1)
    def _():
        for array in arrays:
            array.finish()
        for i in range(seqs):

            @pl.when((core * seqs + i) * share + blk // place.per_part != blk * 2 + core)
            def _(i=i):
                arrived(cot.at[i], cot_s.at[i])

        for t in range(place.per_part):
            here = (place.part * place.per_part + t == blk) & (home == core)

            @pl.when(here)
            def _(t=t):
                arrived(cot_own.at[t], loc.at[4 + place.per_part])

            @pl.when(jnp.logical_not(here))
            def _(t=t):
                arrived(cot_own.at[t], cot_r.at[t])

        arrived(norm_t, loc.at[1])
        arrived(cols_v, loc.at[2 + place.per_part])
        arrived(qkv_v, loc.at[3 + place.per_part])
        for t in range(place.per_part):
            arrived(tok_own.at[t], loc.at[2 + t])

        @pl.when(core == home)
        def _():
            for p in range(blocks):
                arrived(tok_v.at[p], near_s.at[p])

        for i in range(seqs):
            for h in range(per_seq):
                target = (core * seqs + i) * per_seq + h

                @pl.when(target != blk)
                def _(i=i, h=h):
                    arrived(tok.at[i], tok_s.at[i * per_seq + h])

                @pl.when((target == blk) & (core != home))
                def _():
                    arrived(tok_v.at[blk], loc.at[0])


def first_half(sizes, tok, cot, vec, w_qkv, w_out, w_up, w_down, block):
    blocks, lanes, seqs = sizes
    depth, share = lanes // 2, blocks // seqs
    per_part = blocks // share
    rows, model = tok.shape[1:]
    length = blocks * rows
    width = w_qkv.shape[2]
    pairs = width // 384
    low, full = jnp.bfloat16, jnp.float32
    shape = jax.ShapeDtypeStruct
    owners = (blocks, depth, 2)
    in_vmem = pl.BlockSpec(memory_space=pltpu.VMEM)
    return pl.pallas_call(
        functools.partial(first_kernel, sizes, block, pairs),
        grid=(pairs,),
        out_shape=[
            shape((length, 128 * pairs), low),
            shape((pairs, 8, length), full),
            shape((per_part, rows, model), low),
            shape((per_part, rows, model), low),
            shape((model, length), low),
            shape((length, width), low),
            shape((model, width), low),
            shape(vec.shape, full),
            shape(owners + w_qkv.shape, low),
            shape(owners + w_out.shape, low),
            shape(owners + w_up.shape, low),
            shape(owners + w_down.shape, low),
        ],
        in_specs=[ANYWHERE, ANYWHERE, in_vmem] + [ANYWHERE] * 4,
        out_specs=[pl.BlockSpec((length, 128), lambda p: (0, p)), pl.BlockSpec((1, 8, length), lambda p: (p, 0, 0))]
        + [ANYWHERE] * 5
        + [in_vmem]
        + [ANYWHERE] * 4,
        scratch_shapes=[
            pltpu.VMEM((blocks, rows, model), low),
            pltpu.VMEM((length, model), low),
            pltpu.VMEM((model, length), low),
            pltpu.VMEM(owners + w_qkv.shape[1:], low),
            pltpu.VMEM((model, width), full),
            pltpu.VMEM((model, width), low),
            pltpu.VMEM((length, width), low),
            pltpu.VMEM((2, length, 128), low),
            pltpu.VMEM((128, length), low),
            pltpu.VMEM((8, block), full),
            pltpu.VMEM((8, block), full),
            pltpu.VMEM((128, block), full),
            DMA((seqs * share // 2,)),
            DMA((blocks,)),
            DMA((blocks,)),
            DMA((blocks,)),
            DMA((seqs,)),
            DMA((per_part,)),
            DMA((5 + per_part,)),
        ]
        + Total.scratch(sizes, vec.shape)
        + Gather.sems(sizes) * 5,
        compiler_params=pltpu.CompilerParams(collective_id=0, has_side_effects=True, vmem_limit_bytes=VMEM_LIMIT),
    )(tok, cot, vec, w_qkv, w_out, w_up, w_down)


def dot_tn(left, right):
    return lax.dot_general(left, right, (((0,), (0,)), ((), ())), preferred_element_type=jnp.float32)


def centered(values):
    center = jnp.mean(values, axis=-1, keepdims=True)
    offsets = values - center
    spread = jnp.mean(offsets * offsets, axis=-1, keepdims=True)
    inverse = lax.rsqrt(spread + 1e-05)
    return offsets * inverse, inverse


def norm_back(values, grads, gain):
    unit, inverse = centered(values)
    scaled = grads * gain
    first = jnp.mean(scaled, axis=-1, keepdims=True)
    second = jnp.mean(scaled * unit, axis=-1, keepdims=True)
    back = inverse * (scaled - first - unit * second)
    return back, jnp.sum(grads * unit, axis=0, keepdims=True), jnp.sum(grads, axis=0, keepdims=True)


def gelu_parts(x):
    square = x * x
    half = 0.5 + 0.5 * jnp.tanh(0.7978845608028654 * x * (1.0 + 0.044715 * square))
    slope = half + x * (2.0 * half * (1.0 - half)) * (0.7978845608028654 + 0.1070322243 * square)
    return x * half, slope


def mlp_kernel(sizes, cols, tile, chunk, *refs):
    place = Place(*sizes)
    att, tok_own, cot, w_out, w_up, w_down, vec, live = refs[:8]
    result, g_heads, g_mid, g_out, g_up, g_down, g_vec = refs[8:15]
    (att_v, tok_v, cot_v, res_v, out_v, up_v, down_v, mid_v, n2_v, n2t_v, hid_v, slope_v, sum_v, ga_v) = refs[15:29]
    (st_out, st_up, st_down) = refs[29:32]
    a_s, a_r, g_s, g_r, m_s, m_r, loc, up_l, down_l, o_l = refs[32:]
    share, per_part, seqs = place.share, place.per_part, place.seqs
    part, blk, z, core = place.part, place.blk, place.z, place.core
    rows, model = mid_v.shape
    block = rows // per_part
    ff = up_v.shape[1]
    chunks, tiles = ff // chunk, rows // tile
    flat = blk * 2 + core
    partners = [((flat ^ k) // 2, z, (flat ^ k) % 2) for k in range(1, share)]
    slot_of = lax.rem(place.seq, seqs)
    greet(place.peers(False, True))
    for k in range(1, share):
        send(att.at[part ^ k], att_v.at[part], a_s.at[k - 1], a_r.at[k - 1], place.at(*partners[k - 1]))

    def local(src, dst, sem):
        pltpu.make_async_copy(src, dst, sem).start()

    local(att.at[part], att_v.at[part], loc.at[0])
    for t in range(per_part):
        local(tok_own.at[t], tok_v.at[t], loc.at[1 + t])
    local(w_out, out_v, loc.at[1 + per_part])
    local(cot, cot_v, loc.at[2 + per_part])

    def span(f):
        return pl.ds(pl.multiple_of(f * chunk, chunk), chunk)

    for f in range(chunks):
        local(w_up.at[:, pl.ds(f * chunk, chunk)], up_v.at[:, pl.ds(f * chunk, chunk)], up_l.at[f])
        local(w_down.at[pl.ds(f * chunk, chunk)], down_v.at[pl.ds(f * chunk, chunk)], down_l.at[f])

    arrived(att_v.at[part], loc.at[0])
    for t in range(per_part):
        arrived(tok_v.at[t], loc.at[1 + t])
    arrived(out_v, loc.at[1 + per_part])
    for k in range(1, share):
        arrived(att_v.at[part ^ k], a_r.at[k - 1])
    gain, shift = vec[2:3, :], vec[3:4, :]
    per_block = block // tile

    def spot(i):
        return i // per_block, pl.ds(pl.multiple_of(lax.rem(i, per_block) * tile, tile), tile)

    def enter(i, _):
        at = pl.ds(pl.multiple_of(i * tile, tile), tile)
        branch = dot_nn(att_v[0, at, :cols], out_v[:cols, :])
        for g in range(1, share):
            branch = branch + dot_nn(att_v[g, at, :cols], out_v[g * cols : (g + 1) * cols, :])
        t, inside = spot(i)
        middle = tok_v[t, inside, :].astype(jnp.float32) + live[at, :] * branch
        mid_v[at, :] = middle
        unit, _ = centered(middle)
        normed = unit * gain + shift
        n2_v[at, :] = normed.astype(jnp.bfloat16)
        n2t_v[:, at] = normed.T.astype(jnp.bfloat16)
        return 0

    lax.fori_loop(0, tiles, enter, 0)
    sum_v[...] = mid_v[...]

    def up_step(f, _):
        arrived(up_v.at[:, span(f)], up_l.at[f])
        arrived(down_v.at[span(f)], down_l.at[f])
        hidden, slope = gelu_parts(dot_nn(n2_v[...], up_v[:, span(f)]))
        hidden = hidden.astype(jnp.bfloat16)
        hid_v[:, span(f)] = hidden
        slope_v[:, span(f)] = slope.astype(jnp.bfloat16)
        sum_v[...] += dot_nn(hidden, down_v[span(f), :])
        return 0

    lax.fori_loop(0, chunks, up_step, 0)
    for t in range(per_part):
        res_v[t] = sum_v[t * block : (t + 1) * block, :].astype(jnp.bfloat16)
        source = part * per_part + t
        mine = (source == blk) & (place.home == core)

        @pl.when(mine)
        def _(t=t):
            local(res_v.at[t], result.at[slot_of], loc.at[0])

        @pl.when(jnp.logical_not(mine))
        def _(t=t, source=source):
            send(res_v.at[t], result.at[slot_of], m_s.at[t], m_r.at[slot_of], place.at(source, z, place.home))

    arrived(cot_v, loc.at[2 + per_part])
    sum_v[...] = jnp.zeros_like(sum_v)

    def back_step(f, _):
        top = cot_v[...].reshape(rows, model)
        grad_pre = (dot_nt(top, down_v[span(f), :]) * slope_v[:, span(f)].astype(jnp.float32)).astype(jnp.bfloat16)
        now = lax.rem(f, 2)

        @pl.when(f >= 2)
        def _():
            arrived(st_down.at[now], o_l.at[now])
            arrived(st_up.at[now], o_l.at[2 + now])

        st_down[now] = dot_tn(hid_v[:, span(f)], top).astype(jnp.bfloat16)
        st_up[now] = dot_nn(n2t_v[...], grad_pre).astype(jnp.bfloat16)
        local(st_down.at[now], g_down.at[span(f)], o_l.at[now])
        local(st_up.at[now], g_up.at[:, span(f)], o_l.at[2 + now])
        sum_v[...] += dot_nt(grad_pre, up_v[:, span(f)])
        return 0

    lax.fori_loop(0, chunks, back_step, 0)
    g_vec[...] = jnp.zeros_like(g_vec)

    def leave(i, _):
        at = pl.ds(pl.multiple_of(i * tile, tile), tile)
        t, inside = spot(i)
        back, d_gain, d_shift = norm_back(mid_v[at, :], sum_v[at, :], gain)
        g_vec[0:1, :] += d_gain
        g_vec[1:2, :] += d_shift
        total = cot_v[t, inside, :].astype(jnp.float32) + back
        mid_v[at, :] = total
        branch = (live[at, :] * total).astype(jnp.bfloat16)
        n2_v[at, :] = branch
        heads = dot_nt(branch, out_v[...]).astype(jnp.bfloat16)
        for g in range(share):
            if cols == ga_v.shape[2]:
                ga_v[g, at, :] = heads[:, g * cols : (g + 1) * cols]
            else:
                piece = heads[:, g * cols : (g + 1) * cols]
                ga_v[g, at, :] = jnp.concatenate([piece, jnp.zeros((tile, ga_v.shape[2] - cols), jnp.bfloat16)], 1)
        return 0

    lax.fori_loop(0, tiles, leave, 0)
    for k in range(1, share):
        send(ga_v.at[part ^ k], g_heads.at[part], g_s.at[k - 1], g_r.at[k - 1], place.at(*partners[k - 1]))
    local(ga_v.at[part], g_heads.at[part], loc.at[1])
    local(mid_v, g_mid, loc.at[2])
    for g in range(share):
        st_out[g * cols : (g + 1) * cols, :] = dot_tn(att_v[g, :, :cols], n2_v[...]).astype(jnp.bfloat16)
    local(st_out, g_out, loc.at[1 + per_part])
    for n in range(min(2, chunks)):
        arrived(st_down.at[n], o_l.at[n])
        arrived(st_up.at[n], o_l.at[2 + n])
    arrived(st_out, loc.at[1 + per_part])
    arrived(mid_v, loc.at[2])
    arrived(ga_v.at[part], loc.at[1])
    for k in range(1, share):
        arrived(att.at[part ^ k], a_s.at[k - 1])
        arrived(ga_v.at[part ^ k], g_s.at[k - 1])
        arrived(g_heads.at[part ^ k], g_r.at[k - 1])
    for i in range(seqs):
        owner = (core * seqs + i) * share + blk // per_part

        @pl.when(owner != flat)
        def _(i=i):
            arrived(result.at[i], m_r.at[i])

    for t in range(per_part):
        mine = (part * per_part + t == blk) & (place.home == core)

        @pl.when(mine)
        def _(t=t):
            arrived(res_v.at[t], loc.at[0])

        @pl.when(jnp.logical_not(mine))
        def _(t=t):
            arrived(res_v.at[t], m_s.at[t])


def feed_forward(sizes, cols, att, tok_own, cot, w_out, w_up, w_down, vec, live, tile, chunk):
    blocks, lanes, seqs = sizes
    share = blocks // seqs
    per_part = blocks // share
    block, model = tok_own.shape[1:]
    rows = per_part * block
    wide = att.shape[2]
    ff = w_up.shape[1]
    chunks = ff // chunk
    in_vmem = pl.BlockSpec(memory_space=pltpu.VMEM)
    low, full = jnp.bfloat16, jnp.float32
    return pl.pallas_call(
        functools.partial(mlp_kernel, sizes, cols, tile, chunk),
        out_shape=[
            jax.ShapeDtypeStruct((seqs, block, model), low),
            jax.ShapeDtypeStruct((share, rows, wide), low),
            jax.ShapeDtypeStruct((rows, model), full),
            jax.ShapeDtypeStruct((model, model), low),
            jax.ShapeDtypeStruct((model, ff), low),
            jax.ShapeDtypeStruct((ff, model), low),
            jax.ShapeDtypeStruct((8, model), full),
        ],
        in_specs=[ANYWHERE] * 6 + [in_vmem] * 2,
        out_specs=[ANYWHERE] * 6 + [in_vmem],
        scratch_shapes=[
            pltpu.VMEM((share, rows, wide), low),
            pltpu.VMEM((per_part, block, model), low),
            pltpu.VMEM((per_part, block, model), low),
            pltpu.VMEM((per_part, block, model), low),
            pltpu.VMEM((model, model), low),
            pltpu.VMEM((model, ff), low),
            pltpu.VMEM((ff, model), low),
            pltpu.VMEM((rows, model), full),
            pltpu.VMEM((rows, model), low),
            pltpu.VMEM((model, rows), low),
            pltpu.VMEM((rows, ff), low),
            pltpu.VMEM((rows, ff), low),
            pltpu.VMEM((rows, model), full),
            pltpu.VMEM((share, rows, wide), low),
            pltpu.VMEM((model, model), low),
            pltpu.VMEM((2, model, chunk), low),
            pltpu.VMEM((2, chunk, model), low),
            DMA((share,)),
            DMA((share,)),
            DMA((share,)),
            DMA((share,)),
            DMA((per_part,)),
            DMA((seqs,)),
            DMA((3 + per_part,)),
            DMA((chunks,)),
            DMA((chunks,)),
            DMA((4,)),
        ],
        compiler_params=pltpu.CompilerParams(collective_id=4, has_side_effects=True, vmem_limit_bytes=VMEM_LIMIT),
    )(att, tok_own, cot, w_out, w_up, w_down, vec, live)


def last_kernel(sizes, block, pairs, *refs):
    place = Place(*sizes)
    blocks, depth, seqs, share, bits = place.blocks, place.depth, place.seqs, place.share, place.bits
    blk, z, core, part = place.blk, place.z, place.core, place.part
    per_part = place.per_part
    count = 3 + pairs
    q_ref, k_ref, v_ref, g_ref, att_ref, lse_ref = refs[:6]
    big, tok_own, g_mid, norm_t, cols, vec, two = refs[6:9], refs[9], refs[10], refs[11], refs[12], refs[13], refs[14]
    refs = refs[15:]
    sums, tok_out, vec_out, refs = refs[:count], refs[count], refs[count + 1], refs[count + 2 :]
    kh, vh, qh, gh, kt, delta, dqt, dk, dv = refs[:9]
    gq_v, own_v, norm_v, cols_v, tok_v, mid_v, out_v, part_v, got_v, sum_v = refs[9:19]
    p_s, p_r, t_s, t_r, loc = refs[19:24]
    total = Total(place, *refs[24:28], refs[28:34])
    kinds = ["rows"] * 3 + ["columns"] * pairs
    fold = Fold(place, kinds, list(big) + [own_v.at[p] for p in range(pairs)], [], sums, [], refs[34:])
    pair = pl.program_id(0)
    length = q_ref.shape[0]
    rows, model = mid_v.shape
    owned = own_v.shape[4]
    steps = length // block
    per_pair = steps * (steps + 1) // 2
    flat = blk * 2 + core
    partners = [((flat ^ k) // 2, z, (flat ^ k) % 2) for k in range(1, share)]
    slot_of = lax.rem(place.seq, seqs)
    local = lambda src, dst, sem: pltpu.make_async_copy(src, dst, sem).start()

    tasks = []
    units = [(a, k) for a in range(3) for k in fold.order]
    per = 12.0 / len(units)
    for n, (a, k) in enumerate(units):
        tasks.append((8 + 1.2 * per * n, functools.partial(fold.join, a, k)))
        for t in range(bits):
            where = (14 + 2.7 * per * n) if t == 0 else (38 + 8 * t + 1.4 * per * n)
            tasks.append((where, functools.partial(fold.step, a, k, t)))
    for a in range(3):
        tasks.append((72 + 2 * a, functools.partial(fold.total, a)))
    for p in range(pairs - 1):
        third = 85.0 / pairs
        for n, k in enumerate(fold.order):
            tasks.append(((p + 1.1) * third, functools.partial(fold.join, 3 + p, k)))
            for t in range(bits):
                where = (68 if p == pairs - 2 else 60) + 6 * t
                tasks.append((where, functools.partial(fold.step, 3 + p, k, t)))
    tasks = [(where / 85.0, call) for where, call in tasks]
    tasks.sort(key=lambda task: task[0])
    todo = plan(tasks, pairs * per_pair)

    @pl.when(pair == 0)
    def _():
        fold.greet()
        fold.clear()
        for a, k in units:
            fold.start(a, k)
        local(norm_t, norm_v, loc.at[0])
        local(cols, cols_v, loc.at[1])
        local(g_mid, mid_v, loc.at[2])
        local(tok_own, tok_v, loc.at[3])

    split_heads(kh, k_ref[...])
    split_heads(vh, v_ref[...])
    split_heads(qh, q_ref[...])
    split_heads(gh, g_ref[...])
    kt[...] = k_ref[...].astype(jnp.float32).T.astype(jnp.bfloat16)
    prod = (g_ref[...].astype(jnp.float32) * att_ref[...].astype(jnp.float32)).T
    delta[0:1, :] = jnp.sum(prod[:64], axis=0, keepdims=True)
    delta[1:2, :] = jnp.sum(prod[64:], axis=0, keepdims=True)
    dqt[...] = jnp.zeros_like(dqt)

    def k_step(kj, _):
        at = pl.ds(pl.multiple_of(kj * block, block), block)

        def one(qi, masked):
            at_q = pl.ds(pl.multiple_of(qi * block, block), block)
            q_rows = q_ref[at_q, :]
            g_rows = g_ref[at_q, :]
            add_k = add_v = None
            both = [(dot_nt(kh[h, at, :], q_rows), dot_nt(vh[h, at, :], g_rows)) for h in range(2)]
            for h in range(2):
                s, dp = both[h]
                u = s * s + 1.0
                inv = lax.rsqrt(u)
                arg = u * inv - lse_ref[0, h : h + 1, at_q]
                if masked:
                    arg = jnp.where(causal(block, block, kj, qi), arg, -1e30)
                p = jnp.exp(arg)
                sgn = s * inv
                t = inv * inv * (inv - 1.0) + 1.0
                ds = (p * (dp * t - sgn * delta[h : h + 1, at_q])).astype(jnp.bfloat16)
                signed = (p * sgn).astype(jnp.bfloat16)
                one_v = dot_nn(signed, gh[h, at_q, :])
                one_k = dot_nn(ds, qh[h, at_q, :])
                add_v = one_v if h == 0 else add_v + one_v
                add_k = one_k if h == 0 else add_k + one_k
                dqt[64 * h : 64 * h + 64, at_q] += dot_nn(kt[64 * h : 64 * h + 64, at], ds)
            return add_k, add_v

        def more(qi, _):
            @pl.when(qi == kj)
            def _():
                dk[...], dv[...] = one(qi, True)

            @pl.when(qi != kj)
            def _():
                add_k, add_v = one(qi, False)
                dk[...] += add_k
                dv[...] += add_v

            pump(todo, pair * per_pair + kj * steps - kj * (kj - 1) // 2 + qi - kj)
            return 0

        lax.fori_loop(kj, steps, more, 0)
        gq_v[pair, at, 128:256] = dk[...].astype(jnp.bfloat16)
        gq_v[pair, at, 256:384] = dv[...].astype(jnp.bfloat16)
        return 0

    lax.fori_loop(0, steps, k_step, 0)
    gq_v[pair, :, 0:128] = (dqt[...] * 0.125).T.astype(jnp.bfloat16)

    @pl.when(pair == 0)
    def _():
        arrived(norm_v, loc.at[0])
        arrived(cols_v, loc.at[1])
        arrived(mid_v, loc.at[2])
        arrived(tok_v, loc.at[3])

    def weight_grad():
        sum_v[...] = dot_nn(norm_v[...], gq_v[pair])
        for b in range(blocks):
            for d in range(depth):
                for c in range(2):
                    first = ((b * depth + d) * 2 + c) * owned
                    own_v[pair, b, d, c] = sum_v[first : first + owned, :].astype(jnp.bfloat16)
        for p in range(pairs):

            @pl.when(pair == p)
            def _(p=p):
                for k in fold.order:
                    fold.start(3 + p, k)

    @pl.when(pair != pairs - 1)
    def _():
        weight_grad()

    @pl.when(pair == pairs - 1)
    def _():
        mine = 3 + pairs - 1
        tile = min(256, block, rows)

        def input_grad(g, i):
            at = pl.ds(pl.multiple_of(g * rows + i * tile, tile), tile)
            value = dot_nt(gq_v[0, at, :], cols_v[:, 0:384])
            for p in range(1, pairs):
                value = value + dot_nt(gq_v[p, at, :], cols_v[:, p * 384 : (p + 1) * 384])
            return value

        per_block = rows // per_part // tile
        half = rows // per_part
        for t in range(per_part):
            for k in range(1, share):

                def away(i, _, k=k):
                    at = pl.ds(pl.multiple_of(i * tile, tile), tile)
                    part_v[k - 1, at, :] = input_grad(part ^ k, i).astype(jnp.bfloat16)
                    return 0

                lax.fori_loop(t * per_block, (t + 1) * per_block, away, 0)
                piece = pl.ds(t * half, half)
                sems = p_s.at[k - 1, t], p_r.at[k - 1, t]
                send(part_v.at[k - 1, piece], got_v.at[k - 1, piece], *sems, place.at(*partners[k - 1]))
        weight_grad()
        total.stages[0] = jnp.zeros(total.stages.shape[1:], jnp.float32)
        total.stages[0, 2:4, :] = two[0:2, :]
        gain = vec[0:1, :]

        def leave(i, _):
            at = pl.ds(pl.multiple_of(i * tile, tile), tile)
            t = i // per_block
            inside = pl.ds(pl.multiple_of(lax.rem(i, per_block) * tile, tile), tile)
            value = input_grad(part, i)
            for k in range(1, share):
                value = value + got_v[k - 1, at, :].astype(jnp.float32)
            back, d_gain, d_shift = norm_back(tok_v[t, inside, :].astype(jnp.float32), value, gain)
            total.stages[0, 0:1, :] += d_gain
            total.stages[0, 1:2, :] += d_shift
            out_v[t, inside, :] = (mid_v[at, :] + back).astype(jnp.bfloat16)
            return 0

        for t in range(per_part):
            for k in range(1, share):
                arrived(got_v.at[k - 1, pl.ds(t * half, half)], p_r.at[k - 1, t])
            lax.fori_loop(t * per_block, (t + 1) * per_block, leave, 0)
            source = part * per_part + t
            here = (source == blk) & (place.home == core)

            @pl.when(here)
            def _(t=t):
                local(out_v.at[t], tok_out.at[slot_of], loc.at[0])

            @pl.when(jnp.logical_not(here))
            def _(t=t, source=source):
                send(out_v.at[t], tok_out.at[slot_of], t_s.at[t], t_r.at[slot_of], place.at(source, z, place.home))

            if t == 0:
                for k in fold.order:
                    fold.join(mine, k)
        total.start()
        for t in range(bits):
            for k in fold.order:
                fold.step(mine, k, t)
            total.step(t)
        total.step(bits)
        for p in range(pairs):
            fold.total(3 + p)
        vec_out[...] = total.finish()
        fold.finish()
        for k in range(1, share):
            for t in range(per_part):
                arrived(part_v.at[k - 1, pl.ds(t * half, half)], p_s.at[k - 1, t])
        for t in range(per_part):
            here = (part * per_part + t == blk) & (place.home == core)

            @pl.when(here)
            def _(t=t):
                arrived(out_v.at[t], loc.at[0])

            @pl.when(jnp.logical_not(here))
            def _(t=t):
                arrived(out_v.at[t], t_s.at[t])

        for i in range(seqs):
            owner = (core * seqs + i) * share + blk // per_part

            @pl.when(owner != flat)
            def _(i=i):
                arrived(tok_out.at[i], t_r.at[i])


def last_half(sizes, qkv, g_att, att, lse, big, tok_own, g_mid, norm_t, cols, vec, two, block):
    blocks, lanes, seqs = sizes
    depth, share = lanes // 2, blocks // seqs
    length, width = qkv.shape
    pairs = width // 384
    model = cols.shape[0]
    owned = model // (blocks * lanes)
    per_part, rows_in, _ = tok_own.shape
    rows = per_part * rows_in
    low, full = jnp.bfloat16, jnp.float32
    in_vmem = pl.BlockSpec(memory_space=pltpu.VMEM)
    own = jax.ShapeDtypeStruct((blocks, depth, 2, owned, 384), low)
    kinds = ["rows"] * 3 + ["columns"] * pairs
    out, _, scratch = fold_shapes(sizes, list(big) + [own] * pairs, kinds, [])
    return pl.pallas_call(
        functools.partial(last_kernel, sizes, block, pairs),
        grid=(pairs,),
        out_shape=out + [jax.ShapeDtypeStruct((seqs, rows_in, model), low), jax.ShapeDtypeStruct(vec.shape, full)],
        in_specs=[pl.BlockSpec((length, 128), lambda p, n=n: (0, 3 * p + n)) for n in range(3)]
        + [pl.BlockSpec((length, 128), lambda p: (0, p))] * 2
        + [pl.BlockSpec((1, 8, length), lambda p: (p, 0, 0))]
        + [ANYWHERE] * 7
        + [in_vmem] * 2,
        out_specs=[in_vmem] * len(out) + [ANYWHERE, in_vmem],
        scratch_shapes=[pltpu.VMEM((2, length, 128), low)] * 4
        + [
            pltpu.VMEM((128, length), low),
            pltpu.VMEM((8, length), full),
            pltpu.VMEM((128, length), full),
            pltpu.VMEM((block, 128), full),
            pltpu.VMEM((block, 128), full),
            pltpu.VMEM((pairs, length, 384), low),
            pltpu.VMEM((pairs,) + own.shape, low),
            pltpu.VMEM((model, length), low),
            pltpu.VMEM((model, width), low),
            pltpu.VMEM((per_part, rows_in, model), low),
            pltpu.VMEM((rows, model), full),
            pltpu.VMEM((per_part, rows_in, model), low),
            pltpu.VMEM((share - 1, rows, model), low),
            pltpu.VMEM((share - 1, rows, model), low),
            pltpu.VMEM((model, 384), full),
            DMA((share, per_part)),
            DMA((share, per_part)),
            DMA((per_part,)),
            DMA((seqs,)),
            DMA((4,)),
        ]
        + Total.scratch(sizes, vec.shape)
        + scratch,
        compiler_params=pltpu.CompilerParams(collective_id=2, has_side_effects=True, vmem_limit_bytes=63 * 2**20),
    )(qkv, qkv, qkv, g_att, att, lse, *big, tok_own, g_mid, norm_t, cols, vec, two)


def shards(sizes, tokens, seq_len, ln1_gain, ln1_shift, w_qkv, w_out, ln2_gain, ln2_shift, w_up, w_down, cotangent):
    blocks, lanes, seqs = sizes
    place = Place(*sizes)
    share, part = place.share, place.part
    model = tokens.shape[2]
    length = blocks * tokens.shape[1]
    rows = length // share
    owned = w_qkv.shape[0]
    cols = model // share
    wide = -(-cols // 128) * 128

    pairs = wide // 128
    grouped = jnp.pad(w_qkv.reshape(owned, 3, share, cols), ((0, 0), (0, 0), (0, 0), (0, wide - cols)))
    grouped = grouped.reshape(owned, 3, share, pairs, 128)
    grouped = jnp.transpose(grouped, (2, 0, 3, 1, 4)).reshape(share, owned, 3 * wide)
    flat = place.blk * lanes + lax.axis_index("seq")
    vec = jnp.zeros((8, model), jnp.float32)
    own = jnp.stack([ln1_gain, ln1_shift, ln2_gain, ln2_shift]).astype(jnp.float32)
    vec = lax.dynamic_update_slice(vec, own, (0, flat * owned))
    first = (place.blk == 0).astype(jnp.float32)
    vec = lax.dynamic_update_slice(vec, first * seq_len.astype(jnp.float32)[None], (4, lax.axis_index("seq") * seqs))
    outs = first_half(sizes, tokens, cotangent, vec, grouped, w_out, w_up, w_down, min(512, rows))
    att, lse, tok_own, cot_own, norm_t, qkv, qkv_cols, params, _, out_full, up_full, down_full = outs
    out_full, up_full = [a.reshape(model, -1) for a in (out_full, up_full)]
    down_full = down_full.reshape(-1, model)
    my_len = lax.dynamic_index_in_dim(params[4], place.z * 2 * seqs + place.seq, 0, False)

    positions = part * rows + jnp.arange(rows, dtype=jnp.int32)
    live = (positions.astype(jnp.float32) < my_len).astype(jnp.float32)[:, None]
    result, g_heads, grad_mid, grad_out, grad_up, grad_down, two_grads = feed_forward(
        sizes,
        cols,
        att.reshape(share, rows, wide),
        tok_own,
        cot_own,
        out_full,
        up_full,
        down_full,
        params,
        live,
        min(512, tokens.shape[1]),
        min(1024, w_up.shape[1]),
    )

    def cut(values):
        return values.reshape((blocks, lanes // 2, 2, -1) + values.shape[1:])

    done = last_half(
        sizes,
        qkv,
        g_heads.reshape(length, wide),
        att,
        lse,
        [cut(grad_out), cut(grad_up), cut(grad_down)],
        tok_own,
        grad_mid,
        norm_t,
        qkv_cols,
        params,
        two_grads,
        min(512, rows),
    )
    sum_out, sum_up, sum_down, *sum_pairs, grad_tokens, vec_sum = done
    vec_own = lax.dynamic_slice_in_dim(vec_sum, flat * owned, owned, 1)
    sum_qkv = jnp.stack(sum_pairs).reshape(pairs, share, owned, 3, 128)
    sum_qkv = jnp.transpose(sum_qkv, (2, 3, 1, 0, 4)).reshape(owned, 3, share, wide)[..., :cols].reshape(owned, 3 * model)
    return (
        result,
        grad_tokens.astype(jnp.float32),
        vec_own[0],
        vec_own[1],
        sum_qkv,
        sum_out,
        vec_own[2],
        vec_own[3],
        sum_up,
        sum_down,
    )


def solution(mesh):
    blocks, lanes = mesh.shape["blk"], mesh.shape["seq"]
    whole = P(("blk", "seq"))
    rows = P(("blk", "seq"), None)
    tokens = P("seq", "blk", None)

    def run(*args):
        seqs = args[0].shape[0] // lanes
        return jax.shard_map(
            functools.partial(shards, (blocks, lanes, seqs)),
            mesh=mesh,
            in_specs=(tokens, P("seq"), whole, whole, rows, rows, whole, whole, rows, rows, tokens),
            out_specs=(tokens, tokens, whole, whole, rows, rows, whole, whole, rows, rows),
            check_vma=False,
        )(*args)

    return run
```

```python
import functools

import jax
import jax.numpy as jnp
from jax import lax
from jax.experimental import pallas as pl
from jax.experimental.pallas import tpu as pltpu
from jax.sharding import PartitionSpec as P

HEADS = 12
VMEM_LIMIT = 60 * 2**20


MESH = pl.DeviceIdType.MESH
DMA = pltpu.SemaphoreType.DMA
ANYWHERE = pl.BlockSpec(memory_space=pl.ANY)


class Place:
    def __init__(self, blocks, lanes, seqs):
        self.blocks, self.depth, self.seqs = blocks, lanes // 2, seqs
        self.share = blocks // seqs
        self.per_part = blocks // self.share
        self.bits = max(1, blocks.bit_length() - 1)
        self.blk = lax.axis_index("blk")
        lane = lax.axis_index("seq")
        self.z, self.core = lane // 2, lane % 2
        flat = self.blk * 2 + self.core
        self.seq, self.part = flat // self.share, flat % self.share
        self.home = self.seq // seqs
        self.other = lax.rem(self.blk * 2 + 1 - self.core, self.share)

    def at(self, blk, z, core):
        return (blk, z * 2 + core)

    def sibling(self):
        return self.at(self.blk, self.z, 1 - self.core)

    def peers(self, along_z, along_blk):
        out = [self.sibling()]
        if along_z:
            out += [self.at(self.blk, lax.rem(self.z + k, self.depth), self.core) for k in range(1, self.depth)]
        if along_blk:
            for m in range(1, self.blocks):
                out += [self.at(self.blk ^ m, self.z, 0), self.at(self.blk ^ m, self.z, 1)]
        return out

    def bit(self, part, step):
        return 1 << ((part + step) % self.bits)

    def widen(self, k):
        masks, out, seen = [0], [], 0
        for t in range(self.bits):
            bit = self.bit(k, t)
            out.append((bit, list(masks), seen))
            seen += len(masks)
            masks += [m ^ bit for m in masks]
        return out

    def narrow(self, k):
        out, seen = [], 0
        for t in range(self.bits):
            masks = [0]
            for u in range(t + 1, self.bits):
                masks += [m ^ self.bit(k, u) for m in masks]
            out.append((self.bit(k, t), masks, seen))
            seen += len(masks)
        return out


def greet(devices):
    barrier = pltpu.get_barrier_semaphore()
    for device in devices:
        pl.semaphore_signal(barrier, inc=1, device_id=device, device_id_type=MESH)
    pl.semaphore_wait(barrier, len(devices))


def send(src, dst, send_sem, recv_sem, device):
    pltpu.make_async_remote_copy(
        src_ref=src, dst_ref=dst, send_sem=send_sem, recv_sem=recv_sem, device_id=device, device_id_type=MESH
    ).start()


def arrived(ref, sem):
    pltpu.make_async_copy(ref, ref, sem).wait()


class Fold:
    def __init__(self, place, kinds, grads, rows_in, sums, rows_out, scratch):
        self.place, self.kinds, self.grads = place, kinds, grads
        self.rows_in, self.sums, self.rows_out = rows_in, sums, rows_out
        self.count, self.moves = len(kinds), len(rows_in)
        n = self.count
        self.held, self.near, self.wide, self.tall = (scratch[i * n : i * n + n] for i in range(4))
        self.m_s, self.m_r, self.z_s, self.z_r, self.b_s, self.b_r, self.c_s, self.c_r, self.loc = scratch[4 * n :]
        self.order = list(range(1, place.depth)) + [0]
        self.units = [(a, k) for a in range(n) for k in self.order]

    @staticmethod
    def scratch(sizes, chunks, types, kinds, moves):
        blocks, lanes, seqs = sizes
        depth, share, count = lanes // 2, blocks // seqs, len(chunks)
        out = [pltpu.VMEM((blocks, depth) + c, t) for c, t in zip(chunks, types)]
        out += [
            pltpu.VMEM((1, 1, 8, 128) if kind == "columns" else (blocks, depth) + c, t)
            for c, t, kind in zip(chunks, types, kinds)
        ]
        out += [pltpu.VMEM((depth, blocks - 1) + c, t) for c, t in zip(chunks, types)]
        out += [pltpu.VMEM((depth - 1,) + c, t) for c, t in zip(chunks, types)]
        return out + [
            DMA((max(1, moves), blocks // share)),
            DMA((max(1, moves), seqs)),
            DMA((count, depth - 1)),
            DMA((count, depth - 1)),
            DMA((count, depth, blocks - 1)),
            DMA((count, depth, blocks - 1)),
            DMA((count, depth)),
            DMA((count, depth)),
            DMA((count + 1, max(depth, moves))),
        ]

    def level(self, k):
        return lax.rem(self.place.z + k, self.place.depth)

    def greet(self):
        greet(self.place.peers(True, True))

    def clear(self):
        place = self.place
        for a in range(self.count):
            if self.kinds[a] == "columns" and place.share > 2:
                held = self.held[a]
                for g in range(place.share):

                    @pl.when((g != place.part) & (g != place.other))
                    def _(held=held, g=g):
                        held[:, :, g] = jnp.zeros(held.shape[:2] + held.shape[3:], held.dtype)

    def start(self, a, k):
        place = self.place
        if self.kinds[a] == "columns":
            mine = there = self.held[a].at[:, self.level(k), place.part]
        else:
            mine = self.held[a].at[:, self.level(k)]
            there = self.near[a].at[:, self.level(k)]
        theirs = self.grads[a].at[:, self.level(k), 1 - place.core]
        send(theirs, there, self.c_s.at[a, k], self.c_r.at[a, k], place.sibling())
        pltpu.make_async_copy(self.grads[a].at[:, self.level(k), place.core], mine, self.loc.at[a, k]).start()

    def add(self, into, second):
        total = into[...].astype(jnp.float32) + second[...].astype(jnp.float32)
        into[...] = total.astype(into.dtype)

    def forward(self, a, k, t):
        place = self.place
        bit, masks, seen = place.narrow(k)[t]
        for n, m in enumerate(masks):
            sems = self.b_s.at[a, k, seen + n], self.b_r.at[a, k, seen + n]
            block = self.held[a].at[place.blk ^ bit ^ m, self.level(k)]
            send(block, self.wide[a].at[k, seen + n], *sems, place.at(place.blk ^ bit, place.z, place.core))

    def join(self, a, k):
        place = self.place
        if self.kinds[a] == "columns":
            arrived(self.held[a].at[:, self.level(k), place.part], self.loc.at[a, k])
            arrived(self.held[a].at[:, self.level(k), place.other], self.c_r.at[a, k])
        else:
            arrived(self.held[a].at[:, self.level(k)], self.loc.at[a, k])
            arrived(self.near[a].at[:, self.level(k)], self.c_r.at[a, k])

            def one(b, _):
                self.add(self.held[a].at[b, self.level(k)], self.near[a].at[b, self.level(k)])
                return 0

            lax.fori_loop(0, place.blocks, one, 0)
        self.forward(a, k, 0)

    def step(self, a, k, t):
        place = self.place
        bit, masks, seen = place.narrow(k)[t]
        for n, m in enumerate(masks):
            arrived(self.wide[a].at[k, seen + n], self.b_r.at[a, k, seen + n])
            self.add(self.held[a].at[place.blk ^ m, self.level(k)], self.wide[a].at[k, seen + n])
        if t + 1 < place.bits:
            self.forward(a, k, t + 1)
        elif k > 0:
            sems = self.z_s.at[a, k - 1], self.z_r.at[a, k - 1]
            block = self.held[a].at[place.blk, self.level(k)]
            send(block, self.tall[a].at[k - 1], *sems, place.at(place.blk, self.level(k), place.core))

    def total(self, a):
        self.sums[a][...] = self.value(a)

    def value(self, a):
        place = self.place
        value = self.held[a][place.blk, place.z].astype(jnp.float32)
        for k in range(1, place.depth):
            arrived(self.tall[a].at[k - 1], self.z_r.at[a, k - 1])
            value = value + self.tall[a][k - 1].astype(jnp.float32)
        return value

    def rows(self, j):
        place = self.place
        slot = lax.rem(place.seq, place.seqs)
        for t in range(place.per_part):
            source = place.part * place.per_part + t
            mine = (source == place.blk) & (place.home == place.core)

            @pl.when(mine)
            def _(t=t):
                pltpu.make_async_copy(self.rows_in[j].at[t], self.rows_out[j].at[slot], self.loc.at[self.count, j]).start()

            @pl.when(jnp.logical_not(mine))
            def _(t=t, source=source):
                sems = self.m_s.at[j, t], self.m_r.at[j, slot]
                send(self.rows_in[j].at[t], self.rows_out[j].at[slot], *sems, place.at(source, place.z, place.home))

    def finish(self):
        place = self.place
        for a, k in self.units:
            if self.kinds[a] == "columns":
                arrived(self.held[a].at[:, 0, 0], self.c_s.at[a, k])
            else:
                arrived(self.held[a].at[:, 0], self.c_s.at[a, k])
            for n in range(place.blocks - 1):
                arrived(self.held[a].at[0, 0], self.b_s.at[a, k, n])
            if k > 0:
                arrived(self.held[a].at[0, 0], self.z_s.at[a, k - 1])
        for j in range(self.moves):
            for t in range(place.per_part):
                mine = (place.part * place.per_part + t == place.blk) & (place.home == place.core)

                @pl.when(mine)
                def _(j=j, t=t):
                    arrived(self.rows_in[j].at[t], self.loc.at[self.count, j])

                @pl.when(jnp.logical_not(mine))
                def _(j=j, t=t):
                    arrived(self.rows_in[j].at[t], self.m_s.at[j, t])

            for i in range(place.seqs):
                owner = (place.core * place.seqs + i) * place.share + place.blk // place.per_part

                @pl.when(owner != place.blk * 2 + place.core)
                def _(j=j, i=i):
                    arrived(self.rows_out[j].at[i], self.m_r.at[j, i])


def fold_shapes(sizes, grads, kinds, rows):
    blocks, _, seqs = sizes
    share = blocks // seqs
    chunks = [((share,) if kind == "columns" else ()) + g.shape[3:] for g, kind in zip(grads, kinds)]
    scratch = Fold.scratch(sizes, chunks, [g.dtype for g in grads], kinds, len(rows))
    out = [jax.ShapeDtypeStruct(c, jnp.float32) for c in chunks]
    moved = [jax.ShapeDtypeStruct((seqs,) + r.shape[1:], r.dtype) for r in rows]
    return out, moved, scratch


def dot_nt(left, right):
    return lax.dot_general(left, right, (((1,), (1,)), ((), ())), preferred_element_type=jnp.float32)


def dot_nn(left, right):
    return lax.dot_general(left, right, (((1,), (0,)), ((), ())), preferred_element_type=jnp.float32)


def split_heads(dst, src):
    low = lax.broadcasted_iota(jnp.int32, src.shape, 1) < 64
    dst[0] = jnp.where(low, src, jnp.zeros_like(src))
    dst[1] = jnp.where(low, jnp.zeros_like(src), src)


def causal(bk, bq, kj, qi):
    kpos = kj * bk + lax.broadcasted_iota(jnp.int32, (bk, bq), 0)
    qpos = qi * bq + lax.broadcasted_iota(jnp.int32, (bk, bq), 1)
    return kpos <= qpos


def plan(tasks, points):
    out = {}
    for where, call in tasks:
        out.setdefault(min(points - 1, int(where * points)), []).append(call)
    return out


def pump(todo, point):
    for at, calls in todo.items():

        @pl.when(point == at)
        def _(calls=calls):
            for call in calls:
                call()


class Total:
    def __init__(self, place, stages, from_z, from_blk, from_core, sems):
        self.place, self.stages = place, stages
        self.from_z, self.from_blk, self.from_core = from_z, from_blk, from_core
        self.z_s, self.z_r, self.b_s, self.b_r, self.c_s, self.c_r = sems

    @staticmethod
    def scratch(sizes, shape):
        blocks, lanes, _ = sizes
        depth, bits = lanes // 2, max(1, blocks.bit_length() - 1)
        return [
            pltpu.VMEM((2 + bits,) + shape, jnp.float32),
            pltpu.VMEM((depth - 1,) + shape, jnp.float32),
            pltpu.VMEM((bits,) + shape, jnp.float32),
            pltpu.VMEM(shape, jnp.float32),
            DMA((depth - 1,)),
            DMA((depth - 1,)),
            DMA((bits,)),
            DMA((bits,)),
            DMA((1,)),
            DMA((1,)),
        ]

    def start(self):
        place = self.place
        for k in range(1, place.depth):
            target = place.at(place.blk, lax.rem(place.z + k, place.depth), place.core)
            send(self.stages.at[0], self.from_z.at[k - 1], self.z_s.at[k - 1], self.z_r.at[k - 1], target)

    def step(self, n):
        place = self.place
        if n == 0:
            value = self.stages[0]
            for k in range(1, place.depth):
                arrived(self.from_z.at[k - 1], self.z_r.at[k - 1])
                value = value + self.from_z[k - 1]
        else:
            arrived(self.from_blk.at[n - 1], self.b_r.at[n - 1])
            value = self.stages[n] + self.from_blk[n - 1]
        self.stages[n + 1] = value
        if n < place.bits:
            target = place.at(place.blk ^ (1 << n), place.z, place.core)
            send(self.stages.at[n + 1], self.from_blk.at[n], self.b_s.at[n], self.b_r.at[n], target)
        else:
            send(self.stages.at[n + 1], self.from_core, self.c_s.at[0], self.c_r.at[0], place.sibling())

    def finish(self):
        place = self.place
        arrived(self.from_core, self.c_r.at[0])
        value = self.stages[place.bits + 1] + self.from_core[...]
        arrived(self.from_core, self.c_s.at[0])
        for n in range(place.bits):
            arrived(self.from_core, self.b_s.at[n])
        for k in range(1, place.depth):
            arrived(self.from_core, self.z_s.at[k - 1])
        return value


class Gather:
    def __init__(self, place, shard, full, sems, only=None, span=None):
        self.place, self.full, self.only = place, full, only
        self.tail = () if span is None else (pl.ds(*span),)
        self.shard = shard if span is None else shard.at[self.tail[0]]
        self.z_s, self.z_r, self.b_s, self.b_r, self.c_s, self.c_r, self.loc = sems

    @staticmethod
    def sems(sizes):
        blocks, lanes, _ = sizes
        depth = lanes // 2
        return [
            DMA((depth,)),
            DMA((depth,)),
            DMA((depth, blocks - 1)),
            DMA((depth, blocks - 1)),
            DMA((depth,)),
            DMA((depth,)),
            DMA((1 + depth,)),
        ]

    def level(self, k):
        return lax.rem(self.place.z + self.place.depth - k, self.place.depth)

    def lane(self, depth_at, core):
        return self.full.at[(slice(None), depth_at, core) + self.tail]

    def chunk(self, blk, k):
        return self.full.at[(blk, self.level(k), self.place.core) + self.tail]

    def start(self):
        place = self.place
        for k in range(1, place.depth):
            target = place.at(place.blk, lax.rem(place.z + k, place.depth), place.core)
            send(self.shard, self.chunk(place.blk, 0), self.z_s.at[k], self.z_r.at[k], target)

    def keep(self):
        pltpu.make_async_copy(self.shard, self.chunk(self.place.blk, 0), self.loc.at[0]).start()

    def forward(self, k, t):
        place = self.place
        bit, masks, seen = place.widen(k)[t]
        for n, m in enumerate(masks):
            there = self.chunk(place.blk ^ m, k)
            src = self.shard if m == 0 and k == 0 else there
            send(src, there, self.b_s.at[k, seen + n], self.b_r.at[k, seen + n], place.at(place.blk ^ bit, place.z, place.core))

    def climb(self, k):
        if k > 0:
            arrived(self.chunk(self.place.blk, k), self.z_r.at[k])
        self.forward(k, 0)

    def step(self, k, t):
        place = self.place
        bit, masks, seen = place.widen(k)[t]
        for n, m in enumerate(masks):
            arrived(self.chunk(place.blk ^ bit ^ m, k), self.b_r.at[k, seen + n])
        if t + 1 < place.bits:
            self.forward(k, t + 1)
        else:
            self.swap(k)

    def swap(self, k):
        place = self.place
        if k == 0:
            arrived(self.shard, self.loc.at[0])
        if self.only is None:
            held = self.lane(self.level(k), place.core)
            send(held, held, self.c_s.at[k], self.c_r.at[k], place.sibling())
        else:
            there = self.only.at[:, self.level(k), place.core]
            send(self.full.at[:, self.level(k), place.core, place.other], there, self.c_s.at[k], self.c_r.at[k], place.sibling())
            mine = self.full.at[:, self.level(k), place.core, place.part]
            pltpu.make_async_copy(mine, there, self.loc.at[1 + k]).start()

    def wait_swap(self, k):
        place = self.place
        if self.only is None:
            arrived(self.lane(self.level(k), 1 - place.core), self.c_r.at[k])
        else:
            arrived(self.only.at[:, self.level(k), 1 - place.core], self.c_r.at[k])
            arrived(self.only.at[:, self.level(k), place.core], self.loc.at[1 + k])

    def finish(self):
        place = self.place
        for k in range(place.depth):
            if self.only is None:
                self.wait_swap(k)
                arrived(self.lane(0, 0), self.c_s.at[k])
            else:
                arrived(self.only.at[:, 0, 0], self.c_s.at[k])
            if k > 0:
                arrived(self.shard, self.z_s.at[k])
            for n in range(place.blocks - 1):
                arrived(self.shard, self.b_s.at[k, n])


class GatherAcross(Gather):
    def start(self):
        place = self.place
        for m in range(1, place.blocks):
            target = place.at(place.blk ^ m, place.z, place.core)
            send(self.shard, self.chunk(place.blk, 0), self.b_s.at[0, m - 1], self.b_r.at[0, m - 1], target)

    def climb(self):
        place = self.place
        for m in range(1, place.blocks):
            arrived(self.chunk(place.blk ^ m, 0), self.b_r.at[0, m - 1])
        arrived(self.shard, self.loc.at[0])
        held = self.lane(place.z, place.core)
        for k in range(1, place.depth):
            target = place.at(place.blk, lax.rem(place.z + k, place.depth), place.core)
            send(held, held, self.z_s.at[k], self.z_r.at[k], target)
        self.pass_on(0)

    def pass_on(self, k):
        held = self.lane(self.level(k), self.place.core)
        if k > 0:
            arrived(held, self.z_r.at[k])
        send(held, held, self.c_s.at[k], self.c_r.at[k], self.place.sibling())

    def finish(self):
        place = self.place
        for k in range(place.depth):
            self.wait_swap(k)
            arrived(self.lane(0, 0), self.c_s.at[k])
            if k > 0:
                arrived(self.lane(0, 0), self.z_s.at[k])
        for m in range(1, place.blocks):
            arrived(self.shard, self.b_s.at[0, m - 1])


def first_kernel(sizes, block, pairs, *refs):
    place = Place(*sizes)
    tok, cot, vec, w_qkv, w_out, w_up, w_down = refs[:7]
    refs = refs[7:]
    att_ref, lse_ref, att_own, tok_own, cot_own, normed_out, qkv_out, cols_out, vec_out, stage, out_full, up_full, down_full = refs[:13]
    refs = refs[13:]
    tok_v, norm_v, norm_t, chunk_v, w32_v, cols_v, qkv_v, kh, vt, run_m, run_l, run_a, att_v = refs[:13]
    tok_s, tok_r, near_s, near_r, cot_s, cot_r, a_s, a_r, loc = refs[13:22]
    total = Total(place, *refs[22:26], refs[26:32])
    refs = refs[32:]
    late_rows = w_down.shape[0] // 3
    late_rows = late_rows if late_rows % 16 == 0 else 0
    early_rows = w_down.shape[0] - late_rows
    qkv = Gather(place, w_qkv, stage, refs[0:7], chunk_v)
    outw = Gather(place, w_out, out_full, refs[7:14])
    upw = Gather(place, w_up, up_full, refs[14:21])
    downw = GatherAcross(place, w_down, down_full, refs[21:28], span=(0, early_rows))
    climbers = [outw, upw]
    if late_rows:
        climbers.append(Gather(place, w_down, down_full, refs[28:35], span=(early_rows, late_rows)))
    arrays = [qkv, downw] + climbers
    blocks, depth, seqs, share, bits = place.blocks, place.depth, place.seqs, place.share, place.bits
    blk, z, core, home = place.blk, place.z, place.core, place.home
    pair = pl.program_id(0)
    rows, model = tok_v.shape[1:]
    length = blocks * rows
    count = length // block
    owned = w_qkv.shape[1]
    per_seq = share // 2
    local = lambda src, dst, sem: pltpu.make_async_copy(src, dst, sem).start()

    @pl.when(pair == 0)
    def _():
        total.stages[0] = vec[...]
        greet(place.peers(True, True))
        total.start()
        qkv.start()
        for i in range(seqs):
            for h in range(per_seq):
                target = (core * seqs + i) * per_seq + h

                @pl.when(target != blk)
                def _(i=i, h=h, target=target):
                    sems = tok_s.at[i * per_seq + h], tok_r.at[blk]
                    send(tok.at[i], tok_v.at[blk], *sems, place.at(target, z, core))

                @pl.when(target == blk)
                def _(i=i):
                    local(tok.at[i], tok_v.at[blk], loc.at[0])

        qkv.forward(0, 0)
        for array in arrays:
            array.keep()
        for k in range(1, depth):
            qkv.climb(k)
        for array in climbers:
            array.start()
        total.step(0)
        total.step(1)

        @pl.when(core == home)
        def _():
            for p in range(blocks):

                @pl.when(p != blk)
                def _():
                    arrived(tok_v.at[p], tok_r.at[p])

                @pl.when(p == blk)
                def _():
                    arrived(tok_v.at[p], loc.at[0])

                send(tok_v.at[p], tok_v.at[p], near_s.at[p], near_r.at[p], place.sibling())

        for n in range(2, bits + 1):
            total.step(n)
        for t in range(bits):
            for k in range(depth):
                qkv.step(k, t)
            if t == 0:
                downw.start()
        vec_out[...] = total.finish()
        gain, shift = vec_out[0:1, :], vec_out[1:2, :]
        part_rows = min(rows, 128)

        for p in range(blocks):

            @pl.when(core != home)
            def _(p=p):
                arrived(tok_v.at[p], near_r.at[p])

            def norm(i, _, p=p):
                inside = pl.ds(pl.multiple_of(i * part_rows, part_rows), part_rows)
                unit, _ = centered(tok_v[p, inside, :].astype(jnp.float32))
                at = pl.ds(pl.multiple_of(p * rows + i * part_rows, part_rows), part_rows)
                normed = unit * gain + shift
                norm_v[at, :] = normed.astype(jnp.bfloat16)
                norm_t[:, at] = normed.T.astype(jnp.bfloat16)
                return 0

            lax.fori_loop(0, rows // part_rows, norm, 0)
        local(norm_t, normed_out, loc.at[1])
        for t in range(place.per_part):
            local(tok_v.at[place.part * place.per_part + t], tok_own.at[t], loc.at[2 + t])
        downw.climb()
        for array in climbers:
            for k in range(depth):
                array.climb(k)
        for k in range(depth):
            qkv.wait_swap(k)
        for b in range(blocks):
            for d in range(depth):
                for c in range(2):
                    index = (b * depth + d) * 2 + c
                    w32_v[index * owned : (index + 1) * owned, :] = chunk_v[b, d, c].astype(jnp.float32)
        cols_v[...] = w32_v[...].astype(jnp.bfloat16)
        local(cols_v, cols_out, loc.at[2 + place.per_part])

        def project(i, _):
            at = pl.ds(pl.multiple_of(i * block, block), block)
            normed = norm_v[at, :]
            scale = jnp.where(lax.broadcasted_iota(jnp.int32, (1, 384), 1) < 128, 0.125, 1.0)
            for n in range(pairs):
                value = dot_nn(normed, cols_v[:, n * 384 : (n + 1) * 384]) * scale
                qkv_v[at, n * 384 : (n + 1) * 384] = value.astype(jnp.bfloat16)
            return 0

        lax.fori_loop(0, count, project, 0)
        local(qkv_v, qkv_out, loc.at[3 + place.per_part])

    per_pair = count * (count + 1) // 2
    tasks = []
    levels = [(array, k) for array in climbers for k in range(depth)]
    for n, (array, k) in enumerate(levels):
        for t in range(bits):
            where = 0.08 + 0.26 * t + (0.1 + 0.25 * t) * n / len(levels)
            tasks.append((where, functools.partial(array.step, k, t)))
    for k in range(1, depth):
        tasks.append((0.55 + 0.3 * k / depth, functools.partial(downw.pass_on, k)))

    def own_rows():
        for i in range(seqs):
            owner = (core * seqs + i) * share + blk // place.per_part
            slot = lax.rem(blk, place.per_part)

            @pl.when(owner != blk * 2 + core)
            def _(i=i, owner=owner, slot=slot):
                send(cot.at[i], cot_own.at[slot], cot_s.at[i], cot_r.at[slot], place.at(owner // 2, z, owner % 2))

            @pl.when(owner == blk * 2 + core)
            def _(i=i, slot=slot):
                local(cot.at[i], cot_own.at[slot], loc.at[4 + place.per_part])

    tasks.append((0.2, own_rows))
    tasks.sort(key=lambda task: task[0])
    todo = plan(tasks, pairs * per_pair)

    def lanes_of(n):
        return pl.ds(pl.multiple_of(pair * 384 + n * 128, 128), 128)

    split_heads(kh, qkv_v[:, lanes_of(1)])
    vt[...] = qkv_v[:, lanes_of(2)].astype(jnp.float32).T.astype(jnp.bfloat16)

    def q_step(qi, _):
        at_q = pl.ds(pl.multiple_of(qi * block, block), block)
        run_m[...] = jnp.full_like(run_m, -1e30)
        run_l[...] = jnp.zeros_like(run_l)
        run_a[...] = jnp.zeros_like(run_a)

        def one(kj, masked):
            at = pl.ds(pl.multiple_of(kj * block, block), block)
            q_rows = qkv_v[at_q, lanes_of(0)]
            scores = [dot_nt(kh[h, at, :], q_rows) for h in range(2)]
            weighed = []
            for h in range(2):
                peak, so_far = run_m[h : h + 1, :], run_l[h : h + 1, :]
                s = scores[h]
                u = s * s + 1.0
                inv = lax.rsqrt(u)
                mag = u * inv
                if masked:
                    mag = jnp.where(causal(block, block, kj, qi), mag, -1e30)
                new = jnp.maximum(peak, jnp.max(mag, axis=0, keepdims=True))
                p = jnp.exp(mag - new)
                alpha = jnp.exp(peak - new)
                run_m[h : h + 1, :] = new
                run_l[h : h + 1, :] = so_far * alpha + jnp.sum(p, axis=0, keepdims=True)
                weighed.append((alpha, (p * (s * inv)).astype(jnp.bfloat16)))
            for h in range(2):
                alpha, signed = weighed[h]
                head = slice(64 * h, 64 * h + 64)
                run_a[head, :] = run_a[head, :] * alpha + dot_nn(vt[head, at], signed)

        def k_step(kj, _):
            @pl.when(kj == qi)
            def _():
                one(kj, True)

            @pl.when(kj != qi)
            def _():
                one(kj, False)

            pump(todo, pair * per_pair + qi * (qi + 1) // 2 + kj)
            return 0

        lax.fori_loop(0, qi + 1, k_step, 0)
        both = []
        for h in range(2):
            both.append(run_a[64 * h : 64 * h + 64, :] / run_l[h : h + 1, :])
            lse_ref[0, h : h + 1, at_q] = run_m[h : h + 1, :] + jnp.log(run_l[h : h + 1, :])
        joined = jnp.concatenate(both, 0).T.astype(jnp.bfloat16)
        att_ref[at_q, :] = joined
        att_v[pair, at_q, :] = joined
        return 0

    lax.fori_loop(0, count, q_step, 0)
    part, mine = place.part, length // share
    flat = blk * 2 + core

    def piece(p, g):
        return att_v.at[p, pl.ds(pl.multiple_of(g * mine, 16), mine)]

    for p in range(pairs):
        there = att_own.at[part, :, pl.ds(p * 128, 128)]

        @pl.when(pair == p)
        def _(p=p, there=there):
            for k in range(1, share):
                other = flat ^ k
                send(piece(p, part ^ k), there, a_s.at[k, p], a_r.at[k, p], place.at(other // 2, z, other % 2))
            local(piece(p, part), there, a_s.at[0, p])

    @pl.when(pair == pairs - 1)
    def _():
        for p in range(pairs):
            for k in range(share):
                arrived(piece(p, 0), a_s.at[k, p])
                if k > 0:
                    arrived(att_own.at[part ^ k, :, pl.ds(p * 128, 128)], a_r.at[k, p])
        for array in arrays:
            array.finish()
        for i in range(seqs):

            @pl.when((core * seqs + i) * share + blk // place.per_part != blk * 2 + core)
            def _(i=i):
                arrived(cot.at[i], cot_s.at[i])

        for t in range(place.per_part):
            here = (place.part * place.per_part + t == blk) & (home == core)

            @pl.when(here)
            def _(t=t):
                arrived(cot_own.at[t], loc.at[4 + place.per_part])

            @pl.when(jnp.logical_not(here))
            def _(t=t):
                arrived(cot_own.at[t], cot_r.at[t])

        arrived(norm_t, loc.at[1])
        arrived(cols_v, loc.at[2 + place.per_part])
        arrived(qkv_v, loc.at[3 + place.per_part])
        for t in range(place.per_part):
            arrived(tok_own.at[t], loc.at[2 + t])

        @pl.when(core == home)
        def _():
            for p in range(blocks):
                arrived(tok_v.at[p], near_s.at[p])

        for i in range(seqs):
            for h in range(per_seq):
                target = (core * seqs + i) * per_seq + h

                @pl.when(target != blk)
                def _(i=i, h=h):
                    arrived(tok.at[i], tok_s.at[i * per_seq + h])

                @pl.when((target == blk) & (core != home))
                def _():
                    arrived(tok_v.at[blk], loc.at[0])


def first_half(sizes, tok, cot, vec, w_qkv, w_out, w_up, w_down, block):
    blocks, lanes, seqs = sizes
    depth, share = lanes // 2, blocks // seqs
    per_part = blocks // share
    rows, model = tok.shape[1:]
    length = blocks * rows
    width = w_qkv.shape[2]
    pairs = width // 384
    low, full = jnp.bfloat16, jnp.float32
    shape = jax.ShapeDtypeStruct
    owners = (blocks, depth, 2)
    in_vmem = pl.BlockSpec(memory_space=pltpu.VMEM)
    return pl.pallas_call(
        functools.partial(first_kernel, sizes, block, pairs),
        grid=(pairs,),
        out_shape=[
            shape((length, 128 * pairs), low),
            shape((pairs, 8, length), full),
            shape((share, length // share, 128 * pairs), low),
            shape((per_part, rows, model), low),
            shape((per_part, rows, model), low),
            shape((model, length), low),
            shape((length, width), low),
            shape((model, width), low),
            shape(vec.shape, full),
            shape(owners + w_qkv.shape, low),
            shape(owners + w_out.shape, low),
            shape(owners + w_up.shape, low),
            shape(owners + w_down.shape, low),
        ],
        in_specs=[ANYWHERE, ANYWHERE, in_vmem] + [ANYWHERE] * 4,
        out_specs=[pl.BlockSpec((length, 128), lambda p: (0, p)), pl.BlockSpec((1, 8, length), lambda p: (p, 0, 0))]
        + [ANYWHERE] * 6
        + [in_vmem]
        + [ANYWHERE] * 4,
        scratch_shapes=[
            pltpu.VMEM((blocks, rows, model), low),
            pltpu.VMEM((length, model), low),
            pltpu.VMEM((model, length), low),
            pltpu.VMEM(owners + w_qkv.shape[1:], low),
            pltpu.VMEM((model, width), full),
            pltpu.VMEM((model, width), low),
            pltpu.VMEM((length, width), low),
            pltpu.VMEM((2, length, 128), low),
            pltpu.VMEM((128, length), low),
            pltpu.VMEM((8, block), full),
            pltpu.VMEM((8, block), full),
            pltpu.VMEM((128, block), full),
            pltpu.VMEM((pairs, length, 128), low),
            DMA((seqs * share // 2,)),
            DMA((blocks,)),
            DMA((blocks,)),
            DMA((blocks,)),
            DMA((seqs,)),
            DMA((per_part,)),
            DMA((share, pairs)),
            DMA((share, pairs)),
            DMA((5 + per_part,)),
        ]
        + Total.scratch(sizes, vec.shape)
        + Gather.sems(sizes) * 5,
        compiler_params=pltpu.CompilerParams(collective_id=0, has_side_effects=True, vmem_limit_bytes=VMEM_LIMIT),
    )(tok, cot, vec, w_qkv, w_out, w_up, w_down)


def dot_tn(left, right):
    return lax.dot_general(left, right, (((0,), (0,)), ((), ())), preferred_element_type=jnp.float32)


def centered(values):
    center = jnp.mean(values, axis=-1, keepdims=True)
    offsets = values - center
    spread = jnp.mean(offsets * offsets, axis=-1, keepdims=True)
    inverse = lax.rsqrt(spread + 1e-05)
    return offsets * inverse, inverse


def norm_back(values, grads, gain):
    unit, inverse = centered(values)
    scaled = grads * gain
    first = jnp.mean(scaled, axis=-1, keepdims=True)
    second = jnp.mean(scaled * unit, axis=-1, keepdims=True)
    back = inverse * (scaled - first - unit * second)
    return back, jnp.sum(grads * unit, axis=0, keepdims=True), jnp.sum(grads, axis=0, keepdims=True)


def gelu_parts(x):
    square = x * x
    half = 0.5 + 0.5 * jnp.tanh(0.7978845608028654 * x * (1.0 + 0.044715 * square))
    slope = half + x * (2.0 * half * (1.0 - half)) * (0.7978845608028654 + 0.1070322243 * square)
    return x * half, slope


def mlp_kernel(sizes, cols, tile, chunk, *refs):
    place = Place(*sizes)
    att, tok_own, cot, w_out, w_up, w_down, vec = refs[:7]
    refs = refs[7:]
    result, g_heads, g_mid, g_out, g_up, g_down, g_vec = refs[:7]
    (att_v, tok_v, cot_v, res_v, out_v, up_v, down_v, mid_v, n2_v, n2t_v, hid_v, slope_v, sum_v, ga_v) = refs[7:21]
    (st_out, st_up, st_down) = refs[21:24]
    g_s, g_r, m_s, m_r, loc, up_l, down_l, o_l = refs[24:]
    share, per_part, seqs = place.share, place.per_part, place.seqs
    part, blk, z, core = place.part, place.blk, place.z, place.core
    rows, model = mid_v.shape
    block = rows // per_part
    ff = up_v.shape[1]
    chunks, tiles = ff // chunk, rows // tile
    flat = blk * 2 + core
    partners = [((flat ^ k) // 2, z, (flat ^ k) % 2) for k in range(1, share)]
    slot_of = lax.rem(place.seq, seqs)
    greet(place.peers(False, True))
    def local(src, dst, sem):
        pltpu.make_async_copy(src, dst, sem).start()

    local(att, att_v, loc.at[0])
    for t in range(per_part):
        local(tok_own.at[t], tok_v.at[t], loc.at[1 + t])
    local(w_out, out_v, loc.at[1 + per_part])
    local(cot, cot_v, loc.at[2 + per_part])

    def span(f):
        return pl.ds(pl.multiple_of(f * chunk, chunk), chunk)

    for f in range(chunks):
        local(w_up.at[:, pl.ds(f * chunk, chunk)], up_v.at[:, pl.ds(f * chunk, chunk)], up_l.at[f])
        local(w_down.at[pl.ds(f * chunk, chunk)], down_v.at[pl.ds(f * chunk, chunk)], down_l.at[f])

    arrived(att_v, loc.at[0])
    for t in range(per_part):
        arrived(tok_v.at[t], loc.at[1 + t])
    arrived(out_v, loc.at[1 + per_part])
    gain, shift = vec[2:3, :], vec[3:4, :]
    per_block = block // tile

    def spot(i):
        return i // per_block, pl.ds(pl.multiple_of(lax.rem(i, per_block) * tile, tile), tile)

    lane = lax.broadcasted_iota(jnp.int32, (1, model), 1)
    mine_at = z * 2 * seqs + place.seq
    length = jnp.sum(jnp.where(lane == mine_at, vec[4:5, :], 0.0), axis=1, keepdims=True)

    def live(i):
        position = part * rows + i * tile + lax.broadcasted_iota(jnp.int32, (tile, 1), 0)
        return jnp.where(position.astype(jnp.float32) < length, 1.0, 0.0)

    def enter(i, _):
        at = pl.ds(pl.multiple_of(i * tile, tile), tile)
        branch = dot_nn(att_v[0, at, :cols], out_v[:cols, :])
        for g in range(1, share):
            branch = branch + dot_nn(att_v[g, at, :cols], out_v[g * cols : (g + 1) * cols, :])
        t, inside = spot(i)
        middle = tok_v[t, inside, :].astype(jnp.float32) + live(i) * branch
        mid_v[at, :] = middle
        unit, _ = centered(middle)
        normed = unit * gain + shift
        n2_v[at, :] = normed.astype(jnp.bfloat16)
        n2t_v[:, at] = normed.T.astype(jnp.bfloat16)
        return 0

    lax.fori_loop(0, tiles, enter, 0)
    sum_v[...] = mid_v[...]

    def up_step(f, _):
        arrived(up_v.at[:, span(f)], up_l.at[f])
        arrived(down_v.at[span(f)], down_l.at[f])
        hidden, slope = gelu_parts(dot_nn(n2_v[...], up_v[:, span(f)]))
        hidden = hidden.astype(jnp.bfloat16)
        hid_v[:, span(f)] = hidden
        slope_v[:, span(f)] = slope.astype(jnp.bfloat16)
        sum_v[...] += dot_nn(hidden, down_v[span(f), :])
        return 0

    lax.fori_loop(0, chunks, up_step, 0)
    for t in range(per_part):
        res_v[t] = sum_v[t * block : (t + 1) * block, :].astype(jnp.bfloat16)
        source = part * per_part + t
        mine = (source == blk) & (place.home == core)

        @pl.when(mine)
        def _(t=t):
            local(res_v.at[t], result.at[slot_of], loc.at[0])

        @pl.when(jnp.logical_not(mine))
        def _(t=t, source=source):
            send(res_v.at[t], result.at[slot_of], m_s.at[t], m_r.at[slot_of], place.at(source, z, place.home))

    arrived(cot_v, loc.at[2 + per_part])
    sum_v[...] = jnp.zeros_like(sum_v)

    def back_step(f, _):
        top = cot_v[...].reshape(rows, model)
        grad_pre = (dot_nt(top, down_v[span(f), :]) * slope_v[:, span(f)].astype(jnp.float32)).astype(jnp.bfloat16)
        now = lax.rem(f, 2)

        @pl.when(f >= 2)
        def _():
            arrived(st_down.at[now], o_l.at[now])
            arrived(st_up.at[now], o_l.at[2 + now])

        st_down[now] = dot_tn(hid_v[:, span(f)], top).astype(jnp.bfloat16)
        st_up[now] = dot_nn(n2t_v[...], grad_pre).astype(jnp.bfloat16)
        local(st_down.at[now], g_down.at[span(f)], o_l.at[now])
        local(st_up.at[now], g_up.at[:, span(f)], o_l.at[2 + now])
        sum_v[...] += dot_nt(grad_pre, up_v[:, span(f)])
        return 0

    lax.fori_loop(0, chunks, back_step, 0)
    g_vec[...] = jnp.zeros_like(g_vec)

    def leave(i, _):
        at = pl.ds(pl.multiple_of(i * tile, tile), tile)
        t, inside = spot(i)
        back, d_gain, d_shift = norm_back(mid_v[at, :], sum_v[at, :], gain)
        g_vec[0:1, :] += d_gain
        g_vec[1:2, :] += d_shift
        total = cot_v[t, inside, :].astype(jnp.float32) + back
        mid_v[at, :] = total
        branch = (live(i) * total).astype(jnp.bfloat16)
        n2_v[at, :] = branch
        heads = dot_nt(branch, out_v[...]).astype(jnp.bfloat16)
        for g in range(share):
            if cols == ga_v.shape[2]:
                ga_v[g, at, :] = heads[:, g * cols : (g + 1) * cols]
            else:
                piece = heads[:, g * cols : (g + 1) * cols]
                ga_v[g, at, :] = jnp.concatenate([piece, jnp.zeros((tile, ga_v.shape[2] - cols), jnp.bfloat16)], 1)
        return 0

    lax.fori_loop(0, tiles, leave, 0)
    for k in range(1, share):
        send(ga_v.at[part ^ k], g_heads.at[part], g_s.at[k - 1], g_r.at[k - 1], place.at(*partners[k - 1]))
    local(ga_v.at[part], g_heads.at[part], loc.at[1])
    local(mid_v, g_mid, loc.at[2])
    for g in range(share):
        st_out[g * cols : (g + 1) * cols, :] = dot_tn(att_v[g, :, :cols], n2_v[...]).astype(jnp.bfloat16)
    local(st_out, g_out, loc.at[1 + per_part])
    for n in range(min(2, chunks)):
        arrived(st_down.at[n], o_l.at[n])
        arrived(st_up.at[n], o_l.at[2 + n])
    arrived(st_out, loc.at[1 + per_part])
    arrived(mid_v, loc.at[2])
    arrived(ga_v.at[part], loc.at[1])
    for k in range(1, share):
        arrived(ga_v.at[part ^ k], g_s.at[k - 1])
        arrived(g_heads.at[part ^ k], g_r.at[k - 1])
    for i in range(seqs):
        owner = (core * seqs + i) * share + blk // per_part

        @pl.when(owner != flat)
        def _(i=i):
            arrived(result.at[i], m_r.at[i])

    for t in range(per_part):
        mine = (part * per_part + t == blk) & (place.home == core)

        @pl.when(mine)
        def _(t=t):
            arrived(res_v.at[t], loc.at[0])

        @pl.when(jnp.logical_not(mine))
        def _(t=t):
            arrived(res_v.at[t], m_s.at[t])


def feed_forward(sizes, cols, att, tok_own, cot, w_out, w_up, w_down, vec, tile, chunk):
    blocks, lanes, seqs = sizes
    share = blocks // seqs
    per_part = blocks // share
    block, model = tok_own.shape[1:]
    rows = per_part * block
    wide = att.shape[2]
    ff = w_up.shape[1]
    chunks = ff // chunk
    in_vmem = pl.BlockSpec(memory_space=pltpu.VMEM)
    low, full = jnp.bfloat16, jnp.float32
    return pl.pallas_call(
        functools.partial(mlp_kernel, sizes, cols, tile, chunk),
        out_shape=[
            jax.ShapeDtypeStruct((seqs, block, model), low),
            jax.ShapeDtypeStruct((share, rows, wide), low),
            jax.ShapeDtypeStruct((rows, model), full),
            jax.ShapeDtypeStruct((model, model), low),
            jax.ShapeDtypeStruct((model, ff), low),
            jax.ShapeDtypeStruct((ff, model), low),
            jax.ShapeDtypeStruct((8, model), full),
        ],
        in_specs=[ANYWHERE] * 6 + [in_vmem],
        out_specs=[ANYWHERE] * 6 + [in_vmem],
        scratch_shapes=[
            pltpu.VMEM((share, rows, wide), low),
            pltpu.VMEM((per_part, block, model), low),
            pltpu.VMEM((per_part, block, model), low),
            pltpu.VMEM((per_part, block, model), low),
            pltpu.VMEM((model, model), low),
            pltpu.VMEM((model, ff), low),
            pltpu.VMEM((ff, model), low),
            pltpu.VMEM((rows, model), full),
            pltpu.VMEM((rows, model), low),
            pltpu.VMEM((model, rows), low),
            pltpu.VMEM((rows, ff), low),
            pltpu.VMEM((rows, ff), low),
            pltpu.VMEM((rows, model), full),
            pltpu.VMEM((share, rows, wide), low),
            pltpu.VMEM((model, model), low),
            pltpu.VMEM((2, model, chunk), low),
            pltpu.VMEM((2, chunk, model), low),
            DMA((share,)),
            DMA((share,)),
            DMA((per_part,)),
            DMA((seqs,)),
            DMA((3 + per_part,)),
            DMA((chunks,)),
            DMA((chunks,)),
            DMA((4,)),
        ],
        compiler_params=pltpu.CompilerParams(collective_id=4, has_side_effects=True, vmem_limit_bytes=VMEM_LIMIT),
    )(att, tok_own, cot, w_out, w_up, w_down, vec)


def last_kernel(sizes, block, pairs, *refs):
    place = Place(*sizes)
    blocks, depth, seqs, share, bits = place.blocks, place.depth, place.seqs, place.share, place.bits
    blk, z, core, part = place.blk, place.z, place.core, place.part
    per_part = place.per_part
    count = 3 + pairs
    q_ref, k_ref, v_ref, g_ref, att_ref, lse_ref = refs[:6]
    big, tok_own, g_mid, norm_t, cols, vec, two = refs[6:9], refs[9], refs[10], refs[11], refs[12], refs[13], refs[14]
    refs = refs[15:]
    sums, qkv_sum, tok_out, vec_out, refs = refs[:3], refs[3], refs[4], refs[5], refs[6:]
    kh, vh, qh, gh, kt, delta, dqt, dk, dv = refs[:9]
    gq_v, own_v, norm_v, cols_v, tok_v, mid_v, out_v, part_v, got_v, sum_v = refs[9:19]
    p_s, p_r, t_s, t_r, loc = refs[19:24]
    total = Total(place, *refs[24:28], refs[28:34])
    kinds = ["rows"] * 3 + ["columns"] * pairs
    fold = Fold(place, kinds, list(big) + [own_v.at[p] for p in range(pairs)], [], sums, [], refs[34:])
    pair = pl.program_id(0)
    length = q_ref.shape[0]
    rows, model = mid_v.shape
    owned = own_v.shape[4]
    steps = length // block
    per_pair = steps * (steps + 1) // 2
    flat = blk * 2 + core
    partners = [((flat ^ k) // 2, z, (flat ^ k) % 2) for k in range(1, share)]
    slot_of = lax.rem(place.seq, seqs)
    local = lambda src, dst, sem: pltpu.make_async_copy(src, dst, sem).start()

    tasks = []
    units = [(a, k) for a in range(3) for k in fold.order]
    per = 12.0 / len(units)
    for n, (a, k) in enumerate(units):
        tasks.append((8 + 1.2 * per * n, functools.partial(fold.join, a, k)))
        for t in range(bits):
            where = (14 + 2.7 * per * n) if t == 0 else (38 + 8 * t + 1.4 * per * n)
            tasks.append((where, functools.partial(fold.step, a, k, t)))
    for a in range(3):
        tasks.append((72 + 2 * a, functools.partial(fold.total, a)))
    for p in range(pairs - 1):
        third = 85.0 / pairs
        for n, k in enumerate(fold.order):
            tasks.append(((p + 1.1) * third, functools.partial(fold.join, 3 + p, k)))
            for t in range(bits):
                where = (68 if p == pairs - 2 else 60) + 6 * t
                tasks.append((where, functools.partial(fold.step, 3 + p, k, t)))
    tasks = [(where / 85.0, call) for where, call in tasks]
    tasks.sort(key=lambda task: task[0])
    todo = plan(tasks, pairs * per_pair)

    @pl.when(pair == 0)
    def _():
        fold.greet()
        fold.clear()
        for a, k in units:
            fold.start(a, k)
        local(norm_t, norm_v, loc.at[0])
        local(cols, cols_v, loc.at[1])
        local(g_mid, mid_v, loc.at[2])
        local(tok_own, tok_v, loc.at[3])

    split_heads(kh, k_ref[...])
    split_heads(vh, v_ref[...])
    split_heads(qh, q_ref[...])
    split_heads(gh, g_ref[...])
    kt[...] = k_ref[...].astype(jnp.float32).T.astype(jnp.bfloat16)
    prod = (g_ref[...].astype(jnp.float32) * att_ref[...].astype(jnp.float32)).T
    delta[0:1, :] = jnp.sum(prod[:64], axis=0, keepdims=True)
    delta[1:2, :] = jnp.sum(prod[64:], axis=0, keepdims=True)
    dqt[...] = jnp.zeros_like(dqt)

    def k_step(kj, _):
        at = pl.ds(pl.multiple_of(kj * block, block), block)

        def one(qi, masked):
            at_q = pl.ds(pl.multiple_of(qi * block, block), block)
            q_rows = q_ref[at_q, :]
            g_rows = g_ref[at_q, :]
            add_k = add_v = None
            both = [(dot_nt(kh[h, at, :], q_rows), dot_nt(vh[h, at, :], g_rows)) for h in range(2)]
            for h in range(2):
                s, dp = both[h]
                u = s * s + 1.0
                inv = lax.rsqrt(u)
                arg = u * inv - lse_ref[0, h : h + 1, at_q]
                if masked:
                    arg = jnp.where(causal(block, block, kj, qi), arg, -1e30)
                p = jnp.exp(arg)
                sgn = s * inv
                t = inv * inv * (inv - 1.0) + 1.0
                ds = (p * (dp * t - sgn * delta[h : h + 1, at_q])).astype(jnp.bfloat16)
                signed = (p * sgn).astype(jnp.bfloat16)
                one_v = dot_nn(signed, gh[h, at_q, :])
                one_k = dot_nn(ds, qh[h, at_q, :])
                add_v = one_v if h == 0 else add_v + one_v
                add_k = one_k if h == 0 else add_k + one_k
                dqt[64 * h : 64 * h + 64, at_q] += dot_nn(kt[64 * h : 64 * h + 64, at], ds)
            return add_k, add_v

        def more(qi, _):
            @pl.when(qi == kj)
            def _():
                dk[...], dv[...] = one(qi, True)

            @pl.when(qi != kj)
            def _():
                add_k, add_v = one(qi, False)
                dk[...] += add_k
                dv[...] += add_v

            pump(todo, pair * per_pair + kj * steps - kj * (kj - 1) // 2 + qi - kj)
            return 0

        lax.fori_loop(kj, steps, more, 0)
        gq_v[pair, at, 128:256] = dk[...].astype(jnp.bfloat16)
        gq_v[pair, at, 256:384] = dv[...].astype(jnp.bfloat16)
        return 0

    lax.fori_loop(0, steps, k_step, 0)
    gq_v[pair, :, 0:128] = (dqt[...] * 0.125).T.astype(jnp.bfloat16)

    @pl.when(pair == 0)
    def _():
        arrived(norm_v, loc.at[0])
        arrived(cols_v, loc.at[1])
        arrived(mid_v, loc.at[2])
        arrived(tok_v, loc.at[3])

    def weight_grad():
        sum_v[...] = dot_nn(norm_v[...], gq_v[pair])
        for b in range(blocks):
            for d in range(depth):
                for c in range(2):
                    first = ((b * depth + d) * 2 + c) * owned
                    own_v[pair, b, d, c] = sum_v[first : first + owned, :].astype(jnp.bfloat16)
        for p in range(pairs):

            @pl.when(pair == p)
            def _(p=p):
                for k in fold.order:
                    fold.start(3 + p, k)

    @pl.when(pair != pairs - 1)
    def _():
        weight_grad()

    @pl.when(pair == pairs - 1)
    def _():
        mine = 3 + pairs - 1
        tile = min(256, block, rows)

        def input_grad(g, i):
            at = pl.ds(pl.multiple_of(g * rows + i * tile, tile), tile)
            value = dot_nt(gq_v[0, at, :], cols_v[:, 0:384])
            for p in range(1, pairs):
                value = value + dot_nt(gq_v[p, at, :], cols_v[:, p * 384 : (p + 1) * 384])
            return value

        per_block = rows // per_part // tile
        half = rows // per_part
        for t in range(per_part):
            for k in range(1, share):

                def away(i, _, k=k):
                    at = pl.ds(pl.multiple_of(i * tile, tile), tile)
                    part_v[k - 1, at, :] = input_grad(part ^ k, i).astype(jnp.bfloat16)
                    return 0

                lax.fori_loop(t * per_block, (t + 1) * per_block, away, 0)
                piece = pl.ds(t * half, half)
                sems = p_s.at[k - 1, t], p_r.at[k - 1, t]
                send(part_v.at[k - 1, piece], got_v.at[k - 1, piece], *sems, place.at(*partners[k - 1]))
        weight_grad()
        total.stages[0] = jnp.zeros(total.stages.shape[1:], jnp.float32)
        total.stages[0, 2:4, :] = two[0:2, :]
        gain = vec[0:1, :]

        def leave(i, _):
            at = pl.ds(pl.multiple_of(i * tile, tile), tile)
            t = i // per_block
            inside = pl.ds(pl.multiple_of(lax.rem(i, per_block) * tile, tile), tile)
            value = input_grad(part, i)
            for k in range(1, share):
                value = value + got_v[k - 1, at, :].astype(jnp.float32)
            back, d_gain, d_shift = norm_back(tok_v[t, inside, :].astype(jnp.float32), value, gain)
            total.stages[0, 0:1, :] += d_gain
            total.stages[0, 1:2, :] += d_shift
            out_v[t, inside, :] = (mid_v[at, :] + back).astype(jnp.bfloat16)
            return 0

        for t in range(per_part):
            for k in range(1, share):
                arrived(got_v.at[k - 1, pl.ds(t * half, half)], p_r.at[k - 1, t])
            lax.fori_loop(t * per_block, (t + 1) * per_block, leave, 0)
            source = part * per_part + t
            here = (source == blk) & (place.home == core)

            @pl.when(here)
            def _(t=t):
                local(out_v.at[t], tok_out.at[slot_of], loc.at[0])

            @pl.when(jnp.logical_not(here))
            def _(t=t, source=source):
                send(out_v.at[t], tok_out.at[slot_of], t_s.at[t], t_r.at[slot_of], place.at(source, z, place.home))

            if t == 0:
                for k in fold.order:
                    fold.join(mine, k)
        total.start()
        for t in range(bits):
            for k in fold.order:
                fold.step(mine, k, t)
            total.step(t)
        total.step(bits)
        for p in range(pairs):
            value = fold.value(3 + p)
            for g in range(share):
                for n in range(3):
                    first = ((n * share + g) * pairs + p) * 128
                    qkv_sum[:, first : first + 128] = value[g, :, n * 128 : n * 128 + 128]
        vec_out[...] = total.finish()
        fold.finish()
        for k in range(1, share):
            for t in range(per_part):
                arrived(part_v.at[k - 1, pl.ds(t * half, half)], p_s.at[k - 1, t])
        for t in range(per_part):
            here = (part * per_part + t == blk) & (place.home == core)

            @pl.when(here)
            def _(t=t):
                arrived(out_v.at[t], loc.at[0])

            @pl.when(jnp.logical_not(here))
            def _(t=t):
                arrived(out_v.at[t], t_s.at[t])

        for i in range(seqs):
            owner = (core * seqs + i) * share + blk // per_part

            @pl.when(owner != flat)
            def _(i=i):
                arrived(tok_out.at[i], t_r.at[i])


def last_half(sizes, qkv, g_att, att, lse, big, tok_own, g_mid, norm_t, cols, vec, two, block):
    blocks, lanes, seqs = sizes
    depth, share = lanes // 2, blocks // seqs
    length, width = qkv.shape
    pairs = width // 384
    model = cols.shape[0]
    owned = model // (blocks * lanes)
    per_part, rows_in, _ = tok_own.shape
    rows = per_part * rows_in
    low, full = jnp.bfloat16, jnp.float32
    in_vmem = pl.BlockSpec(memory_space=pltpu.VMEM)
    own = jax.ShapeDtypeStruct((blocks, depth, 2, owned, 384), low)
    kinds = ["rows"] * 3 + ["columns"] * pairs
    out, _, scratch = fold_shapes(sizes, list(big) + [own] * pairs, kinds, [])
    return pl.pallas_call(
        functools.partial(last_kernel, sizes, block, pairs),
        grid=(pairs,),
        out_shape=out[:3]
        + [
            jax.ShapeDtypeStruct((owned, share * width), full),
            jax.ShapeDtypeStruct((seqs, rows_in, model), low),
            jax.ShapeDtypeStruct(vec.shape, full),
        ],
        in_specs=[pl.BlockSpec((length, 128), lambda p, n=n: (0, 3 * p + n)) for n in range(3)]
        + [pl.BlockSpec((length, 128), lambda p: (0, p))] * 2
        + [pl.BlockSpec((1, 8, length), lambda p: (p, 0, 0))]
        + [ANYWHERE] * 7
        + [in_vmem] * 2,
        out_specs=[in_vmem] * 4 + [ANYWHERE, in_vmem],
        scratch_shapes=[pltpu.VMEM((2, length, 128), low)] * 4
        + [
            pltpu.VMEM((128, length), low),
            pltpu.VMEM((8, length), full),
            pltpu.VMEM((128, length), full),
            pltpu.VMEM((block, 128), full),
            pltpu.VMEM((block, 128), full),
            pltpu.VMEM((pairs, length, 384), low),
            pltpu.VMEM((pairs,) + own.shape, low),
            pltpu.VMEM((model, length), low),
            pltpu.VMEM((model, width), low),
            pltpu.VMEM((per_part, rows_in, model), low),
            pltpu.VMEM((rows, model), full),
            pltpu.VMEM((per_part, rows_in, model), low),
            pltpu.VMEM((share - 1, rows, model), low),
            pltpu.VMEM((share - 1, rows, model), low),
            pltpu.VMEM((model, 384), full),
            DMA((share, per_part)),
            DMA((share, per_part)),
            DMA((per_part,)),
            DMA((seqs,)),
            DMA((4,)),
        ]
        + Total.scratch(sizes, vec.shape)
        + scratch,
        compiler_params=pltpu.CompilerParams(collective_id=2, has_side_effects=True, vmem_limit_bytes=63 * 2**20),
    )(qkv, qkv, qkv, g_att, att, lse, *big, tok_own, g_mid, norm_t, cols, vec, two)


def shards(sizes, tokens, seq_len, ln1_gain, ln1_shift, w_qkv, w_out, ln2_gain, ln2_shift, w_up, w_down, cotangent):
    blocks, lanes, seqs = sizes
    place = Place(*sizes)
    share, part = place.share, place.part
    model = tokens.shape[2]
    length = blocks * tokens.shape[1]
    rows = length // share
    owned = w_qkv.shape[0]
    cols = model // share
    wide = -(-cols // 128) * 128

    pairs = wide // 128
    grouped = jnp.pad(w_qkv.reshape(owned, 3, share, cols), ((0, 0), (0, 0), (0, 0), (0, wide - cols)))
    grouped = grouped.reshape(owned, 3, share, pairs, 128)
    grouped = jnp.transpose(grouped, (2, 0, 3, 1, 4)).reshape(share, owned, 3 * wide)
    flat = place.blk * lanes + lax.axis_index("seq")
    vec = jnp.zeros((8, model), jnp.float32)
    own = jnp.stack([ln1_gain, ln1_shift, ln2_gain, ln2_shift]).astype(jnp.float32)
    vec = lax.dynamic_update_slice(vec, own, (0, flat * owned))
    first = (place.blk == 0).astype(jnp.float32)
    vec = lax.dynamic_update_slice(vec, first * seq_len.astype(jnp.float32)[None], (4, lax.axis_index("seq") * seqs))
    outs = first_half(sizes, tokens, cotangent, vec, grouped, w_out, w_up, w_down, min(512, rows))
    att, lse, att_own, tok_own, cot_own, norm_t, qkv, qkv_cols, params, _, out_full, up_full, down_full = outs
    out_full, up_full = [a.reshape(model, -1) for a in (out_full, up_full)]
    down_full = down_full.reshape(-1, model)
    result, g_heads, grad_mid, grad_out, grad_up, grad_down, two_grads = feed_forward(
        sizes,
        cols,
        att_own,
        tok_own,
        cot_own,
        out_full,
        up_full,
        down_full,
        params,
        min(512, tokens.shape[1]),
        min(1024, w_up.shape[1]),
    )

    def cut(values):
        return values.reshape((blocks, lanes // 2, 2, -1) + values.shape[1:])

    done = last_half(
        sizes,
        qkv,
        g_heads.reshape(length, wide),
        att,
        lse,
        [cut(grad_out), cut(grad_up), cut(grad_down)],
        tok_own,
        grad_mid,
        norm_t,
        qkv_cols,
        params,
        two_grads,
        min(512, rows),
    )
    sum_out, sum_up, sum_down, sum_qkv, grad_tokens, vec_sum = done
    vec_own = lax.dynamic_slice_in_dim(vec_sum, flat * owned, owned, 1)
    if wide != cols:
        sum_qkv = sum_qkv.reshape(owned, 3, share, wide)[..., :cols].reshape(owned, 3 * model)
    return (
        result,
        grad_tokens.astype(jnp.float32),
        vec_own[0],
        vec_own[1],
        sum_qkv,
        sum_out,
        vec_own[2],
        vec_own[3],
        sum_up,
        sum_down,
    )


def solution(mesh):
    blocks, lanes = mesh.shape["blk"], mesh.shape["seq"]
    whole = P(("blk", "seq"))
    rows = P(("blk", "seq"), None)
    tokens = P("seq", "blk", None)

    def run(*args):
        seqs = args[0].shape[0] // lanes
        return jax.shard_map(
            functools.partial(shards, (blocks, lanes, seqs)),
            mesh=mesh,
            in_specs=(tokens, P("seq"), whole, whole, rows, rows, whole, whole, rows, rows, tokens),
            out_specs=(tokens, tokens, whole, whole, rows, rows, whole, whole, rows, rows),
            check_vma=False,
        )(*args)

    return run
```

```python
import functools

import jax
import jax.numpy as jnp
from jax import lax
from jax.experimental import pallas as pl
from jax.experimental.pallas import tpu as pltpu
from jax.sharding import PartitionSpec as P

HEADS = 12
VMEM_LIMIT = 60 * 2**20


MESH = pl.DeviceIdType.MESH
DMA = pltpu.SemaphoreType.DMA
ANYWHERE = pl.BlockSpec(memory_space=pl.ANY)


class Place:
    def __init__(self, blocks, lanes, seqs):
        self.blocks, self.depth, self.seqs = blocks, lanes // 2, seqs
        self.share = blocks // seqs
        self.per_part = blocks // self.share
        self.bits = max(1, blocks.bit_length() - 1)
        self.blk = lax.axis_index("blk")
        lane = lax.axis_index("seq")
        self.z, self.core = lane // 2, lane % 2
        flat = self.blk * 2 + self.core
        self.seq, self.part = flat // self.share, flat % self.share
        self.home = self.seq // seqs
        self.other = lax.rem(self.blk * 2 + 1 - self.core, self.share)

    def at(self, blk, z, core):
        return (blk, z * 2 + core)

    def sibling(self):
        return self.at(self.blk, self.z, 1 - self.core)

    def peers(self, along_z, along_blk):
        out = [self.sibling()]
        if along_z:
            out += [self.at(self.blk, lax.rem(self.z + k, self.depth), self.core) for k in range(1, self.depth)]
        if along_blk:
            for m in range(1, self.blocks):
                out += [self.at(self.blk ^ m, self.z, 0), self.at(self.blk ^ m, self.z, 1)]
        return out

    def bit(self, part, step):
        return 1 << ((part + step) % self.bits)

    def widen(self, k):
        masks, out, seen = [0], [], 0
        for t in range(self.bits):
            bit = self.bit(k, t)
            out.append((bit, list(masks), seen))
            seen += len(masks)
            masks += [m ^ bit for m in masks]
        return out

    def narrow(self, k):
        out, seen = [], 0
        for t in range(self.bits):
            masks = [0]
            for u in range(t + 1, self.bits):
                masks += [m ^ self.bit(k, u) for m in masks]
            out.append((self.bit(k, t), masks, seen))
            seen += len(masks)
        return out


def greet(devices):
    barrier = pltpu.get_barrier_semaphore()
    for device in devices:
        pl.semaphore_signal(barrier, inc=1, device_id=device, device_id_type=MESH)
    pl.semaphore_wait(barrier, len(devices))


def send(src, dst, send_sem, recv_sem, device):
    pltpu.make_async_remote_copy(
        src_ref=src, dst_ref=dst, send_sem=send_sem, recv_sem=recv_sem, device_id=device, device_id_type=MESH
    ).start()


def arrived(ref, sem):
    pltpu.make_async_copy(ref, ref, sem).wait()


class Fold:
    def __init__(self, place, kinds, grads, rows_in, sums, rows_out, scratch):
        self.place, self.kinds, self.grads = place, kinds, grads
        self.rows_in, self.sums, self.rows_out = rows_in, sums, rows_out
        self.count, self.moves = len(kinds), len(rows_in)
        n = self.count
        self.held, self.near, self.wide, self.tall = (scratch[i * n : i * n + n] for i in range(4))
        self.m_s, self.m_r, self.z_s, self.z_r, self.b_s, self.b_r, self.c_s, self.c_r, self.loc = scratch[4 * n :]
        self.order = list(range(1, place.depth)) + [0]
        self.units = [(a, k) for a in range(n) for k in self.order]

    @staticmethod
    def scratch(sizes, chunks, types, kinds, moves):
        blocks, lanes, seqs = sizes
        depth, share, count = lanes // 2, blocks // seqs, len(chunks)
        out = [pltpu.VMEM((blocks, depth) + c, t) for c, t in zip(chunks, types)]
        out += [
            pltpu.VMEM((1, 1, 8, 128) if kind == "columns" else (blocks, depth) + c, t)
            for c, t, kind in zip(chunks, types, kinds)
        ]
        out += [pltpu.VMEM((depth, blocks - 1) + c, t) for c, t in zip(chunks, types)]
        out += [pltpu.VMEM((depth - 1,) + c, t) for c, t in zip(chunks, types)]
        return out + [
            DMA((max(1, moves), blocks // share)),
            DMA((max(1, moves), seqs)),
            DMA((count, depth - 1)),
            DMA((count, depth - 1)),
            DMA((count, depth, blocks - 1)),
            DMA((count, depth, blocks - 1)),
            DMA((count, depth)),
            DMA((count, depth)),
            DMA((count + 1, max(depth, moves))),
        ]

    def level(self, k):
        return lax.rem(self.place.z + k, self.place.depth)

    def greet(self):
        greet(self.place.peers(True, True))

    def clear(self):
        place = self.place
        for a in range(self.count):
            if self.kinds[a] == "columns" and place.share > 2:
                held = self.held[a]
                for g in range(place.share):

                    @pl.when((g != place.part) & (g != place.other))
                    def _(held=held, g=g):
                        held[:, :, g] = jnp.zeros(held.shape[:2] + held.shape[3:], held.dtype)

    def start(self, a, k):
        place = self.place
        if self.kinds[a] == "columns":
            mine = there = self.held[a].at[:, self.level(k), place.part]
        else:
            mine = self.held[a].at[:, self.level(k)]
            there = self.near[a].at[:, self.level(k)]
        theirs = self.grads[a].at[:, self.level(k), 1 - place.core]
        send(theirs, there, self.c_s.at[a, k], self.c_r.at[a, k], place.sibling())
        pltpu.make_async_copy(self.grads[a].at[:, self.level(k), place.core], mine, self.loc.at[a, k]).start()

    def add(self, into, second):
        total = into[...].astype(jnp.float32) + second[...].astype(jnp.float32)
        into[...] = total.astype(into.dtype)

    def forward(self, a, k, t):
        place = self.place
        bit, masks, seen = place.narrow(k)[t]
        for n, m in enumerate(masks):
            sems = self.b_s.at[a, k, seen + n], self.b_r.at[a, k, seen + n]
            block = self.held[a].at[place.blk ^ bit ^ m, self.level(k)]
            send(block, self.wide[a].at[k, seen + n], *sems, place.at(place.blk ^ bit, place.z, place.core))

    def join(self, a, k):
        place = self.place
        if self.kinds[a] == "columns":
            arrived(self.held[a].at[:, self.level(k), place.part], self.loc.at[a, k])
            arrived(self.held[a].at[:, self.level(k), place.other], self.c_r.at[a, k])
        else:
            arrived(self.held[a].at[:, self.level(k)], self.loc.at[a, k])
            arrived(self.near[a].at[:, self.level(k)], self.c_r.at[a, k])

            def one(b, _):
                self.add(self.held[a].at[b, self.level(k)], self.near[a].at[b, self.level(k)])
                return 0

            lax.fori_loop(0, place.blocks, one, 0)
        self.forward(a, k, 0)

    def step(self, a, k, t):
        place = self.place
        bit, masks, seen = place.narrow(k)[t]
        for n, m in enumerate(masks):
            arrived(self.wide[a].at[k, seen + n], self.b_r.at[a, k, seen + n])
            self.add(self.held[a].at[place.blk ^ m, self.level(k)], self.wide[a].at[k, seen + n])
        if t + 1 < place.bits:
            self.forward(a, k, t + 1)
        elif k > 0:
            sems = self.z_s.at[a, k - 1], self.z_r.at[a, k - 1]
            block = self.held[a].at[place.blk, self.level(k)]
            send(block, self.tall[a].at[k - 1], *sems, place.at(place.blk, self.level(k), place.core))

    def total(self, a):
        self.sums[a][...] = self.value(a)

    def value(self, a):
        place = self.place
        value = self.held[a][place.blk, place.z].astype(jnp.float32)
        for k in range(1, place.depth):
            arrived(self.tall[a].at[k - 1], self.z_r.at[a, k - 1])
            value = value + self.tall[a][k - 1].astype(jnp.float32)
        return value

    def rows(self, j):
        place = self.place
        slot = lax.rem(place.seq, place.seqs)
        for t in range(place.per_part):
            source = place.part * place.per_part + t
            mine = (source == place.blk) & (place.home == place.core)

            @pl.when(mine)
            def _(t=t):
                pltpu.make_async_copy(self.rows_in[j].at[t], self.rows_out[j].at[slot], self.loc.at[self.count, j]).start()

            @pl.when(jnp.logical_not(mine))
            def _(t=t, source=source):
                sems = self.m_s.at[j, t], self.m_r.at[j, slot]
                send(self.rows_in[j].at[t], self.rows_out[j].at[slot], *sems, place.at(source, place.z, place.home))

    def finish(self):
        place = self.place
        for a, k in self.units:
            if self.kinds[a] == "columns":
                arrived(self.held[a].at[:, 0, 0], self.c_s.at[a, k])
            else:
                arrived(self.held[a].at[:, 0], self.c_s.at[a, k])
            for n in range(place.blocks - 1):
                arrived(self.held[a].at[0, 0], self.b_s.at[a, k, n])
            if k > 0:
                arrived(self.held[a].at[0, 0], self.z_s.at[a, k - 1])
        for j in range(self.moves):
            for t in range(place.per_part):
                mine = (place.part * place.per_part + t == place.blk) & (place.home == place.core)

                @pl.when(mine)
                def _(j=j, t=t):
                    arrived(self.rows_in[j].at[t], self.loc.at[self.count, j])

                @pl.when(jnp.logical_not(mine))
                def _(j=j, t=t):
                    arrived(self.rows_in[j].at[t], self.m_s.at[j, t])

            for i in range(place.seqs):
                owner = (place.core * place.seqs + i) * place.share + place.blk // place.per_part

                @pl.when(owner != place.blk * 2 + place.core)
                def _(j=j, i=i):
                    arrived(self.rows_out[j].at[i], self.m_r.at[j, i])


def fold_shapes(sizes, grads, kinds, rows):
    blocks, _, seqs = sizes
    share = blocks // seqs
    chunks = [((share,) if kind == "columns" else ()) + g.shape[3:] for g, kind in zip(grads, kinds)]
    scratch = Fold.scratch(sizes, chunks, [g.dtype for g in grads], kinds, len(rows))
    out = [jax.ShapeDtypeStruct(c, jnp.float32) for c in chunks]
    moved = [jax.ShapeDtypeStruct((seqs,) + r.shape[1:], r.dtype) for r in rows]
    return out, moved, scratch


def dot_nt(left, right):
    return lax.dot_general(left, right, (((1,), (1,)), ((), ())), preferred_element_type=jnp.float32)


def dot_nn(left, right):
    return lax.dot_general(left, right, (((1,), (0,)), ((), ())), preferred_element_type=jnp.float32)


def split_heads(dst, src):
    low = lax.broadcasted_iota(jnp.int32, src.shape, 1) < 64
    dst[0] = jnp.where(low, src, jnp.zeros_like(src))
    dst[1] = jnp.where(low, jnp.zeros_like(src), src)


def causal(bk, bq, kj, qi):
    kpos = kj * bk + lax.broadcasted_iota(jnp.int32, (bk, bq), 0)
    qpos = qi * bq + lax.broadcasted_iota(jnp.int32, (bk, bq), 1)
    return kpos <= qpos


def plan(tasks, points):
    out = {}
    for where, call in tasks:
        out.setdefault(min(points - 1, int(where * points)), []).append(call)
    return out


def pump(todo, point):
    for at, calls in todo.items():

        @pl.when(point == at)
        def _(calls=calls):
            for call in calls:
                call()


class Total:
    def __init__(self, place, stages, from_z, from_blk, from_core, sems):
        self.place, self.stages = place, stages
        self.from_z, self.from_blk, self.from_core = from_z, from_blk, from_core
        self.z_s, self.z_r, self.b_s, self.b_r, self.c_s, self.c_r = sems

    @staticmethod
    def scratch(sizes, shape):
        blocks, lanes, _ = sizes
        depth, bits = lanes // 2, max(1, blocks.bit_length() - 1)
        return [
            pltpu.VMEM((2 + bits,) + shape, jnp.float32),
            pltpu.VMEM((depth - 1,) + shape, jnp.float32),
            pltpu.VMEM((bits,) + shape, jnp.float32),
            pltpu.VMEM(shape, jnp.float32),
            DMA((depth - 1,)),
            DMA((depth - 1,)),
            DMA((bits,)),
            DMA((bits,)),
            DMA((1,)),
            DMA((1,)),
        ]

    def start(self):
        place = self.place
        for k in range(1, place.depth):
            target = place.at(place.blk, lax.rem(place.z + k, place.depth), place.core)
            send(self.stages.at[0], self.from_z.at[k - 1], self.z_s.at[k - 1], self.z_r.at[k - 1], target)

    def step(self, n):
        place = self.place
        if n == 0:
            value = self.stages[0]
            for k in range(1, place.depth):
                arrived(self.from_z.at[k - 1], self.z_r.at[k - 1])
                value = value + self.from_z[k - 1]
        else:
            arrived(self.from_blk.at[n - 1], self.b_r.at[n - 1])
            value = self.stages[n] + self.from_blk[n - 1]
        self.stages[n + 1] = value
        if n < place.bits:
            target = place.at(place.blk ^ (1 << n), place.z, place.core)
            send(self.stages.at[n + 1], self.from_blk.at[n], self.b_s.at[n], self.b_r.at[n], target)
        else:
            send(self.stages.at[n + 1], self.from_core, self.c_s.at[0], self.c_r.at[0], place.sibling())

    def finish(self):
        place = self.place
        arrived(self.from_core, self.c_r.at[0])
        value = self.stages[place.bits + 1] + self.from_core[...]
        arrived(self.from_core, self.c_s.at[0])
        for n in range(place.bits):
            arrived(self.from_core, self.b_s.at[n])
        for k in range(1, place.depth):
            arrived(self.from_core, self.z_s.at[k - 1])
        return value


class Gather:
    def __init__(self, place, shard, full, sems, only=None, span=None):
        self.place, self.full, self.only = place, full, only
        self.tail = () if span is None else (pl.ds(*span),)
        self.shard = shard if span is None else shard.at[self.tail[0]]
        self.z_s, self.z_r, self.b_s, self.b_r, self.c_s, self.c_r, self.loc = sems

    @staticmethod
    def sems(sizes):
        blocks, lanes, _ = sizes
        depth = lanes // 2
        return [
            DMA((depth,)),
            DMA((depth,)),
            DMA((depth, blocks - 1)),
            DMA((depth, blocks - 1)),
            DMA((depth,)),
            DMA((depth,)),
            DMA((1 + depth,)),
        ]

    def level(self, k):
        return lax.rem(self.place.z + self.place.depth - k, self.place.depth)

    def lane(self, depth_at, core):
        return self.full.at[(slice(None), depth_at, core) + self.tail]

    def chunk(self, blk, k):
        return self.full.at[(blk, self.level(k), self.place.core) + self.tail]

    def start(self):
        place = self.place
        for k in range(1, place.depth):
            target = place.at(place.blk, lax.rem(place.z + k, place.depth), place.core)
            send(self.shard, self.chunk(place.blk, 0), self.z_s.at[k], self.z_r.at[k], target)

    def keep(self):
        pltpu.make_async_copy(self.shard, self.chunk(self.place.blk, 0), self.loc.at[0]).start()

    def forward(self, k, t):
        place = self.place
        bit, masks, seen = place.widen(k)[t]
        for n, m in enumerate(masks):
            there = self.chunk(place.blk ^ m, k)
            src = self.shard if m == 0 and k == 0 else there
            send(src, there, self.b_s.at[k, seen + n], self.b_r.at[k, seen + n], place.at(place.blk ^ bit, place.z, place.core))

    def climb(self, k):
        if k > 0:
            arrived(self.chunk(self.place.blk, k), self.z_r.at[k])
        self.forward(k, 0)

    def step(self, k, t):
        place = self.place
        bit, masks, seen = place.widen(k)[t]
        for n, m in enumerate(masks):
            arrived(self.chunk(place.blk ^ bit ^ m, k), self.b_r.at[k, seen + n])
        if t + 1 < place.bits:
            self.forward(k, t + 1)
        else:
            self.swap(k)

    def swap(self, k):
        place = self.place
        if k == 0:
            arrived(self.shard, self.loc.at[0])
        if self.only is None:
            held = self.lane(self.level(k), place.core)
            send(held, held, self.c_s.at[k], self.c_r.at[k], place.sibling())
        else:
            there = self.only.at[:, self.level(k), place.core]
            send(self.full.at[:, self.level(k), place.core, place.other], there, self.c_s.at[k], self.c_r.at[k], place.sibling())
            mine = self.full.at[:, self.level(k), place.core, place.part]
            pltpu.make_async_copy(mine, there, self.loc.at[1 + k]).start()

    def wait_swap(self, k):
        place = self.place
        if self.only is None:
            arrived(self.lane(self.level(k), 1 - place.core), self.c_r.at[k])
        else:
            arrived(self.only.at[:, self.level(k), 1 - place.core], self.c_r.at[k])
            arrived(self.only.at[:, self.level(k), place.core], self.loc.at[1 + k])

    def finish(self):
        place = self.place
        for k in range(place.depth):
            if self.only is None:
                self.wait_swap(k)
                arrived(self.lane(0, 0), self.c_s.at[k])
            else:
                arrived(self.only.at[:, 0, 0], self.c_s.at[k])
            if k > 0:
                arrived(self.shard, self.z_s.at[k])
            for n in range(place.blocks - 1):
                arrived(self.shard, self.b_s.at[k, n])


class GatherAcross(Gather):
    def start(self):
        place = self.place
        for m in range(1, place.blocks):
            target = place.at(place.blk ^ m, place.z, place.core)
            send(self.shard, self.chunk(place.blk, 0), self.b_s.at[0, m - 1], self.b_r.at[0, m - 1], target)

    def climb(self):
        place = self.place
        for m in range(1, place.blocks):
            arrived(self.chunk(place.blk ^ m, 0), self.b_r.at[0, m - 1])
        arrived(self.shard, self.loc.at[0])
        held = self.lane(place.z, place.core)
        for k in range(1, place.depth):
            target = place.at(place.blk, lax.rem(place.z + k, place.depth), place.core)
            send(held, held, self.z_s.at[k], self.z_r.at[k], target)
        self.pass_on(0)

    def pass_on(self, k):
        held = self.lane(self.level(k), self.place.core)
        if k > 0:
            arrived(held, self.z_r.at[k])
        send(held, held, self.c_s.at[k], self.c_r.at[k], self.place.sibling())

    def finish(self):
        place = self.place
        for k in range(place.depth):
            self.wait_swap(k)
            arrived(self.lane(0, 0), self.c_s.at[k])
            if k > 0:
                arrived(self.lane(0, 0), self.z_s.at[k])
        for m in range(1, place.blocks):
            arrived(self.shard, self.b_s.at[0, m - 1])


def first_kernel(sizes, block, pairs, *refs):
    place = Place(*sizes)
    tok, cot, vec, w_qkv, w_out, w_up, w_down = refs[:7]
    refs = refs[7:]
    att_ref, lse_ref, att_own, tok_own, cot_own, normed_out, qkv_out, cols_out, vec_out, stage, out_full, up_full, down_full = refs[:13]
    refs = refs[13:]
    tok_v, norm_v, norm_t, chunk_v, w32_v, cols_v, qkv_v, kh, vt, run_m, run_l, run_a, att_v = refs[:13]
    tok_s, tok_r, near_s, near_r, cot_s, cot_r, a_s, a_r, loc = refs[13:22]
    total = Total(place, *refs[22:26], refs[26:32])
    refs = refs[32:]
    late_rows = w_down.shape[0] // 3
    late_rows = late_rows if late_rows % 16 == 0 else 0
    early_rows = w_down.shape[0] - late_rows
    qkv = Gather(place, w_qkv, stage, refs[0:7], chunk_v)
    outw = Gather(place, w_out, out_full, refs[7:14])
    upw = Gather(place, w_up, up_full, refs[14:21])
    downw = GatherAcross(place, w_down, down_full, refs[21:28], span=(0, early_rows))
    climbers = [outw, upw]
    if late_rows:
        climbers.append(Gather(place, w_down, down_full, refs[28:35], span=(early_rows, late_rows)))
    arrays = [qkv, downw] + climbers
    blocks, depth, seqs, share, bits = place.blocks, place.depth, place.seqs, place.share, place.bits
    blk, z, core, home = place.blk, place.z, place.core, place.home
    pair = pl.program_id(0)
    rows, model = tok_v.shape[1:]
    length = blocks * rows
    count = length // block
    owned = w_qkv.shape[1]
    per_seq = share // 2
    local = lambda src, dst, sem: pltpu.make_async_copy(src, dst, sem).start()

    @pl.when(pair == 0)
    def _():
        total.stages[0] = vec[...]
        greet(place.peers(True, True))
        total.start()
        qkv.start()
        for i in range(seqs):
            for h in range(per_seq):
                target = (core * seqs + i) * per_seq + h

                @pl.when(target != blk)
                def _(i=i, h=h, target=target):
                    sems = tok_s.at[i * per_seq + h], tok_r.at[blk]
                    send(tok.at[i], tok_v.at[blk], *sems, place.at(target, z, core))

                @pl.when(target == blk)
                def _(i=i):
                    local(tok.at[i], tok_v.at[blk], loc.at[0])

        qkv.forward(0, 0)
        for array in arrays:
            array.keep()
        for k in range(1, depth):
            qkv.climb(k)
        for array in climbers:
            array.start()
        total.step(0)
        total.step(1)

        @pl.when(core == home)
        def _():
            for p in range(blocks):

                @pl.when(p != blk)
                def _():
                    arrived(tok_v.at[p], tok_r.at[p])

                @pl.when(p == blk)
                def _():
                    arrived(tok_v.at[p], loc.at[0])

                send(tok_v.at[p], tok_v.at[p], near_s.at[p], near_r.at[p], place.sibling())

        for n in range(2, bits + 1):
            total.step(n)
        for t in range(bits):
            for k in range(depth):
                qkv.step(k, t)
            if t == 0:
                downw.start()
        vec_out[...] = total.finish()
        gain, shift = vec_out[0:1, :], vec_out[1:2, :]
        part_rows = min(rows, 128)

        for p in range(blocks):

            @pl.when(core != home)
            def _(p=p):
                arrived(tok_v.at[p], near_r.at[p])

            def norm(i, _, p=p):
                inside = pl.ds(pl.multiple_of(i * part_rows, part_rows), part_rows)
                unit, _ = centered(tok_v[p, inside, :].astype(jnp.float32))
                at = pl.ds(pl.multiple_of(p * rows + i * part_rows, part_rows), part_rows)
                normed = unit * gain + shift
                norm_v[at, :] = normed.astype(jnp.bfloat16)
                norm_t[:, at] = normed.T.astype(jnp.bfloat16)
                return 0

            lax.fori_loop(0, rows // part_rows, norm, 0)
        local(norm_t, normed_out, loc.at[1])
        for t in range(place.per_part):
            local(tok_v.at[place.part * place.per_part + t], tok_own.at[t], loc.at[2 + t])
        downw.climb()
        for array in climbers:
            for k in range(depth):
                array.climb(k)
        for k in range(depth):
            qkv.wait_swap(k)
        for b in range(blocks):
            for d in range(depth):
                for c in range(2):
                    index = (b * depth + d) * 2 + c
                    w32_v[index * owned : (index + 1) * owned, :] = chunk_v[b, d, c].astype(jnp.float32)
        cols_v[...] = w32_v[...].astype(jnp.bfloat16)
        local(cols_v, cols_out, loc.at[2 + place.per_part])

        def project(i, _):
            at = pl.ds(pl.multiple_of(i * block, block), block)
            normed = norm_v[at, :]
            scale = jnp.where(lax.broadcasted_iota(jnp.int32, (1, 384), 1) < 128, 0.125, 1.0)
            for n in range(pairs):
                value = dot_nn(normed, cols_v[:, n * 384 : (n + 1) * 384]) * scale
                qkv_v[at, n * 384 : (n + 1) * 384] = value.astype(jnp.bfloat16)
            return 0

        lax.fori_loop(0, count, project, 0)
        local(qkv_v, qkv_out, loc.at[3 + place.per_part])

    per_pair = count * (count + 1) // 2
    tasks = []
    levels = [(array, k) for array in climbers for k in range(depth)]
    for n, (array, k) in enumerate(levels):
        for t in range(bits):
            where = 0.08 + 0.26 * t + (0.1 + 0.25 * t) * n / len(levels)
            tasks.append((where, functools.partial(array.step, k, t)))
    for k in range(1, depth):
        tasks.append((0.55 + 0.3 * k / depth, functools.partial(downw.pass_on, k)))

    def own_rows():
        for i in range(seqs):
            owner = (core * seqs + i) * share + blk // place.per_part
            slot = lax.rem(blk, place.per_part)

            @pl.when(owner != blk * 2 + core)
            def _(i=i, owner=owner, slot=slot):
                send(cot.at[i], cot_own.at[slot], cot_s.at[i], cot_r.at[slot], place.at(owner // 2, z, owner % 2))

            @pl.when(owner == blk * 2 + core)
            def _(i=i, slot=slot):
                local(cot.at[i], cot_own.at[slot], loc.at[4 + place.per_part])

    tasks.append((0.2, own_rows))
    tasks.sort(key=lambda task: task[0])
    todo = plan(tasks, pairs * per_pair)

    def lanes_of(n):
        return pl.ds(pl.multiple_of(pair * 384 + n * 128, 128), 128)

    split_heads(kh, qkv_v[:, lanes_of(1)])
    vt[...] = qkv_v[:, lanes_of(2)].astype(jnp.float32).T.astype(jnp.bfloat16)

    def q_step(qi, _):
        at_q = pl.ds(pl.multiple_of(qi * block, block), block)
        run_m[...] = jnp.full_like(run_m, -1e30)
        run_l[...] = jnp.zeros_like(run_l)
        run_a[...] = jnp.zeros_like(run_a)

        def one(kj, masked):
            at = pl.ds(pl.multiple_of(kj * block, block), block)
            q_rows = qkv_v[at_q, lanes_of(0)]
            scores = [dot_nt(kh[h, at, :], q_rows) for h in range(2)]
            weighed = []
            for h in range(2):
                peak, so_far = run_m[h : h + 1, :], run_l[h : h + 1, :]
                s = scores[h]
                u = s * s + 1.0
                inv = lax.rsqrt(u)
                mag = u * inv
                if masked:
                    mag = jnp.where(causal(block, block, kj, qi), mag, -1e30)
                new = jnp.maximum(peak, jnp.max(mag, axis=0, keepdims=True))
                p = jnp.exp(mag - new)
                alpha = jnp.exp(peak - new)
                run_m[h : h + 1, :] = new
                run_l[h : h + 1, :] = so_far * alpha + jnp.sum(p, axis=0, keepdims=True)
                weighed.append((alpha, (p * (s * inv)).astype(jnp.bfloat16)))
            for h in range(2):
                alpha, signed = weighed[h]
                head = slice(64 * h, 64 * h + 64)
                run_a[head, :] = run_a[head, :] * alpha + dot_nn(vt[head, at], signed)

        def k_step(kj, _):
            @pl.when(kj == qi)
            def _():
                one(kj, True)

            @pl.when(kj != qi)
            def _():
                one(kj, False)

            pump(todo, pair * per_pair + qi * (qi + 1) // 2 + kj)
            return 0

        lax.fori_loop(0, qi + 1, k_step, 0)
        both = []
        for h in range(2):
            both.append(run_a[64 * h : 64 * h + 64, :] / run_l[h : h + 1, :])
            lse_ref[0, h : h + 1, at_q] = run_m[h : h + 1, :] + jnp.log(run_l[h : h + 1, :])
        joined = jnp.concatenate(both, 0).T.astype(jnp.bfloat16)
        att_ref[at_q, :] = joined
        att_v[pair, at_q, :] = joined
        return 0

    lax.fori_loop(0, count, q_step, 0)
    part, mine = place.part, length // share
    flat = blk * 2 + core

    def piece(p, g):
        return att_v.at[p, pl.ds(pl.multiple_of(g * mine, 16), mine)]

    for p in range(pairs):
        there = att_own.at[part, :, pl.ds(p * 128, 128)]

        @pl.when(pair == p)
        def _(p=p, there=there):
            for k in range(1, share):
                other = flat ^ k
                send(piece(p, part ^ k), there, a_s.at[k, p], a_r.at[k, p], place.at(other // 2, z, other % 2))
            local(piece(p, part), there, a_s.at[0, p])

    @pl.when(pair == pairs - 1)
    def _():
        for p in range(pairs):
            for k in range(share):
                arrived(piece(p, 0), a_s.at[k, p])
                if k > 0:
                    arrived(att_own.at[part ^ k, :, pl.ds(p * 128, 128)], a_r.at[k, p])
        for array in arrays:
            array.finish()
        for i in range(seqs):

            @pl.when((core * seqs + i) * share + blk // place.per_part != blk * 2 + core)
            def _(i=i):
                arrived(cot.at[i], cot_s.at[i])

        for t in range(place.per_part):
            here = (place.part * place.per_part + t == blk) & (home == core)

            @pl.when(here)
            def _(t=t):
                arrived(cot_own.at[t], loc.at[4 + place.per_part])

            @pl.when(jnp.logical_not(here))
            def _(t=t):
                arrived(cot_own.at[t], cot_r.at[t])

        arrived(norm_t, loc.at[1])
        arrived(cols_v, loc.at[2 + place.per_part])
        arrived(qkv_v, loc.at[3 + place.per_part])
        for t in range(place.per_part):
            arrived(tok_own.at[t], loc.at[2 + t])

        @pl.when(core == home)
        def _():
            for p in range(blocks):
                arrived(tok_v.at[p], near_s.at[p])

        for i in range(seqs):
            for h in range(per_seq):
                target = (core * seqs + i) * per_seq + h

                @pl.when(target != blk)
                def _(i=i, h=h):
                    arrived(tok.at[i], tok_s.at[i * per_seq + h])

                @pl.when((target == blk) & (core != home))
                def _():
                    arrived(tok_v.at[blk], loc.at[0])


def first_half(sizes, tok, cot, vec, w_qkv, w_out, w_up, w_down, block):
    blocks, lanes, seqs = sizes
    depth, share = lanes // 2, blocks // seqs
    per_part = blocks // share
    rows, model = tok.shape[1:]
    length = blocks * rows
    width = w_qkv.shape[2]
    pairs = width // 384
    low, full = jnp.bfloat16, jnp.float32
    shape = jax.ShapeDtypeStruct
    owners = (blocks, depth, 2)
    in_vmem = pl.BlockSpec(memory_space=pltpu.VMEM)
    return pl.pallas_call(
        functools.partial(first_kernel, sizes, block, pairs),
        grid=(pairs,),
        out_shape=[
            shape((length, 128 * pairs), low),
            shape((pairs, 8, length), full),
            shape((share, length // share, 128 * pairs), low),
            shape((per_part, rows, model), low),
            shape((per_part, rows, model), low),
            shape((model, length), low),
            shape((length, width), low),
            shape((model, width), low),
            shape(vec.shape, full),
            shape(owners + w_qkv.shape, low),
            shape(owners + w_out.shape, low),
            shape(owners + w_up.shape, low),
            shape(owners + w_down.shape, low),
        ],
        in_specs=[ANYWHERE, ANYWHERE, in_vmem] + [ANYWHERE] * 4,
        out_specs=[pl.BlockSpec((length, 128), lambda p: (0, p)), pl.BlockSpec((1, 8, length), lambda p: (p, 0, 0))]
        + [ANYWHERE] * 6
        + [in_vmem]
        + [ANYWHERE] * 4,
        scratch_shapes=[
            pltpu.VMEM((blocks, rows, model), low),
            pltpu.VMEM((length, model), low),
            pltpu.VMEM((model, length), low),
            pltpu.VMEM(owners + w_qkv.shape[1:], low),
            pltpu.VMEM((model, width), full),
            pltpu.VMEM((model, width), low),
            pltpu.VMEM((length, width), low),
            pltpu.VMEM((2, length, 128), low),
            pltpu.VMEM((128, length), low),
            pltpu.VMEM((8, block), full),
            pltpu.VMEM((8, block), full),
            pltpu.VMEM((128, block), full),
            pltpu.VMEM((pairs, length, 128), low),
            DMA((seqs * share // 2,)),
            DMA((blocks,)),
            DMA((blocks,)),
            DMA((blocks,)),
            DMA((seqs,)),
            DMA((per_part,)),
            DMA((share, pairs)),
            DMA((share, pairs)),
            DMA((5 + per_part,)),
        ]
        + Total.scratch(sizes, vec.shape)
        + Gather.sems(sizes) * 5,
        compiler_params=pltpu.CompilerParams(collective_id=0, has_side_effects=True, vmem_limit_bytes=VMEM_LIMIT),
    )(tok, cot, vec, w_qkv, w_out, w_up, w_down)


def dot_tn(left, right):
    return lax.dot_general(left, right, (((0,), (0,)), ((), ())), preferred_element_type=jnp.float32)


def centered(values):
    center = jnp.mean(values, axis=-1, keepdims=True)
    offsets = values - center
    spread = jnp.mean(offsets * offsets, axis=-1, keepdims=True)
    inverse = lax.rsqrt(spread + 1e-05)
    return offsets * inverse, inverse


def norm_back(values, grads, gain):
    unit, inverse = centered(values)
    scaled = grads * gain
    first = jnp.mean(scaled, axis=-1, keepdims=True)
    second = jnp.mean(scaled * unit, axis=-1, keepdims=True)
    back = inverse * (scaled - first - unit * second)
    return back, jnp.sum(grads * unit, axis=0, keepdims=True), jnp.sum(grads, axis=0, keepdims=True)


def gelu_parts(x):
    square = x * x
    half = 0.5 + 0.5 * jnp.tanh(0.7978845608028654 * x * (1.0 + 0.044715 * square))
    slope = half + x * (2.0 * half * (1.0 - half)) * (0.7978845608028654 + 0.1070322243 * square)
    return x * half, slope


def mlp_kernel(sizes, cols, tile, chunk, *refs):
    place = Place(*sizes)
    att, tok_own, cot, w_out, w_up, w_down, vec = refs[:7]
    refs = refs[7:]
    result, g_heads, g_mid, g_out, g_up, g_down, g_vec = refs[:7]
    (att_v, tok_v, cot_v, res_v, out_v, up_v, down_v, mid_v, n2_v, n2t_v, hid_v, slope_v, sum_v, ga_v) = refs[7:21]
    (st_out, st_up, st_down) = refs[21:24]
    g_s, g_r, m_s, m_r, loc, up_l, down_l, o_l = refs[24:]
    share, per_part, seqs = place.share, place.per_part, place.seqs
    part, blk, z, core = place.part, place.blk, place.z, place.core
    rows, model = mid_v.shape
    block = rows // per_part
    ff = up_v.shape[1]
    chunks, tiles = ff // chunk, rows // tile
    flat = blk * 2 + core
    partners = [((flat ^ k) // 2, z, (flat ^ k) % 2) for k in range(1, share)]
    slot_of = lax.rem(place.seq, seqs)
    greet(place.peers(False, True))
    def local(src, dst, sem):
        pltpu.make_async_copy(src, dst, sem).start()

    local(att, att_v, loc.at[0])
    for t in range(per_part):
        local(tok_own.at[t], tok_v.at[t], loc.at[1 + t])
    local(w_out, out_v, loc.at[1 + per_part])
    local(cot, cot_v, loc.at[2 + per_part])

    def span(f):
        return pl.ds(pl.multiple_of(f * chunk, chunk), chunk)

    for f in range(chunks):
        local(w_up.at[:, pl.ds(f * chunk, chunk)], up_v.at[:, pl.ds(f * chunk, chunk)], up_l.at[f])
        local(w_down.at[pl.ds(f * chunk, chunk)], down_v.at[pl.ds(f * chunk, chunk)], down_l.at[f])

    arrived(att_v, loc.at[0])
    for t in range(per_part):
        arrived(tok_v.at[t], loc.at[1 + t])
    arrived(out_v, loc.at[1 + per_part])
    gain, shift = vec[2:3, :], vec[3:4, :]
    per_block = block // tile

    def spot(i):
        return i // per_block, pl.ds(pl.multiple_of(lax.rem(i, per_block) * tile, tile), tile)

    lane = lax.broadcasted_iota(jnp.int32, (1, model), 1)
    mine_at = z * 2 * seqs + place.seq
    length = jnp.sum(jnp.where(lane == mine_at, vec[4:5, :], 0.0), axis=1, keepdims=True)

    def live(i):
        position = part * rows + i * tile + lax.broadcasted_iota(jnp.int32, (tile, 1), 0)
        return jnp.where(position.astype(jnp.float32) < length, 1.0, 0.0)

    def enter(i, _):
        at = pl.ds(pl.multiple_of(i * tile, tile), tile)
        branch = dot_nn(att_v[0, at, :cols], out_v[:cols, :])
        for g in range(1, share):
            branch = branch + dot_nn(att_v[g, at, :cols], out_v[g * cols : (g + 1) * cols, :])
        t, inside = spot(i)
        middle = tok_v[t, inside, :].astype(jnp.float32) + live(i) * branch
        mid_v[at, :] = middle
        unit, _ = centered(middle)
        normed = unit * gain + shift
        n2_v[at, :] = normed.astype(jnp.bfloat16)
        n2t_v[:, at] = normed.T.astype(jnp.bfloat16)
        return 0

    lax.fori_loop(0, tiles, enter, 0)
    sum_v[...] = mid_v[...]

    def up_step(f, _):
        arrived(up_v.at[:, span(f)], up_l.at[f])
        arrived(down_v.at[span(f)], down_l.at[f])
        hidden, slope = gelu_parts(dot_nn(n2_v[...], up_v[:, span(f)]))
        hidden = hidden.astype(jnp.bfloat16)
        hid_v[:, span(f)] = hidden
        slope_v[:, span(f)] = slope.astype(jnp.bfloat16)
        sum_v[...] += dot_nn(hidden, down_v[span(f), :])
        return 0

    lax.fori_loop(0, chunks, up_step, 0)
    for t in range(per_part):
        res_v[t] = sum_v[t * block : (t + 1) * block, :].astype(jnp.bfloat16)
        source = part * per_part + t
        mine = (source == blk) & (place.home == core)

        @pl.when(mine)
        def _(t=t):
            local(res_v.at[t], result.at[slot_of], loc.at[0])

        @pl.when(jnp.logical_not(mine))
        def _(t=t, source=source):
            send(res_v.at[t], result.at[slot_of], m_s.at[t], m_r.at[slot_of], place.at(source, z, place.home))

    arrived(cot_v, loc.at[2 + per_part])
    sum_v[...] = jnp.zeros_like(sum_v)

    def back_step(f, _):
        top = cot_v[...].reshape(rows, model)
        grad_pre = (dot_nt(top, down_v[span(f), :]) * slope_v[:, span(f)].astype(jnp.float32)).astype(jnp.bfloat16)
        now = lax.rem(f, 2)

        @pl.when(f >= 2)
        def _():
            arrived(st_down.at[now], o_l.at[now])
            arrived(st_up.at[now], o_l.at[2 + now])

        st_down[now] = dot_tn(hid_v[:, span(f)], top).astype(jnp.bfloat16)
        st_up[now] = dot_nn(n2t_v[...], grad_pre).astype(jnp.bfloat16)
        local(st_down.at[now], g_down.at[span(f)], o_l.at[now])
        local(st_up.at[now], g_up.at[:, span(f)], o_l.at[2 + now])
        sum_v[...] += dot_nt(grad_pre, up_v[:, span(f)])
        return 0

    lax.fori_loop(0, chunks, back_step, 0)
    g_vec[...] = jnp.zeros_like(g_vec)

    def leave(i, _):
        at = pl.ds(pl.multiple_of(i * tile, tile), tile)
        t, inside = spot(i)
        back, d_gain, d_shift = norm_back(mid_v[at, :], sum_v[at, :], gain)
        g_vec[0:1, :] += d_gain
        g_vec[1:2, :] += d_shift
        total = cot_v[t, inside, :].astype(jnp.float32) + back
        mid_v[at, :] = total
        branch = (live(i) * total).astype(jnp.bfloat16)
        n2_v[at, :] = branch
        heads = dot_nt(branch, out_v[...]).astype(jnp.bfloat16)
        for g in range(share):
            if cols == ga_v.shape[2]:
                ga_v[g, at, :] = heads[:, g * cols : (g + 1) * cols]
            else:
                piece = heads[:, g * cols : (g + 1) * cols]
                ga_v[g, at, :] = jnp.concatenate([piece, jnp.zeros((tile, ga_v.shape[2] - cols), jnp.bfloat16)], 1)
        return 0

    lax.fori_loop(0, tiles, leave, 0)
    for k in range(1, share):
        send(ga_v.at[part ^ k], g_heads.at[part], g_s.at[k - 1], g_r.at[k - 1], place.at(*partners[k - 1]))
    local(ga_v.at[part], g_heads.at[part], loc.at[1])
    local(mid_v, g_mid, loc.at[2])
    for g in range(share):
        st_out[g * cols : (g + 1) * cols, :] = dot_tn(att_v[g, :, :cols], n2_v[...]).astype(jnp.bfloat16)
    local(st_out, g_out, loc.at[1 + per_part])
    for n in range(min(2, chunks)):
        arrived(st_down.at[n], o_l.at[n])
        arrived(st_up.at[n], o_l.at[2 + n])
    arrived(st_out, loc.at[1 + per_part])
    arrived(mid_v, loc.at[2])
    arrived(ga_v.at[part], loc.at[1])
    for k in range(1, share):
        arrived(ga_v.at[part ^ k], g_s.at[k - 1])
        arrived(g_heads.at[part ^ k], g_r.at[k - 1])
    for i in range(seqs):
        owner = (core * seqs + i) * share + blk // per_part

        @pl.when(owner != flat)
        def _(i=i):
            arrived(result.at[i], m_r.at[i])

    for t in range(per_part):
        mine = (part * per_part + t == blk) & (place.home == core)

        @pl.when(mine)
        def _(t=t):
            arrived(res_v.at[t], loc.at[0])

        @pl.when(jnp.logical_not(mine))
        def _(t=t):
            arrived(res_v.at[t], m_s.at[t])


def feed_forward(sizes, cols, att, tok_own, cot, w_out, w_up, w_down, vec, tile, chunk):
    blocks, lanes, seqs = sizes
    share = blocks // seqs
    per_part = blocks // share
    block, model = tok_own.shape[1:]
    rows = per_part * block
    wide = att.shape[2]
    ff = w_up.shape[1]
    chunks = ff // chunk
    in_vmem = pl.BlockSpec(memory_space=pltpu.VMEM)
    low, full = jnp.bfloat16, jnp.float32
    return pl.pallas_call(
        functools.partial(mlp_kernel, sizes, cols, tile, chunk),
        out_shape=[
            jax.ShapeDtypeStruct((seqs, block, model), low),
            jax.ShapeDtypeStruct((share, rows, wide), low),
            jax.ShapeDtypeStruct((rows, model), full),
            jax.ShapeDtypeStruct((model, model), low),
            jax.ShapeDtypeStruct((model, ff), low),
            jax.ShapeDtypeStruct((ff, model), low),
            jax.ShapeDtypeStruct((8, model), full),
        ],
        in_specs=[ANYWHERE] * 6 + [in_vmem],
        out_specs=[ANYWHERE] * 6 + [in_vmem],
        scratch_shapes=[
            pltpu.VMEM((share, rows, wide), low),
            pltpu.VMEM((per_part, block, model), low),
            pltpu.VMEM((per_part, block, model), low),
            pltpu.VMEM((per_part, block, model), low),
            pltpu.VMEM((model, model), low),
            pltpu.VMEM((model, ff), low),
            pltpu.VMEM((ff, model), low),
            pltpu.VMEM((rows, model), full),
            pltpu.VMEM((rows, model), low),
            pltpu.VMEM((model, rows), low),
            pltpu.VMEM((rows, ff), low),
            pltpu.VMEM((rows, ff), low),
            pltpu.VMEM((rows, model), full),
            pltpu.VMEM((share, rows, wide), low),
            pltpu.VMEM((model, model), low),
            pltpu.VMEM((2, model, chunk), low),
            pltpu.VMEM((2, chunk, model), low),
            DMA((share,)),
            DMA((share,)),
            DMA((per_part,)),
            DMA((seqs,)),
            DMA((3 + per_part,)),
            DMA((chunks,)),
            DMA((chunks,)),
            DMA((4,)),
        ],
        compiler_params=pltpu.CompilerParams(collective_id=4, has_side_effects=True, vmem_limit_bytes=VMEM_LIMIT),
    )(att, tok_own, cot, w_out, w_up, w_down, vec)


def last_kernel(sizes, block, pairs, *refs):
    place = Place(*sizes)
    blocks, depth, seqs, share, bits = place.blocks, place.depth, place.seqs, place.share, place.bits
    blk, z, core, part = place.blk, place.z, place.core, place.part
    per_part = place.per_part
    count = 3 + pairs
    q_ref, k_ref, v_ref, g_ref, att_ref, lse_ref = refs[:6]
    big, tok_own, g_mid, norm_t, cols, vec, two = refs[6:9], refs[9], refs[10], refs[11], refs[12], refs[13], refs[14]
    refs = refs[15:]
    sums, qkv_sum, tok_out, vec_out, refs = refs[:3], refs[3], refs[4], refs[5], refs[6:]
    kh, vh, qh, gh, kt, delta, dqt, dk, dv = refs[:9]
    gq_v, own_v, norm_v, cols_v, tok_v, mid_v, out_v, part_v, got_v, sum_v = refs[9:19]
    p_s, p_r, t_s, t_r, loc = refs[19:24]
    total = Total(place, *refs[24:28], refs[28:34])
    kinds = ["rows"] * 3 + ["columns"] * pairs
    fold = Fold(place, kinds, list(big) + [own_v.at[p] for p in range(pairs)], [], sums, [], refs[34:])
    pair = pl.program_id(0)
    length = q_ref.shape[0]
    rows, model = mid_v.shape
    owned = own_v.shape[4]
    steps = length // block
    per_pair = steps * (steps + 1) // 2
    flat = blk * 2 + core
    partners = [((flat ^ k) // 2, z, (flat ^ k) % 2) for k in range(1, share)]
    slot_of = lax.rem(place.seq, seqs)
    local = lambda src, dst, sem: pltpu.make_async_copy(src, dst, sem).start()

    tasks = []
    units = [(a, k) for a in range(3) for k in fold.order]
    per = 12.0 / len(units)
    for n, (a, k) in enumerate(units):
        tasks.append((8 + 1.2 * per * n, functools.partial(fold.join, a, k)))
        for t in range(bits):
            where = (14 + 2.7 * per * n) if t == 0 else (38 + 8 * t + 1.4 * per * n)
            tasks.append((where, functools.partial(fold.step, a, k, t)))
    for a in range(3):
        tasks.append((80 + 2 * a, functools.partial(fold.total, a)))
    for p in range(pairs - 1):
        third = 85.0 / pairs
        for n, k in enumerate(fold.order):
            tasks.append(((p + 1.1) * third, functools.partial(fold.join, 3 + p, k)))
            for t in range(bits):
                where = (74 if p == pairs - 2 else 64) + 5 * t
                tasks.append((where, functools.partial(fold.step, 3 + p, k, t)))
    tasks = [(where / 85.0, call) for where, call in tasks]
    tasks.sort(key=lambda task: task[0])
    todo = plan(tasks, pairs * per_pair)

    @pl.when(pair == 0)
    def _():
        fold.greet()
        fold.clear()
        for a, k in units:
            fold.start(a, k)
        local(norm_t, norm_v, loc.at[0])
        local(cols, cols_v, loc.at[1])
        local(g_mid, mid_v, loc.at[2])
        local(tok_own, tok_v, loc.at[3])

    split_heads(kh, k_ref[...])
    split_heads(vh, v_ref[...])
    split_heads(qh, q_ref[...])
    split_heads(gh, g_ref[...])
    kt[...] = k_ref[...].astype(jnp.float32).T.astype(jnp.bfloat16)
    prod = (g_ref[...].astype(jnp.float32) * att_ref[...].astype(jnp.float32)).T
    delta[0:1, :] = jnp.sum(prod[:64], axis=0, keepdims=True)
    delta[1:2, :] = jnp.sum(prod[64:], axis=0, keepdims=True)
    dqt[...] = jnp.zeros_like(dqt)

    def k_step(kj, _):
        at = pl.ds(pl.multiple_of(kj * block, block), block)

        def one(qi, masked):
            at_q = pl.ds(pl.multiple_of(qi * block, block), block)
            q_rows = q_ref[at_q, :]
            g_rows = g_ref[at_q, :]
            add_k = add_v = None
            both = [(dot_nt(kh[h, at, :], q_rows), dot_nt(vh[h, at, :], g_rows)) for h in range(2)]
            for h in range(2):
                s, dp = both[h]
                u = s * s + 1.0
                inv = lax.rsqrt(u)
                arg = u * inv - lse_ref[0, h : h + 1, at_q]
                if masked:
                    arg = jnp.where(causal(block, block, kj, qi), arg, -1e30)
                p = jnp.exp(arg)
                sgn = s * inv
                t = inv * inv * (inv - 1.0) + 1.0
                ds = (p * (dp * t - sgn * delta[h : h + 1, at_q])).astype(jnp.bfloat16)
                signed = (p * sgn).astype(jnp.bfloat16)
                one_v = dot_nn(signed, gh[h, at_q, :])
                one_k = dot_nn(ds, qh[h, at_q, :])
                add_v = one_v if h == 0 else add_v + one_v
                add_k = one_k if h == 0 else add_k + one_k
                dqt[64 * h : 64 * h + 64, at_q] += dot_nn(kt[64 * h : 64 * h + 64, at], ds)
            return add_k, add_v

        def more(qi, _):
            @pl.when(qi == kj)
            def _():
                dk[...], dv[...] = one(qi, True)

            @pl.when(qi != kj)
            def _():
                add_k, add_v = one(qi, False)
                dk[...] += add_k
                dv[...] += add_v

            pump(todo, pair * per_pair + kj * steps - kj * (kj - 1) // 2 + qi - kj)
            return 0

        lax.fori_loop(kj, steps, more, 0)
        gq_v[pair, at, 128:256] = dk[...].astype(jnp.bfloat16)
        gq_v[pair, at, 256:384] = dv[...].astype(jnp.bfloat16)
        return 0

    lax.fori_loop(0, steps, k_step, 0)
    gq_v[pair, :, 0:128] = (dqt[...] * 0.125).T.astype(jnp.bfloat16)

    @pl.when(pair == 0)
    def _():
        arrived(norm_v, loc.at[0])
        arrived(cols_v, loc.at[1])
        arrived(mid_v, loc.at[2])
        arrived(tok_v, loc.at[3])

    def weight_grad():
        sum_v[...] = dot_nn(norm_v[...], gq_v[pair])
        for b in range(blocks):
            for d in range(depth):
                for c in range(2):
                    first = ((b * depth + d) * 2 + c) * owned
                    own_v[pair, b, d, c] = sum_v[first : first + owned, :].astype(jnp.bfloat16)
        for p in range(pairs):

            @pl.when(pair == p)
            def _(p=p):
                for k in fold.order:
                    fold.start(3 + p, k)

    @pl.when(pair != pairs - 1)
    def _():
        weight_grad()

    @pl.when(pair == pairs - 1)
    def _():
        mine = 3 + pairs - 1
        tile = min(256, block, rows)

        def input_grad(g, i):
            at = pl.ds(pl.multiple_of(g * rows + i * tile, tile), tile)
            value = dot_nt(gq_v[0, at, :], cols_v[:, 0:384])
            for p in range(1, pairs):
                value = value + dot_nt(gq_v[p, at, :], cols_v[:, p * 384 : (p + 1) * 384])
            return value

        per_block = rows // per_part // tile
        half = rows // per_part
        for t in range(per_part):
            for k in range(1, share):

                def away(i, _, k=k):
                    at = pl.ds(pl.multiple_of(i * tile, tile), tile)
                    part_v[k - 1, at, :] = input_grad(part ^ k, i).astype(jnp.bfloat16)
                    return 0

                lax.fori_loop(t * per_block, (t + 1) * per_block, away, 0)
                piece = pl.ds(t * half, half)
                sems = p_s.at[k - 1, t], p_r.at[k - 1, t]
                send(part_v.at[k - 1, piece], got_v.at[k - 1, piece], *sems, place.at(*partners[k - 1]))
        weight_grad()
        total.stages[0] = jnp.zeros(total.stages.shape[1:], jnp.float32)
        total.stages[0, 2:4, :] = two[0:2, :]
        gain = vec[0:1, :]

        def leave(i, _):
            at = pl.ds(pl.multiple_of(i * tile, tile), tile)
            t = i // per_block
            inside = pl.ds(pl.multiple_of(lax.rem(i, per_block) * tile, tile), tile)
            value = input_grad(part, i)
            for k in range(1, share):
                value = value + got_v[k - 1, at, :].astype(jnp.float32)
            back, d_gain, d_shift = norm_back(tok_v[t, inside, :].astype(jnp.float32), value, gain)
            total.stages[0, 0:1, :] += d_gain
            total.stages[0, 1:2, :] += d_shift
            out_v[t, inside, :] = (mid_v[at, :] + back).astype(jnp.bfloat16)
            return 0

        for t in range(per_part):
            for k in range(1, share):
                arrived(got_v.at[k - 1, pl.ds(t * half, half)], p_r.at[k - 1, t])
            lax.fori_loop(t * per_block, (t + 1) * per_block, leave, 0)
            source = part * per_part + t
            here = (source == blk) & (place.home == core)

            @pl.when(here)
            def _(t=t):
                local(out_v.at[t], tok_out.at[slot_of], loc.at[0])

            @pl.when(jnp.logical_not(here))
            def _(t=t, source=source):
                send(out_v.at[t], tok_out.at[slot_of], t_s.at[t], t_r.at[slot_of], place.at(source, z, place.home))

            if t == 0:
                for k in fold.order:
                    fold.join(mine, k)
        total.start()
        for t in range(bits):
            for k in fold.order:
                fold.step(mine, k, t)
            total.step(t)
        total.step(bits)
        for p in range(pairs):
            value = fold.value(3 + p)
            for g in range(share):
                for n in range(3):
                    first = ((n * share + g) * pairs + p) * 128
                    qkv_sum[:, first : first + 128] = value[g, :, n * 128 : n * 128 + 128]
        vec_out[...] = total.finish()
        fold.finish()
        for k in range(1, share):
            for t in range(per_part):
                arrived(part_v.at[k - 1, pl.ds(t * half, half)], p_s.at[k - 1, t])
        for t in range(per_part):
            here = (part * per_part + t == blk) & (place.home == core)

            @pl.when(here)
            def _(t=t):
                arrived(out_v.at[t], loc.at[0])

            @pl.when(jnp.logical_not(here))
            def _(t=t):
                arrived(out_v.at[t], t_s.at[t])

        for i in range(seqs):
            owner = (core * seqs + i) * share + blk // per_part

            @pl.when(owner != flat)
            def _(i=i):
                arrived(tok_out.at[i], t_r.at[i])


def last_half(sizes, qkv, g_att, att, lse, big, tok_own, g_mid, norm_t, cols, vec, two, block):
    blocks, lanes, seqs = sizes
    depth, share = lanes // 2, blocks // seqs
    length, width = qkv.shape
    pairs = width // 384
    model = cols.shape[0]
    owned = model // (blocks * lanes)
    per_part, rows_in, _ = tok_own.shape
    rows = per_part * rows_in
    low, full = jnp.bfloat16, jnp.float32
    in_vmem = pl.BlockSpec(memory_space=pltpu.VMEM)
    own = jax.ShapeDtypeStruct((blocks, depth, 2, owned, 384), low)
    kinds = ["rows"] * 3 + ["columns"] * pairs
    out, _, scratch = fold_shapes(sizes, list(big) + [own] * pairs, kinds, [])
    return pl.pallas_call(
        functools.partial(last_kernel, sizes, block, pairs),
        grid=(pairs,),
        out_shape=out[:3]
        + [
            jax.ShapeDtypeStruct((owned, share * width), full),
            jax.ShapeDtypeStruct((seqs, rows_in, model), low),
            jax.ShapeDtypeStruct(vec.shape, full),
        ],
        in_specs=[pl.BlockSpec((length, 128), lambda p, n=n: (0, 3 * p + n)) for n in range(3)]
        + [pl.BlockSpec((length, 128), lambda p: (0, p))] * 2
        + [pl.BlockSpec((1, 8, length), lambda p: (p, 0, 0))]
        + [ANYWHERE] * 7
        + [in_vmem] * 2,
        out_specs=[in_vmem] * 4 + [ANYWHERE, in_vmem],
        scratch_shapes=[pltpu.VMEM((2, length, 128), low)] * 4
        + [
            pltpu.VMEM((128, length), low),
            pltpu.VMEM((8, length), full),
            pltpu.VMEM((128, length), full),
            pltpu.VMEM((block, 128), full),
            pltpu.VMEM((block, 128), full),
            pltpu.VMEM((pairs, length, 384), low),
            pltpu.VMEM((pairs,) + own.shape, low),
            pltpu.VMEM((model, length), low),
            pltpu.VMEM((model, width), low),
            pltpu.VMEM((per_part, rows_in, model), low),
            pltpu.VMEM((rows, model), full),
            pltpu.VMEM((per_part, rows_in, model), low),
            pltpu.VMEM((share - 1, rows, model), low),
            pltpu.VMEM((share - 1, rows, model), low),
            pltpu.VMEM((model, 384), full),
            DMA((share, per_part)),
            DMA((share, per_part)),
            DMA((per_part,)),
            DMA((seqs,)),
            DMA((4,)),
        ]
        + Total.scratch(sizes, vec.shape)
        + scratch,
        compiler_params=pltpu.CompilerParams(collective_id=2, has_side_effects=True, vmem_limit_bytes=63 * 2**20),
    )(qkv, qkv, qkv, g_att, att, lse, *big, tok_own, g_mid, norm_t, cols, vec, two)


def shards(sizes, tokens, seq_len, ln1_gain, ln1_shift, w_qkv, w_out, ln2_gain, ln2_shift, w_up, w_down, cotangent):
    blocks, lanes, seqs = sizes
    place = Place(*sizes)
    share, part = place.share, place.part
    model = tokens.shape[2]
    length = blocks * tokens.shape[1]
    rows = length // share
    owned = w_qkv.shape[0]
    cols = model // share
    wide = -(-cols // 128) * 128

    pairs = wide // 128
    grouped = jnp.pad(w_qkv.reshape(owned, 3, share, cols), ((0, 0), (0, 0), (0, 0), (0, wide - cols)))
    grouped = grouped.reshape(owned, 3, share, pairs, 128)
    grouped = jnp.transpose(grouped, (2, 0, 3, 1, 4)).reshape(share, owned, 3 * wide)
    flat = place.blk * lanes + lax.axis_index("seq")
    vec = jnp.zeros((8, model), jnp.float32)
    own = jnp.stack([ln1_gain, ln1_shift, ln2_gain, ln2_shift]).astype(jnp.float32)
    vec = lax.dynamic_update_slice(vec, own, (0, flat * owned))
    first = (place.blk == 0).astype(jnp.float32)
    vec = lax.dynamic_update_slice(vec, first * seq_len.astype(jnp.float32)[None], (4, lax.axis_index("seq") * seqs))
    outs = first_half(sizes, tokens, cotangent, vec, grouped, w_out, w_up, w_down, min(512, rows))
    att, lse, att_own, tok_own, cot_own, norm_t, qkv, qkv_cols, params, _, out_full, up_full, down_full = outs
    out_full, up_full = [a.reshape(model, -1) for a in (out_full, up_full)]
    down_full = down_full.reshape(-1, model)
    result, g_heads, grad_mid, grad_out, grad_up, grad_down, two_grads = feed_forward(
        sizes,
        cols,
        att_own,
        tok_own,
        cot_own,
        out_full,
        up_full,
        down_full,
        params,
        min(512, tokens.shape[1]),
        min(1024, w_up.shape[1]),
    )

    def cut(values):
        return values.reshape((blocks, lanes // 2, 2, -1) + values.shape[1:])

    done = last_half(
        sizes,
        qkv,
        g_heads.reshape(length, wide),
        att,
        lse,
        [cut(grad_out), cut(grad_up), cut(grad_down)],
        tok_own,
        grad_mid,
        norm_t,
        qkv_cols,
        params,
        two_grads,
        min(512, rows),
    )
    sum_out, sum_up, sum_down, sum_qkv, grad_tokens, vec_sum = done
    vec_own = lax.dynamic_slice_in_dim(vec_sum, flat * owned, owned, 1)
    if wide != cols:
        sum_qkv = sum_qkv.reshape(owned, 3, share, wide)[..., :cols].reshape(owned, 3 * model)
    return (
        result,
        grad_tokens.astype(jnp.float32),
        vec_own[0],
        vec_own[1],
        sum_qkv,
        sum_out,
        vec_own[2],
        vec_own[3],
        sum_up,
        sum_down,
    )


def solution(mesh):
    blocks, lanes = mesh.shape["blk"], mesh.shape["seq"]
    whole = P(("blk", "seq"))
    rows = P(("blk", "seq"), None)
    tokens = P("seq", "blk", None)

    def run(*args):
        seqs = args[0].shape[0] // lanes
        return jax.shard_map(
            functools.partial(shards, (blocks, lanes, seqs)),
            mesh=mesh,
            in_specs=(tokens, P("seq"), whole, whole, rows, rows, whole, whole, rows, rows, tokens),
            out_specs=(tokens, tokens, whole, whole, rows, rows, whole, whole, rows, rows),
            check_vma=False,
        )(*args)

    return run
```

```python
import functools

import jax
import jax.numpy as jnp
from jax import lax
from jax.experimental import pallas as pl
from jax.experimental.pallas import tpu as pltpu
from jax.sharding import PartitionSpec as P

HEADS = 12
VMEM_LIMIT = 60 * 2**20


MESH = pl.DeviceIdType.MESH
DMA = pltpu.SemaphoreType.DMA
ANYWHERE = pl.BlockSpec(memory_space=pl.ANY)


class Place:
    def __init__(self, blocks, lanes, seqs):
        self.blocks, self.depth, self.seqs = blocks, lanes // 2, seqs
        self.share = blocks // seqs
        self.per_part = blocks // self.share
        self.bits = max(1, blocks.bit_length() - 1)
        self.blk = lax.axis_index("blk")
        lane = lax.axis_index("seq")
        self.z, self.core = lane // 2, lane % 2
        flat = self.blk * 2 + self.core
        self.seq, self.part = flat // self.share, flat % self.share
        self.home = self.seq // seqs
        self.other = lax.rem(self.blk * 2 + 1 - self.core, self.share)

    def at(self, blk, z, core):
        return (blk, z * 2 + core)

    def sibling(self):
        return self.at(self.blk, self.z, 1 - self.core)

    def peers(self, along_z, along_blk):
        out = [self.sibling()]
        if along_z:
            out += [self.at(self.blk, lax.rem(self.z + k, self.depth), self.core) for k in range(1, self.depth)]
        if along_blk:
            for m in range(1, self.blocks):
                out += [self.at(self.blk ^ m, self.z, 0), self.at(self.blk ^ m, self.z, 1)]
        return out

    def bit(self, part, step):
        return 1 << ((part + step) % self.bits)

    def widen(self, k):
        masks, out, seen = [0], [], 0
        for t in range(self.bits):
            bit = self.bit(k, t)
            out.append((bit, list(masks), seen))
            seen += len(masks)
            masks += [m ^ bit for m in masks]
        return out

    def narrow(self, k):
        out, seen = [], 0
        for t in range(self.bits):
            masks = [0]
            for u in range(t + 1, self.bits):
                masks += [m ^ self.bit(k, u) for m in masks]
            out.append((self.bit(k, t), masks, seen))
            seen += len(masks)
        return out


def greet(devices):
    barrier = pltpu.get_barrier_semaphore()
    for device in devices:
        pl.semaphore_signal(barrier, inc=1, device_id=device, device_id_type=MESH)
    pl.semaphore_wait(barrier, len(devices))


def send(src, dst, send_sem, recv_sem, device):
    pltpu.make_async_remote_copy(
        src_ref=src, dst_ref=dst, send_sem=send_sem, recv_sem=recv_sem, device_id=device, device_id_type=MESH
    ).start()


def arrived(ref, sem):
    pltpu.make_async_copy(ref, ref, sem).wait()


class Fold:
    def __init__(self, place, kinds, grads, rows_in, sums, rows_out, scratch):
        self.place, self.kinds, self.grads = place, kinds, grads
        self.rows_in, self.sums, self.rows_out = rows_in, sums, rows_out
        self.count, self.moves = len(kinds), len(rows_in)
        n = self.count
        self.held, self.near, self.wide, self.tall = (scratch[i * n : i * n + n] for i in range(4))
        self.m_s, self.m_r, self.z_s, self.z_r, self.b_s, self.b_r, self.c_s, self.c_r, self.loc = scratch[4 * n :]
        self.order = list(range(1, place.depth)) + [0]
        self.units = [(a, k) for a in range(n) for k in self.order]

    @staticmethod
    def scratch(sizes, chunks, types, kinds, moves):
        blocks, lanes, seqs = sizes
        depth, share, count = lanes // 2, blocks // seqs, len(chunks)
        out = [pltpu.VMEM((blocks, depth) + c, t) for c, t in zip(chunks, types)]
        out += [
            pltpu.VMEM((1, 1, 8, 128) if kind == "columns" else (blocks, depth) + c, t)
            for c, t, kind in zip(chunks, types, kinds)
        ]
        out += [pltpu.VMEM((depth, blocks - 1) + c, t) for c, t in zip(chunks, types)]
        out += [pltpu.VMEM((depth - 1,) + c, t) for c, t in zip(chunks, types)]
        return out + [
            DMA((max(1, moves), blocks // share)),
            DMA((max(1, moves), seqs)),
            DMA((count, depth - 1)),
            DMA((count, depth - 1)),
            DMA((count, depth, blocks - 1)),
            DMA((count, depth, blocks - 1)),
            DMA((count, depth)),
            DMA((count, depth)),
            DMA((count + 1, max(depth, moves))),
        ]

    def level(self, k):
        return lax.rem(self.place.z + k, self.place.depth)

    def greet(self):
        greet(self.place.peers(True, True))

    def clear(self):
        place = self.place
        for a in range(self.count):
            if self.kinds[a] == "columns" and place.share > 2:
                held = self.held[a]
                for g in range(place.share):

                    @pl.when((g != place.part) & (g != place.other))
                    def _(held=held, g=g):
                        held[:, :, g] = jnp.zeros(held.shape[:2] + held.shape[3:], held.dtype)

    def start(self, a, k):
        place = self.place
        if self.kinds[a] == "columns":
            mine = there = self.held[a].at[:, self.level(k), place.part]
        else:
            mine = self.held[a].at[:, self.level(k)]
            there = self.near[a].at[:, self.level(k)]
        theirs = self.grads[a].at[:, self.level(k), 1 - place.core]
        send(theirs, there, self.c_s.at[a, k], self.c_r.at[a, k], place.sibling())
        pltpu.make_async_copy(self.grads[a].at[:, self.level(k), place.core], mine, self.loc.at[a, k]).start()

    def add(self, into, second):
        total = into[...].astype(jnp.float32) + second[...].astype(jnp.float32)
        into[...] = total.astype(into.dtype)

    def forward(self, a, k, t):
        place = self.place
        bit, masks, seen = place.narrow(k)[t]
        for n, m in enumerate(masks):
            sems = self.b_s.at[a, k, seen + n], self.b_r.at[a, k, seen + n]
            block = self.held[a].at[place.blk ^ bit ^ m, self.level(k)]
            send(block, self.wide[a].at[k, seen + n], *sems, place.at(place.blk ^ bit, place.z, place.core))

    def join(self, a, k):
        place = self.place
        if self.kinds[a] == "columns":
            arrived(self.held[a].at[:, self.level(k), place.part], self.loc.at[a, k])
            arrived(self.held[a].at[:, self.level(k), place.other], self.c_r.at[a, k])
        else:
            arrived(self.held[a].at[:, self.level(k)], self.loc.at[a, k])
            arrived(self.near[a].at[:, self.level(k)], self.c_r.at[a, k])

            def one(b, _):
                self.add(self.held[a].at[b, self.level(k)], self.near[a].at[b, self.level(k)])
                return 0

            lax.fori_loop(0, place.blocks, one, 0)
        self.forward(a, k, 0)

    def step(self, a, k, t):
        place = self.place
        bit, masks, seen = place.narrow(k)[t]
        for n, m in enumerate(masks):
            arrived(self.wide[a].at[k, seen + n], self.b_r.at[a, k, seen + n])
            self.add(self.held[a].at[place.blk ^ m, self.level(k)], self.wide[a].at[k, seen + n])
        if t + 1 < place.bits:
            self.forward(a, k, t + 1)
        elif k > 0:
            sems = self.z_s.at[a, k - 1], self.z_r.at[a, k - 1]
            block = self.held[a].at[place.blk, self.level(k)]
            send(block, self.tall[a].at[k - 1], *sems, place.at(place.blk, self.level(k), place.core))

    def total(self, a):
        self.sums[a][...] = self.value(a)

    def value(self, a):
        place = self.place
        value = self.held[a][place.blk, place.z].astype(jnp.float32)
        for k in range(1, place.depth):
            arrived(self.tall[a].at[k - 1], self.z_r.at[a, k - 1])
            value = value + self.tall[a][k - 1].astype(jnp.float32)
        return value

    def rows(self, j):
        place = self.place
        slot = lax.rem(place.seq, place.seqs)
        for t in range(place.per_part):
            source = place.part * place.per_part + t
            mine = (source == place.blk) & (place.home == place.core)

            @pl.when(mine)
            def _(t=t):
                pltpu.make_async_copy(self.rows_in[j].at[t], self.rows_out[j].at[slot], self.loc.at[self.count, j]).start()

            @pl.when(jnp.logical_not(mine))
            def _(t=t, source=source):
                sems = self.m_s.at[j, t], self.m_r.at[j, slot]
                send(self.rows_in[j].at[t], self.rows_out[j].at[slot], *sems, place.at(source, place.z, place.home))

    def finish(self):
        place = self.place
        for a, k in self.units:
            if self.kinds[a] == "columns":
                arrived(self.held[a].at[:, 0, 0], self.c_s.at[a, k])
            else:
                arrived(self.held[a].at[:, 0], self.c_s.at[a, k])
            for n in range(place.blocks - 1):
                arrived(self.held[a].at[0, 0], self.b_s.at[a, k, n])
            if k > 0:
                arrived(self.held[a].at[0, 0], self.z_s.at[a, k - 1])
        for j in range(self.moves):
            for t in range(place.per_part):
                mine = (place.part * place.per_part + t == place.blk) & (place.home == place.core)

                @pl.when(mine)
                def _(j=j, t=t):
                    arrived(self.rows_in[j].at[t], self.loc.at[self.count, j])

                @pl.when(jnp.logical_not(mine))
                def _(j=j, t=t):
                    arrived(self.rows_in[j].at[t], self.m_s.at[j, t])

            for i in range(place.seqs):
                owner = (place.core * place.seqs + i) * place.share + place.blk // place.per_part

                @pl.when(owner != place.blk * 2 + place.core)
                def _(j=j, i=i):
                    arrived(self.rows_out[j].at[i], self.m_r.at[j, i])


def fold_shapes(sizes, grads, kinds, rows):
    blocks, _, seqs = sizes
    share = blocks // seqs
    chunks = [((share,) if kind == "columns" else ()) + g.shape[3:] for g, kind in zip(grads, kinds)]
    scratch = Fold.scratch(sizes, chunks, [g.dtype for g in grads], kinds, len(rows))
    out = [jax.ShapeDtypeStruct(c, jnp.float32) for c in chunks]
    moved = [jax.ShapeDtypeStruct((seqs,) + r.shape[1:], r.dtype) for r in rows]
    return out, moved, scratch


def dot_nt(left, right):
    return lax.dot_general(left, right, (((1,), (1,)), ((), ())), preferred_element_type=jnp.float32)


def dot_nn(left, right):
    return lax.dot_general(left, right, (((1,), (0,)), ((), ())), preferred_element_type=jnp.float32)


def split_heads(dst, src):
    low = lax.broadcasted_iota(jnp.int32, src.shape, 1) < 64
    dst[0] = jnp.where(low, src, jnp.zeros_like(src))
    dst[1] = jnp.where(low, jnp.zeros_like(src), src)


def causal(bk, bq, kj, qi):
    kpos = kj * bk + lax.broadcasted_iota(jnp.int32, (bk, bq), 0)
    qpos = qi * bq + lax.broadcasted_iota(jnp.int32, (bk, bq), 1)
    return kpos <= qpos


def plan(tasks, points):
    out = {}
    for where, call in tasks:
        out.setdefault(min(points - 1, int(where * points)), []).append(call)
    return out


def pump(todo, point):
    for at, calls in todo.items():

        @pl.when(point == at)
        def _(calls=calls):
            for call in calls:
                call()


class Total:
    def __init__(self, place, stages, from_z, from_blk, from_core, sems):
        self.place, self.stages = place, stages
        self.from_z, self.from_blk, self.from_core = from_z, from_blk, from_core
        self.z_s, self.z_r, self.b_s, self.b_r, self.c_s, self.c_r = sems

    @staticmethod
    def scratch(sizes, shape):
        blocks, lanes, _ = sizes
        depth, bits = lanes // 2, max(1, blocks.bit_length() - 1)
        return [
            pltpu.VMEM((2 + bits,) + shape, jnp.float32),
            pltpu.VMEM((depth - 1,) + shape, jnp.float32),
            pltpu.VMEM((bits,) + shape, jnp.float32),
            pltpu.VMEM(shape, jnp.float32),
            DMA((depth - 1,)),
            DMA((depth - 1,)),
            DMA((bits,)),
            DMA((bits,)),
            DMA((1,)),
            DMA((1,)),
        ]

    def start(self):
        place = self.place
        for k in range(1, place.depth):
            target = place.at(place.blk, lax.rem(place.z + k, place.depth), place.core)
            send(self.stages.at[0], self.from_z.at[k - 1], self.z_s.at[k - 1], self.z_r.at[k - 1], target)

    def step(self, n):
        place = self.place
        if n == 0:
            value = self.stages[0]
            for k in range(1, place.depth):
                arrived(self.from_z.at[k - 1], self.z_r.at[k - 1])
                value = value + self.from_z[k - 1]
        else:
            arrived(self.from_blk.at[n - 1], self.b_r.at[n - 1])
            value = self.stages[n] + self.from_blk[n - 1]
        self.stages[n + 1] = value
        if n < place.bits:
            target = place.at(place.blk ^ (1 << n), place.z, place.core)
            send(self.stages.at[n + 1], self.from_blk.at[n], self.b_s.at[n], self.b_r.at[n], target)
        else:
            send(self.stages.at[n + 1], self.from_core, self.c_s.at[0], self.c_r.at[0], place.sibling())

    def finish(self):
        place = self.place
        arrived(self.from_core, self.c_r.at[0])
        value = self.stages[place.bits + 1] + self.from_core[...]
        arrived(self.from_core, self.c_s.at[0])
        for n in range(place.bits):
            arrived(self.from_core, self.b_s.at[n])
        for k in range(1, place.depth):
            arrived(self.from_core, self.z_s.at[k - 1])
        return value


class Gather:
    def __init__(self, place, shard, full, sems, only=None, span=None):
        self.place, self.full, self.only = place, full, only
        self.tail = () if span is None else (pl.ds(*span),)
        self.shard = shard if span is None else shard.at[self.tail[0]]
        self.z_s, self.z_r, self.b_s, self.b_r, self.c_s, self.c_r, self.loc = sems

    @staticmethod
    def sems(sizes):
        blocks, lanes, _ = sizes
        depth = lanes // 2
        return [
            DMA((depth,)),
            DMA((depth,)),
            DMA((depth, blocks - 1)),
            DMA((depth, blocks - 1)),
            DMA((depth,)),
            DMA((depth,)),
            DMA((1 + depth,)),
        ]

    def level(self, k):
        return lax.rem(self.place.z + self.place.depth - k, self.place.depth)

    def lane(self, depth_at, core):
        return self.full.at[(slice(None), depth_at, core) + self.tail]

    def chunk(self, blk, k):
        return self.full.at[(blk, self.level(k), self.place.core) + self.tail]

    def start(self):
        place = self.place
        for k in range(1, place.depth):
            target = place.at(place.blk, lax.rem(place.z + k, place.depth), place.core)
            send(self.shard, self.chunk(place.blk, 0), self.z_s.at[k], self.z_r.at[k], target)

    def keep(self):
        pltpu.make_async_copy(self.shard, self.chunk(self.place.blk, 0), self.loc.at[0]).start()

    def forward(self, k, t):
        place = self.place
        bit, masks, seen = place.widen(k)[t]
        for n, m in enumerate(masks):
            there = self.chunk(place.blk ^ m, k)
            src = self.shard if m == 0 and k == 0 else there
            send(src, there, self.b_s.at[k, seen + n], self.b_r.at[k, seen + n], place.at(place.blk ^ bit, place.z, place.core))

    def climb(self, k):
        if k > 0:
            arrived(self.chunk(self.place.blk, k), self.z_r.at[k])
        self.forward(k, 0)

    def step(self, k, t):
        place = self.place
        bit, masks, seen = place.widen(k)[t]
        for n, m in enumerate(masks):
            arrived(self.chunk(place.blk ^ bit ^ m, k), self.b_r.at[k, seen + n])
        if t + 1 < place.bits:
            self.forward(k, t + 1)
        else:
            self.swap(k)

    def swap(self, k):
        place = self.place
        if k == 0:
            arrived(self.shard, self.loc.at[0])
        if self.only is None:
            held = self.lane(self.level(k), place.core)
            send(held, held, self.c_s.at[k], self.c_r.at[k], place.sibling())
        else:
            there = self.only.at[:, self.level(k), place.core]
            send(self.full.at[:, self.level(k), place.core, place.other], there, self.c_s.at[k], self.c_r.at[k], place.sibling())
            mine = self.full.at[:, self.level(k), place.core, place.part]
            pltpu.make_async_copy(mine, there, self.loc.at[1 + k]).start()

    def wait_swap(self, k):
        place = self.place
        if self.only is None:
            arrived(self.lane(self.level(k), 1 - place.core), self.c_r.at[k])
        else:
            arrived(self.only.at[:, self.level(k), 1 - place.core], self.c_r.at[k])
            arrived(self.only.at[:, self.level(k), place.core], self.loc.at[1 + k])

    def finish(self):
        place = self.place
        for k in range(place.depth):
            if self.only is None:
                self.wait_swap(k)
                arrived(self.lane(0, 0), self.c_s.at[k])
            else:
                arrived(self.only.at[:, 0, 0], self.c_s.at[k])
            if k > 0:
                arrived(self.shard, self.z_s.at[k])
            for n in range(place.blocks - 1):
                arrived(self.shard, self.b_s.at[k, n])


class GatherAcross(Gather):
    def start(self):
        place = self.place
        for m in range(1, place.blocks):
            target = place.at(place.blk ^ m, place.z, place.core)
            send(self.shard, self.chunk(place.blk, 0), self.b_s.at[0, m - 1], self.b_r.at[0, m - 1], target)

    def climb(self):
        place = self.place
        for m in range(1, place.blocks):
            arrived(self.chunk(place.blk ^ m, 0), self.b_r.at[0, m - 1])
        arrived(self.shard, self.loc.at[0])
        held = self.lane(place.z, place.core)
        for k in range(1, place.depth):
            target = place.at(place.blk, lax.rem(place.z + k, place.depth), place.core)
            send(held, held, self.z_s.at[k], self.z_r.at[k], target)
        self.pass_on(0)

    def pass_on(self, k):
        held = self.lane(self.level(k), self.place.core)
        if k > 0:
            arrived(held, self.z_r.at[k])
        send(held, held, self.c_s.at[k], self.c_r.at[k], self.place.sibling())

    def finish(self):
        place = self.place
        for k in range(place.depth):
            self.wait_swap(k)
            arrived(self.lane(0, 0), self.c_s.at[k])
            if k > 0:
                arrived(self.lane(0, 0), self.z_s.at[k])
        for m in range(1, place.blocks):
            arrived(self.shard, self.b_s.at[0, m - 1])


def first_kernel(sizes, block, pairs, *refs):
    place = Place(*sizes)
    tok, cot, vec, w_qkv, w_out, w_up, w_down = refs[:7]
    refs = refs[7:]
    att_ref, lse_ref, att_own, tok_own, cot_own, normed_out, qkv_out, cols_out, vec_out, stage, out_full, up_full, down_full = refs[:13]
    refs = refs[13:]
    tok_v, norm_v, norm_t, chunk_v, w32_v, cols_v, qkv_v, kh, vt, run_m, run_l, run_a, att_v = refs[:13]
    tok_s, tok_r, near_s, near_r, cot_s, cot_r, a_s, a_r, loc = refs[13:22]
    total = Total(place, *refs[22:26], refs[26:32])
    refs = refs[32:]
    late_rows = w_down.shape[0] // 3
    late_rows = late_rows if late_rows % 16 == 0 else 0
    early_rows = w_down.shape[0] - late_rows
    qkv = Gather(place, w_qkv, stage, refs[0:7], chunk_v)
    outw = Gather(place, w_out, out_full, refs[7:14])
    upw = Gather(place, w_up, up_full, refs[14:21])
    downw = GatherAcross(place, w_down, down_full, refs[21:28], span=(0, early_rows))
    climbers = [outw, upw]
    if late_rows:
        climbers.append(Gather(place, w_down, down_full, refs[28:35], span=(early_rows, late_rows)))
    arrays = [qkv, downw] + climbers
    blocks, depth, seqs, share, bits = place.blocks, place.depth, place.seqs, place.share, place.bits
    blk, z, core, home = place.blk, place.z, place.core, place.home
    pair = pl.program_id(0)
    rows, model = tok_v.shape[1:]
    length = blocks * rows
    count = length // block
    owned = w_qkv.shape[1]
    per_seq = share // 2
    local = lambda src, dst, sem: pltpu.make_async_copy(src, dst, sem).start()

    @pl.when(pair == 0)
    def _():
        total.stages[0] = vec[...]
        greet(place.peers(True, True))
        total.start()
        qkv.start()
        for i in range(seqs):
            for h in range(per_seq):
                target = (core * seqs + i) * per_seq + h

                @pl.when(target != blk)
                def _(i=i, h=h, target=target):
                    sems = tok_s.at[i * per_seq + h], tok_r.at[blk]
                    send(tok.at[i], tok_v.at[blk], *sems, place.at(target, z, core))

                @pl.when(target == blk)
                def _(i=i):
                    local(tok.at[i], tok_v.at[blk], loc.at[0])

        qkv.forward(0, 0)
        for array in arrays:
            array.keep()
        for k in range(1, depth):
            qkv.climb(k)
        for array in climbers:
            array.start()
        total.step(0)
        total.step(1)

        @pl.when(core == home)
        def _():
            for p in range(blocks):

                @pl.when(p != blk)
                def _():
                    arrived(tok_v.at[p], tok_r.at[p])

                @pl.when(p == blk)
                def _():
                    arrived(tok_v.at[p], loc.at[0])

                send(tok_v.at[p], tok_v.at[p], near_s.at[p], near_r.at[p], place.sibling())

        for n in range(2, bits + 1):
            total.step(n)
        for t in range(bits):
            for k in range(depth):
                qkv.step(k, t)
            if t == 0:
                downw.start()
        vec_out[...] = total.finish()
        gain, shift = vec_out[0:1, :], vec_out[1:2, :]
        part_rows = min(rows, 128)

        for p in range(blocks):

            @pl.when(core != home)
            def _(p=p):
                arrived(tok_v.at[p], near_r.at[p])

            def norm(i, _, p=p):
                inside = pl.ds(pl.multiple_of(i * part_rows, part_rows), part_rows)
                unit, _ = centered(tok_v[p, inside, :].astype(jnp.float32))
                at = pl.ds(pl.multiple_of(p * rows + i * part_rows, part_rows), part_rows)
                normed = unit * gain + shift
                norm_v[at, :] = normed.astype(jnp.bfloat16)
                norm_t[:, at] = normed.T.astype(jnp.bfloat16)
                return 0

            lax.fori_loop(0, rows // part_rows, norm, 0)
        local(norm_t, normed_out, loc.at[1])
        for t in range(place.per_part):
            local(tok_v.at[place.part * place.per_part + t], tok_own.at[t], loc.at[2 + t])
        downw.climb()
        for array in climbers:
            for k in range(depth):
                array.climb(k)
        for k in range(depth):
            qkv.wait_swap(k)
        for b in range(blocks):
            for d in range(depth):
                for c in range(2):
                    index = (b * depth + d) * 2 + c
                    w32_v[index * owned : (index + 1) * owned, :] = chunk_v[b, d, c].astype(jnp.float32)
        cols_v[...] = w32_v[...].astype(jnp.bfloat16)
        local(cols_v, cols_out, loc.at[2 + place.per_part])

        def project(i, _):
            at = pl.ds(pl.multiple_of(i * block, block), block)
            normed = norm_v[at, :]
            scale = jnp.where(lax.broadcasted_iota(jnp.int32, (1, 384), 1) < 128, 0.125, 1.0)
            for n in range(pairs):
                value = dot_nn(normed, cols_v[:, n * 384 : (n + 1) * 384]) * scale
                qkv_v[at, n * 384 : (n + 1) * 384] = value.astype(jnp.bfloat16)
            return 0

        lax.fori_loop(0, count, project, 0)
        local(qkv_v, qkv_out, loc.at[3 + place.per_part])

    per_pair = count * (count + 1) // 2
    tasks = []
    levels = [(array, k) for array in climbers for k in range(depth)]
    for n, (array, k) in enumerate(levels):
        for t in range(bits):
            where = 0.08 + 0.26 * t + (0.1 + 0.25 * t) * n / len(levels)
            tasks.append((where, functools.partial(array.step, k, t)))
    for k in range(1, depth):
        tasks.append((0.55 + 0.3 * k / depth, functools.partial(downw.pass_on, k)))

    def own_rows():
        for i in range(seqs):
            owner = (core * seqs + i) * share + blk // place.per_part
            slot = lax.rem(blk, place.per_part)

            @pl.when(owner != blk * 2 + core)
            def _(i=i, owner=owner, slot=slot):
                send(cot.at[i], cot_own.at[slot], cot_s.at[i], cot_r.at[slot], place.at(owner // 2, z, owner % 2))

            @pl.when(owner == blk * 2 + core)
            def _(i=i, slot=slot):
                local(cot.at[i], cot_own.at[slot], loc.at[4 + place.per_part])

    tasks.append((0.2, own_rows))
    tasks.sort(key=lambda task: task[0])
    todo = plan(tasks, pairs * per_pair)

    def lanes_of(n):
        return pl.ds(pl.multiple_of(pair * 384 + n * 128, 128), 128)

    split_heads(kh, qkv_v[:, lanes_of(1)])
    vt[...] = qkv_v[:, lanes_of(2)].astype(jnp.float32).T.astype(jnp.bfloat16)

    def q_step(qi, _):
        at_q = pl.ds(pl.multiple_of(qi * block, block), block)
        run_m[...] = jnp.full_like(run_m, -1e30)
        run_l[...] = jnp.zeros_like(run_l)
        run_a[...] = jnp.zeros_like(run_a)

        def one(kj, masked):
            at = pl.ds(pl.multiple_of(kj * block, block), block)
            q_rows = qkv_v[at_q, lanes_of(0)]
            scores = [dot_nt(kh[h, at, :], q_rows) for h in range(2)]
            weighed = []
            for h in range(2):
                peak, so_far = run_m[h : h + 1, :], run_l[h : h + 1, :]
                s = scores[h]
                u = s * s + 1.0
                inv = lax.rsqrt(u)
                mag = u * inv
                if masked:
                    mag = jnp.where(causal(block, block, kj, qi), mag, -1e30)
                new = jnp.maximum(peak, jnp.max(mag, axis=0, keepdims=True))
                p = jnp.exp(mag - new)
                alpha = jnp.exp(peak - new)
                run_m[h : h + 1, :] = new
                run_l[h : h + 1, :] = so_far * alpha + jnp.sum(p, axis=0, keepdims=True)
                weighed.append((alpha, (p * (s * inv)).astype(jnp.bfloat16)))
            for h in range(2):
                alpha, signed = weighed[h]
                head = slice(64 * h, 64 * h + 64)
                run_a[head, :] = run_a[head, :] * alpha + dot_nn(vt[head, at], signed)

        def k_step(kj, _):
            @pl.when(kj == qi)
            def _():
                one(kj, True)

            @pl.when(kj != qi)
            def _():
                one(kj, False)

            pump(todo, pair * per_pair + qi * (qi + 1) // 2 + kj)
            return 0

        lax.fori_loop(0, qi + 1, k_step, 0)
        both = []
        for h in range(2):
            both.append(run_a[64 * h : 64 * h + 64, :] / run_l[h : h + 1, :])
            lse_ref[0, h : h + 1, at_q] = run_m[h : h + 1, :] + jnp.log(run_l[h : h + 1, :])
        joined = jnp.concatenate(both, 0).T.astype(jnp.bfloat16)
        att_ref[at_q, :] = joined
        att_v[pair, at_q, :] = joined
        return 0

    lax.fori_loop(0, count, q_step, 0)
    part, mine = place.part, length // share
    flat = blk * 2 + core

    def piece(p, g):
        return att_v.at[p, pl.ds(pl.multiple_of(g * mine, 16), mine)]

    for p in range(pairs):
        there = att_own.at[part, :, pl.ds(p * 128, 128)]

        @pl.when(pair == p)
        def _(p=p, there=there):
            for k in range(1, share):
                other = flat ^ k
                send(piece(p, part ^ k), there, a_s.at[k, p], a_r.at[k, p], place.at(other // 2, z, other % 2))
            local(piece(p, part), there, a_s.at[0, p])

    @pl.when(pair == pairs - 1)
    def _():
        for p in range(pairs):
            for k in range(share):
                arrived(piece(p, 0), a_s.at[k, p])
                if k > 0:
                    arrived(att_own.at[part ^ k, :, pl.ds(p * 128, 128)], a_r.at[k, p])
        for array in arrays:
            array.finish()
        for i in range(seqs):

            @pl.when((core * seqs + i) * share + blk // place.per_part != blk * 2 + core)
            def _(i=i):
                arrived(cot.at[i], cot_s.at[i])

        for t in range(place.per_part):
            here = (place.part * place.per_part + t == blk) & (home == core)

            @pl.when(here)
            def _(t=t):
                arrived(cot_own.at[t], loc.at[4 + place.per_part])

            @pl.when(jnp.logical_not(here))
            def _(t=t):
                arrived(cot_own.at[t], cot_r.at[t])

        arrived(norm_t, loc.at[1])
        arrived(cols_v, loc.at[2 + place.per_part])
        arrived(qkv_v, loc.at[3 + place.per_part])
        for t in range(place.per_part):
            arrived(tok_own.at[t], loc.at[2 + t])

        @pl.when(core == home)
        def _():
            for p in range(blocks):
                arrived(tok_v.at[p], near_s.at[p])

        for i in range(seqs):
            for h in range(per_seq):
                target = (core * seqs + i) * per_seq + h

                @pl.when(target != blk)
                def _(i=i, h=h):
                    arrived(tok.at[i], tok_s.at[i * per_seq + h])

                @pl.when((target == blk) & (core != home))
                def _():
                    arrived(tok_v.at[blk], loc.at[0])


def first_half(sizes, tok, cot, vec, w_qkv, w_out, w_up, w_down, block):
    blocks, lanes, seqs = sizes
    depth, share = lanes // 2, blocks // seqs
    per_part = blocks // share
    rows, model = tok.shape[1:]
    length = blocks * rows
    width = w_qkv.shape[2]
    pairs = width // 384
    low, full = jnp.bfloat16, jnp.float32
    shape = jax.ShapeDtypeStruct
    owners = (blocks, depth, 2)
    in_vmem = pl.BlockSpec(memory_space=pltpu.VMEM)
    return pl.pallas_call(
        functools.partial(first_kernel, sizes, block, pairs),
        grid=(pairs,),
        out_shape=[
            shape((length, 128 * pairs), low),
            shape((pairs, 8, length), full),
            shape((share, length // share, 128 * pairs), low),
            shape((per_part, rows, model), low),
            shape((per_part, rows, model), low),
            shape((model, length), low),
            shape((length, width), low),
            shape((model, width), low),
            shape(vec.shape, full),
            shape(owners + w_qkv.shape, low),
            shape(owners + w_out.shape, low),
            shape(owners + w_up.shape, low),
            shape(owners + w_down.shape, low),
        ],
        in_specs=[ANYWHERE, ANYWHERE, in_vmem] + [ANYWHERE] * 4,
        out_specs=[pl.BlockSpec((length, 128), lambda p: (0, p)), pl.BlockSpec((1, 8, length), lambda p: (p, 0, 0))]
        + [ANYWHERE] * 6
        + [in_vmem]
        + [ANYWHERE] * 4,
        scratch_shapes=[
            pltpu.VMEM((blocks, rows, model), low),
            pltpu.VMEM((length, model), low),
            pltpu.VMEM((model, length), low),
            pltpu.VMEM(owners + w_qkv.shape[1:], low),
            pltpu.VMEM((model, width), full),
            pltpu.VMEM((model, width), low),
            pltpu.VMEM((length, width), low),
            pltpu.VMEM((2, length, 128), low),
            pltpu.VMEM((128, length), low),
            pltpu.VMEM((8, block), full),
            pltpu.VMEM((8, block), full),
            pltpu.VMEM((128, block), full),
            pltpu.VMEM((pairs, length, 128), low),
            DMA((seqs * share // 2,)),
            DMA((blocks,)),
            DMA((blocks,)),
            DMA((blocks,)),
            DMA((seqs,)),
            DMA((per_part,)),
            DMA((share, pairs)),
            DMA((share, pairs)),
            DMA((5 + per_part,)),
        ]
        + Total.scratch(sizes, vec.shape)
        + Gather.sems(sizes) * 5,
        compiler_params=pltpu.CompilerParams(collective_id=0, has_side_effects=True, vmem_limit_bytes=VMEM_LIMIT),
    )(tok, cot, vec, w_qkv, w_out, w_up, w_down)


def dot_tn(left, right):
    return lax.dot_general(left, right, (((0,), (0,)), ((), ())), preferred_element_type=jnp.float32)


def centered(values):
    center = jnp.mean(values, axis=-1, keepdims=True)
    offsets = values - center
    spread = jnp.mean(offsets * offsets, axis=-1, keepdims=True)
    inverse = lax.rsqrt(spread + 1e-05)
    return offsets * inverse, inverse


def norm_back(values, grads, gain):
    unit, inverse = centered(values)
    scaled = grads * gain
    first = jnp.mean(scaled, axis=-1, keepdims=True)
    second = jnp.mean(scaled * unit, axis=-1, keepdims=True)
    back = inverse * (scaled - first - unit * second)
    return back, jnp.sum(grads * unit, axis=0, keepdims=True), jnp.sum(grads, axis=0, keepdims=True)


def gelu_parts(x):
    square = x * x
    half = 0.5 + 0.5 * jnp.tanh(0.7978845608028654 * x * (1.0 + 0.044715 * square))
    slope = half + x * (2.0 * half * (1.0 - half)) * (0.7978845608028654 + 0.1070322243 * square)
    return x * half, slope


def mlp_kernel(sizes, cols, tile, chunk, *refs):
    place = Place(*sizes)
    att, tok_own, cot, w_out, w_up, w_down, vec = refs[:7]
    refs = refs[7:]
    result, g_heads, g_mid, g_out, g_up, g_down, g_vec = refs[:7]
    (att_v, tok_v, cot_v, res_v, out_v, up_v, down_v, mid_v, n2_v, n2t_v, hid_v, slope_v, sum_v, ga_v) = refs[7:21]
    (st_out, st_up, st_down) = refs[21:24]
    g_s, g_r, m_s, m_r, loc, up_l, down_l, o_l = refs[24:]
    share, per_part, seqs = place.share, place.per_part, place.seqs
    part, blk, z, core = place.part, place.blk, place.z, place.core
    rows, model = mid_v.shape
    block = rows // per_part
    ff = up_v.shape[1]
    chunks, tiles = ff // chunk, rows // tile
    flat = blk * 2 + core
    partners = [((flat ^ k) // 2, z, (flat ^ k) % 2) for k in range(1, share)]
    slot_of = lax.rem(place.seq, seqs)
    greet(place.peers(False, True))
    def local(src, dst, sem):
        pltpu.make_async_copy(src, dst, sem).start()

    local(att, att_v, loc.at[0])
    for t in range(per_part):
        local(tok_own.at[t], tok_v.at[t], loc.at[1 + t])
    local(w_out, out_v, loc.at[1 + per_part])
    local(cot, cot_v, loc.at[2 + per_part])

    def span(f):
        return pl.ds(pl.multiple_of(f * chunk, chunk), chunk)

    for f in range(chunks):
        local(w_up.at[:, pl.ds(f * chunk, chunk)], up_v.at[:, pl.ds(f * chunk, chunk)], up_l.at[f])
        local(w_down.at[pl.ds(f * chunk, chunk)], down_v.at[pl.ds(f * chunk, chunk)], down_l.at[f])

    arrived(att_v, loc.at[0])
    for t in range(per_part):
        arrived(tok_v.at[t], loc.at[1 + t])
    arrived(out_v, loc.at[1 + per_part])
    gain, shift = vec[2:3, :], vec[3:4, :]
    per_block = block // tile

    def spot(i):
        return i // per_block, pl.ds(pl.multiple_of(lax.rem(i, per_block) * tile, tile), tile)

    lane = lax.broadcasted_iota(jnp.int32, (1, model), 1)
    mine_at = z * 2 * seqs + place.seq
    length = jnp.sum(jnp.where(lane == mine_at, vec[4:5, :], 0.0), axis=1, keepdims=True)

    def live(i):
        position = part * rows + i * tile + lax.broadcasted_iota(jnp.int32, (tile, 1), 0)
        return jnp.where(position.astype(jnp.float32) < length, 1.0, 0.0)

    def enter(i, _):
        at = pl.ds(pl.multiple_of(i * tile, tile), tile)
        branch = dot_nn(att_v[0, at, :cols], out_v[:cols, :])
        for g in range(1, share):
            branch = branch + dot_nn(att_v[g, at, :cols], out_v[g * cols : (g + 1) * cols, :])
        t, inside = spot(i)
        middle = tok_v[t, inside, :].astype(jnp.float32) + live(i) * branch
        mid_v[at, :] = middle
        unit, _ = centered(middle)
        normed = unit * gain + shift
        n2_v[at, :] = normed.astype(jnp.bfloat16)
        n2t_v[:, at] = normed.T.astype(jnp.bfloat16)
        return 0

    lax.fori_loop(0, tiles, enter, 0)
    sum_v[...] = mid_v[...]

    def up_step(f, _):
        arrived(up_v.at[:, span(f)], up_l.at[f])
        arrived(down_v.at[span(f)], down_l.at[f])
        hidden, slope = gelu_parts(dot_nn(n2_v[...], up_v[:, span(f)]))
        hidden = hidden.astype(jnp.bfloat16)
        hid_v[:, span(f)] = hidden
        slope_v[:, span(f)] = slope.astype(jnp.bfloat16)
        sum_v[...] += dot_nn(hidden, down_v[span(f), :])
        return 0

    lax.fori_loop(0, chunks, up_step, 0)
    for t in range(per_part):
        res_v[t] = sum_v[t * block : (t + 1) * block, :].astype(jnp.bfloat16)
        source = part * per_part + t
        mine = (source == blk) & (place.home == core)

        @pl.when(mine)
        def _(t=t):
            local(res_v.at[t], result.at[slot_of], loc.at[0])

        @pl.when(jnp.logical_not(mine))
        def _(t=t, source=source):
            send(res_v.at[t], result.at[slot_of], m_s.at[t], m_r.at[slot_of], place.at(source, z, place.home))

    arrived(cot_v, loc.at[2 + per_part])
    sum_v[...] = jnp.zeros_like(sum_v)

    def back_step(f, _):
        top = cot_v[...].reshape(rows, model)
        grad_pre = (dot_nt(top, down_v[span(f), :]) * slope_v[:, span(f)].astype(jnp.float32)).astype(jnp.bfloat16)
        now = lax.rem(f, 2)

        @pl.when(f >= 2)
        def _():
            arrived(st_down.at[now], o_l.at[now])
            arrived(st_up.at[now], o_l.at[2 + now])

        st_down[now] = dot_tn(hid_v[:, span(f)], top).astype(jnp.bfloat16)
        st_up[now] = dot_nn(n2t_v[...], grad_pre).astype(jnp.bfloat16)
        local(st_down.at[now], g_down.at[span(f)], o_l.at[now])
        local(st_up.at[now], g_up.at[:, span(f)], o_l.at[2 + now])
        sum_v[...] += dot_nt(grad_pre, up_v[:, span(f)])
        return 0

    lax.fori_loop(0, chunks, back_step, 0)
    g_vec[...] = jnp.zeros_like(g_vec)

    def leave(i, _):
        at = pl.ds(pl.multiple_of(i * tile, tile), tile)
        t, inside = spot(i)
        back, d_gain, d_shift = norm_back(mid_v[at, :], sum_v[at, :], gain)
        g_vec[0:1, :] += d_gain
        g_vec[1:2, :] += d_shift
        total = cot_v[t, inside, :].astype(jnp.float32) + back
        mid_v[at, :] = total
        branch = (live(i) * total).astype(jnp.bfloat16)
        n2_v[at, :] = branch
        heads = dot_nt(branch, out_v[...]).astype(jnp.bfloat16)
        for g in range(share):
            if cols == ga_v.shape[2]:
                ga_v[g, at, :] = heads[:, g * cols : (g + 1) * cols]
            else:
                piece = heads[:, g * cols : (g + 1) * cols]
                ga_v[g, at, :] = jnp.concatenate([piece, jnp.zeros((tile, ga_v.shape[2] - cols), jnp.bfloat16)], 1)
        return 0

    lax.fori_loop(0, tiles, leave, 0)
    for k in range(1, share):
        send(ga_v.at[part ^ k], g_heads.at[part], g_s.at[k - 1], g_r.at[k - 1], place.at(*partners[k - 1]))
    local(ga_v.at[part], g_heads.at[part], loc.at[1])
    local(mid_v, g_mid, loc.at[2])
    for g in range(share):
        st_out[g * cols : (g + 1) * cols, :] = dot_tn(att_v[g, :, :cols], n2_v[...]).astype(jnp.bfloat16)
    local(st_out, g_out, loc.at[1 + per_part])
    for n in range(min(2, chunks)):
        arrived(st_down.at[n], o_l.at[n])
        arrived(st_up.at[n], o_l.at[2 + n])
    arrived(st_out, loc.at[1 + per_part])
    arrived(mid_v, loc.at[2])
    arrived(ga_v.at[part], loc.at[1])
    for k in range(1, share):
        arrived(ga_v.at[part ^ k], g_s.at[k - 1])
        arrived(g_heads.at[part ^ k], g_r.at[k - 1])
    for i in range(seqs):
        owner = (core * seqs + i) * share + blk // per_part

        @pl.when(owner != flat)
        def _(i=i):
            arrived(result.at[i], m_r.at[i])

    for t in range(per_part):
        mine = (part * per_part + t == blk) & (place.home == core)

        @pl.when(mine)
        def _(t=t):
            arrived(res_v.at[t], loc.at[0])

        @pl.when(jnp.logical_not(mine))
        def _(t=t):
            arrived(res_v.at[t], m_s.at[t])


def feed_forward(sizes, cols, att, tok_own, cot, w_out, w_up, w_down, vec, tile, chunk):
    blocks, lanes, seqs = sizes
    share = blocks // seqs
    per_part = blocks // share
    block, model = tok_own.shape[1:]
    rows = per_part * block
    wide = att.shape[2]
    ff = w_up.shape[1]
    chunks = ff // chunk
    in_vmem = pl.BlockSpec(memory_space=pltpu.VMEM)
    low, full = jnp.bfloat16, jnp.float32
    return pl.pallas_call(
        functools.partial(mlp_kernel, sizes, cols, tile, chunk),
        out_shape=[
            jax.ShapeDtypeStruct((seqs, block, model), low),
            jax.ShapeDtypeStruct((share, rows, wide), low),
            jax.ShapeDtypeStruct((rows, model), full),
            jax.ShapeDtypeStruct((model, model), low),
            jax.ShapeDtypeStruct((model, ff), low),
            jax.ShapeDtypeStruct((ff, model), low),
            jax.ShapeDtypeStruct((8, model), full),
        ],
        in_specs=[ANYWHERE] * 6 + [in_vmem],
        out_specs=[ANYWHERE] * 6 + [in_vmem],
        scratch_shapes=[
            pltpu.VMEM((share, rows, wide), low),
            pltpu.VMEM((per_part, block, model), low),
            pltpu.VMEM((per_part, block, model), low),
            pltpu.VMEM((per_part, block, model), low),
            pltpu.VMEM((model, model), low),
            pltpu.VMEM((model, ff), low),
            pltpu.VMEM((ff, model), low),
            pltpu.VMEM((rows, model), full),
            pltpu.VMEM((rows, model), low),
            pltpu.VMEM((model, rows), low),
            pltpu.VMEM((rows, ff), low),
            pltpu.VMEM((rows, ff), low),
            pltpu.VMEM((rows, model), full),
            pltpu.VMEM((share, rows, wide), low),
            pltpu.VMEM((model, model), low),
            pltpu.VMEM((2, model, chunk), low),
            pltpu.VMEM((2, chunk, model), low),
            DMA((share,)),
            DMA((share,)),
            DMA((per_part,)),
            DMA((seqs,)),
            DMA((3 + per_part,)),
            DMA((chunks,)),
            DMA((chunks,)),
            DMA((4,)),
        ],
        compiler_params=pltpu.CompilerParams(collective_id=4, has_side_effects=True, vmem_limit_bytes=VMEM_LIMIT),
    )(att, tok_own, cot, w_out, w_up, w_down, vec)


def last_kernel(sizes, block, pairs, *refs):
    place = Place(*sizes)
    blocks, depth, seqs, share, bits = place.blocks, place.depth, place.seqs, place.share, place.bits
    blk, z, core, part = place.blk, place.z, place.core, place.part
    per_part = place.per_part
    count = 3 + pairs
    q_ref, k_ref, v_ref, g_ref, att_ref, lse_ref = refs[:6]
    big, tok_own, g_mid, norm_t, cols, vec, two = refs[6:9], refs[9], refs[10], refs[11], refs[12], refs[13], refs[14]
    refs = refs[15:]
    sums, qkv_sum, tok_out, vec_out, refs = refs[:3], refs[3], refs[4], refs[5], refs[6:]
    kh, vh, qh, gh, kt, delta, dqt, dk, dv = refs[:9]
    gq_v, own_v, norm_v, cols_v, tok_v, mid_v, out_v, part_v, got_v, sum_v = refs[9:19]
    p_s, p_r, t_s, t_r, loc = refs[19:24]
    total = Total(place, *refs[24:28], refs[28:34])
    kinds = ["rows"] * 3 + ["columns"] * pairs
    fold = Fold(place, kinds, list(big) + [own_v.at[p] for p in range(pairs)], [], sums, [], refs[34:])
    pair = pl.program_id(0)
    length = q_ref.shape[0]
    rows, model = mid_v.shape
    owned = own_v.shape[4]
    steps = length // block
    per_pair = steps * (steps + 1) // 2
    flat = blk * 2 + core
    partners = [((flat ^ k) // 2, z, (flat ^ k) % 2) for k in range(1, share)]
    slot_of = lax.rem(place.seq, seqs)
    local = lambda src, dst, sem: pltpu.make_async_copy(src, dst, sem).start()

    tasks = []
    units = [(a, k) for a in range(3) for k in fold.order]
    per = 12.0 / len(units)
    for n, (a, k) in enumerate(units):
        tasks.append((8 + 1.2 * per * n, functools.partial(fold.join, a, k)))
        for t in range(bits):
            where = (14 + 2.7 * per * n) if t == 0 else (38 + 8 * t + 1.4 * per * n)
            tasks.append((where, functools.partial(fold.step, a, k, t)))
    for a in range(3):
        tasks.append((82 + a, functools.partial(fold.total, a)))
    for p in range(pairs - 1):
        third = 85.0 / pairs
        for n, k in enumerate(fold.order):
            tasks.append(((p + 1.1) * third, functools.partial(fold.join, 3 + p, k)))
            for t in range(bits):
                where = (79 if p == pairs - 2 else 70) + 4 * t
                tasks.append((where, functools.partial(fold.step, 3 + p, k, t)))
    tasks = [(where / 85.0, call) for where, call in tasks]
    tasks.sort(key=lambda task: task[0])
    todo = plan(tasks, pairs * per_pair)

    @pl.when(pair == 0)
    def _():
        fold.greet()
        fold.clear()
        for a, k in units:
            fold.start(a, k)
        local(norm_t, norm_v, loc.at[0])
        local(cols, cols_v, loc.at[1])
        local(g_mid, mid_v, loc.at[2])
        local(tok_own, tok_v, loc.at[3])

    split_heads(kh, k_ref[...])
    split_heads(vh, v_ref[...])
    split_heads(qh, q_ref[...])
    split_heads(gh, g_ref[...])
    kt[...] = k_ref[...].astype(jnp.float32).T.astype(jnp.bfloat16)
    prod = (g_ref[...].astype(jnp.float32) * att_ref[...].astype(jnp.float32)).T
    delta[0:1, :] = jnp.sum(prod[:64], axis=0, keepdims=True)
    delta[1:2, :] = jnp.sum(prod[64:], axis=0, keepdims=True)
    dqt[...] = jnp.zeros_like(dqt)

    def k_step(kj, _):
        at = pl.ds(pl.multiple_of(kj * block, block), block)

        def one(qi, masked):
            at_q = pl.ds(pl.multiple_of(qi * block, block), block)
            q_rows = q_ref[at_q, :]
            g_rows = g_ref[at_q, :]
            add_k = add_v = None
            both = [(dot_nt(kh[h, at, :], q_rows), dot_nt(vh[h, at, :], g_rows)) for h in range(2)]
            for h in range(2):
                s, dp = both[h]
                u = s * s + 1.0
                inv = lax.rsqrt(u)
                arg = u * inv - lse_ref[0, h : h + 1, at_q]
                if masked:
                    arg = jnp.where(causal(block, block, kj, qi), arg, -1e30)
                p = jnp.exp(arg)
                sgn = s * inv
                t = inv * inv * (inv - 1.0) + 1.0
                ds = (p * (dp * t - sgn * delta[h : h + 1, at_q])).astype(jnp.bfloat16)
                signed = (p * sgn).astype(jnp.bfloat16)
                one_v = dot_nn(signed, gh[h, at_q, :])
                one_k = dot_nn(ds, qh[h, at_q, :])
                add_v = one_v if h == 0 else add_v + one_v
                add_k = one_k if h == 0 else add_k + one_k
                dqt[64 * h : 64 * h + 64, at_q] += dot_nn(kt[64 * h : 64 * h + 64, at], ds)
            return add_k, add_v

        def more(qi, _):
            @pl.when(qi == kj)
            def _():
                dk[...], dv[...] = one(qi, True)

            @pl.when(qi != kj)
            def _():
                add_k, add_v = one(qi, False)
                dk[...] += add_k
                dv[...] += add_v

            pump(todo, pair * per_pair + kj * steps - kj * (kj - 1) // 2 + qi - kj)
            return 0

        lax.fori_loop(kj, steps, more, 0)
        gq_v[pair, at, 128:256] = dk[...].astype(jnp.bfloat16)
        gq_v[pair, at, 256:384] = dv[...].astype(jnp.bfloat16)
        return 0

    lax.fori_loop(0, steps, k_step, 0)
    gq_v[pair, :, 0:128] = (dqt[...] * 0.125).T.astype(jnp.bfloat16)

    @pl.when(pair == 0)
    def _():
        arrived(norm_v, loc.at[0])
        arrived(cols_v, loc.at[1])
        arrived(mid_v, loc.at[2])
        arrived(tok_v, loc.at[3])

    def weight_grad():
        sum_v[...] = dot_nn(norm_v[...], gq_v[pair])
        for b in range(blocks):
            for d in range(depth):
                for c in range(2):
                    first = ((b * depth + d) * 2 + c) * owned
                    own_v[pair, b, d, c] = sum_v[first : first + owned, :].astype(jnp.bfloat16)
        for p in range(pairs):

            @pl.when(pair == p)
            def _(p=p):
                for k in fold.order:
                    fold.start(3 + p, k)

    @pl.when(pair != pairs - 1)
    def _():
        weight_grad()

    @pl.when(pair == pairs - 1)
    def _():
        mine = 3 + pairs - 1
        tile = min(256, block, rows)

        def input_grad(g, i):
            at = pl.ds(pl.multiple_of(g * rows + i * tile, tile), tile)
            value = dot_nt(gq_v[0, at, :], cols_v[:, 0:384])
            for p in range(1, pairs):
                value = value + dot_nt(gq_v[p, at, :], cols_v[:, p * 384 : (p + 1) * 384])
            return value

        per_block = rows // per_part // tile
        half = rows // per_part
        for t in range(per_part):
            for k in range(1, share):

                def away(i, _, k=k):
                    at = pl.ds(pl.multiple_of(i * tile, tile), tile)
                    part_v[k - 1, at, :] = input_grad(part ^ k, i).astype(jnp.bfloat16)
                    return 0

                lax.fori_loop(t * per_block, (t + 1) * per_block, away, 0)
                piece = pl.ds(t * half, half)
                sems = p_s.at[k - 1, t], p_r.at[k - 1, t]
                send(part_v.at[k - 1, piece], got_v.at[k - 1, piece], *sems, place.at(*partners[k - 1]))
        weight_grad()
        total.stages[0] = jnp.zeros(total.stages.shape[1:], jnp.float32)
        total.stages[0, 2:4, :] = two[0:2, :]
        gain = vec[0:1, :]

        def leave(i, _):
            at = pl.ds(pl.multiple_of(i * tile, tile), tile)
            t = i // per_block
            inside = pl.ds(pl.multiple_of(lax.rem(i, per_block) * tile, tile), tile)
            value = input_grad(part, i)
            for k in range(1, share):
                value = value + got_v[k - 1, at, :].astype(jnp.float32)
            back, d_gain, d_shift = norm_back(tok_v[t, inside, :].astype(jnp.float32), value, gain)
            total.stages[0, 0:1, :] += d_gain
            total.stages[0, 1:2, :] += d_shift
            out_v[t, inside, :] = (mid_v[at, :] + back).astype(jnp.bfloat16)
            return 0

        for t in range(per_part):
            for k in range(1, share):
                arrived(got_v.at[k - 1, pl.ds(t * half, half)], p_r.at[k - 1, t])
            lax.fori_loop(t * per_block, (t + 1) * per_block, leave, 0)
            source = part * per_part + t
            here = (source == blk) & (place.home == core)

            @pl.when(here)
            def _(t=t):
                local(out_v.at[t], tok_out.at[slot_of], loc.at[0])

            @pl.when(jnp.logical_not(here))
            def _(t=t, source=source):
                send(out_v.at[t], tok_out.at[slot_of], t_s.at[t], t_r.at[slot_of], place.at(source, z, place.home))

            if t == 0:
                for k in fold.order:
                    fold.join(mine, k)
        total.start()
        for t in range(bits):
            for k in fold.order:
                fold.step(mine, k, t)
            total.step(t)
        total.step(bits)
        for p in range(pairs):
            value = fold.value(3 + p)
            for g in range(share):
                for n in range(3):
                    first = ((n * share + g) * pairs + p) * 128
                    qkv_sum[:, first : first + 128] = value[g, :, n * 128 : n * 128 + 128]
        vec_out[...] = total.finish()
        fold.finish()
        for k in range(1, share):
            for t in range(per_part):
                arrived(part_v.at[k - 1, pl.ds(t * half, half)], p_s.at[k - 1, t])
        for t in range(per_part):
            here = (part * per_part + t == blk) & (place.home == core)

            @pl.when(here)
            def _(t=t):
                arrived(out_v.at[t], loc.at[0])

            @pl.when(jnp.logical_not(here))
            def _(t=t):
                arrived(out_v.at[t], t_s.at[t])

        for i in range(seqs):
            owner = (core * seqs + i) * share + blk // per_part

            @pl.when(owner != flat)
            def _(i=i):
                arrived(tok_out.at[i], t_r.at[i])


def last_half(sizes, qkv, g_att, att, lse, big, tok_own, g_mid, norm_t, cols, vec, two, block):
    blocks, lanes, seqs = sizes
    depth, share = lanes // 2, blocks // seqs
    length, width = qkv.shape
    pairs = width // 384
    model = cols.shape[0]
    owned = model // (blocks * lanes)
    per_part, rows_in, _ = tok_own.shape
    rows = per_part * rows_in
    low, full = jnp.bfloat16, jnp.float32
    in_vmem = pl.BlockSpec(memory_space=pltpu.VMEM)
    own = jax.ShapeDtypeStruct((blocks, depth, 2, owned, 384), low)
    kinds = ["rows"] * 3 + ["columns"] * pairs
    out, _, scratch = fold_shapes(sizes, list(big) + [own] * pairs, kinds, [])
    return pl.pallas_call(
        functools.partial(last_kernel, sizes, block, pairs),
        grid=(pairs,),
        out_shape=out[:3]
        + [
            jax.ShapeDtypeStruct((owned, share * width), full),
            jax.ShapeDtypeStruct((seqs, rows_in, model), low),
            jax.ShapeDtypeStruct(vec.shape, full),
        ],
        in_specs=[pl.BlockSpec((length, 128), lambda p, n=n: (0, 3 * p + n)) for n in range(3)]
        + [pl.BlockSpec((length, 128), lambda p: (0, p))] * 2
        + [pl.BlockSpec((1, 8, length), lambda p: (p, 0, 0))]
        + [ANYWHERE] * 7
        + [in_vmem] * 2,
        out_specs=[in_vmem] * 4 + [ANYWHERE, in_vmem],
        scratch_shapes=[pltpu.VMEM((2, length, 128), low)] * 4
        + [
            pltpu.VMEM((128, length), low),
            pltpu.VMEM((8, length), full),
            pltpu.VMEM((128, length), full),
            pltpu.VMEM((block, 128), full),
            pltpu.VMEM((block, 128), full),
            pltpu.VMEM((pairs, length, 384), low),
            pltpu.VMEM((pairs,) + own.shape, low),
            pltpu.VMEM((model, length), low),
            pltpu.VMEM((model, width), low),
            pltpu.VMEM((per_part, rows_in, model), low),
            pltpu.VMEM((rows, model), full),
            pltpu.VMEM((per_part, rows_in, model), low),
            pltpu.VMEM((share - 1, rows, model), low),
            pltpu.VMEM((share - 1, rows, model), low),
            pltpu.VMEM((model, 384), full),
            DMA((share, per_part)),
            DMA((share, per_part)),
            DMA((per_part,)),
            DMA((seqs,)),
            DMA((4,)),
        ]
        + Total.scratch(sizes, vec.shape)
        + scratch,
        compiler_params=pltpu.CompilerParams(collective_id=2, has_side_effects=True, vmem_limit_bytes=63 * 2**20),
    )(qkv, qkv, qkv, g_att, att, lse, *big, tok_own, g_mid, norm_t, cols, vec, two)


def shards(sizes, tokens, seq_len, ln1_gain, ln1_shift, w_qkv, w_out, ln2_gain, ln2_shift, w_up, w_down, cotangent):
    blocks, lanes, seqs = sizes
    place = Place(*sizes)
    share, part = place.share, place.part
    model = tokens.shape[2]
    length = blocks * tokens.shape[1]
    rows = length // share
    owned = w_qkv.shape[0]
    cols = model // share
    wide = -(-cols // 128) * 128

    pairs = wide // 128
    grouped = jnp.pad(w_qkv.reshape(owned, 3, share, cols), ((0, 0), (0, 0), (0, 0), (0, wide - cols)))
    grouped = grouped.reshape(owned, 3, share, pairs, 128)
    grouped = jnp.transpose(grouped, (2, 0, 3, 1, 4)).reshape(share, owned, 3 * wide)
    flat = place.blk * lanes + lax.axis_index("seq")
    vec = jnp.zeros((8, model), jnp.float32)
    own = jnp.stack([ln1_gain, ln1_shift, ln2_gain, ln2_shift]).astype(jnp.float32)
    vec = lax.dynamic_update_slice(vec, own, (0, flat * owned))
    first = (place.blk == 0).astype(jnp.float32)
    vec = lax.dynamic_update_slice(vec, first * seq_len.astype(jnp.float32)[None], (4, lax.axis_index("seq") * seqs))
    outs = first_half(sizes, tokens, cotangent, vec, grouped, w_out, w_up, w_down, min(512, rows))
    att, lse, att_own, tok_own, cot_own, norm_t, qkv, qkv_cols, params, _, out_full, up_full, down_full = outs
    out_full, up_full = [a.reshape(model, -1) for a in (out_full, up_full)]
    down_full = down_full.reshape(-1, model)
    result, g_heads, grad_mid, grad_out, grad_up, grad_down, two_grads = feed_forward(
        sizes,
        cols,
        att_own,
        tok_own,
        cot_own,
        out_full,
        up_full,
        down_full,
        params,
        min(512, tokens.shape[1]),
        min(1024, w_up.shape[1]),
    )

    def cut(values):
        return values.reshape((blocks, lanes // 2, 2, -1) + values.shape[1:])

    done = last_half(
        sizes,
        qkv,
        g_heads.reshape(length, wide),
        att,
        lse,
        [cut(grad_out), cut(grad_up), cut(grad_down)],
        tok_own,
        grad_mid,
        norm_t,
        qkv_cols,
        params,
        two_grads,
        min(512, rows),
    )
    sum_out, sum_up, sum_down, sum_qkv, grad_tokens, vec_sum = done
    vec_own = lax.dynamic_slice_in_dim(vec_sum, flat * owned, owned, 1)
    if wide != cols:
        sum_qkv = sum_qkv.reshape(owned, 3, share, wide)[..., :cols].reshape(owned, 3 * model)
    return (
        result,
        grad_tokens.astype(jnp.float32),
        vec_own[0],
        vec_own[1],
        sum_qkv,
        sum_out,
        vec_own[2],
        vec_own[3],
        sum_up,
        sum_down,
    )


def solution(mesh):
    blocks, lanes = mesh.shape["blk"], mesh.shape["seq"]
    whole = P(("blk", "seq"))
    rows = P(("blk", "seq"), None)
    tokens = P("seq", "blk", None)

    def run(*args):
        seqs = args[0].shape[0] // lanes
        return jax.shard_map(
            functools.partial(shards, (blocks, lanes, seqs)),
            mesh=mesh,
            in_specs=(tokens, P("seq"), whole, whole, rows, rows, whole, whole, rows, rows, tokens),
            out_specs=(tokens, tokens, whole, whole, rows, rows, whole, whole, rows, rows),
            check_vma=False,
        )(*args)

    return run
```
